32 devices in a mesh: dp: 4 (over y, x), head: 8 (over z, core).
Axes of the slice: x: 2, y: 2, z: 4, core: 2. Of those that a mesh axis runs over, the one named last changes fastest.
Arguments:
- token_ids: int32 [8192], P('dp'), may hold values from 0 to 31999
- targets: int32 [8192], P('dp'), may hold values from 0 to 31999
- valid: int32 [8192], P('dp'), may hold values from 0 to 1, as said below
- resets: int32 [512], P('dp'), may hold values from 0 to 1, as said below
- owners: int32 [4, 4], replicated, may hold values from 0 to 3, each once within a row
- emb_master: float32 [32000, 2048], P('head', 'dp')
- emb_first: float32 [32000, 2048], P('head', 'dp'), may hold values from -7.6293945e-06 to 7.6293945e-06
- emb_second: float32 [32000, 2048], P('head', 'dp'), may hold values from 1.1180963e-12 to 4.5583927e-12
- qkv_master: float32 [4, 512, 3, 2048], P('dp', None, None, 'head'), may hold values from -0.125 to 0.125
- qkv_left: float32 [4, 8, 512, 512], P('dp', 'head'), as said below
- qkv_right: float32 [4, 8, 768, 768], P('dp', 'head')
- qkv_left_root: float32 [4, 8, 512, 512], P('dp', 'head')
- qkv_right_root: float32 [4, 8, 768, 768], P('dp', 'head')
- out_master: float32 [4, 2048, 512], P('dp', 'head'), may hold values from -0.125 to 0.125
- out_left: float32 [4, 8, 256, 256], P('dp', 'head')
- out_right: float32 [4, 8, 512, 512], P('dp', 'head')
- out_left_root: float32 [4, 8, 256, 256], P('dp', 'head')
- out_right_root: float32 [4, 8, 512, 512], P('dp', 'head')
- gu_master: float32 [4, 512, 2, 5504], P('dp', None, None, 'head'), may hold values from -0.125 to 0.125
- gu_left: float32 [4, 8, 512, 512], P('dp', 'head')
- gu_right: float32 [4, 8, 1376, 1376], P('dp', 'head')
- gu_left_root: float32 [4, 8, 512, 512], P('dp', 'head')
- gu_right_root: float32 [4, 8, 1376, 1376], P('dp', 'head')
- down_master: float32 [4, 5504, 512], P('dp', 'head'), may hold values from -0.078125 to 0.078125
- down_left: float32 [4, 8, 688, 688], P('dp', 'head')
- down_right: float32 [4, 8, 512, 512], P('dp', 'head')
- down_left_root: float32 [4, 8, 688, 688], P('dp', 'head')
- down_right_root: float32 [4, 8, 512, 512], P('dp', 'head')
- inner_init: float32 [32, 64, 64], P('head'), may hold values from -0.375 to 0.375
- inner_first: float32 [32, 64, 64], P('head'), may hold values from -1.5258789e-05 to 1.5258789e-05
- inner_second: float32 [32, 64, 64], P('head'), may hold values from 4.5583927e-12 to 1.8061556e-11
- gains: float32 [4, 2048], P(None, 'head')
- gains_first: float32 [4, 2048], P(None, 'head'), may hold values from -3.8146973e-05 to 3.8146973e-05
- gains_second: float32 [4, 2048], P(None, 'head'), may hold values from 2.8382444e-11 to 1.1180963e-10
Outputs:
- loss_pair: float32 [2], replicated
- grad_norm: float32 [], replicated
- emb_first_new: float32 [32000, 2048], P('head', 'dp')
- emb_second_new: float32 [32000, 2048], P('head', 'dp')
- emb_new: float32 [32000, 2048], P('head', 'dp')
- qkv_grad: float32 [4, 512, 3, 2048], P('dp', None, None, 'head')
- qkv_left_new: float32 [4, 8, 512, 512], P('dp', 'head')
- qkv_right_new: float32 [4, 8, 768, 768], P('dp', 'head')
- qkv_new: float32 [4, 512, 3, 2048], P('dp', None, None, 'head')
- out_grad: float32 [4, 2048, 512], P('dp', 'head')
- out_left_new: float32 [4, 8, 256, 256], P('dp', 'head')
- out_right_new: float32 [4, 8, 512, 512], P('dp', 'head')
- out_new: float32 [4, 2048, 512], P('dp', 'head')
- gu_grad: float32 [4, 512, 2, 5504], P('dp', None, None, 'head')
- gu_left_new: float32 [4, 8, 512, 512], P('dp', 'head')
- gu_right_new: float32 [4, 8, 1376, 1376], P('dp', 'head')
- gu_new: float32 [4, 512, 2, 5504], P('dp', None, None, 'head')
- down_grad: float32 [4, 5504, 512], P('dp', 'head')
- down_left_new: float32 [4, 8, 688, 688], P('dp', 'head')
- down_right_new: float32 [4, 8, 512, 512], P('dp', 'head')
- down_new: float32 [4, 5504, 512], P('dp', 'head')
- inner_first_new: float32 [32, 64, 64], P('head')
- inner_second_new: float32 [32, 64, 64], P('head')
- inner_new: float32 [32, 64, 64], P('head')
- gains_first_new: float32 [4, 2048], P(None, 'head')
- gains_second_new: float32 [4, 2048], P(None, 'head')
- gains_new: float32 [4, 2048], P(None, 'head')
The draws below stay inside these ranges and needn't reach their ends.
Inputs may be any that keep to these rules, and one draw needn't show every extreme that they name: `valid`: within each sequence the counted positions are a prefix of one or more positions. `resets`: the first mini-batch of every sequence is 1. `owners`: each row is a permutation of the dp indices. `qkv_left`: Symmetric.
All inputs are finite; a program needn't handle non-finite values.
Results may differ from the reference program's by a relative error of at most 0.0085.
The reference program's roundings to bfloat16 on the way count: a program that leaves them out, or rounds other values in their place, can miss the bound.
Values may be sent and summed in bfloat16 or wider, within the bound.
A program may use at most 448 MiB of HBM per device.

```python
import math
import jax
import jax.numpy as jnp
import numpy as np
from jax import lax

D = 2048
H = 32
P_SIZE = 64
FF = 5504
V = 32000
MB = 16
SEQ = 2048
STEP = 10
NSEQ = 4
TOKENS = 8192
CS = 256
QC = 768
FS = 688
GC = 1376
RW = 512
PALL = 116269056
N_DP = 4
N_HEAD = 8


def dominant_matrix(key, shape, level, spread):
    size = shape[-1]
    first, second = jax.random.split(key)
    diagonal = level * jnp.exp(jax.random.uniform(first, shape[:-1], jnp.float32, 0.0, math.log(4.0)))
    noise = jax.random.normal(second, shape, jnp.float32)
    mirrored = (noise + jnp.swapaxes(noise, -1, -2)) * (spread * level / math.sqrt(2.0 * size))
    return mirrored + diagonal[..., None] * jnp.eye(size, dtype=jnp.float32)


def stat_level(count):
    return count * 0.0025 / PALL


def root_level(count):
    return (count * 0.0025 / PALL) ** (-0.25)


def draw_valid(key, part):
    key = jax.random.fold_in(key, 1)
    places = jnp.arange(SEQ, dtype=jnp.int32)
    ranks = jnp.arange(NSEQ, dtype=jnp.int32)
    upper = SEQ // 3 + (SEQ - SEQ // 3) * ranks // max(NSEQ - 1, 1)
    shorter = jax.random.randint(key, (NSEQ,), 0, SEQ // 8 + 1)
    length = jnp.maximum(upper - shorter, 1)
    return (places[None, :] < length[:, None]).astype(jnp.int32).reshape(-1)


def draw_resets(key, part):
    key = jax.random.fold_in(key, 2)
    count = SEQ // MB
    rolled = jax.random.randint(key, (NSEQ, count), 0, 6) == 0
    firsts = jnp.arange(count, dtype=jnp.int32)[None, :] == 0
    return (rolled | firsts).astype(jnp.int32).reshape(-1)


def draw_emb_master(key, part):
    key = jax.random.fold_in(key, 3)
    places = jnp.arange(V, dtype=jnp.float32)[:, None] / (V - 1)
    values = jax.random.normal(key, (V, D), jnp.float32) * (1.0 + 2.0 * places)
    return values / math.sqrt(D)


def draw_gains(key, part):
    key = jax.random.fold_in(key, 4)
    first, second = jax.random.split(key)
    places = jnp.arange(D, dtype=jnp.float32) / D
    ramp = 0.5 + places
    norm_rows = ramp[None, :] * jax.random.uniform(first, (3, D), jnp.float32, 0.8, 1.2)
    rate_row = jax.random.uniform(second, (1, D), jnp.float32, -2.0, 2.0)
    return jnp.concatenate([norm_rows, rate_row], 0)


def draw_qkv_left(key, part):
    key = jax.random.fold_in(key, 11)
    return dominant_matrix(key, (N_DP, N_HEAD, RW, RW), stat_level(QC), 0.6)


def draw_qkv_right(key, part):
    key = jax.random.fold_in(key, 12)
    return dominant_matrix(key, (N_DP, N_HEAD, QC, QC), stat_level(RW), 0.6)


def draw_qkv_left_root(key, part):
    key = jax.random.fold_in(key, 13)
    return dominant_matrix(key, (N_DP, N_HEAD, RW, RW), root_level(QC), 0.6)


def draw_qkv_right_root(key, part):
    key = jax.random.fold_in(key, 14)
    return dominant_matrix(key, (N_DP, N_HEAD, QC, QC), root_level(RW), 0.6)


def draw_out_left(key, part):
    key = jax.random.fold_in(key, 21)
    return dominant_matrix(key, (N_DP, N_HEAD, CS, CS), stat_level(RW), 0.6)


def draw_out_right(key, part):
    key = jax.random.fold_in(key, 22)
    return dominant_matrix(key, (N_DP, N_HEAD, RW, RW), stat_level(CS), 0.6)


def draw_out_left_root(key, part):
    key = jax.random.fold_in(key, 23)
    return dominant_matrix(key, (N_DP, N_HEAD, CS, CS), root_level(RW), 0.6)


def draw_out_right_root(key, part):
    key = jax.random.fold_in(key, 24)
    return dominant_matrix(key, (N_DP, N_HEAD, RW, RW), root_level(CS), 0.6)


def draw_gu_left(key, part):
    key = jax.random.fold_in(key, 31)
    return dominant_matrix(key, (N_DP, N_HEAD, RW, RW), stat_level(GC), 0.6)


def draw_gu_right(key, part):
    key = jax.random.fold_in(key, 32)
    return dominant_matrix(key, (N_DP, N_HEAD, GC, GC), stat_level(RW), 0.6)


def draw_gu_left_root(key, part):
    key = jax.random.fold_in(key, 33)
    return dominant_matrix(key, (N_DP, N_HEAD, RW, RW), root_level(GC), 0.6)


def draw_gu_right_root(key, part):
    key = jax.random.fold_in(key, 34)
    return dominant_matrix(key, (N_DP, N_HEAD, GC, GC), root_level(RW), 0.6)


def draw_down_left(key, part):
    key = jax.random.fold_in(key, 41)
    return dominant_matrix(key, (N_DP, N_HEAD, FS, FS), stat_level(RW), 0.6)


def draw_down_right(key, part):
    key = jax.random.fold_in(key, 42)
    return dominant_matrix(key, (N_DP, N_HEAD, RW, RW), stat_level(FS), 0.6)


def draw_down_left_root(key, part):
    key = jax.random.fold_in(key, 43)
    return dominant_matrix(key, (N_DP, N_HEAD, FS, FS), root_level(RW), 0.6)


def draw_down_right_root(key, part):
    key = jax.random.fold_in(key, 44)
    return dominant_matrix(key, (N_DP, N_HEAD, RW, RW), root_level(FS), 0.6)


def set_ends(entries, stream_key, low, largest):
    extent = entries.shape
    spot = [jax.random.randint(jax.random.fold_in(stream_key, axis), (), 0, extent[axis]) for axis in range(len(extent))]
    entries = entries.at[tuple(spot)].set(low)
    longest = extent.index(max(extent))
    spot[longest] = (spot[longest] + 1) % extent[longest]
    return entries.at[tuple(spot)].set(largest)


def steps_of(own_key, shape, shards, least, largest):
    loudness = 1.0
    for dim, parts in shards:
        steps = jax.random.uniform(jax.random.fold_in(jax.random.fold_in(own_key, 6), dim), (parts,), jnp.float32, least / len(shards), largest / len(shards))
        loudness = loudness * jnp.repeat(jnp.exp(steps), shape[dim] // parts).reshape((-1,) + (1,) * (len(shape) - 1 - dim))
    return loudness


def rank_bounds(amount, slope):
    portions = [(1 << 20) // math.isqrt(rank ** slope) + 1 for rank in range(1, amount + 1)]
    scale = 1 + sum(portions) // (1 << 30)
    return np.cumsum(np.array([max(1, weight // scale) for weight in portions]))


def ranked_ids(rng, extent, count, slope):
    grid = rank_bounds(count, slope)
    lot = jax.random.randint(jax.random.fold_in(rng, 1), extent, 0, int(grid[count - 1]))
    standing = jnp.searchsorted(jnp.asarray(grid, jnp.int32), lot, side="right")
    return jax.random.permutation(jax.random.fold_in(rng, 2), count)[standing].astype(jnp.int32)


def bell_draw(stream_key, shape, width, most, cuts=(), kind=jnp.bfloat16):
    drawn = jax.random.normal(stream_key, shape, jnp.float32) * width
    if len(cuts) > 0:
        drawn = steps_of(stream_key, shape, cuts, -0.22, 0.18) * drawn
    return jnp.clip(drawn, min=-most, max=most).astype(kind)


def setup_inputs(seed: int = 0) -> dict:
    streams_of = jax.random.split(jax.random.key(seed), 35)
    token_ids = set_ends(ranked_ids(streams_of[0], (TOKENS,), V, 2), jax.random.fold_in(streams_of[0], 3), 0, V - 1).astype(jnp.int32)
    targets = set_ends(ranked_ids(streams_of[1], (TOKENS,), V, 2), jax.random.fold_in(streams_of[1], 3), 0, V - 1).astype(jnp.int32)
    valid = draw_valid(jax.random.fold_in(streams_of[34], 71), 0)
    resets = draw_resets(jax.random.fold_in(streams_of[34], 71), 0)
    owners = jax.vmap(lambda own: jax.random.permutation(own, N_DP))(jax.random.split(streams_of[4], 4)).reshape((4, N_DP)).astype(jnp.int32)
    emb_master = draw_emb_master(jax.random.fold_in(streams_of[34], 71), 0)
    emb_first = bell_draw(streams_of[6], (V, D), (0.0056 / PALL ** 0.5), 7.62939453125e-06, ((0, 8), (1, 4)), jnp.float32)
    emb_second = jnp.clip(jnp.exp(math.log(4.558392725784177e-12) - 1.4053426 * jax.random.uniform(streams_of[7], (V, D), jnp.float32) ** steps_of(streams_of[7], (V, D), ((0, 8), (1, 4)), -0.2, 0.2)), 1.1180962839613118e-12, 4.558392725784177e-12)
    qkv_master = bell_draw(streams_of[8], (N_DP, RW, 3, D), D ** -0.5, 0.125, ((0, 4), (3, 8)), jnp.float32)
    qkv_left = draw_qkv_left(jax.random.fold_in(streams_of[34], 71), 0)
    qkv_right = draw_qkv_right(jax.random.fold_in(streams_of[34], 71), 0)
    qkv_left_root = draw_qkv_left_root(jax.random.fold_in(streams_of[34], 71), 0)
    qkv_right_root = draw_qkv_right_root(jax.random.fold_in(streams_of[34], 71), 0)
    out_master = bell_draw(streams_of[13], (N_DP, D, RW), D ** -0.5, 0.125, ((0, 4), (1, 8)), jnp.float32)
    out_left = draw_out_left(jax.random.fold_in(streams_of[34], 71), 0)
    out_right = draw_out_right(jax.random.fold_in(streams_of[34], 71), 0)
    out_left_root = draw_out_left_root(jax.random.fold_in(streams_of[34], 71), 0)
    out_right_root = draw_out_right_root(jax.random.fold_in(streams_of[34], 71), 0)
    gu_master = bell_draw(streams_of[18], (N_DP, RW, 2, FF), D ** -0.5, 0.125, ((0, 4), (3, 8)), jnp.float32)
    gu_left = draw_gu_left(jax.random.fold_in(streams_of[34], 71), 0)
    gu_right = draw_gu_right(jax.random.fold_in(streams_of[34], 71), 0)
    gu_left_root = draw_gu_left_root(jax.random.fold_in(streams_of[34], 71), 0)
    gu_right_root = draw_gu_right_root(jax.random.fold_in(streams_of[34], 71), 0)
    down_master = bell_draw(streams_of[23], (N_DP, FF, RW), FF ** -0.5, 0.078125, ((0, 4), (1, 8)), jnp.float32)
    down_left = draw_down_left(jax.random.fold_in(streams_of[34], 71), 0)
    down_right = draw_down_right(jax.random.fold_in(streams_of[34], 71), 0)
    down_left_root = draw_down_left_root(jax.random.fold_in(streams_of[34], 71), 0)
    down_right_root = draw_down_right_root(jax.random.fold_in(streams_of[34], 71), 0)
    inner_init = bell_draw(streams_of[28], (H, P_SIZE, P_SIZE), (4 * P_SIZE) ** -0.5, 0.375, ((0, 8),), jnp.float32)
    inner_first = bell_draw(streams_of[29], (H, P_SIZE, P_SIZE), (0.011 / PALL ** 0.5), 1.52587890625e-05, ((0, 8),), jnp.float32)
    inner_second = jnp.clip(jnp.exp(math.log(1.806155572325885e-11) - 1.3768156 * jax.random.uniform(streams_of[30], (H, P_SIZE, P_SIZE), jnp.float32) ** steps_of(streams_of[30], (H, P_SIZE, P_SIZE), ((0, 8),), -0.2, 0.2)), 4.558392725784177e-12, 1.806155572325885e-11)
    gains = draw_gains(jax.random.fold_in(streams_of[34], 71), 0)
    gains_first = bell_draw(streams_of[32], (4, D), (0.028 / PALL ** 0.5), 3.814697265625e-05, ((1, 8),), jnp.float32)
    gains_second = jnp.clip(jnp.exp(math.log(1.1180963099821639e-10) - 1.3710269 * jax.random.uniform(streams_of[33], (4, D), jnp.float32) ** steps_of(streams_of[33], (4, D), ((1, 8),), -0.2, 0.2)), 2.8382443964525272e-11, 1.1180963099821639e-10)
    return dict(token_ids=token_ids, targets=targets, valid=valid, resets=resets, owners=owners, emb_master=emb_master, emb_first=emb_first, emb_second=emb_second, qkv_master=qkv_master, qkv_left=qkv_left, qkv_right=qkv_right, qkv_left_root=qkv_left_root, qkv_right_root=qkv_right_root, out_master=out_master, out_left=out_left, out_right=out_right, out_left_root=out_left_root, out_right_root=out_right_root, gu_master=gu_master, gu_left=gu_left, gu_right=gu_right, gu_left_root=gu_left_root, gu_right_root=gu_right_root, down_master=down_master, down_left=down_left, down_right=down_right, down_left_root=down_left_root, down_right_root=down_right_root, inner_init=inner_init, inner_first=inner_first, inner_second=inner_second, gains=gains, gains_first=gains_first, gains_second=gains_second)


EPSILON = 1e-05
CLIP_LIMIT = 0.05
STAT_DECAY = 0.5
MATRIX_RATE = 0.4
TABLE_RATE = 0.3
INITIAL_RATE = 0.05
GAINS_RATE = 0.3
BETA_ONE = 0.9
BETA_TWO = 0.95
ADAM_EPSILON = 1e-08
WEIGHT_DECAY = 0.01
PRECISE = lax.Precision.HIGHEST

@jax.custom_vjp
def low(v):
    return lax.optimization_barrier(v.astype(jnp.bfloat16)).astype(jnp.float32)

@jax.custom_vjp
def low_back(v):
    return v

def low_keep(v):
    return (low(v), None)

def low_pass(kept, grad):
    return (grad,)

def back_keep(v):
    return (v, None)

def back_low(kept, grad):
    return (low(grad),)
low.defvjp(low_keep, low_pass)
low_back.defvjp(back_keep, back_low)

def product(left_side, right_side):
    return jnp.dot(left_side, right_side, precision=PRECISE, preferred_element_type=jnp.float32)

def rms_norm(inputs, gain_row):
    return inputs * lax.rsqrt(lax.optimization_barrier(jnp.mean(inputs * inputs, -1, keepdims=True)) + EPSILON) * gain_row

def mixer(query, key_rows, value_rows, initial, step_rate, markers):
    block_count = query.shape[0] // MB
    head_count = initial.shape[0]
    shaped = [piece.reshape(block_count, MB, head_count, P_SIZE) for piece in (query, key_rows, value_rows)]
    causal = jnp.tril(jnp.ones((MB, MB), jnp.float32))

    def advance(carried, block):
        query_block, key_block, value_block, marker = block
        carried = jnp.where(marker > 0, initial, carried)
        residue = jnp.einsum('thp,hpc->thc', key_block, carried, precision=PRECISE) - (value_block - key_block)
        scaled = residue * step_rate
        scores = jnp.einsum('thp,shp->hts', query_block, key_block, precision=PRECISE) * causal
        output = jnp.einsum('thp,hpc->thc', query_block, carried, precision=PRECISE)
        output = output - jnp.einsum('hts,shc->thc', scores, scaled, precision=PRECISE)
        renewed = carried - jnp.einsum('thp,thc->hpc', key_block, scaled, precision=PRECISE)
        return (renewed, output)
    _, outputs = lax.scan(jax.checkpoint(advance), jnp.zeros_like(initial), (shaped[0], shaped[1], shaped[2], markers))
    return outputs.reshape(query.shape)

def sequence_loss(params, sequence):
    table, w_qkv, w_out, w_gu, w_down, initial, gains = params
    token_row, target_row, valid_row, marker_row = sequence
    table_low = low(table)
    embedded = low_back(table_low[token_row])
    normed_one = low(rms_norm(embedded, gains[0]))
    mixed = low(low_back(product(normed_one, low(w_qkv).reshape(D, 3 * D)))).reshape(SEQ, 3, H, P_SIZE)
    step_rate = jax.nn.sigmoid(gains[3]).reshape(H, P_SIZE) / (8 * P_SIZE)
    inner_out = low(mixer(mixed[:, 0], mixed[:, 1], mixed[:, 2], initial, step_rate, marker_row)).reshape(SEQ, D)
    hidden_one = embedded + low_back(product(inner_out, low(w_out)))
    normed_two = low(rms_norm(hidden_one, gains[1]))
    gate_up = low_back(product(normed_two, low(w_gu).reshape(D, 2 * FF))).reshape(SEQ, 2, FF)
    activated = low(jax.nn.silu(gate_up[:, 0]) * gate_up[:, 1])
    hidden_two = hidden_one + low_back(product(activated, low(w_down)))
    normed_end = low(rms_norm(hidden_two, gains[2]))
    logits = low_back(product(normed_end, table_low.T))
    totals = jax.nn.logsumexp(logits, -1)
    picked = jnp.take_along_axis(logits, target_row[:, None], 1)[:, 0]
    return jnp.sum((totals - picked) * valid_row.astype(jnp.float32))

def row_tiles(matrix):
    split = matrix.reshape(N_DP, RW, matrix.shape[2], N_HEAD, -1)
    return jnp.transpose(split, (0, 3, 1, 2, 4)).reshape(N_DP, N_HEAD, RW, -1)

def row_untile(tiles, kinds):
    split = tiles.reshape(N_DP, N_HEAD, RW, kinds, -1)
    return jnp.transpose(split, (0, 2, 3, 1, 4)).reshape(N_DP, RW, kinds, -1)

def shampoo(tile_w, tile_g, left, right, left_root, right_root):
    new_left = STAT_DECAY * left + (1.0 - STAT_DECAY) * jnp.einsum('abrc,absc->abrs', tile_g, tile_g, precision=PRECISE)
    new_right = STAT_DECAY * right + (1.0 - STAT_DECAY) * jnp.einsum('abrc,abrd->abcd', tile_g, tile_g, precision=PRECISE)
    turned = jnp.einsum('abrs,absc->abrc', left_root, tile_g, precision=PRECISE)
    turned = jnp.einsum('abrc,abcd->abrd', turned, right_root, precision=PRECISE)
    return (new_left, new_right, tile_w - MATRIX_RATE * (turned + WEIGHT_DECAY * tile_w))

def adamw(weight, grad, first, second, step_rate):
    new_first = BETA_ONE * first + (1.0 - BETA_ONE) * grad
    new_second = BETA_TWO * second + (1.0 - BETA_TWO) * grad * grad
    moved = new_first / (1.0 - BETA_ONE ** STEP) / (jnp.sqrt(new_second / (1.0 - BETA_TWO ** STEP)) + ADAM_EPSILON)
    return (new_first, new_second, weight - step_rate * (moved + WEIGHT_DECAY * weight))

def reference(token_ids, targets, valid, resets, owners, emb_master, emb_first, emb_second, qkv_master, qkv_left, qkv_right, qkv_left_root, qkv_right_root, out_master, out_left, out_right, out_left_root, out_right_root, gu_master, gu_left, gu_right, gu_left_root, gu_right_root, down_master, down_left, down_right, down_left_root, down_right_root, inner_init, inner_first, inner_second, gains, gains_first, gains_second):
    order = jnp.argsort(owners, axis=1).astype(jnp.int32)
    w_qkv = qkv_master[owners[0]].reshape(D, 3, D)
    w_out = jnp.swapaxes(out_master[owners[1]], 0, 1).reshape(D, D)
    w_gu = gu_master[owners[2]].reshape(D, 2, FF)
    w_down = jnp.swapaxes(down_master[owners[3]], 0, 1).reshape(FF, D)
    params = (emb_master, w_qkv, w_out, w_gu, w_down, inner_init, gains)
    sequences = (token_ids.reshape(NSEQ, SEQ), targets.reshape(NSEQ, SEQ), valid.reshape(NSEQ, SEQ), resets.reshape(NSEQ, SEQ // MB))

    def accumulate(carried, sequence):
        loss_value, pull = jax.vjp(lambda chosen: sequence_loss(chosen, sequence), params)
        grads = pull(jnp.ones((), jnp.float32))[0]
        return ((carried[0] + loss_value, jax.tree.map(jnp.add, carried[1], grads)), None)
    start = (jnp.zeros((), jnp.float32), jax.tree.map(jnp.zeros_like, params))
    (loss_sum, grads), _ = lax.scan(accumulate, start, sequences)
    count = jnp.sum(valid.astype(jnp.float32))
    g_table, g_qkv, g_out, g_gu, g_down, g_init, g_gains = grads
    slot_qkv = g_qkv.reshape(N_DP, RW, 3, D)[order[0]]
    slot_out = jnp.swapaxes(g_out.reshape(D, N_DP, RW), 0, 1)[order[1]]
    slot_gu = g_gu.reshape(N_DP, RW, 2, FF)[order[2]]
    slot_down = jnp.swapaxes(g_down.reshape(FF, N_DP, RW), 0, 1)[order[3]]
    pieces = (g_table, slot_qkv, slot_out, slot_gu, slot_down, g_init, g_gains)
    squares = sum((jnp.sum(piece * piece) for piece in pieces))
    grad_norm = jnp.sqrt(squares) / count
    factor = jnp.minimum(1.0, CLIP_LIMIT / grad_norm) / count
    c_table, c_qkv, c_out, c_gu, c_down, c_init, c_gains = [piece * factor for piece in pieces]
    qkv_l, qkv_r, qkv_w = shampoo(row_tiles(qkv_master), row_tiles(c_qkv), qkv_left, qkv_right, qkv_left_root, qkv_right_root)
    out_l, out_r, out_w = shampoo(out_master.reshape(N_DP, N_HEAD, CS, RW), c_out.reshape(N_DP, N_HEAD, CS, RW), out_left, out_right, out_left_root, out_right_root)
    gu_l, gu_r, gu_w = shampoo(row_tiles(gu_master), row_tiles(c_gu), gu_left, gu_right, gu_left_root, gu_right_root)
    down_l, down_r, down_w = shampoo(down_master.reshape(N_DP, N_HEAD, FS, RW), c_down.reshape(N_DP, N_HEAD, FS, RW), down_left, down_right, down_left_root, down_right_root)
    table_m, table_v, table_w = adamw(emb_master, c_table, emb_first, emb_second, TABLE_RATE)
    init_m, init_v, init_w = adamw(inner_init, c_init, inner_first, inner_second, INITIAL_RATE)
    gain_m, gain_v, gain_w = adamw(gains, c_gains, gains_first, gains_second, GAINS_RATE)
    return (jnp.stack([loss_sum, count]), grad_norm, table_m, table_v, table_w, c_qkv, qkv_l, qkv_r, row_untile(qkv_w, 3), c_out, out_l, out_r, out_w.reshape(N_DP, D, RW), c_gu, gu_l, gu_r, row_untile(gu_w, 2), c_down, down_l, down_r, down_w.reshape(N_DP, FF, RW), init_m, init_v, init_w, gain_m, gain_v, gain_w)
```

```python
import jax
import jax.numpy as jnp
from jax import lax
from jax.experimental import pallas as pl
from jax.experimental.pallas import tpu as pltpu
from jax.sharding import PartitionSpec as P

D = 2048
P_SIZE = 64
MB = 16
STEP = 10


EPSILON = 1e-05
CLIP_LIMIT = 0.05
STAT_DECAY = 0.5
MATRIX_RATE = 0.4
TABLE_RATE = 0.3
INITIAL_RATE = 0.05
GAINS_RATE = 0.3
BETA_ONE = 0.9
BETA_TWO = 0.95
ADAM_EPSILON = 1e-08
WEIGHT_DECAY = 0.01


def head_total(values):
    return lax.psum(values, "head")


def spread(rows):
    return lax.all_gather(rows, "head", axis=1, tiled=True)


def spread_grad(rows):
    return lax.all_gather(rows, "head", axis=1, tiled=True)


def fold(partial_value):
    low = partial_value.astype(jnp.bfloat16)
    return lax.psum_scatter(low, "head", scatter_dimension=1, tiled=True).astype(jnp.float32)


def norm_forward(inputs, gain_row):
    scale = lax.rsqrt(head_total(jnp.sum(inputs * inputs, -1)) / D + EPSILON)
    return ((inputs * scale[:, None] * gain_row).astype(jnp.bfloat16), scale)


def norm_backward(inputs, scale, gain_row, upstream):
    normed = inputs * scale[:, None]
    weighted = upstream * gain_row
    inner = head_total(jnp.sum(weighted * normed, -1)) / D
    return (scale[:, None] * (weighted - normed * inner[:, None]), jnp.sum(upstream * normed, 0))


CHUNK = 64
PAIR = 2 * P_SIZE


def dot_ab(left, right):
    return lax.dot_general(left, right, (((1,), (0,)), ((), ())), preferred_element_type=jnp.float32)


def dot_abt(left, right):
    return lax.dot_general(left, right, (((1,), (1,)), ((), ())), preferred_element_type=jnp.float32)


def dot_atb(left, right):
    return lax.dot_general(left, right, (((0,), (0,)), ((), ())), preferred_element_type=jnp.float32)


def halves_of(value):
    high = value.astype(jnp.bfloat16)
    return (high, (value - high.astype(jnp.float32)).astype(jnp.bfloat16))


def wide(form, left, right):
    lefts = left if isinstance(left, tuple) else (left,)
    rights = right if isinstance(right, tuple) else (right,)
    total = form(lefts[0], rights[0])
    if len(rights) > 1:
        total = total + form(lefts[0], rights[1])
    if len(lefts) > 1:
        total = total + form(lefts[1], rights[0])
    return total


def each(pieces, change):
    return tuple(change(piece) for piece in pieces) if isinstance(pieces, tuple) else change(pieces)


def mixer_masks(resets, tokens):
    per_chunk = CHUNK // MB
    chunks = tokens // CHUNK
    segment = jnp.cumsum(resets.reshape(chunks, per_chunk), axis=1)
    segment = jnp.repeat(segment, MB, axis=1)
    same = segment[:, :, None] == segment[:, None, :]
    spot = jnp.arange(CHUNK, dtype=jnp.int32)
    causal = (spot[None, :] <= spot[:, None])[None]
    earlier = ((spot[None, :] // MB) < (spot[:, None] // MB))[None]
    causal = (same & causal).astype(jnp.float32)
    earlier = (same & earlier).astype(jnp.float32)
    first = (segment == 0).astype(jnp.float32).reshape(tokens, 1)
    last = (segment == segment[:, -1:]).astype(jnp.float32).reshape(tokens, 1)
    anew = (segment[:, -1] > 0).astype(jnp.float32)
    first = jnp.broadcast_to(first, (tokens, PAIR))
    last = jnp.broadcast_to(last, (tokens, PAIR))
    anew = jnp.broadcast_to(anew[:, None, None], (chunks, 8, PAIR))
    return causal, earlier, first, last, anew


def lane_helpers(rows):
    lanes = lax.broadcasted_iota(jnp.int32, (rows, PAIR), 1)
    low_lane = lanes < P_SIZE
    low_half = low_lane.astype(jnp.float32)
    high_half = 1.0 - low_half

    def stack(pieces):
        def one(piece):
            kind = piece.dtype
            return jnp.concatenate(
                [piece * low_half.astype(kind), piece * high_half.astype(kind)], 0
            )

        return each(pieces, one)

    def pick(product):
        return jnp.where(low_lane, product[:rows], product[rows:])

    return stack, pick


def diagonal_blocks():
    rows = lax.broadcasted_iota(jnp.int32, (PAIR, PAIR), 0) // P_SIZE
    columns = lax.broadcasted_iota(jnp.int32, (PAIR, PAIR), 1) // P_SIZE
    return (rows == columns).astype(jnp.float32)


def solve(matrix, rate_row, value, pick):
    rows = value.shape[0]
    powers = [(matrix, rate_row)]
    reach = 2
    while reach < CHUNK // MB:
        last, rate = powers[-1]
        low, high = halves_of(last[:rows]), halves_of(last[rows:])
        powers.append(
            (
                jnp.concatenate([wide(dot_ab, low, low), wide(dot_ab, high, high)], 0),
                rate * rate,
            )
        )
        reach = 2 * reach
    for index in range(len(powers) - 1, -1, -1):
        factor, rate = powers[index]
        moved = pick(wide(dot_ab, halves_of(factor), halves_of(value * rate)))
        value = value - moved if index == 0 else value + moved
    return value


def mixer_forward_kernel(
    qkv_ref,
    rate_ref,
    initial_ref,
    causal_ref,
    earlier_ref,
    first_ref,
    last_ref,
    anew_ref,
    z_ref,
    residue_ref,
    states_ref,
    state,
):
    pairs = initial_ref.shape[0]
    width = pairs * PAIR

    @pl.when(pl.program_id(0) == 0)
    def _():
        state[...] = jnp.zeros_like(state)

    stack, pick = lane_helpers(CHUNK)
    blocks = diagonal_blocks()
    causal = causal_ref[0]
    causal = jnp.concatenate([causal, causal], 0)
    earlier = earlier_ref[0]
    earlier = jnp.concatenate([earlier, earlier], 0)
    first = first_ref[...] > 0.0
    last = last_ref[...]
    anew = anew_ref[0, 0:1, :]
    for pair in range(pairs):
        lanes = slice(pair * PAIR, (pair + 1) * PAIR)
        query = qkv_ref[:, lanes]
        key = qkv_ref[:, width + pair * PAIR : width + (pair + 1) * PAIR]
        value = qkv_ref[:, 2 * width + pair * PAIR : 2 * width + (pair + 1) * PAIR]
        rate = rate_ref[0:1, lanes]
        begin = state[pair]
        initial = initial_ref[pair]
        states_ref[0, pair] = begin
        products = dot_abt(jnp.concatenate([stack(key), stack(query)], 0), key)
        ties = products[: 2 * CHUNK] * earlier
        scores = products[2 * CHUNK :] * causal
        both = jnp.concatenate([key, query], 0)
        seen = wide(dot_ab, both, halves_of(begin))
        fresh = wide(dot_ab, both, halves_of(initial))
        key_seen = jnp.where(first, seen[:CHUNK], fresh[:CHUNK])
        query_seen = jnp.where(first, seen[CHUNK:], fresh[CHUNK:])
        key_wide = key.astype(jnp.float32)
        residue = solve(ties, rate, key_seen - (value.astype(jnp.float32) - key_wide), pick)
        residue_ref[:, lanes] = residue
        scaled = residue * rate
        scaled_parts = halves_of(scaled)
        output = query_seen - pick(wide(dot_ab, halves_of(scores), scaled_parts))
        z_ref[:, lanes] = output.astype(jnp.bfloat16)
        key_last = (key_wide * last).astype(jnp.bfloat16)
        base = jnp.where(anew > 0.0, initial, begin)
        state[pair] = base - blocks * wide(dot_atb, key_last, scaled_parts)


def mixer_backward_kernel(
    qkv_ref,
    rate_ref,
    initial_ref,
    causal_ref,
    earlier_ref,
    causal_turned_ref,
    earlier_turned_ref,
    first_ref,
    last_ref,
    anew_ref,
    residue_ref,
    states_ref,
    upstream_ref,
    grad_ref,
    grad_initial_ref,
    grad_rate_ref,
    carried,
):
    pairs = initial_ref.shape[0]
    width = pairs * PAIR

    @pl.when(pl.program_id(0) == 0)
    def _():
        carried[...] = jnp.zeros_like(carried)
        grad_initial_ref[...] = jnp.zeros_like(grad_initial_ref)
        grad_rate_ref[...] = jnp.zeros_like(grad_rate_ref)

    stack, pick = lane_helpers(CHUNK)
    blocks = diagonal_blocks()

    def doubled(ref):
        return jnp.concatenate([ref[0], ref[0]], 0)

    causal, earlier = doubled(causal_ref), doubled(earlier_ref)
    causal_turned, earlier_turned = doubled(causal_turned_ref), doubled(earlier_turned_ref)
    first_wide = first_ref[...]
    first = first_wide > 0.0
    last = last_ref[...]
    anew = anew_ref[0, 0:1, :]
    low = jnp.bfloat16
    for pair in range(pairs):
        lanes = slice(pair * PAIR, (pair + 1) * PAIR)
        query = qkv_ref[:, lanes]
        key = qkv_ref[:, width + pair * PAIR : width + (pair + 1) * PAIR]
        rate = rate_ref[0:1, lanes]
        begin = halves_of(states_ref[0, pair])
        initial = halves_of(initial_ref[pair])
        after = carried[pair]
        after_parts = halves_of(after)
        residue = residue_ref[:, lanes]
        scaled = halves_of(residue * rate)
        upstream = upstream_ref[:, lanes]
        upstream_parts = halves_of(upstream)
        key_wide = key.astype(jnp.float32)
        query_wide = query.astype(jnp.float32)
        key_last = (key_wide * last).astype(low)
        key_stack = stack(key)
        products = dot_abt(key_stack, jnp.concatenate([key, query], 0))
        ties_turned = products[:, :CHUNK] * earlier_turned
        scores_turned = products[:, CHUNK:] * causal_turned
        pulled = pick(wide(dot_ab, halves_of(scores_turned), upstream_parts))
        pulled = pulled + wide(dot_ab, key_last, after_parts)
        grad_scaled = solve(ties_turned, rate, -pulled, pick)
        grad_rate_ref[0:1, lanes] += jnp.sum(grad_scaled * residue, 0, keepdims=True)
        grad_residue = grad_scaled * rate
        residue_parts = halves_of(grad_residue)
        joined = tuple(
            jnp.concatenate([one, two], 0) for one, two in zip(upstream_parts, residue_parts)
        )
        scaled_stack = stack(scaled)
        turned = wide(dot_abt, scaled_stack, joined)
        straight = wide(
            dot_abt,
            tuple(
                jnp.concatenate([stack(one), stack(two)], 0)
                for one, two in zip(upstream_parts, residue_parts)
            ),
            scaled,
        )
        grad_scores = -straight[: 2 * CHUNK] * causal
        grad_scores_turned = -turned[:, :CHUNK] * causal_turned
        grad_ties = -(straight[2 * CHUNK :] * earlier + turned[:, CHUNK:] * earlier_turned)
        seen = wide(dot_abt, joined, begin)
        fresh = wide(dot_abt, joined, initial)
        grad_query = jnp.where(first, seen[:CHUNK], fresh[:CHUNK])
        grad_query = grad_query + pick(wide(dot_ab, halves_of(grad_scores), key))
        grad_key = jnp.where(first, seen[CHUNK:], fresh[CHUNK:]) + grad_residue
        grad_key = grad_key + pick(
            wide(dot_ab, halves_of(grad_scores_turned), query)
            + wide(dot_ab, halves_of(grad_ties), key)
        )
        grad_key = grad_key - last * wide(dot_abt, scaled, after_parts)
        grad_ref[:, lanes] = grad_query.astype(low)
        grad_ref[:, width + pair * PAIR : width + (pair + 1) * PAIR] = grad_key.astype(low)
        grad_ref[:, 2 * width + pair * PAIR : 2 * width + (pair + 1) * PAIR] = (
            -grad_residue
        ).astype(low)
        fronts = jnp.concatenate([query_wide * first_wide, key_wide * first_wide], 0).astype(low)
        backs = jnp.concatenate(
            [query_wide * (1.0 - first_wide), key_wide * (1.0 - first_wide)], 0
        ).astype(low)
        kept_after = jnp.where(anew > 0.0, 0.0, after)
        carried[pair] = kept_after + blocks * wide(dot_atb, fronts, joined)
        grad_initial_ref[pair] += (after - kept_after) + blocks * wide(dot_atb, backs, joined)


def pair_blocks(matrices):
    heads = matrices.shape[0]
    split = matrices.reshape(heads // 2, 2, P_SIZE, P_SIZE)
    empty = jnp.zeros_like(split[:, 0])
    upper = jnp.concatenate([split[:, 0], empty], 2)
    lower = jnp.concatenate([empty, split[:, 1]], 2)
    return jnp.concatenate([upper, lower], 1)


def head_blocks(pairs):
    return jnp.stack([pairs[:, :P_SIZE, :P_SIZE], pairs[:, P_SIZE:, P_SIZE:]], 1).reshape(
        -1, P_SIZE, P_SIZE
    )


def mixer_forward(qkv, rate, initial, masks):
    tokens = qkv.shape[0]
    width = rate.shape[1]
    pairs = initial.shape[0]
    chunks = tokens // CHUNK
    whole = lambda shape: pl.BlockSpec(shape, lambda i: (0,) * len(shape))
    square = pl.BlockSpec((1, CHUNK, CHUNK), lambda i: (i, 0, 0))
    column = pl.BlockSpec((CHUNK, PAIR), lambda i: (i, 0))
    causal, earlier, first, last, anew = masks
    return pl.pallas_call(
        mixer_forward_kernel,
        grid=(chunks,),
        in_specs=[
            pl.BlockSpec((CHUNK, 3 * width), lambda i: (i, 0)),
            whole((1, width)),
            whole((pairs, PAIR, PAIR)),
            square,
            square,
            column,
            column,
            pl.BlockSpec((1, 8, PAIR), lambda i: (i, 0, 0)),
        ],
        out_specs=[
            pl.BlockSpec((CHUNK, width), lambda i: (i, 0)),
            pl.BlockSpec((CHUNK, width), lambda i: (i, 0)),
            pl.BlockSpec((1, pairs, PAIR, PAIR), lambda i: (i, 0, 0, 0)),
        ],
        out_shape=[
            jax.ShapeDtypeStruct((tokens, width), jnp.bfloat16),
            jax.ShapeDtypeStruct((tokens, width), jnp.float32),
            jax.ShapeDtypeStruct((chunks, pairs, PAIR, PAIR), jnp.float32),
        ],
        scratch_shapes=[pltpu.VMEM((pairs, PAIR, PAIR), jnp.float32)],
        compiler_params=pltpu.CompilerParams(
            dimension_semantics=("arbitrary",), vmem_limit_bytes=32 * 1024 * 1024
        ),
        name="inner_forward",
    )(qkv, rate, initial, causal, earlier, first, last, anew)


def mixer_backward(qkv, rate, initial, masks, residue, states, upstream):
    tokens = qkv.shape[0]
    width = rate.shape[1]
    pairs = initial.shape[0]
    chunks = tokens // CHUNK
    whole = lambda shape: pl.BlockSpec(shape, lambda i: (0,) * len(shape))
    square = pl.BlockSpec((1, CHUNK, CHUNK), lambda i: (chunks - 1 - i, 0, 0))
    column = pl.BlockSpec((CHUNK, PAIR), lambda i: (chunks - 1 - i, 0))
    rows = lambda size: pl.BlockSpec((CHUNK, size), lambda i: (chunks - 1 - i, 0))
    causal, earlier, first, last, anew = masks
    return pl.pallas_call(
        mixer_backward_kernel,
        grid=(chunks,),
        in_specs=[
            rows(3 * width),
            whole((1, width)),
            whole((pairs, PAIR, PAIR)),
            square,
            square,
            square,
            square,
            column,
            column,
            pl.BlockSpec((1, 8, PAIR), lambda i: (chunks - 1 - i, 0, 0)),
            rows(width),
            pl.BlockSpec((1, pairs, PAIR, PAIR), lambda i: (chunks - 1 - i, 0, 0, 0)),
            rows(width),
        ],
        out_specs=[rows(3 * width), whole((pairs, PAIR, PAIR)), whole((1, width))],
        out_shape=[
            jax.ShapeDtypeStruct((tokens, 3 * width), jnp.bfloat16),
            jax.ShapeDtypeStruct((pairs, PAIR, PAIR), jnp.float32),
            jax.ShapeDtypeStruct((1, width), jnp.float32),
        ],
        scratch_shapes=[pltpu.VMEM((pairs, PAIR, PAIR), jnp.float32)],
        compiler_params=pltpu.CompilerParams(
            dimension_semantics=("arbitrary",), vmem_limit_bytes=32 * 1024 * 1024
        ),
        name="inner_backward",
    )(
        qkv,
        rate,
        initial,
        causal,
        earlier,
        jnp.swapaxes(causal, 1, 2),
        jnp.swapaxes(earlier, 1, 2),
        first,
        last,
        anew,
        residue,
        states,
        upstream,
    )


def shampoo(tile_w, tile_g, left, right, left_root, right_root):
    low_g = tile_g.astype(jnp.bfloat16)

    def product(form, one, two):
        return jnp.einsum(
            form,
            one.astype(jnp.bfloat16),
            two.astype(jnp.bfloat16),
            preferred_element_type=jnp.float32,
        )

    new_left = STAT_DECAY * left + (1.0 - STAT_DECAY) * product("abrc,absc->abrs", low_g, low_g)
    new_right = STAT_DECAY * right + (1.0 - STAT_DECAY) * product("abrc,abrd->abcd", low_g, low_g)
    turned = product("abrs,absc->abrc", left_root, low_g)
    turned = product("abrc,abcd->abrd", turned, right_root)
    return (new_left, new_right, tile_w - MATRIX_RATE * (turned + WEIGHT_DECAY * tile_w))


def refresh(master, grad, left, right, left_root, right_root):
    rows = master.shape[1]
    new_left, new_right, new_w = shampoo(
        master.reshape(1, 1, rows, -1),
        grad.reshape(1, 1, rows, -1),
        left,
        right,
        left_root,
        right_root,
    )
    return (grad, new_left, new_right, new_w.reshape(master.shape))


def adamw(weight, grad, first, second, step_rate):
    new_first = BETA_ONE * first + (1.0 - BETA_ONE) * grad
    new_second = BETA_TWO * second + (1.0 - BETA_TWO) * grad * grad
    moved = (
        new_first
        / (1.0 - BETA_ONE**STEP)
        / (jnp.sqrt(new_second / (1.0 - BETA_TWO**STEP)) + ADAM_EPSILON)
    )
    return (new_first, new_second, weight - step_rate * (moved + WEIGHT_DECAY * weight))


def layer_forward(token_ids, targets, valid, resets, weights, inner_init, gains, head_index):
    w_qkv, w_out, w_gu, w_down, table = weights
    vocab_part = table.shape[0]
    columns = jnp.arange(vocab_part, dtype=jnp.int32)
    local_ids = token_ids - head_index * vocab_part
    inside = (local_ids >= 0) & (local_ids < vocab_part)
    looked = jnp.take(table, jnp.clip(local_ids, 0, vocab_part - 1), axis=0)
    looked_rows = jnp.where(inside[:, None], looked.astype(jnp.float32), 0.0)
    embedded = lax.psum_scatter(
        looked_rows.astype(jnp.bfloat16), "head", scatter_dimension=1, tiled=True
    ).astype(jnp.float32)
    normed_one, scale_one = norm_forward(embedded, gains[0])
    full_one = spread(normed_one)
    mixed = jnp.dot(full_one, w_qkv, preferred_element_type=jnp.float32).astype(jnp.bfloat16)
    tokens = mixed.shape[0]
    step_rate = jax.nn.sigmoid(gains[3:4]) / (8 * P_SIZE)
    masks = mixer_masks(resets, tokens)
    initial_pairs = pair_blocks(inner_init)
    inner_low, residue, states = mixer_forward(mixed, step_rate, initial_pairs, masks)
    hidden_one = embedded + fold(jnp.dot(inner_low, w_out, preferred_element_type=jnp.float32))
    normed_two, scale_two = norm_forward(hidden_one, gains[1])
    full_two = spread(normed_two)
    gate_up = jnp.dot(full_two, w_gu, preferred_element_type=jnp.float32)

    def swiglu(paired):
        halves = paired.reshape(tokens, 2, -1)
        return jax.nn.silu(halves[:, 0]) * halves[:, 1]

    activated, act_pull = jax.vjp(swiglu, gate_up)
    act_low = activated.astype(jnp.bfloat16)
    hidden_two = hidden_one + fold(jnp.dot(act_low, w_down, preferred_element_type=jnp.float32))
    normed_end, scale_end = norm_forward(hidden_two, gains[2])
    full_end = spread(normed_end)
    logits = jnp.einsum("td,vd->tv", full_end, table, preferred_element_type=jnp.float32)
    peak = jnp.max(logits, -1)
    target_hits = columns[None, :] == (targets - head_index * vocab_part)[:, None]
    stats = lax.all_gather(
        jnp.stack(
            [
                peak,
                jnp.sum(jnp.exp(logits - peak[:, None]), -1),
                jnp.sum(jnp.where(target_hits, logits, 0.0), -1),
            ]
        ),
        "head",
        axis=0,
    )
    highest = jnp.max(stats[:, 0], 0)
    exp_sum = jnp.sum(stats[:, 1] * jnp.exp(stats[:, 0] - highest[None]), 0)
    target_logit = jnp.sum(stats[:, 2], 0)
    totals = highest + jnp.log(exp_sum)
    counted = valid.astype(jnp.float32)
    kept = (
        embedded,
        scale_one,
        full_one,
        (mixed, step_rate, initial_pairs, masks, residue, states),
        inner_low,
        hidden_one,
        scale_two,
        full_two,
        act_pull,
        act_low,
        hidden_two,
        scale_end,
        full_end,
        logits,
        totals,
        target_hits,
        counted,
        local_ids,
    )
    return (jnp.sum((totals - target_logit) * counted), jnp.sum(counted), kept)


def layer_backward(kept, weights, gains):
    (
        embedded,
        scale_one,
        full_one,
        inner_kept,
        inner_low,
        hidden_one,
        scale_two,
        full_two,
        act_pull,
        act_low,
        hidden_two,
        scale_end,
        full_end,
        logits,
        totals,
        target_hits,
        counted,
        local_ids,
    ) = kept
    w_qkv, w_out, w_gu, w_down, table = weights
    tokens = logits.shape[0]
    d_logits = (
        (jnp.exp(logits - totals[:, None]) - target_hits.astype(jnp.float32)) * counted[:, None]
    ).astype(jnp.bfloat16)
    grad_table = jnp.einsum("tv,td->vd", d_logits, full_end, preferred_element_type=jnp.float32)
    d_end = fold(jnp.dot(d_logits, table, preferred_element_type=jnp.float32))
    d_two, gain_end = norm_backward(hidden_two, scale_end, gains[2], d_end)
    d_down_in = spread_grad(d_two.astype(jnp.bfloat16))
    grad_down = jnp.einsum("tf,td->fd", act_low, d_down_in, preferred_element_type=jnp.float32)
    d_act = jnp.einsum("td,fd->tf", d_down_in, w_down, preferred_element_type=jnp.float32)
    d_gate_up = act_pull(d_act)[0].astype(jnp.bfloat16)
    grad_gu = jnp.einsum("td,tc->dc", full_two, d_gate_up, preferred_element_type=jnp.float32)
    d_two_norm = fold(jnp.einsum("tc,dc->td", d_gate_up, w_gu, preferred_element_type=jnp.float32))
    d_middle, gain_two = norm_backward(hidden_one, scale_two, gains[1], d_two_norm)
    d_one = d_two + d_middle
    d_out_in = spread_grad(d_one.astype(jnp.bfloat16))
    grad_out = jnp.einsum("tc,td->cd", inner_low, d_out_in, preferred_element_type=jnp.float32)
    d_inner = jnp.einsum("td,cd->tc", d_out_in, w_out, preferred_element_type=jnp.float32)
    d_mixed, grad_pairs, grad_step = mixer_backward(*inner_kept, d_inner)
    grad_init = head_blocks(grad_pairs)
    gate = jax.nn.sigmoid(gains[3])
    grad_rate = grad_step[0] * gate * (1.0 - gate) / (8 * P_SIZE)
    grad_qkv = jnp.einsum("td,tc->dc", full_one, d_mixed, preferred_element_type=jnp.float32)
    d_one_norm = fold(jnp.einsum("tc,dc->td", d_mixed, w_qkv, preferred_element_type=jnp.float32))
    d_base, gain_one = norm_backward(embedded, scale_one, gains[0], d_one_norm)
    d_embed = spread_grad((d_one + d_base).astype(jnp.bfloat16))
    columns = jnp.arange(table.shape[0], dtype=jnp.int32)
    id_onehot = (columns[None, :] == local_ids[:, None]).astype(jnp.bfloat16)
    grad_table = grad_table + jnp.einsum(
        "tv,td->vd", id_onehot, d_embed, preferred_element_type=jnp.float32
    )
    grad_gains = jnp.stack([gain_one, gain_two, gain_end, grad_rate], 0)
    return (grad_qkv, grad_out, grad_gu, grad_down, grad_table, grad_init, grad_gains)


def shards(
    token_ids,
    targets,
    valid,
    resets,
    owners,
    emb_master,
    emb_first,
    emb_second,
    qkv_master,
    qkv_left,
    qkv_right,
    qkv_left_root,
    qkv_right_root,
    out_master,
    out_left,
    out_right,
    out_left_root,
    out_right_root,
    gu_master,
    gu_left,
    gu_right,
    gu_left_root,
    gu_right_root,
    down_master,
    down_left,
    down_right,
    down_left_root,
    down_right_root,
    inner_init,
    inner_first,
    inner_second,
    gains,
    gains_first,
    gains_second,
):
    gathered = (
        lax.all_gather(qkv_master.astype(jnp.bfloat16), "dp", axis=0, tiled=True),
        lax.all_gather(out_master.astype(jnp.bfloat16), "dp", axis=0, tiled=True),
        lax.all_gather(gu_master.astype(jnp.bfloat16), "dp", axis=0, tiled=True),
        lax.all_gather(down_master.astype(jnp.bfloat16), "dp", axis=0, tiled=True),
        lax.all_gather(emb_master.astype(jnp.bfloat16), "dp", axis=1, tiled=True),
    )
    w_qkv = jnp.take(gathered[0], owners[0], axis=0).reshape(D, -1)
    w_out = jnp.take(gathered[1], owners[1], axis=0)
    w_out = jnp.swapaxes(w_out, 0, 1).reshape(w_out.shape[1], D)
    w_gu = jnp.take(gathered[2], owners[2], axis=0).reshape(D, -1)
    w_down = jnp.take(gathered[3], owners[3], axis=0)
    w_down = jnp.swapaxes(w_down, 0, 1).reshape(w_down.shape[1], D)
    weights = (w_qkv, w_out, w_gu, w_down, gathered[4])
    head_index = lax.axis_index("head")
    loss_local, count_local, kept = layer_forward(
        token_ids, targets, valid, resets, weights, inner_init, gains, head_index
    )
    loss_sum, count = lax.psum((loss_local, count_local), "dp")
    grad_qkv, grad_out, grad_gu, grad_down, grad_table, grad_init, grad_gains = layer_backward(
        kept, weights, gains
    )
    parts = lax.axis_size("dp")
    order = jnp.argsort(owners, axis=1)
    slot_qkv = jnp.take(grad_qkv.reshape(parts, -1, 3, grad_qkv.shape[1] // 3), order[0], axis=0)
    slot_out = jnp.take(
        jnp.swapaxes(grad_out.reshape(grad_out.shape[0], parts, -1), 0, 1), order[1], axis=0
    )
    slot_gu = jnp.take(grad_gu.reshape(parts, -1, 2, grad_gu.shape[1] // 2), order[2], axis=0)
    slot_down = jnp.take(
        jnp.swapaxes(grad_down.reshape(grad_down.shape[0], parts, -1), 0, 1), order[3], axis=0
    )
    low = jnp.bfloat16
    owned = tuple(
        lax.psum_scatter(piece.astype(low), "dp", scatter_dimension=0, tiled=True).astype(
            jnp.float32
        )
        for piece in (slot_qkv, slot_out, slot_gu, slot_down)
    )
    owned = owned + (
        lax.psum_scatter(grad_table.astype(low), "dp", scatter_dimension=1, tiled=True).astype(
            jnp.float32
        ),
    )
    small = lax.psum((grad_init, grad_gains), "dp")
    first_dp = (lax.axis_index("dp") == 0).astype(jnp.float32)
    squares = sum((jnp.sum(piece * piece) for piece in owned))
    squares = squares + first_dp * (jnp.sum(small[0] * small[0]) + jnp.sum(small[1] * small[1]))
    squares_all = lax.psum(squares, ("dp", "head"))
    grad_norm = jnp.sqrt(squares_all) / count
    factor = jnp.minimum(1.0, CLIP_LIMIT / grad_norm) / count
    qkv_out = refresh(
        qkv_master, owned[0] * factor, qkv_left, qkv_right, qkv_left_root, qkv_right_root
    )
    out_out = refresh(
        out_master, owned[1] * factor, out_left, out_right, out_left_root, out_right_root
    )
    gu_out = refresh(gu_master, owned[2] * factor, gu_left, gu_right, gu_left_root, gu_right_root)
    down_out = refresh(
        down_master, owned[3] * factor, down_left, down_right, down_left_root, down_right_root
    )
    table_out = adamw(emb_master, owned[4] * factor, emb_first, emb_second, TABLE_RATE)
    init_out = adamw(inner_init, small[0] * factor, inner_first, inner_second, INITIAL_RATE)
    gain_out = adamw(gains, small[1] * factor, gains_first, gains_second, GAINS_RATE)
    return (
        (jnp.stack([loss_sum, count]), grad_norm)
        + table_out
        + qkv_out
        + out_out
        + gu_out
        + down_out
        + init_out
        + gain_out
    )


def solution(mesh):
    placed = (
        P("dp"),
        P("dp"),
        P("dp"),
        P("dp"),
        P(),
        P("head", "dp"),
        P("head", "dp"),
        P("head", "dp"),
        P("dp", None, None, "head"),
        P("dp", "head", None, None),
        P("dp", "head", None, None),
        P("dp", "head", None, None),
        P("dp", "head", None, None),
        P("dp", "head", None),
        P("dp", "head", None, None),
        P("dp", "head", None, None),
        P("dp", "head", None, None),
        P("dp", "head", None, None),
        P("dp", None, None, "head"),
        P("dp", "head", None, None),
        P("dp", "head", None, None),
        P("dp", "head", None, None),
        P("dp", "head", None, None),
        P("dp", "head", None),
        P("dp", "head", None, None),
        P("dp", "head", None, None),
        P("dp", "head", None, None),
        P("dp", "head", None, None),
        P("head", None, None),
        P("head", None, None),
        P("head", None, None),
        P(None, "head"),
        P(None, "head"),
        P(None, "head"),
    )
    return jax.shard_map(
        shards,
        mesh=mesh,
        in_specs=placed,
        out_specs=(
            P(),
            P(),
            P("head", "dp"),
            P("head", "dp"),
            P("head", "dp"),
            P("dp", None, None, "head"),
            P("dp", "head", None, None),
            P("dp", "head", None, None),
            P("dp", None, None, "head"),
            P("dp", "head", None),
            P("dp", "head", None, None),
            P("dp", "head", None, None),
            P("dp", "head", None),
            P("dp", None, None, "head"),
            P("dp", "head", None, None),
            P("dp", "head", None, None),
            P("dp", None, None, "head"),
            P("dp", "head", None),
            P("dp", "head", None, None),
            P("dp", "head", None, None),
            P("dp", "head", None),
            P("head", None, None),
            P("head", None, None),
            P("head", None, None),
            P(None, "head"),
            P(None, "head"),
            P(None, "head"),
        ),
        check_vma=False,
    )
```

```python
import functools

import jax
import jax.numpy as jnp
from jax import lax
from jax.experimental import pallas as pl
from jax.experimental.pallas import tpu as pltpu
from jax.sharding import PartitionSpec as P

D = 2048
P_SIZE = 64
MB = 16
STEP = 10


EPSILON = 1e-05
CLIP_LIMIT = 0.05
STAT_DECAY = 0.5
MATRIX_RATE = 0.4
TABLE_RATE = 0.3
INITIAL_RATE = 0.05
GAINS_RATE = 0.3
BETA_ONE = 0.9
BETA_TWO = 0.95
ADAM_EPSILON = 1e-08
WEIGHT_DECAY = 0.01


CHUNK = 64
PAIR = 2 * P_SIZE


def dot_ab(left, right):
    return lax.dot_general(left, right, (((1,), (0,)), ((), ())), preferred_element_type=jnp.float32)


def dot_abt(left, right):
    return lax.dot_general(left, right, (((1,), (1,)), ((), ())), preferred_element_type=jnp.float32)


def dot_atb(left, right):
    return lax.dot_general(left, right, (((0,), (0,)), ((), ())), preferred_element_type=jnp.float32)


def halves_of(value):
    high = value.astype(jnp.bfloat16)
    return (high, (value - high.astype(jnp.float32)).astype(jnp.bfloat16))


def wide(form, left, right):
    lefts = left if isinstance(left, tuple) else (left,)
    rights = right if isinstance(right, tuple) else (right,)
    total = form(lefts[0], rights[0])
    if len(rights) > 1:
        total = total + form(lefts[0], rights[1])
    if len(lefts) > 1:
        total = total + form(lefts[1], rights[0])
    return total


def each(pieces, change):
    return tuple(change(piece) for piece in pieces) if isinstance(pieces, tuple) else change(pieces)


def mixer_masks(resets, tokens):
    per_chunk = CHUNK // MB
    chunks = tokens // CHUNK
    segment = jnp.cumsum(resets.reshape(chunks, per_chunk), axis=1)
    segment = jnp.repeat(segment, MB, axis=1)
    same = segment[:, :, None] == segment[:, None, :]
    spot = jnp.arange(CHUNK, dtype=jnp.int32)
    causal = (spot[None, :] <= spot[:, None])[None]
    earlier = ((spot[None, :] // MB) < (spot[:, None] // MB))[None]
    causal = (same & causal).astype(jnp.float32)
    earlier = (same & earlier).astype(jnp.float32)
    first = (segment == 0).astype(jnp.float32).reshape(tokens, 1)
    last = (segment == segment[:, -1:]).astype(jnp.float32).reshape(tokens, 1)
    anew = (segment[:, -1] > 0).astype(jnp.float32)
    first = jnp.broadcast_to(first, (tokens, PAIR))
    last = jnp.broadcast_to(last, (tokens, PAIR))
    anew = jnp.broadcast_to(anew[:, None, None], (chunks, 8, PAIR))
    return causal, earlier, first, last, anew


def lane_helpers(rows):
    lanes = lax.broadcasted_iota(jnp.int32, (rows, PAIR), 1)
    low_lane = lanes < P_SIZE
    low_half = low_lane.astype(jnp.float32)
    high_half = 1.0 - low_half

    def stack(pieces):
        def one(piece):
            kind = piece.dtype
            return jnp.concatenate(
                [piece * low_half.astype(kind), piece * high_half.astype(kind)], 0
            )

        return each(pieces, one)

    def pick(product):
        return jnp.where(low_lane, product[:rows], product[rows:])

    return stack, pick


def diagonal_blocks():
    rows = lax.broadcasted_iota(jnp.int32, (PAIR, PAIR), 0) // P_SIZE
    columns = lax.broadcasted_iota(jnp.int32, (PAIR, PAIR), 1) // P_SIZE
    return (rows == columns).astype(jnp.float32)


def solve(matrix, rate_row, value, pick):
    rows = value.shape[0]
    powers = [(matrix, rate_row)]
    reach = 2
    while reach < CHUNK // MB:
        last, rate = powers[-1]
        low, high = halves_of(last[:rows]), halves_of(last[rows:])
        powers.append(
            (
                jnp.concatenate([wide(dot_ab, low, low), wide(dot_ab, high, high)], 0),
                rate * rate,
            )
        )
        reach = 2 * reach
    for index in range(len(powers) - 1, -1, -1):
        factor, rate = powers[index]
        moved = pick(wide(dot_ab, halves_of(factor), halves_of(value * rate)))
        value = value - moved if index == 0 else value + moved
    return value


def mixer_forward_kernel(
    qkv_ref,
    rate_ref,
    initial_ref,
    causal_ref,
    earlier_ref,
    first_ref,
    last_ref,
    anew_ref,
    z_ref,
    residue_ref,
    states_ref,
    state,
):
    pairs = initial_ref.shape[0]
    width = pairs * PAIR

    @pl.when(pl.program_id(0) == 0)
    def _():
        state[...] = jnp.zeros_like(state)

    stack, pick = lane_helpers(CHUNK)
    blocks = diagonal_blocks()
    causal = causal_ref[0]
    causal = jnp.concatenate([causal, causal], 0)
    earlier = earlier_ref[0]
    earlier = jnp.concatenate([earlier, earlier], 0)
    first = first_ref[...] > 0.0
    last = last_ref[...]
    anew = anew_ref[0, 0:1, :]
    for pair in range(pairs):
        lanes = slice(pair * PAIR, (pair + 1) * PAIR)
        query = qkv_ref[:, lanes]
        key = qkv_ref[:, width + pair * PAIR : width + (pair + 1) * PAIR]
        value = qkv_ref[:, 2 * width + pair * PAIR : 2 * width + (pair + 1) * PAIR]
        rate = rate_ref[0:1, lanes]
        begin = state[pair]
        initial = initial_ref[pair]
        states_ref[0, pair] = begin
        products = dot_abt(jnp.concatenate([stack(key), stack(query)], 0), key)
        ties = products[: 2 * CHUNK] * earlier
        scores = products[2 * CHUNK :] * causal
        both = jnp.concatenate([key, query], 0)
        seen = wide(dot_ab, both, halves_of(begin))
        fresh = wide(dot_ab, both, halves_of(initial))
        key_seen = jnp.where(first, seen[:CHUNK], fresh[:CHUNK])
        query_seen = jnp.where(first, seen[CHUNK:], fresh[CHUNK:])
        key_wide = key.astype(jnp.float32)
        residue = solve(ties, rate, key_seen - (value.astype(jnp.float32) - key_wide), pick)
        residue_ref[:, lanes] = residue
        scaled = residue * rate
        scaled_parts = halves_of(scaled)
        output = query_seen - pick(wide(dot_ab, halves_of(scores), scaled_parts))
        z_ref[:, lanes] = output.astype(jnp.bfloat16)
        key_last = (key_wide * last).astype(jnp.bfloat16)
        base = jnp.where(anew > 0.0, initial, begin)
        state[pair] = base - blocks * wide(dot_atb, key_last, scaled_parts)


def mixer_backward_kernel(
    qkv_ref,
    rate_ref,
    initial_ref,
    causal_ref,
    earlier_ref,
    causal_turned_ref,
    earlier_turned_ref,
    first_ref,
    last_ref,
    anew_ref,
    residue_ref,
    states_ref,
    upstream_ref,
    grad_ref,
    grad_initial_ref,
    grad_rate_ref,
    carried,
):
    pairs = initial_ref.shape[0]
    width = pairs * PAIR

    @pl.when(pl.program_id(0) == 0)
    def _():
        carried[...] = jnp.zeros_like(carried)
        grad_initial_ref[...] = jnp.zeros_like(grad_initial_ref)
        grad_rate_ref[...] = jnp.zeros_like(grad_rate_ref)

    stack, pick = lane_helpers(CHUNK)
    blocks = diagonal_blocks()

    def doubled(ref):
        return jnp.concatenate([ref[0], ref[0]], 0)

    causal, earlier = doubled(causal_ref), doubled(earlier_ref)
    causal_turned, earlier_turned = doubled(causal_turned_ref), doubled(earlier_turned_ref)
    first_wide = first_ref[...]
    first = first_wide > 0.0
    last = last_ref[...]
    anew = anew_ref[0, 0:1, :]
    low = jnp.bfloat16
    for pair in range(pairs):
        lanes = slice(pair * PAIR, (pair + 1) * PAIR)
        query = qkv_ref[:, lanes]
        key = qkv_ref[:, width + pair * PAIR : width + (pair + 1) * PAIR]
        rate = rate_ref[0:1, lanes]
        begin = halves_of(states_ref[0, pair])
        initial = halves_of(initial_ref[pair])
        after = carried[pair]
        after_parts = halves_of(after)
        residue = residue_ref[:, lanes]
        scaled = halves_of(residue * rate)
        upstream = upstream_ref[:, lanes]
        upstream_parts = halves_of(upstream)
        key_wide = key.astype(jnp.float32)
        query_wide = query.astype(jnp.float32)
        key_last = (key_wide * last).astype(low)
        key_stack = stack(key)
        products = dot_abt(key_stack, jnp.concatenate([key, query], 0))
        ties_turned = products[:, :CHUNK] * earlier_turned
        scores_turned = products[:, CHUNK:] * causal_turned
        pulled = pick(wide(dot_ab, halves_of(scores_turned), upstream_parts))
        pulled = pulled + wide(dot_ab, key_last, after_parts)
        grad_scaled = solve(ties_turned, rate, -pulled, pick)
        grad_rate_ref[0:1, lanes] += jnp.sum(grad_scaled * residue, 0, keepdims=True)
        grad_residue = grad_scaled * rate
        residue_parts = halves_of(grad_residue)
        joined = tuple(
            jnp.concatenate([one, two], 0) for one, two in zip(upstream_parts, residue_parts)
        )
        scaled_stack = stack(scaled)
        turned = wide(dot_abt, scaled_stack, joined)
        straight = wide(
            dot_abt,
            tuple(
                jnp.concatenate([stack(one), stack(two)], 0)
                for one, two in zip(upstream_parts, residue_parts)
            ),
            scaled,
        )
        grad_scores = -straight[: 2 * CHUNK] * causal
        grad_scores_turned = -turned[:, :CHUNK] * causal_turned
        grad_ties = -(straight[2 * CHUNK :] * earlier + turned[:, CHUNK:] * earlier_turned)
        seen = wide(dot_abt, joined, begin)
        fresh = wide(dot_abt, joined, initial)
        grad_query = jnp.where(first, seen[:CHUNK], fresh[:CHUNK])
        grad_query = grad_query + pick(wide(dot_ab, halves_of(grad_scores), key))
        grad_key = jnp.where(first, seen[CHUNK:], fresh[CHUNK:]) + grad_residue
        grad_key = grad_key + pick(
            wide(dot_ab, halves_of(grad_scores_turned), query)
            + wide(dot_ab, halves_of(grad_ties), key)
        )
        grad_key = grad_key - last * wide(dot_abt, scaled, after_parts)
        grad_ref[:, lanes] = grad_query.astype(low)
        grad_ref[:, width + pair * PAIR : width + (pair + 1) * PAIR] = grad_key.astype(low)
        grad_ref[:, 2 * width + pair * PAIR : 2 * width + (pair + 1) * PAIR] = (
            -grad_residue
        ).astype(low)
        fronts = jnp.concatenate([query_wide * first_wide, key_wide * first_wide], 0).astype(low)
        backs = jnp.concatenate(
            [query_wide * (1.0 - first_wide), key_wide * (1.0 - first_wide)], 0
        ).astype(low)
        kept_after = jnp.where(anew > 0.0, 0.0, after)
        carried[pair] = kept_after + blocks * wide(dot_atb, fronts, joined)
        grad_initial_ref[pair] += (after - kept_after) + blocks * wide(dot_atb, backs, joined)


def pair_blocks(matrices):
    heads = matrices.shape[0]
    split = matrices.reshape(heads // 2, 2, P_SIZE, P_SIZE)
    empty = jnp.zeros_like(split[:, 0])
    upper = jnp.concatenate([split[:, 0], empty], 2)
    lower = jnp.concatenate([empty, split[:, 1]], 2)
    return jnp.concatenate([upper, lower], 1)


def head_blocks(pairs):
    return jnp.stack([pairs[:, :P_SIZE, :P_SIZE], pairs[:, P_SIZE:, P_SIZE:]], 1).reshape(
        -1, P_SIZE, P_SIZE
    )


def mixer_forward(qkv, rate, initial, masks):
    tokens = qkv.shape[0]
    width = rate.shape[1]
    pairs = initial.shape[0]
    chunks = tokens // CHUNK
    whole = lambda shape: pl.BlockSpec(shape, lambda i: (0,) * len(shape))
    square = pl.BlockSpec((1, CHUNK, CHUNK), lambda i: (i, 0, 0))
    column = pl.BlockSpec((CHUNK, PAIR), lambda i: (i, 0))
    causal, earlier, first, last, anew = masks
    return pl.pallas_call(
        mixer_forward_kernel,
        grid=(chunks,),
        in_specs=[
            pl.BlockSpec((CHUNK, 3 * width), lambda i: (i, 0)),
            whole((1, width)),
            whole((pairs, PAIR, PAIR)),
            square,
            square,
            column,
            column,
            pl.BlockSpec((1, 8, PAIR), lambda i: (i, 0, 0)),
        ],
        out_specs=[
            pl.BlockSpec((CHUNK, width), lambda i: (i, 0)),
            pl.BlockSpec((CHUNK, width), lambda i: (i, 0)),
            pl.BlockSpec((1, pairs, PAIR, PAIR), lambda i: (i, 0, 0, 0)),
        ],
        out_shape=[
            jax.ShapeDtypeStruct((tokens, width), jnp.bfloat16),
            jax.ShapeDtypeStruct((tokens, width), jnp.float32),
            jax.ShapeDtypeStruct((chunks, pairs, PAIR, PAIR), jnp.float32),
        ],
        scratch_shapes=[pltpu.VMEM((pairs, PAIR, PAIR), jnp.float32)],
        compiler_params=pltpu.CompilerParams(
            dimension_semantics=("arbitrary",), vmem_limit_bytes=32 * 1024 * 1024
        ),
        name="inner_forward",
    )(qkv, rate, initial, causal, earlier, first, last, anew)


def mixer_backward(qkv, rate, initial, masks, residue, states, upstream):
    tokens = qkv.shape[0]
    width = rate.shape[1]
    pairs = initial.shape[0]
    chunks = tokens // CHUNK
    whole = lambda shape: pl.BlockSpec(shape, lambda i: (0,) * len(shape))
    square = pl.BlockSpec((1, CHUNK, CHUNK), lambda i: (chunks - 1 - i, 0, 0))
    column = pl.BlockSpec((CHUNK, PAIR), lambda i: (chunks - 1 - i, 0))
    rows = lambda size: pl.BlockSpec((CHUNK, size), lambda i: (chunks - 1 - i, 0))
    causal, earlier, first, last, anew = masks
    return pl.pallas_call(
        mixer_backward_kernel,
        grid=(chunks,),
        in_specs=[
            rows(3 * width),
            whole((1, width)),
            whole((pairs, PAIR, PAIR)),
            square,
            square,
            square,
            square,
            column,
            column,
            pl.BlockSpec((1, 8, PAIR), lambda i: (chunks - 1 - i, 0, 0)),
            rows(width),
            pl.BlockSpec((1, pairs, PAIR, PAIR), lambda i: (chunks - 1 - i, 0, 0, 0)),
            rows(width),
        ],
        out_specs=[rows(3 * width), whole((pairs, PAIR, PAIR)), whole((1, width))],
        out_shape=[
            jax.ShapeDtypeStruct((tokens, 3 * width), jnp.bfloat16),
            jax.ShapeDtypeStruct((pairs, PAIR, PAIR), jnp.float32),
            jax.ShapeDtypeStruct((1, width), jnp.float32),
        ],
        scratch_shapes=[pltpu.VMEM((pairs, PAIR, PAIR), jnp.float32)],
        compiler_params=pltpu.CompilerParams(
            dimension_semantics=("arbitrary",), vmem_limit_bytes=32 * 1024 * 1024
        ),
        name="inner_backward",
    )(
        qkv,
        rate,
        initial,
        causal,
        earlier,
        jnp.swapaxes(causal, 1, 2),
        jnp.swapaxes(earlier, 1, 2),
        first,
        last,
        anew,
        residue,
        states,
        upstream,
    )


ROWS = 128
MESH = pl.DeviceIdType.MESH


def across(column, size):
    return jnp.swapaxes(jnp.broadcast_to(column, (size, size)), 0, 1)[:8]


def down(row, size, width):
    turned = jnp.swapaxes(jnp.broadcast_to(row[:1], (size, size)), 0, 1)
    return jnp.concatenate([turned] * (width // size), 1) if width > size else turned[:, :width]


def transit_kernel(mode, turned, parts, *refs):
    refs = list(refs)
    left_hbm, right_ref, inputs_ref, gain_ref = refs[:4]
    refs = refs[4:]
    if mode == "norm":
        own_ref, full_ref, scale_ref = refs[:3]
        refs = refs[3:]
    else:
        given_scale_ref = refs[0]
        added_ref = None
        refs = refs[1:]
        if mode == "grad_add":
            added_ref = refs[0]
            refs = refs[1:]
        own_ref, full_ref, gain_grad_ref = refs[:3]
        refs = refs[3:]
    (
        left_buf,
        partial,
        pair_out,
        pair_in,
        from_low,
        from_high,
        total,
        sums_out,
        sums_in,
        left_sem,
        pair_out_sem,
        pair_in_sem,
        low_out_sem,
        low_in_sem,
        high_out_sem,
        high_in_sem,
        sums_out_sem,
        sums_in_sem,
        up_out_sem,
        up_in_sem,
        down_out_sem,
        down_in_sem,
        twin_out_sem,
        twin_in_sem,
    ) = refs
    places = parts // 2
    tokens, size = own_ref.shape
    chunks = tokens // ROWS
    ring = partial.shape[0]
    me = lax.axis_index("head")
    core = lax.rem(me, 2)
    spot = me // 2
    twin = {"head": me + 1 - 2 * core}
    upper = {"head": lax.rem(me + 2, parts)}
    lower = {"head": lax.rem(me + parts - 2, parts)}

    def rows_of(chunk):
        return pl.ds(pl.multiple_of(chunk * ROWS, ROWS), ROWS)

    def shard(index):
        return pl.ds(pl.multiple_of(index * size, 128), size)

    def remote(source, target, out_sem, in_sem, device):
        return pltpu.make_async_remote_copy(
            src_ref=source,
            dst_ref=target,
            send_sem=out_sem,
            recv_sem=in_sem,
            device_id=device,
            device_id_type=MESH,
        )

    def left_copy(chunk):
        return pltpu.make_async_copy(
            left_hbm.at[rows_of(chunk)], left_buf.at[lax.rem(chunk, 2)], left_sem.at[lax.rem(chunk, 2)]
        )

    barrier = pltpu.get_barrier_semaphore()
    for offset in range(1, parts):
        pl.semaphore_signal(
            barrier, inc=1, device_id={"head": lax.rem(me + offset, parts)}, device_id_type=MESH
        )
    left_copy(0).start()
    if mode != "norm":
        gain_grad_ref[...] = jnp.zeros_like(gain_grad_ref)
    pl.semaphore_wait(barrier, parts - 1)

    def valid(chunk):
        return jnp.logical_and(chunk >= 0, chunk < chunks)

    def pair_copy(chunk):
        slot = lax.rem(chunk, ring)
        return remote(
            pair_out.at[slot], pair_in.at[slot], pair_out_sem.at[slot], pair_in_sem.at[slot], twin
        )

    def rise(chunk, place):
        slot = lax.rem(chunk, ring)
        part = from_low.at[slot, :, pl.ds((place + 1) * size, (places - 1 - place) * size)]
        return remote(part, part, low_out_sem.at[slot], low_in_sem.at[slot], upper)

    def fall(chunk, place):
        slot = lax.rem(chunk, ring)
        part = from_high.at[slot, :, pl.ds(0, place * size)]
        return remote(part, part, high_out_sem.at[slot], high_in_sem.at[slot], lower)

    def sums_copy(chunk, offset):
        slot = lax.rem(chunk, ring)
        return remote(
            sums_out.at[slot],
            sums_in.at[slot, offset - 1],
            sums_out_sem.at[slot, offset - 1],
            sums_in_sem.at[slot],
            {"head": lax.rem(me + offset, parts)},
        )

    def climb(chunk, source, hop):
        part = full_ref.at[rows_of(chunk), shard(2 * source + core)]
        return remote(
            part, part, up_out_sem.at[chunk, hop - 1], up_in_sem.at[chunk, hop - 1], upper
        )

    def sink(chunk, source, hop):
        part = full_ref.at[rows_of(chunk), shard(2 * source + core)]
        return remote(
            part, part, down_out_sem.at[chunk, hop - 1], down_in_sem.at[chunk, hop - 1], lower
        )

    def mirror(chunk, source):
        part = full_ref.at[rows_of(chunk), shard(2 * source + core)]
        return remote(part, part, twin_out_sem.at[chunk, source], twin_in_sem.at[chunk], twin)

    def relay(step):
        for hop in range(1, places):
            chunk = step - places - 1 - hop
            source = spot - hop

            @pl.when(jnp.logical_and(valid(chunk), source >= 0))
            def _():
                climb(chunk, source, hop).wait_recv()
                if hop < places - 1:

                    @pl.when(spot < places - 1)
                    def _():
                        climb(chunk, source, hop + 1).start()

                mirror(chunk, source).start()

            source_high = spot + hop

            @pl.when(jnp.logical_and(valid(chunk), source_high < places))
            def _():
                sink(chunk, source_high, hop).wait_recv()
                if hop < places - 1:

                    @pl.when(spot > 0)
                    def _():
                        sink(chunk, source_high, hop + 1).start()

                mirror(chunk, source_high).start()

    def finish_shard(step):
        chunk = step - places - 1

        @pl.when(valid(chunk))
        def _():
            slot = lax.rem(chunk, ring)
            rows = rows_of(chunk)
            pltpu.make_async_copy(sums_in.at[slot], sums_in.at[slot], sums_in_sem.at[slot]).wait()
            summed = sums_out[slot]
            for offset in range(1, parts):
                summed = summed + sums_in[slot, offset - 1]
            gain = gain_ref[0:1, :]
            if mode == "norm":
                scale = lax.rsqrt(summed / D + EPSILON)
                scale_ref[chunk] = scale
                result = own_ref[rows, :] * down(scale, ROWS, size) * gain
            else:
                scale = down(given_scale_ref[chunk], ROWS, size)
                normed = inputs_ref[rows, :] * scale
                inner = down(summed / D, ROWS, size)
                result = scale * (own_ref[rows, :] * gain - normed * inner)
                if mode == "grad_add":
                    result = result + added_ref[rows, :]
                own_ref[rows, :] = result
            full_ref[rows, shard(me)] = result.astype(jnp.bfloat16)
            mirror(chunk, spot).start()

            @pl.when(spot < places - 1)
            def _():
                climb(chunk, spot, 1).start()

            @pl.when(spot > 0)
            def _():
                sink(chunk, spot, 1).start()

    def add_pair(step):
        chunk = step - 1

        @pl.when(valid(chunk))
        def _():
            slot = lax.rem(chunk, ring)
            pair_copy(chunk).wait_recv()
            partial[slot] = partial[slot] + pair_in[slot].astype(jnp.float32)

    def pass_on(step):
        for place in range(places):
            if place < places - 1:
                up_chunk = step - 1 - place

                @pl.when(jnp.logical_and(valid(up_chunk), spot == place))
                def _():
                    slot = lax.rem(up_chunk, ring)
                    above = pl.ds((place + 1) * size, (places - 1 - place) * size)
                    values = partial[slot, :, above]
                    if place > 0:
                        rise(up_chunk, place - 1).wait_recv()
                        values = values + from_low[slot, :, above].astype(jnp.float32)
                    from_low[slot, :, above] = values.astype(jnp.bfloat16)
                    rise(up_chunk, place).start()

            if place > 0:
                down_chunk = step - places + place

                @pl.when(jnp.logical_and(valid(down_chunk), spot == place))
                def _():
                    slot = lax.rem(down_chunk, ring)
                    below = pl.ds(0, place * size)
                    values = partial[slot, :, below]
                    if place < places - 1:
                        fall(down_chunk, place + 1).wait_recv()
                        values = values + from_high[slot, :, below].astype(jnp.float32)
                    from_high[slot, :, below] = values.astype(jnp.bfloat16)
                    fall(down_chunk, place).start()

    def settle(step):
        chunk = step - places - 1

        @pl.when(valid(chunk))
        def _():
            pair_copy(chunk).wait_send()
            for place in range(places):

                @pl.when(spot == place)
                def _():
                    if place < places - 1:
                        rise(chunk, place).wait_send()
                    if place > 0:
                        fall(chunk, place).wait_send()

            for offset in range(1, parts):
                sums_copy(chunk, offset).wait_send()

    def sum_shard(step):
        chunk = step - places

        @pl.when(valid(chunk))
        def _():
            slot = lax.rem(chunk, ring)
            rows = rows_of(chunk)
            mine = shard(spot)

            @pl.when(spot == places - 1)
            def _():
                rise(chunk, places - 2).wait_recv()

            @pl.when(spot == 0)
            def _():
                fall(chunk, 1).wait_recv()

            total[...] = partial[slot, :, mine]

            @pl.when(spot > 0)
            def _():
                total[...] += from_low[slot, :, mine].astype(jnp.float32)

            @pl.when(spot < places - 1)
            def _():
                total[...] += from_high[slot, :, mine].astype(jnp.float32)

            value = total[...]
            if mode == "norm":
                value = value + inputs_ref[rows, :]
                column = jnp.sum(value * value, 1, keepdims=True)
            else:
                scale = down(given_scale_ref[chunk], ROWS, size)
                normed = inputs_ref[rows, :] * scale
                gain_grad_ref[0:1, :] += jnp.sum(value * normed, 0, keepdims=True)
                column = jnp.sum(value * gain_ref[0:1, :] * normed, 1, keepdims=True)
            own_ref[rows, :] = value
            sums_out[slot] = across(column, ROWS)
            for offset in range(1, parts):
                sums_copy(chunk, offset).start()

    def produce(step):
        chunk = step

        @pl.when(valid(chunk))
        def _():
            slot = lax.rem(chunk, ring)
            half = lax.rem(chunk, 2)
            left_copy(chunk).wait()

            @pl.when(chunk + 1 < chunks)
            def _():
                left_copy(chunk + 1).start()

            def term(index):
                if turned:
                    return dot_abt(left_buf[half], right_ref[shard(index), :])
                return dot_ab(left_buf[half], right_ref[:, shard(index)])

            for place in range(places):
                lanes = pl.ds(place * size, size)
                pair_out[slot, :, lanes] = term(2 * place + 1 - core).astype(jnp.bfloat16)
            pair_copy(chunk).start()
            for place in range(places):
                lanes = pl.ds(place * size, size)
                partial[slot, :, lanes] = term(2 * place + core)

    def close(step):
        chunk = step - 2 * places - 1

        @pl.when(valid(chunk))
        def _():
            arrived = full_ref.at[rows_of(chunk), pl.ds(0, places * size)]
            pltpu.make_async_copy(arrived, arrived, twin_in_sem.at[chunk]).wait()
            for source in range(places):
                mirror(chunk, source).wait_send()
            for hop in range(1, places):
                source = spot - hop + 1

                @pl.when(jnp.logical_and(source >= 0, spot < places - 1))
                def _():
                    climb(chunk, source, hop).wait_send()

                source_high = spot + hop - 1

                @pl.when(jnp.logical_and(source_high < places, spot > 0))
                def _():
                    sink(chunk, source_high, hop).wait_send()

    def advance(step, carried):
        relay(step)
        finish_shard(step)
        add_pair(step)
        pass_on(step)
        settle(step)
        sum_shard(step)
        produce(step)
        close(step)
        return carried

    lax.fori_loop(0, chunks + 2 * places + 1, advance, 0)


def transit(mode, number, parts, left, right, inputs, gain, scale=None, added=None, turned=False):
    tokens, size = inputs.shape
    depth = left.shape[1]
    width = parts * size
    chunks = tokens // ROWS
    places = parts // 2
    ring = min(chunks, 2 * places)
    dma = pltpu.SemaphoreType.DMA
    low = jnp.bfloat16
    vmem = pl.BlockSpec(memory_space=pltpu.VMEM)
    operands = [left, right, inputs, gain]
    specs = [pl.BlockSpec(memory_space=pl.ANY), vmem, vmem, vmem]
    shapes = [
        jax.ShapeDtypeStruct((tokens, size), jnp.float32),
        jax.ShapeDtypeStruct((tokens, width), low),
    ]
    if mode == "norm":
        shapes.append(jax.ShapeDtypeStruct((chunks, 8, ROWS), jnp.float32))
    else:
        operands.append(scale)
        specs.append(vmem)
        if mode == "grad_add":
            operands.append(added)
            specs.append(vmem)
        shapes.append(jax.ShapeDtypeStruct((8, size), jnp.float32))
    span = places * size
    hops = max(places - 1, 1)
    return pl.pallas_call(
        functools.partial(transit_kernel, mode, turned, parts),
        in_specs=specs,
        out_specs=[vmem] * len(shapes),
        out_shape=shapes,
        scratch_shapes=[
            pltpu.VMEM((2, ROWS, depth), low),
            pltpu.VMEM((ring, ROWS, span), jnp.float32),
            pltpu.VMEM((ring, ROWS, span), low),
            pltpu.VMEM((ring, ROWS, span), low),
            pltpu.VMEM((ring, ROWS, span), low),
            pltpu.VMEM((ring, ROWS, span), low),
            pltpu.VMEM((ROWS, size), jnp.float32),
            pltpu.VMEM((ring, 8, ROWS), jnp.float32),
            pltpu.VMEM((ring, parts - 1, 8, ROWS), jnp.float32),
            dma((2,)),
            dma((ring,)),
            dma((ring,)),
            dma((ring,)),
            dma((ring,)),
            dma((ring,)),
            dma((ring,)),
            dma((ring, parts - 1)),
            dma((ring,)),
            dma((chunks, hops)),
            dma((chunks, hops)),
            dma((chunks, hops)),
            dma((chunks, hops)),
            dma((chunks, places)),
            dma((chunks,)),
        ],
        compiler_params=pltpu.CompilerParams(
            collective_id=number, has_side_effects=True, vmem_limit_bytes=60 * 1024 * 1024
        ),
        cost_estimate=pl.CostEstimate(
            flops=2 * tokens * depth * width,
            bytes_accessed=2 * (tokens * depth + depth * width + tokens * width),
            transcendentals=0,
        ),
        name="transit_" + mode,
    )(*operands)


def shampoo(tile_w, tile_g, left, right, left_root, right_root):
    low_g = tile_g.astype(jnp.bfloat16)

    def product(form, one, two):
        return jnp.einsum(
            form,
            one.astype(jnp.bfloat16),
            two.astype(jnp.bfloat16),
            preferred_element_type=jnp.float32,
        )

    new_left = STAT_DECAY * left + (1.0 - STAT_DECAY) * product("abrc,absc->abrs", low_g, low_g)
    new_right = STAT_DECAY * right + (1.0 - STAT_DECAY) * product("abrc,abrd->abcd", low_g, low_g)
    turned = product("abrs,absc->abrc", left_root, low_g)
    turned = product("abrc,abcd->abrd", turned, right_root)
    return (new_left, new_right, tile_w - MATRIX_RATE * (turned + WEIGHT_DECAY * tile_w))


def refresh(master, grad, left, right, left_root, right_root):
    rows = master.shape[1]
    new_left, new_right, new_w = shampoo(
        master.reshape(1, 1, rows, -1),
        grad.reshape(1, 1, rows, -1),
        left,
        right,
        left_root,
        right_root,
    )
    return (grad, new_left, new_right, new_w.reshape(master.shape))


def adamw(weight, grad, first, second, step_rate):
    new_first = BETA_ONE * first + (1.0 - BETA_ONE) * grad
    new_second = BETA_TWO * second + (1.0 - BETA_TWO) * grad * grad
    moved = (
        new_first
        / (1.0 - BETA_ONE**STEP)
        / (jnp.sqrt(new_second / (1.0 - BETA_TWO**STEP)) + ADAM_EPSILON)
    )
    return (new_first, new_second, weight - step_rate * (moved + WEIGHT_DECAY * weight))


def layer_forward(token_ids, targets, valid, resets, weights, inner_init, gains, head_index):
    w_qkv, w_out, w_gu, w_down, table = weights
    parts = lax.axis_size("head")
    vocab_part = table.shape[0]
    tokens = token_ids.shape[0]
    columns = jnp.arange(vocab_part, dtype=jnp.int32)
    local_ids = token_ids - head_index * vocab_part
    id_onehot = (columns[None, :] == local_ids[:, None]).astype(jnp.bfloat16)
    nothing = jnp.zeros((tokens, gains.shape[1]), jnp.float32)
    embedded, full_one, scale_one = transit(
        "norm", 1, parts, id_onehot, table, nothing, gains[0:1]
    )
    mixed = jnp.dot(full_one, w_qkv, preferred_element_type=jnp.float32).astype(jnp.bfloat16)
    step_rate = jax.nn.sigmoid(gains[3:4]) / (8 * P_SIZE)
    masks = mixer_masks(resets, tokens)
    initial_pairs = pair_blocks(inner_init)
    inner_low, residue, states = mixer_forward(mixed, step_rate, initial_pairs, masks)
    hidden_one, full_two, scale_two = transit(
        "norm", 2, parts, inner_low, w_out, embedded, gains[1:2]
    )
    gate_up = jnp.dot(full_two, w_gu, preferred_element_type=jnp.float32)

    def swiglu(paired):
        halves = paired.reshape(tokens, 2, -1)
        return jax.nn.silu(halves[:, 0]) * halves[:, 1]

    activated, act_pull = jax.vjp(swiglu, gate_up)
    act_low = activated.astype(jnp.bfloat16)
    hidden_two, full_end, scale_end = transit(
        "norm", 3, parts, act_low, w_down, hidden_one, gains[2:3]
    )
    logits = jnp.einsum("td,vd->tv", full_end, table, preferred_element_type=jnp.float32)
    peak = jnp.max(logits, -1)
    target_hits = columns[None, :] == (targets - head_index * vocab_part)[:, None]
    stats = lax.all_gather(
        jnp.stack(
            [
                peak,
                jnp.sum(jnp.exp(logits - peak[:, None]), -1),
                jnp.sum(jnp.where(target_hits, logits, 0.0), -1),
            ]
        ),
        "head",
        axis=0,
    )
    highest = jnp.max(stats[:, 0], 0)
    exp_sum = jnp.sum(stats[:, 1] * jnp.exp(stats[:, 0] - highest[None]), 0)
    target_logit = jnp.sum(stats[:, 2], 0)
    totals = highest + jnp.log(exp_sum)
    counted = valid.astype(jnp.float32)
    d_logits = (
        (jnp.exp(logits - totals[:, None]) - target_hits.astype(jnp.float32)) * counted[:, None]
    ).astype(jnp.bfloat16)
    kept = (
        embedded,
        scale_one,
        full_one,
        (mixed, step_rate, initial_pairs, masks, residue, states),
        inner_low,
        hidden_one,
        scale_two,
        full_two,
        act_pull,
        act_low,
        hidden_two,
        scale_end,
        full_end,
        d_logits,
        id_onehot,
    )
    return (jnp.sum((totals - target_logit) * counted), jnp.sum(counted), kept)


def layer_backward(kept, weights, gains):
    (
        embedded,
        scale_one,
        full_one,
        inner_kept,
        inner_low,
        hidden_one,
        scale_two,
        full_two,
        act_pull,
        act_low,
        hidden_two,
        scale_end,
        full_end,
        d_logits,
        id_onehot,
    ) = kept
    w_qkv, w_out, w_gu, w_down, table = weights
    parts = lax.axis_size("head")
    d_two, d_down_in, gain_end = transit(
        "grad", 4, parts, d_logits, table, hidden_two, gains[2:3], scale_end
    )
    grad_table = jnp.einsum("tv,td->vd", d_logits, full_end, preferred_element_type=jnp.float32)
    d_act = jnp.einsum("td,fd->tf", d_down_in, w_down, preferred_element_type=jnp.float32)
    d_gate_up = act_pull(d_act)[0].astype(jnp.bfloat16)
    d_one, d_out_in, gain_two = transit(
        "grad_add", 5, parts, d_gate_up, w_gu, hidden_one, gains[1:2], scale_two, d_two, True
    )
    grad_down = jnp.einsum("tf,td->fd", act_low, d_down_in, preferred_element_type=jnp.float32)
    grad_gu = jnp.einsum("td,tc->dc", full_two, d_gate_up, preferred_element_type=jnp.float32)
    d_inner = jnp.einsum("td,cd->tc", d_out_in, w_out, preferred_element_type=jnp.float32)
    d_mixed, grad_pairs, grad_step = mixer_backward(*inner_kept, d_inner)
    grad_init = head_blocks(grad_pairs)
    gate = jax.nn.sigmoid(gains[3])
    grad_rate = grad_step[0] * gate * (1.0 - gate) / (8 * P_SIZE)
    _, d_embed, gain_one = transit(
        "grad_add", 6, parts, d_mixed, w_qkv, embedded, gains[0:1], scale_one, d_one, True
    )
    grad_out = jnp.einsum("tc,td->cd", inner_low, d_out_in, preferred_element_type=jnp.float32)
    grad_qkv = jnp.einsum("td,tc->dc", full_one, d_mixed, preferred_element_type=jnp.float32)
    grad_table = grad_table + jnp.einsum(
        "tv,td->vd", id_onehot, d_embed, preferred_element_type=jnp.float32
    )
    grad_gains = jnp.stack([gain_one[0], gain_two[0], gain_end[0], grad_rate], 0)
    return (grad_qkv, grad_out, grad_gu, grad_down, grad_table, grad_init, grad_gains)


def shards(
    token_ids,
    targets,
    valid,
    resets,
    owners,
    emb_master,
    emb_first,
    emb_second,
    qkv_master,
    qkv_left,
    qkv_right,
    qkv_left_root,
    qkv_right_root,
    out_master,
    out_left,
    out_right,
    out_left_root,
    out_right_root,
    gu_master,
    gu_left,
    gu_right,
    gu_left_root,
    gu_right_root,
    down_master,
    down_left,
    down_right,
    down_left_root,
    down_right_root,
    inner_init,
    inner_first,
    inner_second,
    gains,
    gains_first,
    gains_second,
):
    gathered = (
        lax.all_gather(qkv_master.astype(jnp.bfloat16), "dp", axis=0, tiled=True),
        lax.all_gather(out_master.astype(jnp.bfloat16), "dp", axis=0, tiled=True),
        lax.all_gather(gu_master.astype(jnp.bfloat16), "dp", axis=0, tiled=True),
        lax.all_gather(down_master.astype(jnp.bfloat16), "dp", axis=0, tiled=True),
        lax.all_gather(emb_master.astype(jnp.bfloat16), "dp", axis=1, tiled=True),
    )
    w_qkv = jnp.take(gathered[0], owners[0], axis=0).reshape(D, -1)
    w_out = jnp.take(gathered[1], owners[1], axis=0)
    w_out = jnp.swapaxes(w_out, 0, 1).reshape(w_out.shape[1], D)
    w_gu = jnp.take(gathered[2], owners[2], axis=0).reshape(D, -1)
    w_down = jnp.take(gathered[3], owners[3], axis=0)
    w_down = jnp.swapaxes(w_down, 0, 1).reshape(w_down.shape[1], D)
    weights = (w_qkv, w_out, w_gu, w_down, gathered[4])
    head_index = lax.axis_index("head")
    loss_local, count_local, kept = layer_forward(
        token_ids, targets, valid, resets, weights, inner_init, gains, head_index
    )
    loss_sum, count = lax.psum((loss_local, count_local), "dp")
    grad_qkv, grad_out, grad_gu, grad_down, grad_table, grad_init, grad_gains = layer_backward(
        kept, weights, gains
    )
    parts = lax.axis_size("dp")
    order = jnp.argsort(owners, axis=1)
    slot_qkv = jnp.take(grad_qkv.reshape(parts, -1, 3, grad_qkv.shape[1] // 3), order[0], axis=0)
    slot_out = jnp.take(
        jnp.swapaxes(grad_out.reshape(grad_out.shape[0], parts, -1), 0, 1), order[1], axis=0
    )
    slot_gu = jnp.take(grad_gu.reshape(parts, -1, 2, grad_gu.shape[1] // 2), order[2], axis=0)
    slot_down = jnp.take(
        jnp.swapaxes(grad_down.reshape(grad_down.shape[0], parts, -1), 0, 1), order[3], axis=0
    )
    low = jnp.bfloat16
    owned = tuple(
        lax.psum_scatter(piece.astype(low), "dp", scatter_dimension=0, tiled=True).astype(
            jnp.float32
        )
        for piece in (slot_qkv, slot_out, slot_gu, slot_down)
    )
    owned = owned + (
        lax.psum_scatter(grad_table.astype(low), "dp", scatter_dimension=1, tiled=True).astype(
            jnp.float32
        ),
    )
    small = lax.psum((grad_init, grad_gains), "dp")
    first_dp = (lax.axis_index("dp") == 0).astype(jnp.float32)
    squares = sum((jnp.sum(piece * piece) for piece in owned))
    squares = squares + first_dp * (jnp.sum(small[0] * small[0]) + jnp.sum(small[1] * small[1]))
    squares_all = lax.psum(squares, ("dp", "head"))
    grad_norm = jnp.sqrt(squares_all) / count
    factor = jnp.minimum(1.0, CLIP_LIMIT / grad_norm) / count
    qkv_out = refresh(
        qkv_master, owned[0] * factor, qkv_left, qkv_right, qkv_left_root, qkv_right_root
    )
    out_out = refresh(
        out_master, owned[1] * factor, out_left, out_right, out_left_root, out_right_root
    )
    gu_out = refresh(gu_master, owned[2] * factor, gu_left, gu_right, gu_left_root, gu_right_root)
    down_out = refresh(
        down_master, owned[3] * factor, down_left, down_right, down_left_root, down_right_root
    )
    table_out = adamw(emb_master, owned[4] * factor, emb_first, emb_second, TABLE_RATE)
    init_out = adamw(inner_init, small[0] * factor, inner_first, inner_second, INITIAL_RATE)
    gain_out = adamw(gains, small[1] * factor, gains_first, gains_second, GAINS_RATE)
    return (
        (jnp.stack([loss_sum, count]), grad_norm)
        + table_out
        + qkv_out
        + out_out
        + gu_out
        + down_out
        + init_out
        + gain_out
    )


def solution(mesh):
    placed = (
        P("dp"),
        P("dp"),
        P("dp"),
        P("dp"),
        P(),
        P("head", "dp"),
        P("head", "dp"),
        P("head", "dp"),
        P("dp", None, None, "head"),
        P("dp", "head", None, None),
        P("dp", "head", None, None),
        P("dp", "head", None, None),
        P("dp", "head", None, None),
        P("dp", "head", None),
        P("dp", "head", None, None),
        P("dp", "head", None, None),
        P("dp", "head", None, None),
        P("dp", "head", None, None),
        P("dp", None, None, "head"),
        P("dp", "head", None, None),
        P("dp", "head", None, None),
        P("dp", "head", None, None),
        P("dp", "head", None, None),
        P("dp", "head", None),
        P("dp", "head", None, None),
        P("dp", "head", None, None),
        P("dp", "head", None, None),
        P("dp", "head", None, None),
        P("head", None, None),
        P("head", None, None),
        P("head", None, None),
        P(None, "head"),
        P(None, "head"),
        P(None, "head"),
    )
    return jax.shard_map(
        shards,
        mesh=mesh,
        in_specs=placed,
        out_specs=(
            P(),
            P(),
            P("head", "dp"),
            P("head", "dp"),
            P("head", "dp"),
            P("dp", None, None, "head"),
            P("dp", "head", None, None),
            P("dp", "head", None, None),
            P("dp", None, None, "head"),
            P("dp", "head", None),
            P("dp", "head", None, None),
            P("dp", "head", None, None),
            P("dp", "head", None),
            P("dp", None, None, "head"),
            P("dp", "head", None, None),
            P("dp", "head", None, None),
            P("dp", None, None, "head"),
            P("dp", "head", None),
            P("dp", "head", None, None),
            P("dp", "head", None, None),
            P("dp", "head", None),
            P("head", None, None),
            P("head", None, None),
            P("head", None, None),
            P(None, "head"),
            P(None, "head"),
            P(None, "head"),
        ),
        check_vma=False,
    )
```

```python
import functools

import jax
import jax.numpy as jnp
from jax import lax
from jax.experimental import pallas as pl
from jax.experimental.pallas import tpu as pltpu
from jax.sharding import PartitionSpec as P

D = 2048
P_SIZE = 64
MB = 16
STEP = 10


EPSILON = 1e-05
CLIP_LIMIT = 0.05
STAT_DECAY = 0.5
MATRIX_RATE = 0.4
TABLE_RATE = 0.3
INITIAL_RATE = 0.05
GAINS_RATE = 0.3
BETA_ONE = 0.9
BETA_TWO = 0.95
ADAM_EPSILON = 1e-08
WEIGHT_DECAY = 0.01


CHUNK = 64
PAIR = 2 * P_SIZE


def dot_ab(left, right):
    return lax.dot_general(left, right, (((1,), (0,)), ((), ())), preferred_element_type=jnp.float32)


def dot_abt(left, right):
    return lax.dot_general(left, right, (((1,), (1,)), ((), ())), preferred_element_type=jnp.float32)


def dot_atb(left, right):
    return lax.dot_general(left, right, (((0,), (0,)), ((), ())), preferred_element_type=jnp.float32)


def halves_of(value):
    high = value.astype(jnp.bfloat16)
    return (high, (value - high.astype(jnp.float32)).astype(jnp.bfloat16))


def wide(form, left, right):
    lefts = left if isinstance(left, tuple) else (left,)
    rights = right if isinstance(right, tuple) else (right,)
    total = form(lefts[0], rights[0])
    if len(rights) > 1:
        total = total + form(lefts[0], rights[1])
    if len(lefts) > 1:
        total = total + form(lefts[1], rights[0])
    return total


def each(pieces, change):
    return tuple(change(piece) for piece in pieces) if isinstance(pieces, tuple) else change(pieces)


def mixer_masks(resets, tokens):
    per_chunk = CHUNK // MB
    chunks = tokens // CHUNK
    segment = jnp.cumsum(resets.reshape(chunks, per_chunk), axis=1)
    segment = jnp.repeat(segment, MB, axis=1)
    same = segment[:, :, None] == segment[:, None, :]
    spot = jnp.arange(CHUNK, dtype=jnp.int32)
    causal = (spot[None, :] <= spot[:, None])[None]
    earlier = ((spot[None, :] // MB) < (spot[:, None] // MB))[None]
    causal = (same & causal).astype(jnp.float32)
    earlier = (same & earlier).astype(jnp.float32)
    first = (segment == 0).astype(jnp.float32).reshape(tokens, 1)
    last = (segment == segment[:, -1:]).astype(jnp.float32).reshape(tokens, 1)
    anew = (segment[:, -1] > 0).astype(jnp.float32)
    first = jnp.broadcast_to(first, (tokens, PAIR))
    last = jnp.broadcast_to(last, (tokens, PAIR))
    anew = jnp.broadcast_to(anew[:, None, None], (chunks, 8, PAIR))
    return causal, earlier, first, last, anew


def lane_helpers(rows):
    lanes = lax.broadcasted_iota(jnp.int32, (rows, PAIR), 1)
    low_lane = lanes < P_SIZE
    low_half = low_lane.astype(jnp.float32)
    high_half = 1.0 - low_half

    def stack(pieces):
        def one(piece):
            kind = piece.dtype
            return jnp.concatenate(
                [piece * low_half.astype(kind), piece * high_half.astype(kind)], 0
            )

        return each(pieces, one)

    def pick(product):
        return jnp.where(low_lane, product[:rows], product[rows:])

    return stack, pick


def diagonal_blocks():
    rows = lax.broadcasted_iota(jnp.int32, (PAIR, PAIR), 0) // P_SIZE
    columns = lax.broadcasted_iota(jnp.int32, (PAIR, PAIR), 1) // P_SIZE
    return (rows == columns).astype(jnp.float32)


def solve(matrix, rate_row, value, pick):
    rows = value.shape[0]
    powers = [(matrix, rate_row)]
    reach = 2
    while reach < CHUNK // MB:
        last, rate = powers[-1]
        low, high = halves_of(last[:rows]), halves_of(last[rows:])
        powers.append(
            (
                jnp.concatenate([wide(dot_ab, low, low), wide(dot_ab, high, high)], 0),
                rate * rate,
            )
        )
        reach = 2 * reach
    for index in range(len(powers) - 1, -1, -1):
        factor, rate = powers[index]
        moved = pick(wide(dot_ab, halves_of(factor), halves_of(value * rate)))
        value = value - moved if index == 0 else value + moved
    return value


def mixer_forward_kernel(
    qkv_ref,
    rate_ref,
    initial_ref,
    causal_ref,
    earlier_ref,
    first_ref,
    last_ref,
    anew_ref,
    z_ref,
    residue_ref,
    states_ref,
    state,
):
    pairs = initial_ref.shape[0]
    width = pairs * PAIR

    @pl.when(pl.program_id(0) == 0)
    def _():
        state[...] = jnp.zeros_like(state)

    stack, pick = lane_helpers(CHUNK)
    blocks = diagonal_blocks()
    causal = causal_ref[0]
    causal = jnp.concatenate([causal, causal], 0)
    earlier = earlier_ref[0]
    earlier = jnp.concatenate([earlier, earlier], 0)
    first = first_ref[...] > 0.0
    last = last_ref[...]
    anew = anew_ref[0, 0:1, :]
    for pair in range(pairs):
        lanes = slice(pair * PAIR, (pair + 1) * PAIR)
        query = qkv_ref[:, lanes]
        key = qkv_ref[:, width + pair * PAIR : width + (pair + 1) * PAIR]
        value = qkv_ref[:, 2 * width + pair * PAIR : 2 * width + (pair + 1) * PAIR]
        rate = rate_ref[0:1, lanes]
        begin = state[pair]
        initial = initial_ref[pair]
        states_ref[0, pair] = begin
        products = dot_abt(jnp.concatenate([stack(key), stack(query)], 0), key)
        ties = products[: 2 * CHUNK] * earlier
        scores = products[2 * CHUNK :] * causal
        both = jnp.concatenate([key, query], 0)
        seen = wide(dot_ab, both, halves_of(begin))
        fresh = wide(dot_ab, both, halves_of(initial))
        key_seen = jnp.where(first, seen[:CHUNK], fresh[:CHUNK])
        query_seen = jnp.where(first, seen[CHUNK:], fresh[CHUNK:])
        key_wide = key.astype(jnp.float32)
        residue = solve(ties, rate, key_seen - (value.astype(jnp.float32) - key_wide), pick)
        residue_ref[:, lanes] = residue
        scaled = residue * rate
        scaled_parts = halves_of(scaled)
        output = query_seen - pick(wide(dot_ab, halves_of(scores), scaled_parts))
        z_ref[:, lanes] = output.astype(jnp.bfloat16)
        key_last = (key_wide * last).astype(jnp.bfloat16)
        base = jnp.where(anew > 0.0, initial, begin)
        state[pair] = base - blocks * wide(dot_atb, key_last, scaled_parts)


def mixer_backward_kernel(
    qkv_ref,
    rate_ref,
    initial_ref,
    causal_ref,
    earlier_ref,
    causal_turned_ref,
    earlier_turned_ref,
    first_ref,
    last_ref,
    anew_ref,
    residue_ref,
    states_ref,
    upstream_ref,
    grad_ref,
    grad_initial_ref,
    grad_rate_ref,
    carried,
):
    pairs = initial_ref.shape[0]
    width = pairs * PAIR

    @pl.when(pl.program_id(0) == 0)
    def _():
        carried[...] = jnp.zeros_like(carried)
        grad_initial_ref[...] = jnp.zeros_like(grad_initial_ref)
        grad_rate_ref[...] = jnp.zeros_like(grad_rate_ref)

    stack, pick = lane_helpers(CHUNK)
    blocks = diagonal_blocks()

    def doubled(ref):
        return jnp.concatenate([ref[0], ref[0]], 0)

    causal, earlier = doubled(causal_ref), doubled(earlier_ref)
    causal_turned, earlier_turned = doubled(causal_turned_ref), doubled(earlier_turned_ref)
    first_wide = first_ref[...]
    first = first_wide > 0.0
    last = last_ref[...]
    anew = anew_ref[0, 0:1, :]
    low = jnp.bfloat16
    for pair in range(pairs):
        lanes = slice(pair * PAIR, (pair + 1) * PAIR)
        query = qkv_ref[:, lanes]
        key = qkv_ref[:, width + pair * PAIR : width + (pair + 1) * PAIR]
        rate = rate_ref[0:1, lanes]
        begin = halves_of(states_ref[0, pair])
        initial = halves_of(initial_ref[pair])
        after = carried[pair]
        after_parts = halves_of(after)
        residue = residue_ref[:, lanes]
        scaled = halves_of(residue * rate)
        upstream = upstream_ref[:, lanes]
        upstream_parts = halves_of(upstream)
        key_wide = key.astype(jnp.float32)
        query_wide = query.astype(jnp.float32)
        key_last = (key_wide * last).astype(low)
        key_stack = stack(key)
        products = dot_abt(key_stack, jnp.concatenate([key, query], 0))
        ties_turned = products[:, :CHUNK] * earlier_turned
        scores_turned = products[:, CHUNK:] * causal_turned
        pulled = pick(wide(dot_ab, halves_of(scores_turned), upstream_parts))
        pulled = pulled + wide(dot_ab, key_last, after_parts)
        grad_scaled = solve(ties_turned, rate, -pulled, pick)
        grad_rate_ref[0:1, lanes] += jnp.sum(grad_scaled * residue, 0, keepdims=True)
        grad_residue = grad_scaled * rate
        residue_parts = halves_of(grad_residue)
        joined = tuple(
            jnp.concatenate([one, two], 0) for one, two in zip(upstream_parts, residue_parts)
        )
        scaled_stack = stack(scaled)
        turned = wide(dot_abt, scaled_stack, joined)
        straight = wide(
            dot_abt,
            tuple(
                jnp.concatenate([stack(one), stack(two)], 0)
                for one, two in zip(upstream_parts, residue_parts)
            ),
            scaled,
        )
        grad_scores = -straight[: 2 * CHUNK] * causal
        grad_scores_turned = -turned[:, :CHUNK] * causal_turned
        grad_ties = -(straight[2 * CHUNK :] * earlier + turned[:, CHUNK:] * earlier_turned)
        seen = wide(dot_abt, joined, begin)
        fresh = wide(dot_abt, joined, initial)
        grad_query = jnp.where(first, seen[:CHUNK], fresh[:CHUNK])
        grad_query = grad_query + pick(wide(dot_ab, halves_of(grad_scores), key))
        grad_key = jnp.where(first, seen[CHUNK:], fresh[CHUNK:]) + grad_residue
        grad_key = grad_key + pick(
            wide(dot_ab, halves_of(grad_scores_turned), query)
            + wide(dot_ab, halves_of(grad_ties), key)
        )
        grad_key = grad_key - last * wide(dot_abt, scaled, after_parts)
        grad_ref[:, lanes] = grad_query.astype(low)
        grad_ref[:, width + pair * PAIR : width + (pair + 1) * PAIR] = grad_key.astype(low)
        grad_ref[:, 2 * width + pair * PAIR : 2 * width + (pair + 1) * PAIR] = (
            -grad_residue
        ).astype(low)
        fronts = jnp.concatenate([query_wide * first_wide, key_wide * first_wide], 0).astype(low)
        backs = jnp.concatenate(
            [query_wide * (1.0 - first_wide), key_wide * (1.0 - first_wide)], 0
        ).astype(low)
        kept_after = jnp.where(anew > 0.0, 0.0, after)
        carried[pair] = kept_after + blocks * wide(dot_atb, fronts, joined)
        grad_initial_ref[pair] += (after - kept_after) + blocks * wide(dot_atb, backs, joined)


def pair_blocks(matrices):
    heads = matrices.shape[0]
    split = matrices.reshape(heads // 2, 2, P_SIZE, P_SIZE)
    empty = jnp.zeros_like(split[:, 0])
    upper = jnp.concatenate([split[:, 0], empty], 2)
    lower = jnp.concatenate([empty, split[:, 1]], 2)
    return jnp.concatenate([upper, lower], 1)


def head_blocks(pairs):
    return jnp.stack([pairs[:, :P_SIZE, :P_SIZE], pairs[:, P_SIZE:, P_SIZE:]], 1).reshape(
        -1, P_SIZE, P_SIZE
    )


def mixer_forward(qkv, rate, initial, masks):
    tokens = qkv.shape[0]
    width = rate.shape[1]
    pairs = initial.shape[0]
    chunks = tokens // CHUNK
    whole = lambda shape: pl.BlockSpec(shape, lambda i: (0,) * len(shape))
    square = pl.BlockSpec((1, CHUNK, CHUNK), lambda i: (i, 0, 0))
    column = pl.BlockSpec((CHUNK, PAIR), lambda i: (i, 0))
    causal, earlier, first, last, anew = masks
    return pl.pallas_call(
        mixer_forward_kernel,
        grid=(chunks,),
        in_specs=[
            pl.BlockSpec((CHUNK, 3 * width), lambda i: (i, 0)),
            whole((1, width)),
            whole((pairs, PAIR, PAIR)),
            square,
            square,
            column,
            column,
            pl.BlockSpec((1, 8, PAIR), lambda i: (i, 0, 0)),
        ],
        out_specs=[
            pl.BlockSpec((CHUNK, width), lambda i: (i, 0)),
            pl.BlockSpec((CHUNK, width), lambda i: (i, 0)),
            pl.BlockSpec((1, pairs, PAIR, PAIR), lambda i: (i, 0, 0, 0)),
        ],
        out_shape=[
            jax.ShapeDtypeStruct((tokens, width), jnp.bfloat16),
            jax.ShapeDtypeStruct((tokens, width), jnp.float32),
            jax.ShapeDtypeStruct((chunks, pairs, PAIR, PAIR), jnp.float32),
        ],
        scratch_shapes=[pltpu.VMEM((pairs, PAIR, PAIR), jnp.float32)],
        compiler_params=pltpu.CompilerParams(
            dimension_semantics=("arbitrary",), vmem_limit_bytes=32 * 1024 * 1024
        ),
        name="inner_forward",
    )(qkv, rate, initial, causal, earlier, first, last, anew)


def mixer_backward(qkv, rate, initial, masks, residue, states, upstream):
    tokens = qkv.shape[0]
    width = rate.shape[1]
    pairs = initial.shape[0]
    chunks = tokens // CHUNK
    whole = lambda shape: pl.BlockSpec(shape, lambda i: (0,) * len(shape))
    square = pl.BlockSpec((1, CHUNK, CHUNK), lambda i: (chunks - 1 - i, 0, 0))
    column = pl.BlockSpec((CHUNK, PAIR), lambda i: (chunks - 1 - i, 0))
    rows = lambda size: pl.BlockSpec((CHUNK, size), lambda i: (chunks - 1 - i, 0))
    causal, earlier, first, last, anew = masks
    return pl.pallas_call(
        mixer_backward_kernel,
        grid=(chunks,),
        in_specs=[
            rows(3 * width),
            whole((1, width)),
            whole((pairs, PAIR, PAIR)),
            square,
            square,
            square,
            square,
            column,
            column,
            pl.BlockSpec((1, 8, PAIR), lambda i: (chunks - 1 - i, 0, 0)),
            rows(width),
            pl.BlockSpec((1, pairs, PAIR, PAIR), lambda i: (chunks - 1 - i, 0, 0, 0)),
            rows(width),
        ],
        out_specs=[rows(3 * width), whole((pairs, PAIR, PAIR)), whole((1, width))],
        out_shape=[
            jax.ShapeDtypeStruct((tokens, 3 * width), jnp.bfloat16),
            jax.ShapeDtypeStruct((pairs, PAIR, PAIR), jnp.float32),
            jax.ShapeDtypeStruct((1, width), jnp.float32),
        ],
        scratch_shapes=[pltpu.VMEM((pairs, PAIR, PAIR), jnp.float32)],
        compiler_params=pltpu.CompilerParams(
            dimension_semantics=("arbitrary",), vmem_limit_bytes=32 * 1024 * 1024
        ),
        name="inner_backward",
    )(
        qkv,
        rate,
        initial,
        causal,
        earlier,
        jnp.swapaxes(causal, 1, 2),
        jnp.swapaxes(earlier, 1, 2),
        first,
        last,
        anew,
        residue,
        states,
        upstream,
    )


ROWS = 128
LAG = 2
MESH = pl.DeviceIdType.MESH


def across(column, size):
    return jnp.swapaxes(jnp.broadcast_to(column, (size, size)), 0, 1)[:8]


def down(row, size, width):
    turned = jnp.swapaxes(jnp.broadcast_to(row[:1], (size, size)), 0, 1)
    return jnp.concatenate([turned] * (width // size), 1) if width > size else turned[:, :width]


def transit_kernel(mode, form, parts, slabs, names, *all_refs):
    ref = dict(zip(names, all_refs))
    full_ref, partial, total = ref["full"], ref["partial"], ref["total"]
    pair_out, pair_in = ref["pair_out"], ref["pair_in"]
    from_low, from_high = ref["from_low"], ref["from_high"]
    places = parts // 2
    cross = form in ("lookup", "table")
    summing = mode != "plain"
    size = total.shape[1]
    ring = partial.shape[0]
    me = lax.axis_index("head")
    mine_dp = lax.axis_index("dp")
    core = lax.rem(me, 2)
    spot = me // 2
    twin = {"head": me + 1 - 2 * core}
    upper = {"head": lax.rem(me + 2, parts)}
    lower = {"head": lax.rem(me + parts - 2, parts)}
    chunks = ref["up_in_sem"].shape[0]
    sum_at = LAG * places
    finish_at = sum_at + (LAG if summing else 0)
    reach_at = finish_at + LAG * (places - 1)
    close_at = reach_at + (2 * LAG if cross else LAG)

    def rows_of(chunk):
        return pl.ds(pl.multiple_of(chunk * ROWS, ROWS), ROWS)

    def shard(index):
        return pl.ds(pl.multiple_of(index * size, 128), size)

    def remote(source, target, out_sem, in_sem, device):
        return pltpu.make_async_remote_copy(
            src_ref=source,
            dst_ref=target,
            send_sem=out_sem,
            recv_sem=in_sem,
            device_id=device,
            device_id_type=MESH,
        )

    def left_copy(chunk):
        half = lax.rem(chunk, 2)
        return pltpu.make_async_copy(
            ref["left"].at[rows_of(chunk)], ref["left_buf"].at[half], ref["left_sem"].at[half]
        )

    barrier = pltpu.get_barrier_semaphore()
    for offset in range(1, parts):
        pl.semaphore_signal(
            barrier, inc=1, device_id={"head": lax.rem(me + offset, parts)}, device_id_type=MESH
        )
    if cross:
        for offset in range(1, slabs):
            pl.semaphore_signal(
                barrier,
                inc=1,
                device_id={"dp": lax.rem(mine_dp + offset, slabs)},
                device_id_type=MESH,
            )
    if form != "lookup":
        left_copy(0).start()
    if mode in ("grad", "grad_add"):
        ref["gain_grad"][...] = jnp.zeros_like(ref["gain_grad"])
    if form == "table":
        ref["table_grad"][...] = jnp.zeros_like(ref["table_grad"])
    pl.semaphore_wait(barrier, parts - 1 + (slabs - 1 if cross else 0))

    def valid(chunk):
        return jnp.logical_and(chunk >= 0, chunk < chunks)

    def pair_copy(chunk):
        slot = lax.rem(chunk, ring)
        return remote(
            pair_out.at[slot],
            pair_in.at[slot],
            ref["pair_out_sem"].at[slot],
            ref["pair_in_sem"].at[slot],
            twin,
        )

    def rise(chunk, place):
        slot = lax.rem(chunk, ring)
        part = from_low.at[slot, :, pl.ds((place + 1) * size, (places - 1 - place) * size)]
        return remote(part, part, ref["low_out_sem"].at[slot], ref["low_in_sem"].at[slot], upper)

    def fall(chunk, place):
        slot = lax.rem(chunk, ring)
        part = from_high.at[slot, :, pl.ds(0, place * size)]
        return remote(part, part, ref["high_out_sem"].at[slot], ref["high_in_sem"].at[slot], lower)

    def sums_copy(chunk, offset):
        slot = lax.rem(chunk, ring)
        return remote(
            ref["sums_out"].at[slot],
            ref["sums_in"].at[slot, offset - 1],
            ref["sums_out_sem"].at[slot, offset - 1],
            ref["sums_in_sem"].at[slot],
            {"head": lax.rem(me + offset, parts)},
        )

    def piece(chunk, source):
        if cross:
            return ref["stage"].at[rows_of(chunk), shard(source)]
        return full_ref.at[rows_of(chunk), shard(2 * source + core)]

    def climb(chunk, source, hop):
        part = piece(chunk, source)
        return remote(
            part,
            part,
            ref["up_out_sem"].at[chunk, hop - 1],
            ref["up_in_sem"].at[chunk, hop - 1],
            upper,
        )

    def sink(chunk, source, hop):
        part = piece(chunk, source)
        return remote(
            part,
            part,
            ref["down_out_sem"].at[chunk, hop - 1],
            ref["down_in_sem"].at[chunk, hop - 1],
            lower,
        )

    def target(chunk, giver):
        if form == "lookup":
            return full_ref.at[rows_of(chunk), shard(2 * giver + core)]
        return full_ref.at[chunk, rows_of(giver), shard(core)]

    def mirror(chunk, index):
        part = target(chunk, index) if cross else piece(chunk, index)
        return remote(
            part, part, ref["twin_out_sem"].at[chunk, index], ref["twin_in_sem"].at[chunk], twin
        )

    def hand_over(chunk, source):
        return remote(
            piece(chunk, source),
            target(chunk, mine_dp),
            ref["cross_out_sem"].at[chunk, source],
            ref["cross_in_sem"].at[chunk, mine_dp],
            {"dp": source},
        )

    def have(chunk, source):
        if not cross:
            mirror(chunk, source).start()
            return

        @pl.when(source != mine_dp)
        def _():
            hand_over(chunk, source).start()

        @pl.when(source == mine_dp)
        def _():
            values = ref["stage"][rows_of(chunk), shard(source)]
            if form == "lookup":
                full_ref[rows_of(chunk), shard(2 * mine_dp + core)] = values
            else:
                full_ref[chunk, rows_of(mine_dp), shard(core)] = values
            mirror(chunk, mine_dp).start()

    def receive(step):
        for hop in range(places):
            chunk = step - finish_at - LAG * (hop + 1)

            @pl.when(jnp.logical_and(valid(chunk), jnp.abs(spot - mine_dp) == hop))
            def _():
                for offset in range(1, slabs):
                    giver = lax.rem(mine_dp + offset, slabs)
                    part = target(chunk, giver)
                    remote(
                        part,
                        part,
                        ref["cross_out_sem"].at[chunk, giver],
                        ref["cross_in_sem"].at[chunk, giver],
                        twin,
                    ).wait_recv()
                    mirror(chunk, giver).start()

    def relay(step):
        for hop in range(1, places):
            chunk = step - finish_at - LAG * hop
            source = spot - hop

            @pl.when(jnp.logical_and(valid(chunk), source >= 0))
            def _():
                climb(chunk, source, hop).wait_recv()
                if hop < places - 1:

                    @pl.when(spot < places - 1)
                    def _():
                        climb(chunk, source, hop + 1).start()

                have(chunk, source)

            source_high = spot + hop

            @pl.when(jnp.logical_and(valid(chunk), source_high < places))
            def _():
                sink(chunk, source_high, hop).wait_recv()
                if hop < places - 1:

                    @pl.when(spot > 0)
                    def _():
                        sink(chunk, source_high, hop + 1).start()

                have(chunk, source_high)

    def finish_shard(step):
        chunk = step - finish_at

        @pl.when(valid(chunk))
        def _():
            slot = lax.rem(chunk, ring)
            rows = rows_of(chunk)
            if summing:
                sums_in = ref["sums_in"]
                pltpu.make_async_copy(
                    sums_in.at[slot], sums_in.at[slot], ref["sums_in_sem"].at[slot]
                ).wait()
                summed = ref["sums_out"][slot]
                for offset in range(1, parts):
                    summed = summed + sums_in[slot, offset - 1]
                gain = ref["gain"][0:1, :]
            if mode == "plain":
                result = total[...]
            elif mode == "norm":
                scale = lax.rsqrt(summed / D + EPSILON)
                ref["scale"][chunk] = scale
                result = ref["own"][rows, :] * down(scale, ROWS, size) * gain
            else:
                scale = down(ref["scale"][chunk], ROWS, size)
                normed = ref["inputs"][rows, :] * scale
                inner = down(summed / D, ROWS, size)
                result = scale * (ref["own"][rows, :] * gain - normed * inner)
                if mode == "grad_add":
                    result = result + ref["added"][rows, :]
                if form != "table":
                    ref["own"][rows, :] = result
            if cross:
                ref["stage"][rows, shard(spot)] = result.astype(jnp.bfloat16)
            else:
                full_ref[rows, shard(me)] = result.astype(jnp.bfloat16)

            @pl.when(spot < places - 1)
            def _():
                climb(chunk, spot, 1).start()

            @pl.when(spot > 0)
            def _():
                sink(chunk, spot, 1).start()

            have(chunk, spot)

    def add_pair(step):
        chunk = step - LAG

        @pl.when(valid(chunk))
        def _():
            slot = lax.rem(chunk, ring)
            pair_copy(chunk).wait_recv()
            partial[slot] = partial[slot] + pair_in[slot].astype(jnp.float32)

    def pass_on(step):
        for place in range(places):
            if place < places - 1:
                up_chunk = step - LAG * (1 + place)

                @pl.when(jnp.logical_and(valid(up_chunk), spot == place))
                def _():
                    slot = lax.rem(up_chunk, ring)
                    above = pl.ds((place + 1) * size, (places - 1 - place) * size)
                    values = partial[slot, :, above]
                    if place > 0:
                        rise(up_chunk, place - 1).wait_recv()
                        values = values + from_low[slot, :, above].astype(jnp.float32)
                    from_low[slot, :, above] = values.astype(jnp.bfloat16)
                    rise(up_chunk, place).start()

            if place > 0:
                down_chunk = step - LAG * (places - place)

                @pl.when(jnp.logical_and(valid(down_chunk), spot == place))
                def _():
                    slot = lax.rem(down_chunk, ring)
                    below = pl.ds(0, place * size)
                    values = partial[slot, :, below]
                    if place < places - 1:
                        fall(down_chunk, place + 1).wait_recv()
                        values = values + from_high[slot, :, below].astype(jnp.float32)
                    from_high[slot, :, below] = values.astype(jnp.bfloat16)
                    fall(down_chunk, place).start()

    def settle(step):
        chunk = step - sum_at - LAG

        @pl.when(valid(chunk))
        def _():
            pair_copy(chunk).wait_send()
            for place in range(places):

                @pl.when(spot == place)
                def _():
                    if place < places - 1:
                        rise(chunk, place).wait_send()
                    if place > 0:
                        fall(chunk, place).wait_send()

            if summing:
                for offset in range(1, parts):
                    sums_copy(chunk, offset).wait_send()

    def sum_shard(step):
        chunk = step - sum_at

        @pl.when(valid(chunk))
        def _():
            slot = lax.rem(chunk, ring)
            rows = rows_of(chunk)
            mine = shard(spot)

            @pl.when(spot == places - 1)
            def _():
                rise(chunk, places - 2).wait_recv()

            @pl.when(spot == 0)
            def _():
                fall(chunk, 1).wait_recv()

            total[...] = partial[slot, :, mine]

            @pl.when(spot > 0)
            def _():
                total[...] += from_low[slot, :, mine].astype(jnp.float32)

            @pl.when(spot < places - 1)
            def _():
                total[...] += from_high[slot, :, mine].astype(jnp.float32)

            if not summing:
                return
            value = total[...]
            if mode == "norm":
                value = value + ref["inputs"][rows, :]
                column = jnp.sum(value * value, 1, keepdims=True)
            else:
                scale = down(ref["scale"][chunk], ROWS, size)
                normed = ref["inputs"][rows, :] * scale
                ref["gain_grad"][0:1, :] += jnp.sum(value * normed, 0, keepdims=True)
                column = jnp.sum(value * ref["gain"][0:1, :] * normed, 1, keepdims=True)
            ref["own"][rows, :] = value
            ref["sums_out"][slot] = across(column, ROWS)
            for offset in range(1, parts):
                sums_copy(chunk, offset).start()

    def produce(step):
        chunk = step

        @pl.when(valid(chunk))
        def _():
            slot = lax.rem(chunk, ring)
            right_ref = ref["right"]
            if form == "lookup":
                entries = right_ref.shape[0]
                for group in range(slabs):
                    ids = ref["ids"][group, rows_of(chunk), 0:1]
                    spots = lax.broadcasted_iota(jnp.int32, (ROWS, entries), 1)
                    hits = (spots == ids).astype(jnp.bfloat16)
                    lanes = pl.ds(group * size, size)
                    pair_out[slot, :, lanes] = dot_ab(hits, right_ref[:, shard(1 - core)]).astype(
                        jnp.bfloat16
                    )
                    partial[slot, :, lanes] = dot_ab(hits, right_ref[:, shard(core)])
                pair_copy(chunk).start()
                return
            half = lax.rem(chunk, 2)
            left_copy(chunk).wait()

            @pl.when(chunk + 1 < chunks)
            def _():
                left_copy(chunk + 1).start()

            def term(index):
                if form in ("turned", "table"):
                    return dot_abt(ref["left_buf"][half], right_ref[shard(index), :])
                return dot_ab(ref["left_buf"][half], right_ref[:, shard(index)])

            for place in range(places):
                lanes = pl.ds(place * size, size)
                pair_out[slot, :, lanes] = term(2 * place + 1 - core).astype(jnp.bfloat16)
            pair_copy(chunk).start()
            for place in range(places):
                lanes = pl.ds(place * size, size)
                partial[slot, :, lanes] = term(2 * place + core)

    def close(step):
        chunk = step - close_at

        @pl.when(valid(chunk))
        def _():
            if form == "table":
                arrived = full_ref.at[chunk, :, pl.ds(0, size)]
            else:
                arrived = full_ref.at[rows_of(chunk), pl.ds(0, places * size)]
            pltpu.make_async_copy(arrived, arrived, ref["twin_in_sem"].at[chunk]).wait()
            for index in range(places):
                mirror(chunk, index).wait_send()
            if cross:
                for offset in range(1, slabs):
                    hand_over(chunk, lax.rem(mine_dp + offset, slabs)).wait_send()
            for hop in range(1, places):
                source = spot - hop + 1

                @pl.when(jnp.logical_and(source >= 0, spot < places - 1))
                def _():
                    climb(chunk, source, hop).wait_send()

                source_high = spot + hop - 1

                @pl.when(jnp.logical_and(source_high < places, spot > 0))
                def _():
                    sink(chunk, source_high, hop).wait_send()

            if form == "table":
                table_grad = ref["table_grad"]
                entries = table_grad.shape[0]
                pieces = 5 if entries % 80 == 0 else 1
                block = entries // pieces
                ids = ref["ids"][chunk, 0:1, :]
                values = full_ref[chunk]
                for index in range(pieces):
                    spots = index * block + lax.broadcasted_iota(
                        jnp.int32, (block, ids.shape[1]), 0
                    )
                    hits = (spots == ids).astype(jnp.bfloat16)
                    span = pl.ds(index * block, block)
                    table_grad[span, :] += dot_ab(hits, values)

    def advance(step, carried):
        relay(step)
        if summing:
            finish_shard(step)
        if cross:
            receive(step)
        add_pair(step)
        pass_on(step)
        settle(step)
        sum_shard(step)
        if not summing:
            finish_shard(step)
        produce(step)
        close(step)
        return carried

    lax.fori_loop(0, chunks + close_at, advance, 0)


def transit(
    mode,
    form,
    number,
    parts,
    slabs,
    right,
    tokens,
    size,
    left=None,
    inputs=None,
    gain=None,
    scale=None,
    added=None,
    ids=None,
    entries=None,
):
    chunks = tokens // ROWS
    places = parts // 2
    cross = form in ("lookup", "table")
    summing = mode != "plain"
    ring = min(chunks, LAG * (places + 1) + 2) if summing else chunks
    dma = pltpu.SemaphoreType.DMA
    low, wide_kind = jnp.bfloat16, jnp.float32
    vmem = pl.BlockSpec(memory_space=pltpu.VMEM)
    operands, specs, outputs, scratch = {}, [], {}, {}

    def take(name, array, spec=vmem):
        operands[name] = array
        specs.append(spec)

    take("right", right)
    if left is not None:
        take("left", left, pl.BlockSpec(memory_space=pl.ANY))
    if ids is not None:
        take("ids", ids)
    if summing:
        take("inputs", inputs)
        take("gain", gain)
    if mode in ("grad", "grad_add"):
        take("scale", scale)
    if mode == "grad_add":
        take("added", added)

    if summing and form != "table":
        outputs["own"] = ((tokens, size), wide_kind)
    if form != "table":
        outputs["full"] = ((tokens, parts * size), low)
    if mode == "norm":
        outputs["scale"] = ((chunks, 8, ROWS), wide_kind)
    if mode in ("grad", "grad_add"):
        outputs["gain_grad"] = ((8, size), wide_kind)
    if form == "table":
        outputs["table_grad"] = ((entries, 2 * size), wide_kind)

    span = places * size
    hops = max(places - 1, 1)
    if form == "table":
        scratch["own"] = pltpu.VMEM((tokens, size), wide_kind)
        scratch["full"] = pltpu.VMEM((chunks, slabs * ROWS, 2 * size), low)
    if left is not None:
        scratch["left_buf"] = pltpu.VMEM((2, ROWS, left.shape[1]), low)
        scratch["left_sem"] = dma((2,))
    if cross:
        scratch["stage"] = pltpu.VMEM((tokens, span), low)
        scratch["cross_out_sem"] = dma((chunks, slabs))
        scratch["cross_in_sem"] = dma((chunks, slabs))
    if summing:
        scratch["sums_out"] = pltpu.VMEM((ring, 8, ROWS), wide_kind)
        scratch["sums_in"] = pltpu.VMEM((ring, parts - 1, 8, ROWS), wide_kind)
        scratch["sums_out_sem"] = dma((ring, parts - 1))
        scratch["sums_in_sem"] = dma((ring,))
    scratch["total"] = pltpu.VMEM((ROWS, size), wide_kind)
    scratch["partial"] = pltpu.VMEM((ring, ROWS, span), wide_kind)
    for name in ("pair_out", "pair_in", "from_low", "from_high"):
        scratch[name] = pltpu.VMEM((ring, ROWS, span), low)
    for name in ("pair_out", "pair_in", "low_out", "low_in", "high_out", "high_in"):
        scratch[name + "_sem"] = dma((ring,))
    for name in ("up_out", "up_in", "down_out", "down_in"):
        scratch[name + "_sem"] = dma((chunks, hops))
    scratch["twin_out_sem"] = dma((chunks, places))
    scratch["twin_in_sem"] = dma((chunks,))

    depth = right.shape[1] if form in ("turned", "table") else right.shape[0]
    names = tuple(operands) + tuple(outputs) + tuple(scratch)
    results = pl.pallas_call(
        functools.partial(transit_kernel, mode, form, parts, slabs, names),
        in_specs=specs,
        out_specs=[vmem] * len(outputs),
        out_shape=[jax.ShapeDtypeStruct(shape, kind) for shape, kind in outputs.values()],
        scratch_shapes=list(scratch.values()),
        compiler_params=pltpu.CompilerParams(
            collective_id=number, has_side_effects=True, vmem_limit_bytes=60 * 1024 * 1024
        ),
        cost_estimate=pl.CostEstimate(
            flops=2 * tokens * depth * parts * size,
            bytes_accessed=128 * tokens * parts * size,
            transcendentals=0,
        ),
        name="transit_" + form,
    )(*operands.values())
    return dict(zip(outputs, results))


def shampoo(tile_w, tile_g, left, right, left_root, right_root):
    low_g = tile_g.astype(jnp.bfloat16)

    def product(form, one, two):
        return jnp.einsum(
            form,
            one.astype(jnp.bfloat16),
            two.astype(jnp.bfloat16),
            preferred_element_type=jnp.float32,
        )

    new_left = STAT_DECAY * left + (1.0 - STAT_DECAY) * product("abrc,absc->abrs", low_g, low_g)
    new_right = STAT_DECAY * right + (1.0 - STAT_DECAY) * product("abrc,abrd->abcd", low_g, low_g)
    turned = product("abrs,absc->abrc", left_root, low_g)
    turned = product("abrc,abcd->abrd", turned, right_root)
    return (new_left, new_right, tile_w - MATRIX_RATE * (turned + WEIGHT_DECAY * tile_w))


def refresh(master, grad, left, right, left_root, right_root):
    rows = master.shape[1]
    new_left, new_right, new_w = shampoo(
        master.reshape(1, 1, rows, -1),
        grad.reshape(1, 1, rows, -1),
        left,
        right,
        left_root,
        right_root,
    )
    return (grad, new_left, new_right, new_w.reshape(master.shape))


def adamw(weight, grad, first, second, step_rate):
    new_first = BETA_ONE * first + (1.0 - BETA_ONE) * grad
    new_second = BETA_TWO * second + (1.0 - BETA_TWO) * grad * grad
    moved = (
        new_first
        / (1.0 - BETA_ONE**STEP)
        / (jnp.sqrt(new_second / (1.0 - BETA_TWO**STEP)) + ADAM_EPSILON)
    )
    return (new_first, new_second, weight - step_rate * (moved + WEIGHT_DECAY * weight))


def layer_forward(
    token_ids, targets, valid, resets, emb_low, weights, inner_init, gains, head_index
):
    w_qkv, w_out, w_gu, w_down, table = weights
    parts, slabs = lax.axis_size("head"), lax.axis_size("dp")
    vocab_part = table.shape[0]
    tokens, size = token_ids.shape[0], gains.shape[1]
    chunks = tokens // ROWS
    columns = jnp.arange(vocab_part, dtype=jnp.int32)
    local_ids = lax.all_gather(token_ids, "dp", axis=0) - head_index * vocab_part
    spread_ids = jnp.broadcast_to(local_ids[:, :, None], (slabs, tokens, 128))
    first = transit("plain", "lookup", 1, parts, slabs, emb_low, tokens, size, ids=spread_ids)
    low_embedded = first["full"]
    wide_embedded = low_embedded.astype(jnp.float32)
    scale_one = lax.rsqrt(jnp.mean(wide_embedded * wide_embedded, -1) + EPSILON)
    gain_one = lax.all_gather(gains[0], "head", axis=0, tiled=True)
    full_one = (wide_embedded * scale_one[:, None] * gain_one[None]).astype(jnp.bfloat16)
    embedded = lax.dynamic_slice_in_dim(low_embedded, head_index * size, size, 1)
    embedded = embedded.astype(jnp.float32)
    scale_one = jnp.broadcast_to(scale_one.reshape(chunks, 1, ROWS), (chunks, 8, ROWS))
    mixed = jnp.dot(full_one, w_qkv, preferred_element_type=jnp.float32).astype(jnp.bfloat16)
    step_rate = jax.nn.sigmoid(gains[3:4]) / (8 * P_SIZE)
    masks = mixer_masks(resets, tokens)
    initial_pairs = pair_blocks(inner_init)
    inner_low, residue, states = mixer_forward(mixed, step_rate, initial_pairs, masks)
    second = transit(
        "norm",
        "rows",
        2,
        parts,
        slabs,
        w_out,
        tokens,
        size,
        left=inner_low,
        inputs=embedded,
        gain=gains[1:2],
    )
    hidden_one, full_two, scale_two = second["own"], second["full"], second["scale"]
    gate_up = jnp.dot(full_two, w_gu, preferred_element_type=jnp.float32)

    def swiglu(paired):
        halves = paired.reshape(tokens, 2, -1)
        return jax.nn.silu(halves[:, 0]) * halves[:, 1]

    activated, act_pull = jax.vjp(swiglu, gate_up)
    act_low = activated.astype(jnp.bfloat16)
    third = transit(
        "norm",
        "rows",
        3,
        parts,
        slabs,
        w_down,
        tokens,
        size,
        left=act_low,
        inputs=hidden_one,
        gain=gains[2:3],
    )
    hidden_two, full_end, scale_end = third["own"], third["full"], third["scale"]
    logits = jnp.einsum("td,vd->tv", full_end, table, preferred_element_type=jnp.float32)
    peak = jnp.max(logits, -1)
    target_hits = columns[None, :] == (targets - head_index * vocab_part)[:, None]
    stats = lax.all_gather(
        jnp.stack(
            [
                peak,
                jnp.sum(jnp.exp(logits - peak[:, None]), -1),
                jnp.sum(jnp.where(target_hits, logits, 0.0), -1),
            ]
        ),
        "head",
        axis=0,
    )
    highest = jnp.max(stats[:, 0], 0)
    exp_sum = jnp.sum(stats[:, 1] * jnp.exp(stats[:, 0] - highest[None]), 0)
    target_logit = jnp.sum(stats[:, 2], 0)
    totals = highest + jnp.log(exp_sum)
    counted = valid.astype(jnp.float32)
    d_logits = (
        (jnp.exp(logits - totals[:, None]) - target_hits.astype(jnp.float32)) * counted[:, None]
    ).astype(jnp.bfloat16)
    kept = (
        embedded,
        scale_one,
        full_one,
        (mixed, step_rate, initial_pairs, masks, residue, states),
        inner_low,
        hidden_one,
        scale_two,
        full_two,
        act_pull,
        act_low,
        hidden_two,
        scale_end,
        full_end,
        d_logits,
        local_ids,
    )
    return (jnp.sum((totals - target_logit) * counted), jnp.sum(counted), kept)


def slots_of(grad, order, kinds):
    parts = lax.axis_size("dp")
    shaped = grad.astype(jnp.bfloat16).reshape(parts, -1, kinds, grad.shape[1] // kinds)
    return jnp.take(shaped, order, axis=0, mode="clip")


def column_slots_of(grad, order):
    parts = lax.axis_size("dp")
    shaped = grad.astype(jnp.bfloat16).reshape(grad.shape[0], parts, -1)
    return jnp.take(jnp.swapaxes(shaped, 0, 1), order, axis=0, mode="clip")


def scatter_dp(grad, dimension):
    return lax.psum_scatter(grad, "dp", scatter_dimension=dimension, tiled=True)


def layer_backward(kept, weights, gains, order):
    (
        embedded,
        scale_one,
        full_one,
        inner_kept,
        inner_low,
        hidden_one,
        scale_two,
        full_two,
        act_pull,
        act_low,
        hidden_two,
        scale_end,
        full_end,
        d_logits,
        local_ids,
    ) = kept
    w_qkv, w_out, w_gu, w_down, table = weights
    parts, slabs = lax.axis_size("head"), lax.axis_size("dp")
    tokens, size = embedded.shape
    chunks = tokens // ROWS
    wide_kind = jnp.float32
    fourth = transit(
        "grad",
        "rows",
        4,
        parts,
        slabs,
        table,
        tokens,
        size,
        left=d_logits,
        inputs=hidden_two,
        gain=gains[2:3],
        scale=scale_end,
    )
    d_two, d_down_in = fourth["own"], fourth["full"]
    grad_table = jnp.einsum("tv,td->vd", d_logits, full_end, preferred_element_type=wide_kind)
    grad_table = grad_table.astype(jnp.bfloat16)
    d_act = jnp.einsum("td,fd->tf", d_down_in, w_down, preferred_element_type=wide_kind)
    d_gate_up = act_pull(d_act)[0].astype(jnp.bfloat16)
    grad_down = jnp.einsum("tf,td->fd", act_low, d_down_in, preferred_element_type=wide_kind)
    slot_down = column_slots_of(grad_down, order[3])
    d_gate_up, grad_table, slot_down = lax.optimization_barrier(
        (d_gate_up, grad_table, slot_down)
    )
    owned_table = scatter_dp(grad_table, 1)
    owned_down = scatter_dp(slot_down, 0)
    fifth = transit(
        "grad_add",
        "turned",
        5,
        parts,
        slabs,
        w_gu,
        tokens,
        size,
        left=d_gate_up,
        inputs=hidden_one,
        gain=gains[1:2],
        scale=scale_two,
        added=d_two,
    )
    d_one, d_out_in = fifth["own"], fifth["full"]
    d_inner = jnp.einsum("td,cd->tc", d_out_in, w_out, preferred_element_type=wide_kind)
    grad_gu = jnp.einsum("td,tc->dc", full_two, d_gate_up, preferred_element_type=wide_kind)
    slot_gu = slots_of(grad_gu, order[2], 2)
    d_inner, slot_gu = lax.optimization_barrier((d_inner, slot_gu))
    owned_gu = scatter_dp(slot_gu, 0)
    d_mixed, grad_pairs, grad_step = mixer_backward(*inner_kept, d_inner)
    grad_init = head_blocks(grad_pairs)
    gate = jax.nn.sigmoid(gains[3])
    grad_rate = grad_step[0] * gate * (1.0 - gate) / (8 * P_SIZE)
    grad_out = jnp.einsum("tc,td->cd", inner_low, d_out_in, preferred_element_type=wide_kind)
    grad_qkv = jnp.einsum("td,tc->dc", full_one, d_mixed, preferred_element_type=wide_kind)
    slot_out = column_slots_of(grad_out, order[1])
    slot_qkv = slots_of(grad_qkv, order[0], 3)
    d_mixed, slot_out, slot_qkv = lax.optimization_barrier((d_mixed, slot_out, slot_qkv))
    owned_out = scatter_dp(slot_out, 0)
    owned_qkv = scatter_dp(slot_qkv, 0)
    row_ids = jnp.swapaxes(local_ids.reshape(slabs, chunks, ROWS), 0, 1)
    row_ids = jnp.broadcast_to(
        row_ids.reshape(chunks, 1, slabs * ROWS), (chunks, 8, slabs * ROWS)
    )
    sixth = transit(
        "grad_add",
        "table",
        6,
        parts,
        slabs,
        w_qkv,
        tokens,
        size,
        left=d_mixed,
        inputs=embedded,
        gain=gains[0:1],
        scale=scale_one,
        added=d_one,
        ids=row_ids,
        entries=table.shape[0],
    )
    owned_table = owned_table.astype(wide_kind) + sixth["table_grad"]
    gain_rows = [sixth["gain_grad"][0], fifth["gain_grad"][0], fourth["gain_grad"][0], grad_rate]
    owned = tuple(
        piece.astype(wide_kind) for piece in (owned_qkv, owned_out, owned_gu, owned_down)
    )
    return owned + (owned_table,), grad_init, jnp.stack(gain_rows, 0)


def shards(
    token_ids,
    targets,
    valid,
    resets,
    owners,
    emb_master,
    emb_first,
    emb_second,
    qkv_master,
    qkv_left,
    qkv_right,
    qkv_left_root,
    qkv_right_root,
    out_master,
    out_left,
    out_right,
    out_left_root,
    out_right_root,
    gu_master,
    gu_left,
    gu_right,
    gu_left_root,
    gu_right_root,
    down_master,
    down_left,
    down_right,
    down_left_root,
    down_right_root,
    inner_init,
    inner_first,
    inner_second,
    gains,
    gains_first,
    gains_second,
):
    low = jnp.bfloat16
    emb_low = emb_master.astype(low)
    gathered = (
        lax.all_gather(qkv_master.astype(low), "dp", axis=0, tiled=True),
        lax.all_gather(out_master.astype(low), "dp", axis=0, tiled=True),
        lax.all_gather(gu_master.astype(low), "dp", axis=0, tiled=True),
        lax.all_gather(down_master.astype(low), "dp", axis=0, tiled=True),
        lax.all_gather(emb_low, "dp", axis=1, tiled=True),
    )
    w_qkv = jnp.take(gathered[0], owners[0], axis=0, mode="clip").reshape(D, -1)
    w_out = jnp.take(gathered[1], owners[1], axis=0, mode="clip")
    w_out = jnp.swapaxes(w_out, 0, 1).reshape(w_out.shape[1], D)
    w_gu = jnp.take(gathered[2], owners[2], axis=0, mode="clip").reshape(D, -1)
    w_down = jnp.take(gathered[3], owners[3], axis=0, mode="clip")
    w_down = jnp.swapaxes(w_down, 0, 1).reshape(w_down.shape[1], D)
    weights = (w_qkv, w_out, w_gu, w_down, gathered[4])
    head_index = lax.axis_index("head")
    loss_local, count_local, kept = layer_forward(
        token_ids, targets, valid, resets, emb_low, weights, inner_init, gains, head_index
    )
    loss_sum, count = lax.psum((loss_local, count_local), "dp")
    order = jnp.argsort(owners, axis=1)
    owned, grad_init, grad_gains = layer_backward(kept, weights, gains, order)
    small = lax.psum((grad_init, grad_gains), "dp")
    first_dp = (lax.axis_index("dp") == 0).astype(jnp.float32)
    squares = sum((jnp.sum(piece * piece) for piece in owned))
    squares = squares + first_dp * (jnp.sum(small[0] * small[0]) + jnp.sum(small[1] * small[1]))
    squares_all = lax.psum(squares, ("dp", "head"))
    grad_norm = jnp.sqrt(squares_all) / count
    factor = jnp.minimum(1.0, CLIP_LIMIT / grad_norm) / count
    qkv_out = refresh(
        qkv_master, owned[0] * factor, qkv_left, qkv_right, qkv_left_root, qkv_right_root
    )
    out_out = refresh(
        out_master, owned[1] * factor, out_left, out_right, out_left_root, out_right_root
    )
    gu_out = refresh(gu_master, owned[2] * factor, gu_left, gu_right, gu_left_root, gu_right_root)
    down_out = refresh(
        down_master, owned[3] * factor, down_left, down_right, down_left_root, down_right_root
    )
    table_out = adamw(emb_master, owned[4] * factor, emb_first, emb_second, TABLE_RATE)
    init_out = adamw(inner_init, small[0] * factor, inner_first, inner_second, INITIAL_RATE)
    gain_out = adamw(gains, small[1] * factor, gains_first, gains_second, GAINS_RATE)
    return (
        (jnp.stack([loss_sum, count]), grad_norm)
        + table_out
        + qkv_out
        + out_out
        + gu_out
        + down_out
        + init_out
        + gain_out
    )


def solution(mesh):
    placed = (
        P("dp"),
        P("dp"),
        P("dp"),
        P("dp"),
        P(),
        P("head", "dp"),
        P("head", "dp"),
        P("head", "dp"),
        P("dp", None, None, "head"),
        P("dp", "head", None, None),
        P("dp", "head", None, None),
        P("dp", "head", None, None),
        P("dp", "head", None, None),
        P("dp", "head", None),
        P("dp", "head", None, None),
        P("dp", "head", None, None),
        P("dp", "head", None, None),
        P("dp", "head", None, None),
        P("dp", None, None, "head"),
        P("dp", "head", None, None),
        P("dp", "head", None, None),
        P("dp", "head", None, None),
        P("dp", "head", None, None),
        P("dp", "head", None),
        P("dp", "head", None, None),
        P("dp", "head", None, None),
        P("dp", "head", None, None),
        P("dp", "head", None, None),
        P("head", None, None),
        P("head", None, None),
        P("head", None, None),
        P(None, "head"),
        P(None, "head"),
        P(None, "head"),
    )
    return jax.shard_map(
        shards,
        mesh=mesh,
        in_specs=placed,
        out_specs=(
            P(),
            P(),
            P("head", "dp"),
            P("head", "dp"),
            P("head", "dp"),
            P("dp", None, None, "head"),
            P("dp", "head", None, None),
            P("dp", "head", None, None),
            P("dp", None, None, "head"),
            P("dp", "head", None),
            P("dp", "head", None, None),
            P("dp", "head", None, None),
            P("dp", "head", None),
            P("dp", None, None, "head"),
            P("dp", "head", None, None),
            P("dp", "head", None, None),
            P("dp", None, None, "head"),
            P("dp", "head", None),
            P("dp", "head", None, None),
            P("dp", "head", None, None),
            P("dp", "head", None),
            P("head", None, None),
            P("head", None, None),
            P("head", None, None),
            P(None, "head"),
            P(None, "head"),
            P(None, "head"),
        ),
        check_vma=False,
    )
```

```python
import functools

import jax
import jax.numpy as jnp
from jax import lax
from jax.experimental import pallas as pl
from jax.experimental.pallas import tpu as pltpu
from jax.sharding import PartitionSpec as P

D = 2048
P_SIZE = 64
MB = 16
STEP = 10


EPSILON = 1e-05
CLIP_LIMIT = 0.05
STAT_DECAY = 0.5
MATRIX_RATE = 0.4
TABLE_RATE = 0.3
INITIAL_RATE = 0.05
GAINS_RATE = 0.3
BETA_ONE = 0.9
BETA_TWO = 0.95
ADAM_EPSILON = 1e-08
WEIGHT_DECAY = 0.01


CHUNK = 64
PAIR = 2 * P_SIZE


def dot_ab(left, right):
    return lax.dot_general(left, right, (((1,), (0,)), ((), ())), preferred_element_type=jnp.float32)


def dot_abt(left, right):
    return lax.dot_general(left, right, (((1,), (1,)), ((), ())), preferred_element_type=jnp.float32)


def dot_atb(left, right):
    return lax.dot_general(left, right, (((0,), (0,)), ((), ())), preferred_element_type=jnp.float32)


def halves_of(value):
    high = value.astype(jnp.bfloat16)
    return (high, (value - high.astype(jnp.float32)).astype(jnp.bfloat16))


def wide(form, left, right):
    lefts = left if isinstance(left, tuple) else (left,)
    rights = right if isinstance(right, tuple) else (right,)
    total = form(lefts[0], rights[0])
    if len(rights) > 1:
        total = total + form(lefts[0], rights[1])
    if len(lefts) > 1:
        total = total + form(lefts[1], rights[0])
    return total


def each(pieces, change):
    return tuple(change(piece) for piece in pieces) if isinstance(pieces, tuple) else change(pieces)


def mixer_masks(resets, tokens):
    per_chunk = CHUNK // MB
    chunks = tokens // CHUNK
    segment = jnp.cumsum(resets.reshape(chunks, per_chunk), axis=1)
    segment = jnp.repeat(segment, MB, axis=1)
    same = segment[:, :, None] == segment[:, None, :]
    spot = jnp.arange(CHUNK, dtype=jnp.int32)
    causal = (spot[None, :] <= spot[:, None])[None]
    earlier = ((spot[None, :] // MB) < (spot[:, None] // MB))[None]
    causal = (same & causal).astype(jnp.float32)
    earlier = (same & earlier).astype(jnp.float32)
    first = (segment == 0).astype(jnp.float32).reshape(tokens, 1)
    last = (segment == segment[:, -1:]).astype(jnp.float32).reshape(tokens, 1)
    anew = (segment[:, -1] > 0).astype(jnp.float32)
    first = jnp.broadcast_to(first, (tokens, PAIR))
    last = jnp.broadcast_to(last, (tokens, PAIR))
    anew = jnp.broadcast_to(anew[:, None, None], (chunks, 8, PAIR))
    return causal, earlier, first, last, anew


def lane_helpers(rows):
    lanes = lax.broadcasted_iota(jnp.int32, (rows, PAIR), 1)
    low_lane = lanes < P_SIZE
    low_half = low_lane.astype(jnp.float32)
    high_half = 1.0 - low_half

    def stack(pieces):
        def one(piece):
            kind = piece.dtype
            return jnp.concatenate(
                [piece * low_half.astype(kind), piece * high_half.astype(kind)], 0
            )

        return each(pieces, one)

    def pick(product):
        return jnp.where(low_lane, product[:rows], product[rows:])

    return stack, pick


def diagonal_blocks():
    rows = lax.broadcasted_iota(jnp.int32, (PAIR, PAIR), 0) // P_SIZE
    columns = lax.broadcasted_iota(jnp.int32, (PAIR, PAIR), 1) // P_SIZE
    return (rows == columns).astype(jnp.float32)


def solve(matrix, rate_row, value, pick):
    rows = value.shape[0]
    powers = [(matrix, rate_row)]
    reach = 2
    while reach < CHUNK // MB:
        last, rate = powers[-1]
        low, high = halves_of(last[:rows]), halves_of(last[rows:])
        powers.append(
            (
                jnp.concatenate([wide(dot_ab, low, low), wide(dot_ab, high, high)], 0),
                rate * rate,
            )
        )
        reach = 2 * reach
    for index in range(len(powers) - 1, -1, -1):
        factor, rate = powers[index]
        moved = pick(wide(dot_ab, halves_of(factor), halves_of(value * rate)))
        value = value - moved if index == 0 else value + moved
    return value


def mixer_forward_kernel(
    qkv_ref,
    rate_ref,
    initial_ref,
    causal_ref,
    earlier_ref,
    first_ref,
    last_ref,
    anew_ref,
    z_ref,
    residue_ref,
    states_ref,
    state,
):
    pairs = initial_ref.shape[0]
    width = pairs * PAIR

    @pl.when(pl.program_id(0) == 0)
    def _():
        state[...] = jnp.zeros_like(state)

    stack, pick = lane_helpers(CHUNK)
    blocks = diagonal_blocks()
    causal = causal_ref[0]
    causal = jnp.concatenate([causal, causal], 0)
    earlier = earlier_ref[0]
    earlier = jnp.concatenate([earlier, earlier], 0)
    first = first_ref[...] > 0.0
    last = last_ref[...]
    anew = anew_ref[0, 0:1, :]
    for pair in range(pairs):
        lanes = slice(pair * PAIR, (pair + 1) * PAIR)
        query = qkv_ref[:, lanes]
        key = qkv_ref[:, width + pair * PAIR : width + (pair + 1) * PAIR]
        value = qkv_ref[:, 2 * width + pair * PAIR : 2 * width + (pair + 1) * PAIR]
        rate = rate_ref[0:1, lanes]
        begin = state[pair]
        initial = initial_ref[pair]
        states_ref[0, pair] = begin
        products = dot_abt(jnp.concatenate([stack(key), stack(query)], 0), key)
        ties = products[: 2 * CHUNK] * earlier
        scores = products[2 * CHUNK :] * causal
        both = jnp.concatenate([key, query], 0)
        seen = wide(dot_ab, both, halves_of(begin))
        fresh = wide(dot_ab, both, halves_of(initial))
        key_seen = jnp.where(first, seen[:CHUNK], fresh[:CHUNK])
        query_seen = jnp.where(first, seen[CHUNK:], fresh[CHUNK:])
        key_wide = key.astype(jnp.float32)
        residue = solve(ties, rate, key_seen - (value.astype(jnp.float32) - key_wide), pick)
        residue_ref[:, lanes] = residue
        scaled = residue * rate
        scaled_parts = halves_of(scaled)
        output = query_seen - pick(wide(dot_ab, halves_of(scores), scaled_parts))
        z_ref[:, lanes] = output.astype(jnp.bfloat16)
        key_last = (key_wide * last).astype(jnp.bfloat16)
        base = jnp.where(anew > 0.0, initial, begin)
        state[pair] = base - blocks * wide(dot_atb, key_last, scaled_parts)


def mixer_backward_kernel(
    qkv_ref,
    rate_ref,
    initial_ref,
    causal_ref,
    earlier_ref,
    causal_turned_ref,
    earlier_turned_ref,
    first_ref,
    last_ref,
    anew_ref,
    residue_ref,
    states_ref,
    upstream_ref,
    grad_ref,
    grad_initial_ref,
    grad_rate_ref,
    carried,
):
    pairs = initial_ref.shape[0]
    width = pairs * PAIR

    @pl.when(pl.program_id(0) == 0)
    def _():
        carried[...] = jnp.zeros_like(carried)
        grad_initial_ref[...] = jnp.zeros_like(grad_initial_ref)
        grad_rate_ref[...] = jnp.zeros_like(grad_rate_ref)

    stack, pick = lane_helpers(CHUNK)
    blocks = diagonal_blocks()

    def doubled(ref):
        return jnp.concatenate([ref[0], ref[0]], 0)

    causal, earlier = doubled(causal_ref), doubled(earlier_ref)
    causal_turned, earlier_turned = doubled(causal_turned_ref), doubled(earlier_turned_ref)
    first_wide = first_ref[...]
    first = first_wide > 0.0
    last = last_ref[...]
    anew = anew_ref[0, 0:1, :]
    low = jnp.bfloat16
    for pair in range(pairs):
        lanes = slice(pair * PAIR, (pair + 1) * PAIR)
        query = qkv_ref[:, lanes]
        key = qkv_ref[:, width + pair * PAIR : width + (pair + 1) * PAIR]
        rate = rate_ref[0:1, lanes]
        begin = halves_of(states_ref[0, pair])
        initial = halves_of(initial_ref[pair])
        after = carried[pair]
        after_parts = halves_of(after)
        residue = residue_ref[:, lanes]
        scaled = halves_of(residue * rate)
        upstream = upstream_ref[:, lanes]
        upstream_parts = halves_of(upstream)
        key_wide = key.astype(jnp.float32)
        query_wide = query.astype(jnp.float32)
        key_last = (key_wide * last).astype(low)
        key_stack = stack(key)
        products = dot_abt(key_stack, jnp.concatenate([key, query], 0))
        ties_turned = products[:, :CHUNK] * earlier_turned
        scores_turned = products[:, CHUNK:] * causal_turned
        pulled = pick(wide(dot_ab, halves_of(scores_turned), upstream_parts))
        pulled = pulled + wide(dot_ab, key_last, after_parts)
        grad_scaled = solve(ties_turned, rate, -pulled, pick)
        grad_rate_ref[0:1, lanes] += jnp.sum(grad_scaled * residue, 0, keepdims=True)
        grad_residue = grad_scaled * rate
        residue_parts = halves_of(grad_residue)
        joined = tuple(
            jnp.concatenate([one, two], 0) for one, two in zip(upstream_parts, residue_parts)
        )
        scaled_stack = stack(scaled)
        turned = wide(dot_abt, scaled_stack, joined)
        straight = wide(
            dot_abt,
            tuple(
                jnp.concatenate([stack(one), stack(two)], 0)
                for one, two in zip(upstream_parts, residue_parts)
            ),
            scaled,
        )
        grad_scores = -straight[: 2 * CHUNK] * causal
        grad_scores_turned = -turned[:, :CHUNK] * causal_turned
        grad_ties = -(straight[2 * CHUNK :] * earlier + turned[:, CHUNK:] * earlier_turned)
        seen = wide(dot_abt, joined, begin)
        fresh = wide(dot_abt, joined, initial)
        grad_query = jnp.where(first, seen[:CHUNK], fresh[:CHUNK])
        grad_query = grad_query + pick(wide(dot_ab, halves_of(grad_scores), key))
        grad_key = jnp.where(first, seen[CHUNK:], fresh[CHUNK:]) + grad_residue
        grad_key = grad_key + pick(
            wide(dot_ab, halves_of(grad_scores_turned), query)
            + wide(dot_ab, halves_of(grad_ties), key)
        )
        grad_key = grad_key - last * wide(dot_abt, scaled, after_parts)
        grad_ref[:, lanes] = grad_query.astype(low)
        grad_ref[:, width + pair * PAIR : width + (pair + 1) * PAIR] = grad_key.astype(low)
        grad_ref[:, 2 * width + pair * PAIR : 2 * width + (pair + 1) * PAIR] = (
            -grad_residue
        ).astype(low)
        fronts = jnp.concatenate([query_wide * first_wide, key_wide * first_wide], 0).astype(low)
        backs = jnp.concatenate(
            [query_wide * (1.0 - first_wide), key_wide * (1.0 - first_wide)], 0
        ).astype(low)
        kept_after = jnp.where(anew > 0.0, 0.0, after)
        carried[pair] = kept_after + blocks * wide(dot_atb, fronts, joined)
        grad_initial_ref[pair] += (after - kept_after) + blocks * wide(dot_atb, backs, joined)


def pair_blocks(matrices):
    heads = matrices.shape[0]
    split = matrices.reshape(heads // 2, 2, P_SIZE, P_SIZE)
    empty = jnp.zeros_like(split[:, 0])
    upper = jnp.concatenate([split[:, 0], empty], 2)
    lower = jnp.concatenate([empty, split[:, 1]], 2)
    return jnp.concatenate([upper, lower], 1)


def head_blocks(pairs):
    return jnp.stack([pairs[:, :P_SIZE, :P_SIZE], pairs[:, P_SIZE:, P_SIZE:]], 1).reshape(
        -1, P_SIZE, P_SIZE
    )


def mixer_forward(qkv, rate, initial, masks):
    tokens = qkv.shape[0]
    width = rate.shape[1]
    pairs = initial.shape[0]
    chunks = tokens // CHUNK
    whole = lambda shape: pl.BlockSpec(shape, lambda i: (0,) * len(shape))
    square = pl.BlockSpec((1, CHUNK, CHUNK), lambda i: (i, 0, 0))
    column = pl.BlockSpec((CHUNK, PAIR), lambda i: (i, 0))
    causal, earlier, first, last, anew = masks
    return pl.pallas_call(
        mixer_forward_kernel,
        grid=(chunks,),
        in_specs=[
            pl.BlockSpec((CHUNK, 3 * width), lambda i: (i, 0)),
            whole((1, width)),
            whole((pairs, PAIR, PAIR)),
            square,
            square,
            column,
            column,
            pl.BlockSpec((1, 8, PAIR), lambda i: (i, 0, 0)),
        ],
        out_specs=[
            pl.BlockSpec((CHUNK, width), lambda i: (i, 0)),
            pl.BlockSpec((CHUNK, width), lambda i: (i, 0)),
            pl.BlockSpec((1, pairs, PAIR, PAIR), lambda i: (i, 0, 0, 0)),
        ],
        out_shape=[
            jax.ShapeDtypeStruct((tokens, width), jnp.bfloat16),
            jax.ShapeDtypeStruct((tokens, width), jnp.float32),
            jax.ShapeDtypeStruct((chunks, pairs, PAIR, PAIR), jnp.float32),
        ],
        scratch_shapes=[pltpu.VMEM((pairs, PAIR, PAIR), jnp.float32)],
        compiler_params=pltpu.CompilerParams(
            dimension_semantics=("arbitrary",), vmem_limit_bytes=32 * 1024 * 1024
        ),
        cost_estimate=pl.CostEstimate(
            flops=0, bytes_accessed=90000 * tokens, transcendentals=0
        ),
        name="inner_forward",
    )(qkv, rate, initial, causal, earlier, first, last, anew)


def mixer_backward(qkv, rate, initial, masks, residue, states, upstream):
    tokens = qkv.shape[0]
    width = rate.shape[1]
    pairs = initial.shape[0]
    chunks = tokens // CHUNK
    whole = lambda shape: pl.BlockSpec(shape, lambda i: (0,) * len(shape))
    square = pl.BlockSpec((1, CHUNK, CHUNK), lambda i: (chunks - 1 - i, 0, 0))
    column = pl.BlockSpec((CHUNK, PAIR), lambda i: (chunks - 1 - i, 0))
    rows = lambda size: pl.BlockSpec((CHUNK, size), lambda i: (chunks - 1 - i, 0))
    causal, earlier, first, last, anew = masks
    return pl.pallas_call(
        mixer_backward_kernel,
        grid=(chunks,),
        in_specs=[
            rows(3 * width),
            whole((1, width)),
            whole((pairs, PAIR, PAIR)),
            square,
            square,
            square,
            square,
            column,
            column,
            pl.BlockSpec((1, 8, PAIR), lambda i: (chunks - 1 - i, 0, 0)),
            rows(width),
            pl.BlockSpec((1, pairs, PAIR, PAIR), lambda i: (chunks - 1 - i, 0, 0, 0)),
            rows(width),
        ],
        out_specs=[rows(3 * width), whole((pairs, PAIR, PAIR)), whole((1, width))],
        out_shape=[
            jax.ShapeDtypeStruct((tokens, 3 * width), jnp.bfloat16),
            jax.ShapeDtypeStruct((pairs, PAIR, PAIR), jnp.float32),
            jax.ShapeDtypeStruct((1, width), jnp.float32),
        ],
        scratch_shapes=[pltpu.VMEM((pairs, PAIR, PAIR), jnp.float32)],
        compiler_params=pltpu.CompilerParams(
            dimension_semantics=("arbitrary",), vmem_limit_bytes=32 * 1024 * 1024
        ),
        cost_estimate=pl.CostEstimate(
            flops=0, bytes_accessed=140000 * tokens, transcendentals=0
        ),
        name="inner_backward",
    )(
        qkv,
        rate,
        initial,
        causal,
        earlier,
        jnp.swapaxes(causal, 1, 2),
        jnp.swapaxes(earlier, 1, 2),
        first,
        last,
        anew,
        residue,
        states,
        upstream,
    )


ROWS = 64
LAG = 2
MESH = pl.DeviceIdType.MESH


def across(column):
    return jnp.swapaxes(jnp.broadcast_to(column, (column.shape[0], 128)), 0, 1)[:8]


def down(row, width):
    turned = jnp.swapaxes(jnp.broadcast_to(row[:1], (128, row.shape[1])), 0, 1)
    return jnp.concatenate([turned] * (width // 128), 1) if width > 128 else turned


def transit_kernel(mode, form, parts, slabs, names, *all_refs):
    ref = dict(zip(names, all_refs))
    full_ref, partial, total = ref["full"], ref["partial"], ref["total"]
    pair_out, pair_in = ref["pair_out"], ref["pair_in"]
    from_low, from_high = ref["from_low"], ref["from_high"]
    places = parts // 2
    cross = form in ("lookup", "table")
    summing = mode != "plain"
    size = total.shape[1]
    ring = partial.shape[0]
    me = lax.axis_index("head")
    mine_dp = lax.axis_index("dp")
    core = lax.rem(me, 2)
    spot = me // 2
    twin = {"head": me + 1 - 2 * core}
    upper = {"head": lax.rem(me + 2, parts)}
    lower = {"head": lax.rem(me + parts - 2, parts)}
    chunks = ref["up_in_sem"].shape[0]
    sum_at = LAG * places
    finish_at = sum_at + (LAG if summing else 0)
    reach_at = finish_at + LAG * (places - 1)
    close_at = reach_at + (2 * LAG if cross else LAG)

    def rows_of(chunk):
        return pl.ds(pl.multiple_of(chunk * ROWS, ROWS), ROWS)

    def shard(index):
        return pl.ds(pl.multiple_of(index * size, 128), size)

    def remote(source, target, out_sem, in_sem, device):
        return pltpu.make_async_remote_copy(
            src_ref=source,
            dst_ref=target,
            send_sem=out_sem,
            recv_sem=in_sem,
            device_id=device,
            device_id_type=MESH,
        )

    def left_copy(chunk):
        half = lax.rem(chunk, 2)
        return pltpu.make_async_copy(
            ref["left"].at[rows_of(chunk)], ref["left_buf"].at[half], ref["left_sem"].at[half]
        )

    barrier = pltpu.get_barrier_semaphore()
    for offset in range(1, parts):
        pl.semaphore_signal(
            barrier, inc=1, device_id={"head": lax.rem(me + offset, parts)}, device_id_type=MESH
        )
    if cross:
        for offset in range(1, slabs):
            pl.semaphore_signal(
                barrier,
                inc=1,
                device_id={"dp": lax.rem(mine_dp + offset, slabs)},
                device_id_type=MESH,
            )
    if form != "lookup":
        left_copy(0).start()
    if mode in ("grad", "grad_add"):
        ref["gain_grad"][...] = jnp.zeros_like(ref["gain_grad"])
    if form == "table":
        ref["table_grad"][...] = jnp.zeros_like(ref["table_grad"])
    pl.semaphore_wait(barrier, parts - 1 + (slabs - 1 if cross else 0))

    def valid(chunk):
        return jnp.logical_and(chunk >= 0, chunk < chunks)

    def pair_copy(chunk):
        slot = lax.rem(chunk, ring)
        return remote(
            pair_out.at[slot],
            pair_in.at[slot],
            ref["pair_out_sem"].at[slot],
            ref["pair_in_sem"].at[slot],
            twin,
        )

    def rise(chunk, place):
        slot = lax.rem(chunk, ring)
        part = from_low.at[slot, :, pl.ds((place + 1) * size, (places - 1 - place) * size)]
        return remote(part, part, ref["low_out_sem"].at[slot], ref["low_in_sem"].at[slot], upper)

    def fall(chunk, place):
        slot = lax.rem(chunk, ring)
        part = from_high.at[slot, :, pl.ds(0, place * size)]
        return remote(part, part, ref["high_out_sem"].at[slot], ref["high_in_sem"].at[slot], lower)

    def sums_copy(chunk, offset):
        slot = lax.rem(chunk, ring)
        return remote(
            ref["sums_out"].at[slot],
            ref["sums_in"].at[slot, offset - 1],
            ref["sums_out_sem"].at[slot],
            ref["sums_in_sem"].at[slot],
            {"head": lax.rem(me + offset, parts)},
        )

    def piece(chunk, source):
        if cross:
            return ref["stage"].at[rows_of(chunk), shard(source)]
        return full_ref.at[rows_of(chunk), shard(2 * source + core)]

    def climb(chunk, source, hop):
        part = piece(chunk, source)
        return remote(
            part,
            part,
            ref["up_out_sem"].at[chunk, hop - 1],
            ref["up_in_sem"].at[chunk, hop - 1],
            upper,
        )

    def sink(chunk, source, hop):
        part = piece(chunk, source)
        return remote(
            part,
            part,
            ref["down_out_sem"].at[chunk, hop - 1],
            ref["down_in_sem"].at[chunk, hop - 1],
            lower,
        )

    def target(chunk, giver):
        if form == "lookup":
            return full_ref.at[rows_of(chunk), shard(2 * giver + core)]
        return full_ref.at[chunk // 2, rows_of(lax.rem(chunk, 2) * slabs + giver), shard(core)]

    def mirror(chunk, index):
        part = target(chunk, index) if cross else piece(chunk, index)
        return remote(
            part, part, ref["twin_out_sem"].at[chunk], ref["twin_in_sem"].at[chunk], twin
        )

    def hand_over(chunk, source):
        return remote(
            piece(chunk, source),
            target(chunk, mine_dp),
            ref["cross_out_sem"].at[chunk, source],
            ref["cross_in_sem"].at[chunk, mine_dp],
            {"dp": source},
        )

    def have(chunk, source):
        if not cross:
            mirror(chunk, source).start()
            return

        @pl.when(source != mine_dp)
        def _():
            hand_over(chunk, source).start()

        @pl.when(source == mine_dp)
        def _():
            values = ref["stage"][rows_of(chunk), shard(source)]
            if form == "lookup":
                full_ref[rows_of(chunk), shard(2 * mine_dp + core)] = values
            else:
                place_rows = rows_of(lax.rem(chunk, 2) * slabs + mine_dp)
                full_ref[chunk // 2, place_rows, shard(core)] = values
            mirror(chunk, mine_dp).start()

    def receive(step):
        for hop in range(places):
            chunk = step - finish_at - LAG * (hop + 1)

            @pl.when(jnp.logical_and(valid(chunk), jnp.abs(spot - mine_dp) == hop))
            def _():
                for offset in range(1, slabs):
                    giver = lax.rem(mine_dp + offset, slabs)
                    part = target(chunk, giver)
                    remote(
                        part,
                        part,
                        ref["cross_out_sem"].at[chunk, giver],
                        ref["cross_in_sem"].at[chunk, giver],
                        twin,
                    ).wait_recv()
                    mirror(chunk, giver).start()

    def relay(step):
        for hop in range(1, places):
            chunk = step - finish_at - LAG * hop
            source = spot - hop

            @pl.when(jnp.logical_and(valid(chunk), source >= 0))
            def _():
                climb(chunk, source, hop).wait_recv()
                if hop < places - 1:

                    @pl.when(spot < places - 1)
                    def _():
                        climb(chunk, source, hop + 1).start()

                have(chunk, source)

            source_high = spot + hop

            @pl.when(jnp.logical_and(valid(chunk), source_high < places))
            def _():
                sink(chunk, source_high, hop).wait_recv()
                if hop < places - 1:

                    @pl.when(spot > 0)
                    def _():
                        sink(chunk, source_high, hop + 1).start()

                have(chunk, source_high)

    def finish_shard(step):
        chunk = step - finish_at

        @pl.when(valid(chunk))
        def _():
            slot = lax.rem(chunk, ring)
            rows = rows_of(chunk)
            if summing:
                sums_in = ref["sums_in"]
                pltpu.make_async_copy(
                    sums_in.at[slot], sums_in.at[slot], ref["sums_in_sem"].at[slot]
                ).wait()
                summed = ref["sums_out"][slot]
                for offset in range(1, parts):
                    summed = summed + sums_in[slot, offset - 1]
                gain = ref["gain"][0:1, :]
            if mode == "plain":
                result = total[...]
            elif mode == "norm":
                scale = lax.rsqrt(summed / D + EPSILON)
                ref["scale"][chunk] = scale
                result = ref["own"][rows, :] * down(scale, size) * gain
            else:
                scale = down(ref["scale"][chunk], size)
                normed = ref["inputs"][rows, :] * scale
                inner = down(summed / D, size)
                result = scale * (ref["own"][rows, :] * gain - normed * inner)
                if mode == "grad_add":
                    result = result + ref["added"][rows, :]
                if form != "table":
                    ref["own"][rows, :] = result
            if cross:
                ref["stage"][rows, shard(spot)] = result.astype(jnp.bfloat16)
            else:
                full_ref[rows, shard(me)] = result.astype(jnp.bfloat16)

            @pl.when(spot < places - 1)
            def _():
                climb(chunk, spot, 1).start()

            @pl.when(spot > 0)
            def _():
                sink(chunk, spot, 1).start()

            have(chunk, spot)

    def add_pair(step):
        chunk = step - LAG

        @pl.when(valid(chunk))
        def _():
            slot = lax.rem(chunk, ring)
            pair_copy(chunk).wait_recv()
            partial[slot] = partial[slot] + pair_in[slot].astype(jnp.float32)

    def pass_on(step):
        for place in range(places):
            if place < places - 1:
                up_chunk = step - LAG * (1 + place)

                @pl.when(jnp.logical_and(valid(up_chunk), spot == place))
                def _():
                    slot = lax.rem(up_chunk, ring)
                    above = pl.ds((place + 1) * size, (places - 1 - place) * size)
                    values = partial[slot, :, above]
                    if place > 0:
                        rise(up_chunk, place - 1).wait_recv()
                        values = values + from_low[slot, :, above].astype(jnp.float32)
                    from_low[slot, :, above] = values.astype(jnp.bfloat16)
                    rise(up_chunk, place).start()

            if place > 0:
                down_chunk = step - LAG * (places - place)

                @pl.when(jnp.logical_and(valid(down_chunk), spot == place))
                def _():
                    slot = lax.rem(down_chunk, ring)
                    below = pl.ds(0, place * size)
                    values = partial[slot, :, below]
                    if place < places - 1:
                        fall(down_chunk, place + 1).wait_recv()
                        values = values + from_high[slot, :, below].astype(jnp.float32)
                    from_high[slot, :, below] = values.astype(jnp.bfloat16)
                    fall(down_chunk, place).start()

    def settle(step):
        chunk = step - sum_at - LAG

        @pl.when(valid(chunk))
        def _():
            pair_copy(chunk).wait_send()
            for place in range(places):

                @pl.when(spot == place)
                def _():
                    if place < places - 1:
                        rise(chunk, place).wait_send()
                    if place > 0:
                        fall(chunk, place).wait_send()

            if summing:
                slot = lax.rem(chunk, ring)
                sums_in = ref["sums_in"]
                pltpu.make_async_copy(
                    sums_in.at[slot], sums_in.at[slot], ref["sums_out_sem"].at[slot]
                ).wait()

    def sum_shard(step):
        chunk = step - sum_at

        @pl.when(valid(chunk))
        def _():
            slot = lax.rem(chunk, ring)
            rows = rows_of(chunk)
            mine = shard(spot)

            @pl.when(spot == places - 1)
            def _():
                rise(chunk, places - 2).wait_recv()

            @pl.when(spot == 0)
            def _():
                fall(chunk, 1).wait_recv()

            total[...] = partial[slot, :, mine]

            @pl.when(spot > 0)
            def _():
                total[...] += from_low[slot, :, mine].astype(jnp.float32)

            @pl.when(spot < places - 1)
            def _():
                total[...] += from_high[slot, :, mine].astype(jnp.float32)

            if not summing:
                return
            value = total[...]
            if mode == "norm":
                value = value + ref["inputs"][rows, :]
                column = jnp.sum(value * value, 1, keepdims=True)
            else:
                scale = down(ref["scale"][chunk], size)
                normed = ref["inputs"][rows, :] * scale
                ref["gain_grad"][0:1, :] += jnp.sum(value * normed, 0, keepdims=True)
                column = jnp.sum(value * ref["gain"][0:1, :] * normed, 1, keepdims=True)
            ref["own"][rows, :] = value
            ref["sums_out"][slot] = across(column)
            for offset in range(1, parts):
                sums_copy(chunk, offset).start()

    def produce(step):
        chunk = step

        @pl.when(valid(chunk))
        def _():
            slot = lax.rem(chunk, ring)
            right_ref = ref["right"]
            if form == "lookup":
                entries = right_ref.shape[0]
                ids = jnp.concatenate(
                    [ref["ids"][group, rows_of(chunk), 0:1] for group in range(slabs)], 0
                )
                spots = lax.broadcasted_iota(jnp.int32, (slabs * ROWS, entries), 1)
                hits = (spots == ids).astype(jnp.bfloat16)
                other = dot_ab(hits, right_ref[:, shard(1 - core)]).astype(jnp.bfloat16)
                for group in range(slabs):
                    pair_out[slot, :, pl.ds(group * size, size)] = other[
                        group * ROWS : (group + 1) * ROWS
                    ]
                pair_copy(chunk).start()
                here = dot_ab(hits, right_ref[:, shard(core)])
                for group in range(slabs):
                    partial[slot, :, pl.ds(group * size, size)] = here[
                        group * ROWS : (group + 1) * ROWS
                    ]
                return
            half = lax.rem(chunk, 2)
            left_copy(chunk).wait()

            @pl.when(chunk + 1 < chunks)
            def _():
                left_copy(chunk + 1).start()

            def term(index):
                if form in ("turned", "table"):
                    return dot_abt(ref["left_buf"][half], right_ref[shard(index), :])
                return dot_ab(ref["left_buf"][half], right_ref[:, shard(index)])

            for place in range(places):
                lanes = pl.ds(place * size, size)
                pair_out[slot, :, lanes] = term(2 * place + 1 - core).astype(jnp.bfloat16)
            pair_copy(chunk).start()
            for place in range(places):
                lanes = pl.ds(place * size, size)
                partial[slot, :, lanes] = term(2 * place + core)

    def close(step):
        chunk = step - close_at

        @pl.when(valid(chunk))
        def _():
            if form == "table":
                arrived = full_ref.at[chunk // 2, pl.ds(0, slabs * ROWS), pl.ds(0, size)]
            else:
                arrived = full_ref.at[rows_of(chunk), pl.ds(0, places * size)]
            pltpu.make_async_copy(arrived, arrived, ref["twin_in_sem"].at[chunk]).wait()
            pltpu.make_async_copy(arrived, arrived, ref["twin_out_sem"].at[chunk]).wait()
            if cross:
                for offset in range(1, slabs):
                    hand_over(chunk, lax.rem(mine_dp + offset, slabs)).wait_send()
            for hop in range(1, places):
                source = spot - hop + 1

                @pl.when(jnp.logical_and(source >= 0, spot < places - 1))
                def _():
                    climb(chunk, source, hop).wait_send()

                source_high = spot + hop - 1

                @pl.when(jnp.logical_and(source_high < places, spot > 0))
                def _():
                    sink(chunk, source_high, hop).wait_send()

            if form == "table":
                @pl.when(lax.rem(chunk, 2) == 1)
                def _():
                    table_grad = ref["table_grad"]
                    entries = table_grad.shape[0]
                    pieces = 5 if entries % 80 == 0 else 1
                    block = entries // pieces
                    ids = ref["ids"][chunk // 2, 0:1, :]
                    values = full_ref[chunk // 2]
                    for index in range(pieces):
                        spots = index * block + lax.broadcasted_iota(
                            jnp.int32, (block, ids.shape[1]), 0
                        )
                        hits = (spots == ids).astype(jnp.bfloat16)
                        span = pl.ds(index * block, block)
                        table_grad[span, :] += dot_ab(hits, values)

    def advance(step, carried):
        relay(step)
        if summing:
            finish_shard(step)
        if cross:
            receive(step)
        add_pair(step)
        pass_on(step)
        settle(step)
        sum_shard(step)
        if not summing:
            finish_shard(step)
        produce(step)
        close(step)
        return carried

    lax.fori_loop(0, chunks + close_at, advance, 0)


def transit(
    mode,
    form,
    number,
    parts,
    slabs,
    right,
    tokens,
    size,
    left=None,
    inputs=None,
    gain=None,
    scale=None,
    added=None,
    ids=None,
    entries=None,
):
    chunks = tokens // ROWS
    places = parts // 2
    cross = form in ("lookup", "table")
    summing = mode != "plain"
    ring = min(chunks, LAG * (places + 1) + 2) if summing else chunks
    dma = pltpu.SemaphoreType.DMA
    low, wide_kind = jnp.bfloat16, jnp.float32
    vmem = pl.BlockSpec(memory_space=pltpu.VMEM)
    operands, specs, outputs, scratch = {}, [], {}, {}

    def take(name, array, spec=vmem):
        operands[name] = array
        specs.append(spec)

    take("right", right)
    if left is not None:
        take("left", left, pl.BlockSpec(memory_space=pl.ANY))
    if ids is not None:
        take("ids", ids)
    if summing:
        take("inputs", inputs)
        take("gain", gain)
    if mode in ("grad", "grad_add"):
        take("scale", scale)
    if mode == "grad_add":
        take("added", added)

    if summing and form != "table":
        outputs["own"] = ((tokens, size), wide_kind)
    if form != "table":
        outputs["full"] = ((tokens, parts * size), low)
    if mode == "norm":
        outputs["scale"] = ((chunks, 8, ROWS), wide_kind)
    if mode in ("grad", "grad_add"):
        outputs["gain_grad"] = ((8, size), wide_kind)
    if form == "table":
        outputs["table_grad"] = ((entries, 2 * size), wide_kind)

    span = places * size
    hops = max(places - 1, 1)
    if form == "table":
        scratch["own"] = pltpu.VMEM((tokens, size), wide_kind)
        scratch["full"] = pltpu.VMEM((chunks // 2, 2 * slabs * ROWS, 2 * size), low)
    if left is not None:
        scratch["left_buf"] = pltpu.VMEM((2, ROWS, left.shape[1]), low)
        scratch["left_sem"] = dma((2,))
    if cross:
        scratch["stage"] = pltpu.VMEM((tokens, span), low)
        scratch["cross_out_sem"] = dma((chunks, slabs))
        scratch["cross_in_sem"] = dma((chunks, slabs))
    if summing:
        scratch["sums_out"] = pltpu.VMEM((ring, 8, ROWS), wide_kind)
        scratch["sums_in"] = pltpu.VMEM((ring, parts - 1, 8, ROWS), wide_kind)
        scratch["sums_out_sem"] = dma((ring,))
        scratch["sums_in_sem"] = dma((ring,))
    scratch["total"] = pltpu.VMEM((ROWS, size), wide_kind)
    scratch["partial"] = pltpu.VMEM((ring, ROWS, span), wide_kind)
    for name in ("pair_out", "pair_in", "from_low", "from_high"):
        scratch[name] = pltpu.VMEM((ring, ROWS, span), low)
    for name in ("pair_out", "pair_in", "low_out", "low_in", "high_out", "high_in"):
        scratch[name + "_sem"] = dma((ring,))
    for name in ("up_out", "up_in", "down_out", "down_in"):
        scratch[name + "_sem"] = dma((chunks, hops))
    scratch["twin_out_sem"] = dma((chunks,))
    scratch["twin_in_sem"] = dma((chunks,))

    depth = right.shape[1] if form in ("turned", "table") else right.shape[0]
    names = tuple(operands) + tuple(outputs) + tuple(scratch)
    results = pl.pallas_call(
        functools.partial(transit_kernel, mode, form, parts, slabs, names),
        in_specs=specs,
        out_specs=[vmem] * len(outputs),
        out_shape=[jax.ShapeDtypeStruct(shape, kind) for shape, kind in outputs.values()],
        scratch_shapes=list(scratch.values()),
        compiler_params=pltpu.CompilerParams(
            collective_id=number, has_side_effects=True, vmem_limit_bytes=60 * 1024 * 1024
        ),
        cost_estimate=pl.CostEstimate(
            flops=2 * tokens * depth * parts * size,
            bytes_accessed=128 * tokens * parts * size,
            transcendentals=0,
        ),
        name="transit_" + form,
    )(*operands.values())
    return dict(zip(outputs, results))


def share_kernel(axes, block_ref, all_ref, out_sem, in_sem):
    counts = [lax.axis_size(axis) for axis in axes]
    places = [lax.axis_index(axis) for axis in axes]
    members = 1
    me = 0
    for count, place in zip(counts, places):
        members = members * count
        me = me * count + place

    def partner(offset):
        device, rest = {}, offset
        for axis, count, place in reversed(list(zip(axes, counts, places))):
            device[axis] = lax.rem(place + lax.rem(rest, count), count)
            rest = rest // count
        return device

    def send(offset):
        return pltpu.make_async_remote_copy(
            src_ref=block_ref,
            dst_ref=all_ref.at[me],
            send_sem=out_sem,
            recv_sem=in_sem,
            device_id=partner(offset),
            device_id_type=MESH,
        )

    barrier = pltpu.get_barrier_semaphore()

    def greet(offset, carried):
        pl.semaphore_signal(barrier, inc=1, device_id=partner(offset), device_id_type=MESH)
        return carried

    def start(offset, carried):
        send(offset).start()
        return carried

    lax.fori_loop(1, members, greet, 0)
    all_ref[me] = block_ref[...]
    pl.semaphore_wait(barrier, members - 1)
    lax.fori_loop(1, members, start, 0)
    arrived = all_ref.at[pl.ds(0, members - 1)]
    pltpu.make_async_copy(arrived, arrived, in_sem).wait()
    pltpu.make_async_copy(arrived, arrived, out_sem).wait()


def share(number, block, axes):
    members = 1
    for axis in axes:
        members = members * lax.axis_size(axis)
    vmem = pl.BlockSpec(memory_space=pltpu.VMEM)
    return pl.pallas_call(
        functools.partial(share_kernel, axes),
        in_specs=[vmem],
        out_specs=vmem,
        out_shape=jax.ShapeDtypeStruct((members,) + block.shape, block.dtype),
        scratch_shapes=[pltpu.SemaphoreType.DMA, pltpu.SemaphoreType.DMA],
        compiler_params=pltpu.CompilerParams(
            collective_id=number, has_side_effects=True, vmem_limit_bytes=16 * 1024 * 1024
        ),
        cost_estimate=pl.CostEstimate(
            flops=0, bytes_accessed=16 * 1024 * 1024, transcendentals=0
        ),
        name="share",
    )(block)


SCORE_ROWS = 256


def scores_kernel(rows_ref, table_ref, goal_ref, logits_ref, stats_ref):
    entries = table_ref.shape[0]
    edges = list(range(0, entries, 1024)) + [entries]
    peak = jnp.full((SCORE_ROWS, 1), -jnp.inf, jnp.float32)
    for low, high in zip(edges, edges[1:]):
        values = dot_abt(rows_ref[...], table_ref[low:high, :])
        logits_ref[:, low:high] = values
        peak = jnp.maximum(peak, jnp.max(values, 1, keepdims=True))
    exp_sum = jnp.zeros((SCORE_ROWS, 1), jnp.float32)
    picked = jnp.zeros((SCORE_ROWS, 1), jnp.float32)
    goal = goal_ref[:, 0:1]
    for low, high in zip(edges, edges[1:]):
        values = logits_ref[:, low:high]
        exp_sum = exp_sum + jnp.sum(jnp.exp(values - peak), 1, keepdims=True)
        spots = low + lax.broadcasted_iota(jnp.int32, values.shape, 1)
        picked = picked + jnp.sum(jnp.where(spots == goal, values, 0.0), 1, keepdims=True)
    stats_ref[0] = jnp.broadcast_to(peak, (SCORE_ROWS, 128))
    stats_ref[1] = jnp.broadcast_to(exp_sum, (SCORE_ROWS, 128))
    stats_ref[2] = jnp.broadcast_to(picked, (SCORE_ROWS, 128))


def scores(rows, table, goals):
    tokens, width = rows.shape
    entries = table.shape[0]
    return pl.pallas_call(
        scores_kernel,
        grid=(tokens // SCORE_ROWS,),
        in_specs=[
            pl.BlockSpec((SCORE_ROWS, width), lambda i: (i, 0)),
            pl.BlockSpec(memory_space=pltpu.VMEM),
            pl.BlockSpec((SCORE_ROWS, 128), lambda i: (i, 0)),
        ],
        out_specs=[
            pl.BlockSpec((SCORE_ROWS, entries), lambda i: (i, 0)),
            pl.BlockSpec((3, SCORE_ROWS, 128), lambda i: (0, i, 0)),
        ],
        out_shape=[
            jax.ShapeDtypeStruct((tokens, entries), jnp.float32),
            jax.ShapeDtypeStruct((3, tokens, 128), jnp.float32),
        ],
        compiler_params=pltpu.CompilerParams(
            dimension_semantics=("arbitrary",), vmem_limit_bytes=56 * 1024 * 1024
        ),
        cost_estimate=pl.CostEstimate(
            flops=2 * tokens * entries * width,
            bytes_accessed=2 * entries * width + 4 * tokens * entries,
            transcendentals=tokens * entries,
        ),
        name="scores",
    )(rows, table, goals)


def shampoo(tile_w, tile_g, left, right, left_root, right_root):
    low_g = tile_g.astype(jnp.bfloat16)

    def product(form, one, two):
        return jnp.einsum(
            form,
            one.astype(jnp.bfloat16),
            two.astype(jnp.bfloat16),
            preferred_element_type=jnp.float32,
        )

    new_left = STAT_DECAY * left + (1.0 - STAT_DECAY) * product("abrc,absc->abrs", low_g, low_g)
    new_right = STAT_DECAY * right + (1.0 - STAT_DECAY) * product("abrc,abrd->abcd", low_g, low_g)
    turned = product("abrs,absc->abrc", left_root, low_g)
    turned = product("abrc,abcd->abrd", turned, right_root)
    return (new_left, new_right, tile_w - MATRIX_RATE * (turned + WEIGHT_DECAY * tile_w))


def refresh(master, grad, left, right, left_root, right_root):
    rows = master.shape[1]
    new_left, new_right, new_w = shampoo(
        master.reshape(1, 1, rows, -1),
        grad.reshape(1, 1, rows, -1),
        left,
        right,
        left_root,
        right_root,
    )
    return (grad.reshape(master.shape), new_left, new_right, new_w.reshape(master.shape))


def adamw(weight, grad, first, second, step_rate):
    new_first = BETA_ONE * first + (1.0 - BETA_ONE) * grad
    new_second = BETA_TWO * second + (1.0 - BETA_TWO) * grad * grad
    moved = (
        new_first
        / (1.0 - BETA_ONE**STEP)
        / (jnp.sqrt(new_second / (1.0 - BETA_TWO**STEP)) + ADAM_EPSILON)
    )
    return (new_first, new_second, weight - step_rate * (moved + WEIGHT_DECAY * weight))


def layer_forward(
    local_ids, targets, valid, resets, emb_low, weights, inner_init, gains, gain_one, head_index
):
    w_qkv, w_out, w_gu, w_down, table = weights
    parts, slabs = lax.axis_size("head"), lax.axis_size("dp")
    vocab_part = table.shape[0]
    tokens, size = targets.shape[0], gains.shape[1]
    chunks = tokens // ROWS
    columns = jnp.arange(vocab_part, dtype=jnp.int32)
    spread_ids = jnp.broadcast_to(local_ids[:, :, None], (slabs, tokens, 128))
    first = transit("plain", "lookup", 1, parts, slabs, emb_low, tokens, size, ids=spread_ids)
    low_embedded = first["full"]
    wide_embedded = low_embedded.astype(jnp.float32)
    scale_one = lax.rsqrt(jnp.mean(wide_embedded * wide_embedded, -1) + EPSILON)
    full_one = (wide_embedded * scale_one[:, None] * gain_one[None]).astype(jnp.bfloat16)
    embedded = lax.dynamic_slice_in_dim(low_embedded, head_index * size, size, 1)
    embedded = embedded.astype(jnp.float32)
    scale_one = jnp.broadcast_to(scale_one.reshape(chunks, 1, ROWS), (chunks, 8, ROWS))
    mixed = jnp.dot(full_one, w_qkv, preferred_element_type=jnp.float32).astype(jnp.bfloat16)
    step_rate = jax.nn.sigmoid(gains[3:4]) / (8 * P_SIZE)
    masks = mixer_masks(resets, tokens)
    initial_pairs = pair_blocks(inner_init)
    inner_low, residue, states = mixer_forward(mixed, step_rate, initial_pairs, masks)
    second = transit(
        "norm",
        "rows",
        2,
        parts,
        slabs,
        w_out,
        tokens,
        size,
        left=inner_low,
        inputs=embedded,
        gain=gains[1:2],
    )
    hidden_one, full_two, scale_two = second["own"], second["full"], second["scale"]
    gate_up = jnp.dot(full_two, w_gu, preferred_element_type=jnp.float32)

    def swiglu(paired):
        halves = paired.reshape(tokens, 2, -1)
        return jax.nn.silu(halves[:, 0]) * halves[:, 1]

    activated, act_pull = jax.vjp(swiglu, gate_up)
    act_low = activated.astype(jnp.bfloat16)
    third = transit(
        "norm",
        "rows",
        3,
        parts,
        slabs,
        w_down,
        tokens,
        size,
        left=act_low,
        inputs=hidden_one,
        gain=gains[2:3],
    )
    hidden_two, full_end, scale_end = third["own"], third["full"], third["scale"]
    local_targets = targets - head_index * vocab_part
    target_hits = columns[None, :] == local_targets[:, None]
    logits, stats = scores(
        full_end, table, jnp.broadcast_to(local_targets[:, None], (tokens, 128))
    )
    stats = share(7, stats[:, :, 0].reshape(-1, 128), ("head",)).reshape(parts, 3, tokens)
    highest = jnp.max(stats[:, 0], 0)
    exp_sum = jnp.sum(stats[:, 1] * jnp.exp(stats[:, 0] - highest[None]), 0)
    target_logit = jnp.sum(stats[:, 2], 0)
    totals = highest + jnp.log(exp_sum)
    counted = valid.astype(jnp.float32)
    d_logits = (
        (jnp.exp(logits - totals[:, None]) - target_hits.astype(jnp.float32)) * counted[:, None]
    ).astype(jnp.bfloat16)
    kept = (
        embedded,
        scale_one,
        full_one,
        (mixed, step_rate, initial_pairs, masks, residue, states),
        inner_low,
        hidden_one,
        scale_two,
        full_two,
        act_pull,
        act_low,
        hidden_two,
        scale_end,
        full_end,
        d_logits,
        local_ids,
    )
    return (jnp.sum((totals - target_logit) * counted), jnp.sum(counted), kept)


def slots_of(grad, order):
    parts = lax.axis_size("dp")
    shaped = grad.astype(jnp.bfloat16).reshape(parts, -1, grad.shape[1])
    return jnp.take(shaped, order, axis=0, mode="clip")


def column_slots_of(grad, order):
    parts = lax.axis_size("dp")
    shaped = grad.astype(jnp.bfloat16).reshape(grad.shape[0], parts, -1)
    return jnp.take(jnp.swapaxes(shaped, 0, 1), order, axis=0, mode="clip")


def scatter_dp(grad, dimension):
    return lax.psum_scatter(grad, "dp", scatter_dimension=dimension, tiled=True)


def layer_backward(kept, weights, gains, order):
    (
        embedded,
        scale_one,
        full_one,
        inner_kept,
        inner_low,
        hidden_one,
        scale_two,
        full_two,
        act_pull,
        act_low,
        hidden_two,
        scale_end,
        full_end,
        d_logits,
        local_ids,
    ) = kept
    w_qkv, w_out, w_gu, w_down, table = weights
    parts, slabs = lax.axis_size("head"), lax.axis_size("dp")
    tokens, size = embedded.shape
    chunks = tokens // ROWS
    wide_kind = jnp.float32
    fourth = transit(
        "grad",
        "rows",
        4,
        parts,
        slabs,
        table,
        tokens,
        size,
        left=d_logits,
        inputs=hidden_two,
        gain=gains[2:3],
        scale=scale_end,
    )
    d_two, d_down_in = fourth["own"], fourth["full"]
    grad_table = jnp.einsum("tv,td->vd", d_logits, full_end, preferred_element_type=wide_kind)
    grad_table = grad_table.astype(jnp.bfloat16)
    d_act = jnp.einsum("td,fd->tf", d_down_in, w_down, preferred_element_type=wide_kind)
    d_gate_up = act_pull(d_act)[0].astype(jnp.bfloat16)
    grad_down = jnp.einsum("tf,td->fd", act_low, d_down_in, preferred_element_type=wide_kind)
    slot_down = column_slots_of(grad_down, order[3])
    d_gate_up, grad_table, slot_down = lax.optimization_barrier(
        (d_gate_up, grad_table, slot_down)
    )
    owned_table = scatter_dp(grad_table, 1)
    owned_down = scatter_dp(slot_down, 0)
    fifth = transit(
        "grad_add",
        "turned",
        5,
        parts,
        slabs,
        w_gu,
        tokens,
        size,
        left=d_gate_up,
        inputs=hidden_one,
        gain=gains[1:2],
        scale=scale_two,
        added=d_two,
    )
    d_one, d_out_in = fifth["own"], fifth["full"]
    d_out_in, owned_down = lax.optimization_barrier((d_out_in, owned_down))
    d_inner = jnp.einsum("td,cd->tc", d_out_in, w_out, preferred_element_type=wide_kind)
    grad_gu = jnp.einsum("td,tc->dc", full_two, d_gate_up, preferred_element_type=wide_kind)
    slot_gu = slots_of(grad_gu, order[2])
    d_inner, slot_gu = lax.optimization_barrier((d_inner, slot_gu))
    owned_gu = scatter_dp(slot_gu, 0)
    d_mixed, grad_pairs, grad_step = mixer_backward(*inner_kept, d_inner)
    grad_init = head_blocks(grad_pairs)
    gate = jax.nn.sigmoid(gains[3])
    grad_rate = grad_step[0] * gate * (1.0 - gate) / (8 * P_SIZE)
    grad_out = jnp.einsum("tc,td->cd", inner_low, d_out_in, preferred_element_type=wide_kind)
    grad_qkv = jnp.einsum("td,tc->dc", full_one, d_mixed, preferred_element_type=wide_kind)
    slot_out = column_slots_of(grad_out, order[1])
    slot_qkv = slots_of(grad_qkv, order[0])
    d_mixed, slot_out, slot_qkv, owned_table, owned_gu = lax.optimization_barrier(
        (d_mixed, slot_out, slot_qkv, owned_table, owned_gu)
    )
    owned_out = scatter_dp(slot_out, 0)
    owned_qkv = scatter_dp(slot_qkv, 0)
    row_ids = jnp.moveaxis(local_ids.reshape(slabs, chunks // 2, 2, ROWS), 0, 2)
    row_ids = jnp.broadcast_to(
        row_ids.reshape(chunks // 2, 1, 2 * slabs * ROWS), (chunks // 2, 8, 2 * slabs * ROWS)
    )
    sixth = transit(
        "grad_add",
        "table",
        6,
        parts,
        slabs,
        w_qkv,
        tokens,
        size,
        left=d_mixed,
        inputs=embedded,
        gain=gains[0:1],
        scale=scale_one,
        added=d_one,
        ids=row_ids,
        entries=table.shape[0],
    )
    owned_table = owned_table.astype(wide_kind) + sixth["table_grad"]
    gain_rows = [sixth["gain_grad"][0], fifth["gain_grad"][0], fourth["gain_grad"][0], grad_rate]
    owned = tuple(
        piece.astype(wide_kind) for piece in (owned_qkv, owned_out, owned_gu, owned_down)
    )
    return owned + (owned_table,), grad_init, jnp.stack(gain_rows, 0)


def shards(
    token_ids,
    targets,
    valid,
    resets,
    owners,
    emb_master,
    emb_first,
    emb_second,
    qkv_master,
    qkv_left,
    qkv_right,
    qkv_left_root,
    qkv_right_root,
    out_master,
    out_left,
    out_right,
    out_left_root,
    out_right_root,
    gu_master,
    gu_left,
    gu_right,
    gu_left_root,
    gu_right_root,
    down_master,
    down_left,
    down_right,
    down_left_root,
    down_right_root,
    inner_init,
    inner_first,
    inner_second,
    gains,
    gains_first,
    gains_second,
):
    low = jnp.bfloat16
    dp_size, head_size = lax.axis_size("dp"), lax.axis_size("head")
    head_index = lax.axis_index("head")
    ids_rows = token_ids.astype(jnp.float32).reshape(-1, 128)
    gain_rows = jnp.pad(gains[0].reshape(-1, 128), ((0, 8 - gains.shape[1] // 128), (0, 0)))
    opening = share(8, jnp.concatenate([ids_rows, gain_rows], 0), ("dp", "head"))
    opening = opening.reshape(dp_size, head_size, -1, 128)
    local_ids = opening[:, 0, : ids_rows.shape[0]].reshape(dp_size, -1).astype(jnp.int32)
    local_ids = local_ids - head_index * emb_master.shape[0]
    gain_one = opening[0, :, ids_rows.shape[0] :].reshape(head_size, -1)
    gain_one = gain_one[:, : gains.shape[1]].reshape(-1)
    emb_low = emb_master.astype(low)

    def flat(array):
        return array.reshape(array.shape[1], -1)

    gathered = (
        lax.all_gather(flat(qkv_master).astype(low), "dp", axis=0),
        lax.all_gather(out_master.astype(low), "dp", axis=0, tiled=True),
        lax.all_gather(flat(gu_master).astype(low), "dp", axis=0),
        lax.all_gather(down_master.astype(low), "dp", axis=0, tiled=True),
        lax.all_gather(emb_low, "dp", axis=1, tiled=True),
    )
    w_qkv = jnp.take(gathered[0], owners[0], axis=0, mode="clip").reshape(D, -1)
    w_out = jnp.take(gathered[1], owners[1], axis=0, mode="clip")
    w_out = jnp.swapaxes(w_out, 0, 1).reshape(w_out.shape[1], D)
    w_gu = jnp.take(gathered[2], owners[2], axis=0, mode="clip").reshape(D, -1)
    w_down = jnp.take(gathered[3], owners[3], axis=0, mode="clip")
    w_down = jnp.swapaxes(w_down, 0, 1).reshape(w_down.shape[1], D)
    weights = (w_qkv, w_out, w_gu, w_down, gathered[4])
    loss_local, count_local, kept = layer_forward(
        local_ids, targets, valid, resets, emb_low, weights, inner_init, gains, gain_one, head_index
    )
    order = jnp.argsort(owners, axis=1)
    owned, grad_init, grad_gains = layer_backward(kept, weights, gains, order)
    init_rows = grad_init.size // 128
    numbers = jnp.zeros((8, 128), jnp.float32).at[0, 0].set(loss_local).at[0, 1].set(count_local)
    pieces = (grad_init.reshape(-1, 128), grad_gains.reshape(-1, 128), numbers)
    small = jnp.sum(share(9, jnp.concatenate(pieces, 0), ("dp",)), 0)
    loss_sum, count = small[-8, 0], small[-8, 1]
    small = (
        small[:init_rows].reshape(grad_init.shape),
        small[init_rows:-8].reshape(grad_gains.shape),
    )
    first_dp = (lax.axis_index("dp") == 0).astype(jnp.float32)
    squares = sum((jnp.sum(piece * piece) for piece in owned))
    squares = squares + first_dp * (jnp.sum(small[0] * small[0]) + jnp.sum(small[1] * small[1]))
    squares = share(10, jnp.broadcast_to(squares, (8, 128)), ("dp", "head"))
    squares_all = jnp.sum(squares[:, 0, 0])
    grad_norm = jnp.sqrt(squares_all) / count
    factor = jnp.minimum(1.0, CLIP_LIMIT / grad_norm) / count
    qkv_out = refresh(
        qkv_master, owned[0] * factor, qkv_left, qkv_right, qkv_left_root, qkv_right_root
    )
    out_out = refresh(
        out_master, owned[1] * factor, out_left, out_right, out_left_root, out_right_root
    )
    gu_out = refresh(gu_master, owned[2] * factor, gu_left, gu_right, gu_left_root, gu_right_root)
    down_out = refresh(
        down_master, owned[3] * factor, down_left, down_right, down_left_root, down_right_root
    )
    table_out = adamw(emb_master, owned[4] * factor, emb_first, emb_second, TABLE_RATE)
    init_out = adamw(inner_init, small[0] * factor, inner_first, inner_second, INITIAL_RATE)
    gain_out = adamw(gains, small[1] * factor, gains_first, gains_second, GAINS_RATE)
    return (
        (jnp.stack([loss_sum, count]), grad_norm)
        + table_out
        + qkv_out
        + out_out
        + gu_out
        + down_out
        + init_out
        + gain_out
    )


def solution(mesh):
    placed = (
        P("dp"),
        P("dp"),
        P("dp"),
        P("dp"),
        P(),
        P("head", "dp"),
        P("head", "dp"),
        P("head", "dp"),
        P("dp", None, None, "head"),
        P("dp", "head", None, None),
        P("dp", "head", None, None),
        P("dp", "head", None, None),
        P("dp", "head", None, None),
        P("dp", "head", None),
        P("dp", "head", None, None),
        P("dp", "head", None, None),
        P("dp", "head", None, None),
        P("dp", "head", None, None),
        P("dp", None, None, "head"),
        P("dp", "head", None, None),
        P("dp", "head", None, None),
        P("dp", "head", None, None),
        P("dp", "head", None, None),
        P("dp", "head", None),
        P("dp", "head", None, None),
        P("dp", "head", None, None),
        P("dp", "head", None, None),
        P("dp", "head", None, None),
        P("head", None, None),
        P("head", None, None),
        P("head", None, None),
        P(None, "head"),
        P(None, "head"),
        P(None, "head"),
    )
    return jax.shard_map(
        shards,
        mesh=mesh,
        in_specs=placed,
        out_specs=(
            P(),
            P(),
            P("head", "dp"),
            P("head", "dp"),
            P("head", "dp"),
            P("dp", None, None, "head"),
            P("dp", "head", None, None),
            P("dp", "head", None, None),
            P("dp", None, None, "head"),
            P("dp", "head", None),
            P("dp", "head", None, None),
            P("dp", "head", None, None),
            P("dp", "head", None),
            P("dp", None, None, "head"),
            P("dp", "head", None, None),
            P("dp", "head", None, None),
            P("dp", None, None, "head"),
            P("dp", "head", None),
            P("dp", "head", None, None),
            P("dp", "head", None, None),
            P("dp", "head", None),
            P("head", None, None),
            P("head", None, None),
            P("head", None, None),
            P(None, "head"),
            P(None, "head"),
            P(None, "head"),
        ),
        check_vma=False,
    )
```

```python
import functools

import jax
import jax.numpy as jnp
from jax import lax
from jax.experimental import pallas as pl
from jax.experimental.pallas import tpu as pltpu
from jax.sharding import PartitionSpec as P

D = 2048
P_SIZE = 64
MB = 16
STEP = 10


EPSILON = 1e-05
CLIP_LIMIT = 0.05
STAT_DECAY = 0.5
MATRIX_RATE = 0.4
TABLE_RATE = 0.3
INITIAL_RATE = 0.05
GAINS_RATE = 0.3
BETA_ONE = 0.9
BETA_TWO = 0.95
ADAM_EPSILON = 1e-08
WEIGHT_DECAY = 0.01


CHUNK = 64
PAIR = 2 * P_SIZE


def dot_ab(left, right):
    return lax.dot_general(left, right, (((1,), (0,)), ((), ())), preferred_element_type=jnp.float32)


def dot_abt(left, right):
    return lax.dot_general(left, right, (((1,), (1,)), ((), ())), preferred_element_type=jnp.float32)


def dot_atb(left, right):
    return lax.dot_general(left, right, (((0,), (0,)), ((), ())), preferred_element_type=jnp.float32)


def halves_of(value):
    high = value.astype(jnp.bfloat16)
    return (high, (value - high.astype(jnp.float32)).astype(jnp.bfloat16))


def wide(form, left, right):
    lefts = left if isinstance(left, tuple) else (left,)
    rights = right if isinstance(right, tuple) else (right,)
    total = form(lefts[0], rights[0])
    if len(rights) > 1:
        total = total + form(lefts[0], rights[1])
    if len(lefts) > 1:
        total = total + form(lefts[1], rights[0])
    return total


def each(pieces, change):
    return tuple(change(piece) for piece in pieces) if isinstance(pieces, tuple) else change(pieces)


def mixer_masks(resets, tokens):
    per_chunk = CHUNK // MB
    chunks = tokens // CHUNK
    segment = jnp.cumsum(resets.reshape(chunks, per_chunk), axis=1)
    segment = jnp.repeat(segment, MB, axis=1)
    same = segment[:, :, None] == segment[:, None, :]
    spot = jnp.arange(CHUNK, dtype=jnp.int32)
    causal = (spot[None, :] <= spot[:, None])[None]
    earlier = ((spot[None, :] // MB) < (spot[:, None] // MB))[None]
    causal = (same & causal).astype(jnp.float32)
    earlier = (same & earlier).astype(jnp.float32)
    first = (segment == 0).astype(jnp.float32).reshape(tokens, 1)
    last = (segment == segment[:, -1:]).astype(jnp.float32).reshape(tokens, 1)
    anew = (segment[:, -1] > 0).astype(jnp.float32)
    first = jnp.broadcast_to(first, (tokens, PAIR))
    last = jnp.broadcast_to(last, (tokens, PAIR))
    anew = jnp.broadcast_to(anew[:, None, None], (chunks, 8, PAIR))
    return causal, earlier, first, last, anew


def lane_helpers(rows):
    lanes = lax.broadcasted_iota(jnp.int32, (rows, PAIR), 1)
    low_lane = lanes < P_SIZE
    low_half = low_lane.astype(jnp.float32)
    high_half = 1.0 - low_half

    def stack(pieces):
        def one(piece):
            kind = piece.dtype
            return jnp.concatenate(
                [piece * low_half.astype(kind), piece * high_half.astype(kind)], 0
            )

        return each(pieces, one)

    def pick(product):
        return jnp.where(low_lane, product[:rows], product[rows:])

    return stack, pick


def diagonal_blocks():
    rows = lax.broadcasted_iota(jnp.int32, (PAIR, PAIR), 0) // P_SIZE
    columns = lax.broadcasted_iota(jnp.int32, (PAIR, PAIR), 1) // P_SIZE
    return (rows == columns).astype(jnp.float32)


def solve(matrix, rate_row, value, pick):
    rows = value.shape[0]
    powers = [(matrix, rate_row)]
    reach = 2
    while reach < CHUNK // MB:
        last, rate = powers[-1]
        low, high = halves_of(last[:rows]), halves_of(last[rows:])
        powers.append(
            (
                jnp.concatenate([wide(dot_ab, low, low), wide(dot_ab, high, high)], 0),
                rate * rate,
            )
        )
        reach = 2 * reach
    for index in range(len(powers) - 1, -1, -1):
        factor, rate = powers[index]
        moved = pick(wide(dot_ab, halves_of(factor), halves_of(value * rate)))
        value = value - moved if index == 0 else value + moved
    return value


def mixer_forward_chunk(
    qkv_ref,
    rate_ref,
    initial_ref,
    causal_ref,
    earlier_ref,
    first_ref,
    last_ref,
    anew_ref,
    z_ref,
    residue_ref,
    states_ref,
    state,
):
    pairs = initial_ref.shape[0]
    width = pairs * PAIR

    stack, pick = lane_helpers(CHUNK)
    blocks = diagonal_blocks()
    causal = causal_ref[0]
    causal = jnp.concatenate([causal, causal], 0)
    earlier = earlier_ref[0]
    earlier = jnp.concatenate([earlier, earlier], 0)
    first = first_ref[...] > 0.0
    last = last_ref[...]
    anew = anew_ref[0, 0:1, :]
    for pair in range(pairs):
        lanes = slice(pair * PAIR, (pair + 1) * PAIR)
        query = qkv_ref[:, lanes]
        key = qkv_ref[:, width + pair * PAIR : width + (pair + 1) * PAIR]
        value = qkv_ref[:, 2 * width + pair * PAIR : 2 * width + (pair + 1) * PAIR]
        rate = rate_ref[0:1, lanes]
        begin = state[pair]
        initial = initial_ref[pair]
        states_ref[0, pair] = begin
        products = dot_abt(jnp.concatenate([stack(key), stack(query)], 0), key)
        ties = products[: 2 * CHUNK] * earlier
        scores = products[2 * CHUNK :] * causal
        both = jnp.concatenate([key, query], 0)
        seen = wide(dot_ab, both, halves_of(begin))
        fresh = wide(dot_ab, both, halves_of(initial))
        key_seen = jnp.where(first, seen[:CHUNK], fresh[:CHUNK])
        query_seen = jnp.where(first, seen[CHUNK:], fresh[CHUNK:])
        key_wide = key.astype(jnp.float32)
        residue = solve(ties, rate, key_seen - (value.astype(jnp.float32) - key_wide), pick)
        residue_ref[:, lanes] = residue
        scaled = residue * rate
        scaled_parts = halves_of(scaled)
        output = query_seen - pick(wide(dot_ab, halves_of(scores), scaled_parts))
        z_ref[:, lanes] = output.astype(jnp.bfloat16)
        key_last = (key_wide * last).astype(jnp.bfloat16)
        base = jnp.where(anew > 0.0, initial, begin)
        state[pair] = base - blocks * wide(dot_atb, key_last, scaled_parts)


def mixer_backward_kernel(
    qkv_ref,
    rate_ref,
    initial_ref,
    causal_ref,
    earlier_ref,
    causal_turned_ref,
    earlier_turned_ref,
    first_ref,
    last_ref,
    anew_ref,
    residue_ref,
    states_ref,
    upstream_ref,
    grad_ref,
    grad_initial_ref,
    grad_rate_ref,
    carried,
):
    pairs = initial_ref.shape[0]
    width = pairs * PAIR

    @pl.when(pl.program_id(0) == 0)
    def _():
        carried[...] = jnp.zeros_like(carried)
        grad_initial_ref[...] = jnp.zeros_like(grad_initial_ref)
        grad_rate_ref[...] = jnp.zeros_like(grad_rate_ref)

    stack, pick = lane_helpers(CHUNK)
    blocks = diagonal_blocks()

    def doubled(ref):
        return jnp.concatenate([ref[0], ref[0]], 0)

    causal, earlier = doubled(causal_ref), doubled(earlier_ref)
    causal_turned, earlier_turned = doubled(causal_turned_ref), doubled(earlier_turned_ref)
    first_wide = first_ref[...]
    first = first_wide > 0.0
    last = last_ref[...]
    anew = anew_ref[0, 0:1, :]
    low = jnp.bfloat16
    for pair in range(pairs):
        lanes = slice(pair * PAIR, (pair + 1) * PAIR)
        query = qkv_ref[:, lanes]
        key = qkv_ref[:, width + pair * PAIR : width + (pair + 1) * PAIR]
        rate = rate_ref[0:1, lanes]
        begin = halves_of(states_ref[0, pair])
        initial = halves_of(initial_ref[pair])
        after = carried[pair]
        after_parts = halves_of(after)
        residue = residue_ref[:, lanes]
        scaled = halves_of(residue * rate)
        upstream = upstream_ref[:, lanes]
        upstream_parts = halves_of(upstream)
        key_wide = key.astype(jnp.float32)
        query_wide = query.astype(jnp.float32)
        key_last = (key_wide * last).astype(low)
        key_stack = stack(key)
        products = dot_abt(key_stack, jnp.concatenate([key, query], 0))
        ties_turned = products[:, :CHUNK] * earlier_turned
        scores_turned = products[:, CHUNK:] * causal_turned
        pulled = pick(wide(dot_ab, halves_of(scores_turned), upstream_parts))
        pulled = pulled + wide(dot_ab, key_last, after_parts)
        grad_scaled = solve(ties_turned, rate, -pulled, pick)
        grad_rate_ref[0:1, lanes] += jnp.sum(grad_scaled * residue, 0, keepdims=True)
        grad_residue = grad_scaled * rate
        residue_parts = halves_of(grad_residue)
        joined = tuple(
            jnp.concatenate([one, two], 0) for one, two in zip(upstream_parts, residue_parts)
        )
        scaled_stack = stack(scaled)
        turned = wide(dot_abt, scaled_stack, joined)
        straight = wide(
            dot_abt,
            tuple(
                jnp.concatenate([stack(one), stack(two)], 0)
                for one, two in zip(upstream_parts, residue_parts)
            ),
            scaled,
        )
        grad_scores = -straight[: 2 * CHUNK] * causal
        grad_scores_turned = -turned[:, :CHUNK] * causal_turned
        grad_ties = -(straight[2 * CHUNK :] * earlier + turned[:, CHUNK:] * earlier_turned)
        seen = wide(dot_abt, joined, begin)
        fresh = wide(dot_abt, joined, initial)
        grad_query = jnp.where(first, seen[:CHUNK], fresh[:CHUNK])
        grad_query = grad_query + pick(wide(dot_ab, halves_of(grad_scores), key))
        grad_key = jnp.where(first, seen[CHUNK:], fresh[CHUNK:]) + grad_residue
        grad_key = grad_key + pick(
            wide(dot_ab, halves_of(grad_scores_turned), query)
            + wide(dot_ab, halves_of(grad_ties), key)
        )
        grad_key = grad_key - last * wide(dot_abt, scaled, after_parts)
        grad_ref[:, lanes] = grad_query.astype(low)
        grad_ref[:, width + pair * PAIR : width + (pair + 1) * PAIR] = grad_key.astype(low)
        grad_ref[:, 2 * width + pair * PAIR : 2 * width + (pair + 1) * PAIR] = (
            -grad_residue
        ).astype(low)
        fronts = jnp.concatenate([query_wide * first_wide, key_wide * first_wide], 0).astype(low)
        backs = jnp.concatenate(
            [query_wide * (1.0 - first_wide), key_wide * (1.0 - first_wide)], 0
        ).astype(low)
        kept_after = jnp.where(anew > 0.0, 0.0, after)
        carried[pair] = kept_after + blocks * wide(dot_atb, fronts, joined)
        grad_initial_ref[pair] += (after - kept_after) + blocks * wide(dot_atb, backs, joined)


def pair_blocks(matrices):
    heads = matrices.shape[0]
    split = matrices.reshape(heads // 2, 2, P_SIZE, P_SIZE)
    empty = jnp.zeros_like(split[:, 0])
    upper = jnp.concatenate([split[:, 0], empty], 2)
    lower = jnp.concatenate([empty, split[:, 1]], 2)
    return jnp.concatenate([upper, lower], 1)


def head_blocks(pairs):
    return jnp.stack([pairs[:, :P_SIZE, :P_SIZE], pairs[:, P_SIZE:, P_SIZE:]], 1).reshape(
        -1, P_SIZE, P_SIZE
    )


def mixer_backward(qkv, rate, initial, masks, residue, states, upstream):
    tokens = qkv.shape[0]
    width = rate.shape[1]
    pairs = initial.shape[0]
    chunks = tokens // CHUNK
    whole = lambda shape: pl.BlockSpec(shape, lambda i: (0,) * len(shape))
    square = pl.BlockSpec((1, CHUNK, CHUNK), lambda i: (chunks - 1 - i, 0, 0))
    column = pl.BlockSpec((CHUNK, PAIR), lambda i: (chunks - 1 - i, 0))
    rows = lambda size: pl.BlockSpec((CHUNK, size), lambda i: (chunks - 1 - i, 0))
    causal, earlier, first, last, anew = masks
    return pl.pallas_call(
        mixer_backward_kernel,
        grid=(chunks,),
        in_specs=[
            rows(3 * width),
            whole((1, width)),
            whole((pairs, PAIR, PAIR)),
            square,
            square,
            square,
            square,
            column,
            column,
            pl.BlockSpec((1, 8, PAIR), lambda i: (chunks - 1 - i, 0, 0)),
            rows(width),
            pl.BlockSpec((1, pairs, PAIR, PAIR), lambda i: (chunks - 1 - i, 0, 0, 0)),
            rows(width),
        ],
        out_specs=[rows(3 * width), whole((pairs, PAIR, PAIR)), whole((1, width))],
        out_shape=[
            jax.ShapeDtypeStruct((tokens, 3 * width), jnp.bfloat16),
            jax.ShapeDtypeStruct((pairs, PAIR, PAIR), jnp.float32),
            jax.ShapeDtypeStruct((1, width), jnp.float32),
        ],
        scratch_shapes=[pltpu.VMEM((pairs, PAIR, PAIR), jnp.float32)],
        compiler_params=pltpu.CompilerParams(
            dimension_semantics=("arbitrary",), vmem_limit_bytes=32 * 1024 * 1024
        ),
        cost_estimate=pl.CostEstimate(
            flops=0, bytes_accessed=140000 * tokens, transcendentals=0
        ),
        name="inner_backward",
    )(
        qkv,
        rate,
        initial,
        causal,
        earlier,
        jnp.swapaxes(causal, 1, 2),
        jnp.swapaxes(earlier, 1, 2),
        first,
        last,
        anew,
        residue,
        states,
        upstream,
    )


ROWS = 64
LAG = 2
MESH = pl.DeviceIdType.MESH


def across(column):
    return jnp.swapaxes(jnp.broadcast_to(column, (column.shape[0], 128)), 0, 1)[:8]


def down(row, width):
    turned = jnp.swapaxes(jnp.broadcast_to(row[:1], (128, row.shape[1])), 0, 1)
    return jnp.concatenate([turned] * (width // 128), 1) if width > 128 else turned


def transit_kernel(mode, form, parts, slabs, names, *all_refs):
    ref = dict(zip(names, all_refs))
    full_ref, partial, total = ref["full"], ref["partial"], ref["total"]
    pair_out, pair_in = ref["pair_out"], ref["pair_in"]
    from_low, from_high = ref["from_low"], ref["from_high"]
    places = parts // 2
    cross = form in ("lookup", "table")
    summing = mode != "plain"
    size = total.shape[1]
    ring, band = partial.shape[0], partial.shape[1]
    me = lax.axis_index("head")
    mine_dp = lax.axis_index("dp")
    core = lax.rem(me, 2)
    spot = me // 2
    twin = {"head": me + 1 - 2 * core}
    upper = {"head": lax.rem(me + 2, parts)}
    lower = {"head": lax.rem(me + parts - 2, parts)}
    chunks = ref["up_in_sem"].shape[0]
    sum_at = LAG * places
    finish_at = sum_at + (LAG if summing else 0)
    reach_at = finish_at + LAG * (places - 1)
    close_at = reach_at + (2 * LAG if cross else LAG)

    def rows_of(chunk):
        return pl.ds(pl.multiple_of(chunk * band, band), band)

    def shard(index):
        return pl.ds(pl.multiple_of(index * size, 128), size)

    def remote(source, target, out_sem, in_sem, device):
        return pltpu.make_async_remote_copy(
            src_ref=source,
            dst_ref=target,
            send_sem=out_sem,
            recv_sem=in_sem,
            device_id=device,
            device_id_type=MESH,
        )

    def left_copy(chunk):
        half = lax.rem(chunk, 2)
        return pltpu.make_async_copy(
            ref["left"].at[rows_of(chunk)], ref["left_buf"].at[half], ref["left_sem"].at[half]
        )

    barrier = pltpu.get_barrier_semaphore()
    for offset in range(1, parts):
        pl.semaphore_signal(
            barrier, inc=1, device_id={"head": lax.rem(me + offset, parts)}, device_id_type=MESH
        )
    if cross:
        for offset in range(1, slabs):
            pl.semaphore_signal(
                barrier,
                inc=1,
                device_id={"dp": lax.rem(mine_dp + offset, slabs)},
                device_id_type=MESH,
            )
    if form in ("rows", "turned", "table"):
        left_copy(0).start()
    if mode in ("grad", "grad_add"):
        ref["gain_grad"][...] = jnp.zeros_like(ref["gain_grad"])
    if form == "table":
        ref["table_grad"][...] = jnp.zeros_like(ref["table_grad"])
    pl.semaphore_wait(barrier, parts - 1 + (slabs - 1 if cross else 0))

    def valid(chunk):
        return jnp.logical_and(chunk >= 0, chunk < chunks)

    def pair_copy(chunk):
        slot = lax.rem(chunk, ring)
        return remote(
            pair_out.at[slot],
            pair_in.at[slot],
            ref["pair_out_sem"].at[slot],
            ref["pair_in_sem"].at[slot],
            twin,
        )

    def rise(chunk, place):
        slot = lax.rem(chunk, ring)
        part = from_low.at[slot, :, pl.ds((place + 1) * size, (places - 1 - place) * size)]
        return remote(part, part, ref["low_out_sem"].at[slot], ref["low_in_sem"].at[slot], upper)

    def fall(chunk, place):
        slot = lax.rem(chunk, ring)
        part = from_high.at[slot, :, pl.ds(0, place * size)]
        return remote(part, part, ref["high_out_sem"].at[slot], ref["high_in_sem"].at[slot], lower)

    def sums_copy(chunk, offset):
        slot = lax.rem(chunk, ring)
        return remote(
            ref["sums_out"].at[slot],
            ref["sums_in"].at[slot, offset - 1],
            ref["sums_out_sem"].at[slot],
            ref["sums_in_sem"].at[slot],
            {"head": lax.rem(me + offset, parts)},
        )

    def piece(chunk, source):
        if cross:
            return ref["stage"].at[rows_of(chunk), shard(source)]
        return full_ref.at[rows_of(chunk), shard(2 * source + core)]

    def climb(chunk, source, hop):
        part = piece(chunk, source)
        return remote(
            part,
            part,
            ref["up_out_sem"].at[chunk, hop - 1],
            ref["up_in_sem"].at[chunk, hop - 1],
            upper,
        )

    def sink(chunk, source, hop):
        part = piece(chunk, source)
        return remote(
            part,
            part,
            ref["down_out_sem"].at[chunk, hop - 1],
            ref["down_in_sem"].at[chunk, hop - 1],
            lower,
        )

    def target(chunk, giver):
        if form == "lookup":
            return full_ref.at[rows_of(chunk), shard(2 * giver + core)]
        return full_ref.at[chunk // 2, rows_of(lax.rem(chunk, 2) * slabs + giver), shard(core)]

    def mirror(chunk, index):
        part = target(chunk, index) if cross else piece(chunk, index)
        return remote(
            part, part, ref["twin_out_sem"].at[chunk], ref["twin_in_sem"].at[chunk], twin
        )

    def hand_over(chunk, source):
        return remote(
            piece(chunk, source),
            target(chunk, mine_dp),
            ref["cross_out_sem"].at[chunk, source],
            ref["cross_in_sem"].at[chunk, mine_dp],
            {"dp": source},
        )

    def have(chunk, source):
        if not cross:
            mirror(chunk, source).start()
            return

        @pl.when(source != mine_dp)
        def _():
            hand_over(chunk, source).start()

        @pl.when(source == mine_dp)
        def _():
            values = ref["stage"][rows_of(chunk), shard(source)]
            if form == "lookup":
                full_ref[rows_of(chunk), shard(2 * mine_dp + core)] = values
            else:
                place_rows = rows_of(lax.rem(chunk, 2) * slabs + mine_dp)
                full_ref[chunk // 2, place_rows, shard(core)] = values
            mirror(chunk, mine_dp).start()

    def receive(step):
        for hop in range(places):
            chunk = step - finish_at - LAG * (hop + 1)

            @pl.when(jnp.logical_and(valid(chunk), jnp.abs(spot - mine_dp) == hop))
            def _():
                for offset in range(1, slabs):
                    giver = lax.rem(mine_dp + offset, slabs)
                    part = target(chunk, giver)
                    remote(
                        part,
                        part,
                        ref["cross_out_sem"].at[chunk, giver],
                        ref["cross_in_sem"].at[chunk, giver],
                        twin,
                    ).wait_recv()
                    mirror(chunk, giver).start()

    def relay(step):
        for hop in range(1, places):
            chunk = step - finish_at - LAG * hop
            source = spot - hop

            @pl.when(jnp.logical_and(valid(chunk), source >= 0))
            def _():
                climb(chunk, source, hop).wait_recv()
                if hop < places - 1:

                    @pl.when(spot < places - 1)
                    def _():
                        climb(chunk, source, hop + 1).start()

                have(chunk, source)

            source_high = spot + hop

            @pl.when(jnp.logical_and(valid(chunk), source_high < places))
            def _():
                sink(chunk, source_high, hop).wait_recv()
                if hop < places - 1:

                    @pl.when(spot > 0)
                    def _():
                        sink(chunk, source_high, hop + 1).start()

                have(chunk, source_high)

    def finish_shard(step):
        chunk = step - finish_at

        @pl.when(valid(chunk))
        def _():
            slot = lax.rem(chunk, ring)
            rows = rows_of(chunk)
            if summing:
                sums_in = ref["sums_in"]
                pltpu.make_async_copy(
                    sums_in.at[slot], sums_in.at[slot], ref["sums_in_sem"].at[slot]
                ).wait()
                summed = ref["sums_out"][slot]
                for offset in range(1, parts):
                    summed = summed + sums_in[slot, offset - 1]
                gain = ref["gain"][0:1, :]
            if mode == "plain":
                result = total[...]
            elif mode == "norm":
                scale = lax.rsqrt(summed / D + EPSILON)
                ref["scale"][chunk] = scale
                result = ref["own"][rows, :] * down(scale, size) * gain
            else:
                scale = down(ref["scale"][chunk], size)
                normed = ref["inputs"][rows, :] * scale
                inner = down(summed / D, size)
                result = scale * (ref["own"][rows, :] * gain - normed * inner)
                if mode == "grad_add":
                    result = result + ref["added"][rows, :]
                if form != "table":
                    ref["own"][rows, :] = result
            if cross:
                ref["stage"][rows, shard(spot)] = result.astype(jnp.bfloat16)
            else:
                full_ref[rows, shard(me)] = result.astype(jnp.bfloat16)

            @pl.when(spot < places - 1)
            def _():
                climb(chunk, spot, 1).start()

            @pl.when(spot > 0)
            def _():
                sink(chunk, spot, 1).start()

            have(chunk, spot)

    def add_pair(step):
        chunk = step - LAG

        @pl.when(valid(chunk))
        def _():
            slot = lax.rem(chunk, ring)
            pair_copy(chunk).wait_recv()
            partial[slot] = partial[slot] + pair_in[slot].astype(jnp.float32)

    def pass_on(step):
        for place in range(places):
            if place < places - 1:
                up_chunk = step - LAG * (1 + place)

                @pl.when(jnp.logical_and(valid(up_chunk), spot == place))
                def _():
                    slot = lax.rem(up_chunk, ring)
                    above = pl.ds((place + 1) * size, (places - 1 - place) * size)
                    values = partial[slot, :, above]
                    if place > 0:
                        rise(up_chunk, place - 1).wait_recv()
                        values = values + from_low[slot, :, above].astype(jnp.float32)
                    from_low[slot, :, above] = values.astype(jnp.bfloat16)
                    rise(up_chunk, place).start()

            if place > 0:
                down_chunk = step - LAG * (places - place)

                @pl.when(jnp.logical_and(valid(down_chunk), spot == place))
                def _():
                    slot = lax.rem(down_chunk, ring)
                    below = pl.ds(0, place * size)
                    values = partial[slot, :, below]
                    if place < places - 1:
                        fall(down_chunk, place + 1).wait_recv()
                        values = values + from_high[slot, :, below].astype(jnp.float32)
                    from_high[slot, :, below] = values.astype(jnp.bfloat16)
                    fall(down_chunk, place).start()

    def settle(step):
        chunk = step - sum_at - LAG

        @pl.when(valid(chunk))
        def _():
            pair_copy(chunk).wait_send()
            for place in range(places):

                @pl.when(spot == place)
                def _():
                    if place < places - 1:
                        rise(chunk, place).wait_send()
                    if place > 0:
                        fall(chunk, place).wait_send()

            if summing:
                slot = lax.rem(chunk, ring)
                sums_in = ref["sums_in"]
                pltpu.make_async_copy(
                    sums_in.at[slot], sums_in.at[slot], ref["sums_out_sem"].at[slot]
                ).wait()

    def sum_shard(step):
        chunk = step - sum_at

        @pl.when(valid(chunk))
        def _():
            slot = lax.rem(chunk, ring)
            rows = rows_of(chunk)
            mine = shard(spot)

            @pl.when(spot == places - 1)
            def _():
                rise(chunk, places - 2).wait_recv()

            @pl.when(spot == 0)
            def _():
                fall(chunk, 1).wait_recv()

            total[...] = partial[slot, :, mine]

            @pl.when(spot > 0)
            def _():
                total[...] += from_low[slot, :, mine].astype(jnp.float32)

            @pl.when(spot < places - 1)
            def _():
                total[...] += from_high[slot, :, mine].astype(jnp.float32)

            if not summing:
                return
            value = total[...]
            if mode == "norm":
                value = value + ref["inputs"][rows, :]
                column = jnp.sum(value * value, 1, keepdims=True)
            else:
                scale = down(ref["scale"][chunk], size)
                normed = ref["inputs"][rows, :] * scale
                ref["gain_grad"][0:1, :] += jnp.sum(value * normed, 0, keepdims=True)
                column = jnp.sum(value * ref["gain"][0:1, :] * normed, 1, keepdims=True)
            ref["own"][rows, :] = value
            ref["sums_out"][slot] = across(column)
            for offset in range(1, parts):
                sums_copy(chunk, offset).start()

    def produce(step):
        chunk = step

        @pl.when(valid(chunk))
        def _():
            slot = lax.rem(chunk, ring)
            right_ref = ref["right"]
            if form == "lookup":
                entries = right_ref.shape[0]
                ids = jnp.concatenate(
                    [ref["ids"][group, rows_of(chunk), 0:1] for group in range(slabs)], 0
                )
                spots = lax.broadcasted_iota(jnp.int32, (slabs * band, entries), 1)
                hits = (spots == ids).astype(jnp.bfloat16)
                other = dot_ab(hits, right_ref[:, shard(1 - core)]).astype(jnp.bfloat16)
                for group in range(slabs):
                    pair_out[slot, :, pl.ds(group * size, size)] = other[
                        group * band : (group + 1) * band
                    ]
                pair_copy(chunk).start()
                here = dot_ab(hits, right_ref[:, shard(core)])
                for group in range(slabs):
                    partial[slot, :, pl.ds(group * size, size)] = here[
                        group * band : (group + 1) * band
                    ]
                return
            half = lax.rem(chunk, 2)
            if form == "mixer":
                one = pl.ds(chunk, 1)
                here = rows_of(chunk)

                @pl.when(chunk == 0)
                def _():
                    ref["state"][...] = jnp.zeros_like(ref["state"])

                mixer_forward_chunk(
                    ref["qkv"].at[here],
                    ref["rate"],
                    ref["initial"],
                    ref["causal"].at[one],
                    ref["earlier"].at[one],
                    ref["first"].at[here],
                    ref["last"].at[here],
                    ref["anew"].at[one],
                    ref["z"].at[here],
                    ref["residue"].at[here],
                    ref["states"].at[one],
                    ref["state"],
                )
            else:
                left_copy(chunk).wait()

                @pl.when(chunk + 1 < chunks)
                def _():
                    left_copy(chunk + 1).start()

            def term(index):
                if form == "mixer":
                    return dot_ab(ref["z"][rows_of(chunk), :], right_ref[:, shard(index)])
                if form in ("turned", "table"):
                    return dot_abt(ref["left_buf"][half], right_ref[shard(index), :])
                return dot_ab(ref["left_buf"][half], right_ref[:, shard(index)])

            for place in range(places):
                lanes = pl.ds(place * size, size)
                pair_out[slot, :, lanes] = term(2 * place + 1 - core).astype(jnp.bfloat16)
            pair_copy(chunk).start()
            for place in range(places):
                lanes = pl.ds(place * size, size)
                partial[slot, :, lanes] = term(2 * place + core)

    def close(step):
        chunk = step - close_at

        @pl.when(valid(chunk))
        def _():
            if form == "table":
                arrived = full_ref.at[chunk // 2, pl.ds(0, slabs * band), pl.ds(0, size)]
            else:
                arrived = full_ref.at[rows_of(chunk), pl.ds(0, places * size)]
            pltpu.make_async_copy(arrived, arrived, ref["twin_in_sem"].at[chunk]).wait()
            pltpu.make_async_copy(arrived, arrived, ref["twin_out_sem"].at[chunk]).wait()
            if cross:
                for offset in range(1, slabs):
                    hand_over(chunk, lax.rem(mine_dp + offset, slabs)).wait_send()
            for hop in range(1, places):
                source = spot - hop + 1

                @pl.when(jnp.logical_and(source >= 0, spot < places - 1))
                def _():
                    climb(chunk, source, hop).wait_send()

                source_high = spot + hop - 1

                @pl.when(jnp.logical_and(source_high < places, spot > 0))
                def _():
                    sink(chunk, source_high, hop).wait_send()

            if form == "table":
                @pl.when(lax.rem(chunk, 2) == 1)
                def _():
                    table_grad = ref["table_grad"]
                    entries = table_grad.shape[0]
                    pieces = 5 if entries % 80 == 0 else 1
                    block = entries // pieces
                    ids = ref["ids"][chunk // 2, 0:1, :]
                    values = full_ref[chunk // 2]
                    for index in range(pieces):
                        spots = index * block + lax.broadcasted_iota(
                            jnp.int32, (block, ids.shape[1]), 0
                        )
                        hits = (spots == ids).astype(jnp.bfloat16)
                        span = pl.ds(index * block, block)
                        table_grad[span, :] += dot_ab(hits, values)

    def advance(step, carried):
        relay(step)
        if summing:
            finish_shard(step)
        if cross:
            receive(step)
        add_pair(step)
        pass_on(step)
        settle(step)
        sum_shard(step)
        if not summing:
            finish_shard(step)
        produce(step)
        close(step)
        return carried

    lax.fori_loop(0, chunks + close_at, advance, 0)


def transit(
    mode,
    form,
    number,
    parts,
    slabs,
    right,
    tokens,
    size,
    left=None,
    inputs=None,
    gain=None,
    scale=None,
    added=None,
    ids=None,
    entries=None,
    mixer=None,
    band=ROWS,
):
    chunks = tokens // band
    places = parts // 2
    cross = form in ("lookup", "table")
    summing = mode != "plain"
    ring = min(chunks, LAG * (places + 1) + 2) if summing else chunks
    dma = pltpu.SemaphoreType.DMA
    low, wide_kind = jnp.bfloat16, jnp.float32
    vmem = pl.BlockSpec(memory_space=pltpu.VMEM)
    operands, specs, outputs, scratch = {}, [], {}, {}

    def take(name, array, spec=vmem):
        operands[name] = array
        specs.append(spec)

    take("right", right)
    if left is not None:
        take("left", left, pl.BlockSpec(memory_space=pl.ANY))
    if ids is not None:
        take("ids", ids)
    if mixer is not None:
        for name, array in mixer.items():
            take(name, array)
        pairs, width = mixer["initial"].shape[0], mixer["rate"].shape[1]
    if summing:
        take("inputs", inputs)
        take("gain", gain)
    if mode in ("grad", "grad_add"):
        take("scale", scale)
    if mode == "grad_add":
        take("added", added)

    if summing and form != "table":
        outputs["own"] = ((tokens, size), wide_kind)
    if form != "table":
        outputs["full"] = ((tokens, parts * size), low)
    if mode == "norm":
        outputs["scale"] = ((chunks, 8, band), wide_kind)
    if mode in ("grad", "grad_add"):
        outputs["gain_grad"] = ((8, size), wide_kind)
    if form == "table":
        outputs["table_grad"] = ((entries, 2 * size), wide_kind)

    if mixer is not None:
        outputs["z"] = ((tokens, width), low)
        outputs["residue"] = ((tokens, width), wide_kind)
        outputs["states"] = ((chunks, pairs, PAIR, PAIR), wide_kind)
        scratch["state"] = pltpu.VMEM((pairs, PAIR, PAIR), wide_kind)
    span = places * size
    hops = max(places - 1, 1)
    if form == "table":
        scratch["own"] = pltpu.VMEM((tokens, size), wide_kind)
        scratch["full"] = pltpu.VMEM((chunks // 2, 2 * slabs * band, 2 * size), low)
    if left is not None:
        scratch["left_buf"] = pltpu.VMEM((2, band, left.shape[1]), low)
        scratch["left_sem"] = dma((2,))
    if cross:
        scratch["stage"] = pltpu.VMEM((tokens, span), low)
        scratch["cross_out_sem"] = dma((chunks, slabs))
        scratch["cross_in_sem"] = dma((chunks, slabs))
    if summing:
        scratch["sums_out"] = pltpu.VMEM((ring, 8, band), wide_kind)
        scratch["sums_in"] = pltpu.VMEM((ring, parts - 1, 8, band), wide_kind)
        scratch["sums_out_sem"] = dma((ring,))
        scratch["sums_in_sem"] = dma((ring,))
    scratch["total"] = pltpu.VMEM((band, size), wide_kind)
    scratch["partial"] = pltpu.VMEM((ring, band, span), wide_kind)
    for name in ("pair_out", "pair_in", "from_low", "from_high"):
        scratch[name] = pltpu.VMEM((ring, band, span), low)
    for name in ("pair_out", "pair_in", "low_out", "low_in", "high_out", "high_in"):
        scratch[name + "_sem"] = dma((ring,))
    for name in ("up_out", "up_in", "down_out", "down_in"):
        scratch[name + "_sem"] = dma((chunks, hops))
    scratch["twin_out_sem"] = dma((chunks,))
    scratch["twin_in_sem"] = dma((chunks,))

    depth = right.shape[1] if form in ("turned", "table") else right.shape[0]
    names = tuple(operands) + tuple(outputs) + tuple(scratch)
    results = pl.pallas_call(
        functools.partial(transit_kernel, mode, form, parts, slabs, names),
        in_specs=specs,
        out_specs=[vmem] * len(outputs),
        out_shape=[jax.ShapeDtypeStruct(shape, kind) for shape, kind in outputs.values()],
        scratch_shapes=list(scratch.values()),
        compiler_params=pltpu.CompilerParams(
            collective_id=number, has_side_effects=True, vmem_limit_bytes=60 * 1024 * 1024
        ),
        cost_estimate=pl.CostEstimate(
            flops=2 * tokens * depth * parts * size,
            bytes_accessed=128 * tokens * parts * size,
            transcendentals=0,
        ),
        name="transit_" + form,
    )(*operands.values())
    return dict(zip(outputs, results))


def share_kernel(axes, block_ref, all_ref, out_sem, in_sem):
    counts = [lax.axis_size(axis) for axis in axes]
    places = [lax.axis_index(axis) for axis in axes]
    members = 1
    me = 0
    for count, place in zip(counts, places):
        members = members * count
        me = me * count + place

    def partner(offset):
        device, rest = {}, offset
        for axis, count, place in reversed(list(zip(axes, counts, places))):
            device[axis] = lax.rem(place + lax.rem(rest, count), count)
            rest = rest // count
        return device

    def send(offset):
        return pltpu.make_async_remote_copy(
            src_ref=block_ref,
            dst_ref=all_ref.at[me],
            send_sem=out_sem,
            recv_sem=in_sem,
            device_id=partner(offset),
            device_id_type=MESH,
        )

    barrier = pltpu.get_barrier_semaphore()

    def greet(offset, carried):
        pl.semaphore_signal(barrier, inc=1, device_id=partner(offset), device_id_type=MESH)
        return carried

    def start(offset, carried):
        send(offset).start()
        return carried

    lax.fori_loop(1, members, greet, 0)
    all_ref[me] = block_ref[...]
    pl.semaphore_wait(barrier, members - 1)
    lax.fori_loop(1, members, start, 0)
    arrived = all_ref.at[pl.ds(0, members - 1)]
    pltpu.make_async_copy(arrived, arrived, in_sem).wait()
    pltpu.make_async_copy(arrived, arrived, out_sem).wait()


def share(number, block, axes):
    members = 1
    for axis in axes:
        members = members * lax.axis_size(axis)
    vmem = pl.BlockSpec(memory_space=pltpu.VMEM)
    return pl.pallas_call(
        functools.partial(share_kernel, axes),
        in_specs=[vmem],
        out_specs=vmem,
        out_shape=jax.ShapeDtypeStruct((members,) + block.shape, block.dtype),
        scratch_shapes=[pltpu.SemaphoreType.DMA, pltpu.SemaphoreType.DMA],
        compiler_params=pltpu.CompilerParams(
            collective_id=number, has_side_effects=True, vmem_limit_bytes=16 * 1024 * 1024
        ),
        cost_estimate=pl.CostEstimate(
            flops=0, bytes_accessed=16 * 1024 * 1024, transcendentals=0
        ),
        name="share",
    )(block)


SCORE_ROWS = 256


def scores_kernel(rows_ref, table_ref, goal_ref, logits_ref, stats_ref):
    entries = table_ref.shape[0]
    edges = list(range(0, entries, 1024)) + [entries]
    peak = jnp.full((SCORE_ROWS, 1), -jnp.inf, jnp.float32)
    for low, high in zip(edges, edges[1:]):
        values = dot_abt(rows_ref[...], table_ref[low:high, :])
        logits_ref[:, low:high] = values
        peak = jnp.maximum(peak, jnp.max(values, 1, keepdims=True))
    exp_sum = jnp.zeros((SCORE_ROWS, 1), jnp.float32)
    picked = jnp.zeros((SCORE_ROWS, 1), jnp.float32)
    goal = goal_ref[:, 0:1]
    for low, high in zip(edges, edges[1:]):
        values = logits_ref[:, low:high]
        exp_sum = exp_sum + jnp.sum(jnp.exp(values - peak), 1, keepdims=True)
        spots = low + lax.broadcasted_iota(jnp.int32, values.shape, 1)
        picked = picked + jnp.sum(jnp.where(spots == goal, values, 0.0), 1, keepdims=True)
    stats_ref[0] = jnp.broadcast_to(peak, (SCORE_ROWS, 128))
    stats_ref[1] = jnp.broadcast_to(exp_sum, (SCORE_ROWS, 128))
    stats_ref[2] = jnp.broadcast_to(picked, (SCORE_ROWS, 128))


def scores(rows, table, goals):
    tokens, width = rows.shape
    entries = table.shape[0]
    return pl.pallas_call(
        scores_kernel,
        grid=(tokens // SCORE_ROWS,),
        in_specs=[
            pl.BlockSpec((SCORE_ROWS, width), lambda i: (i, 0)),
            pl.BlockSpec(memory_space=pltpu.VMEM),
            pl.BlockSpec((SCORE_ROWS, 128), lambda i: (i, 0)),
        ],
        out_specs=[
            pl.BlockSpec((SCORE_ROWS, entries), lambda i: (i, 0)),
            pl.BlockSpec((3, SCORE_ROWS, 128), lambda i: (0, i, 0)),
        ],
        out_shape=[
            jax.ShapeDtypeStruct((tokens, entries), jnp.float32),
            jax.ShapeDtypeStruct((3, tokens, 128), jnp.float32),
        ],
        compiler_params=pltpu.CompilerParams(
            dimension_semantics=("arbitrary",), vmem_limit_bytes=56 * 1024 * 1024
        ),
        cost_estimate=pl.CostEstimate(
            flops=2 * tokens * entries * width,
            bytes_accessed=2 * entries * width + 4 * tokens * entries,
            transcendentals=tokens * entries,
        ),
        name="scores",
    )(rows, table, goals)


def shampoo(tile_w, tile_g, left, right, left_root, right_root):
    low_g = tile_g.astype(jnp.bfloat16)

    def product(form, one, two):
        return jnp.einsum(
            form,
            one.astype(jnp.bfloat16),
            two.astype(jnp.bfloat16),
            preferred_element_type=jnp.float32,
        )

    new_left = STAT_DECAY * left + (1.0 - STAT_DECAY) * product("abrc,absc->abrs", low_g, low_g)
    new_right = STAT_DECAY * right + (1.0 - STAT_DECAY) * product("abrc,abrd->abcd", low_g, low_g)
    turned = product("abrs,absc->abrc", left_root, low_g)
    turned = product("abrc,abcd->abrd", turned, right_root)
    return (new_left, new_right, tile_w - MATRIX_RATE * (turned + WEIGHT_DECAY * tile_w))


def refresh(master, grad, left, right, left_root, right_root):
    rows = master.shape[1]
    new_left, new_right, new_w = shampoo(
        master.reshape(1, 1, rows, -1),
        grad.reshape(1, 1, rows, -1),
        left,
        right,
        left_root,
        right_root,
    )
    return (grad.reshape(master.shape), new_left, new_right, new_w.reshape(master.shape))


def adamw(weight, grad, first, second, step_rate):
    new_first = BETA_ONE * first + (1.0 - BETA_ONE) * grad
    new_second = BETA_TWO * second + (1.0 - BETA_TWO) * grad * grad
    moved = (
        new_first
        / (1.0 - BETA_ONE**STEP)
        / (jnp.sqrt(new_second / (1.0 - BETA_TWO**STEP)) + ADAM_EPSILON)
    )
    return (new_first, new_second, weight - step_rate * (moved + WEIGHT_DECAY * weight))


def layer_forward(
    local_ids, targets, valid, resets, emb_low, weights, inner_init, gains, gain_one, head_index
):
    w_qkv, w_out, w_gu, w_down, table = weights
    parts, slabs = lax.axis_size("head"), lax.axis_size("dp")
    vocab_part = table.shape[0]
    tokens, size = targets.shape[0], gains.shape[1]
    chunks = tokens // ROWS
    columns = jnp.arange(vocab_part, dtype=jnp.int32)
    spread_ids = jnp.broadcast_to(local_ids[:, :, None], (slabs, tokens, 128))
    first = transit("plain", "lookup", 1, parts, slabs, emb_low, tokens, size, ids=spread_ids)
    low_embedded = first["full"]
    wide_embedded = low_embedded.astype(jnp.float32)
    scale_one = lax.rsqrt(jnp.mean(wide_embedded * wide_embedded, -1) + EPSILON)
    full_one = (wide_embedded * scale_one[:, None] * gain_one[None]).astype(jnp.bfloat16)
    embedded = lax.dynamic_slice_in_dim(low_embedded, head_index * size, size, 1)
    embedded = embedded.astype(jnp.float32)
    scale_one = jnp.broadcast_to(scale_one.reshape(chunks, 1, ROWS), (chunks, 8, ROWS))
    mixed = jnp.dot(full_one, w_qkv, preferred_element_type=jnp.float32).astype(jnp.bfloat16)
    step_rate = jax.nn.sigmoid(gains[3:4]) / (8 * P_SIZE)
    masks = mixer_masks(resets, tokens)
    initial_pairs = pair_blocks(inner_init)
    causal, earlier, before, after, anew = masks
    second = transit(
        "norm",
        "mixer",
        2,
        parts,
        slabs,
        w_out,
        tokens,
        size,
        mixer=dict(
            qkv=mixed,
            rate=step_rate,
            initial=initial_pairs,
            causal=causal,
            earlier=earlier,
            first=before,
            last=after,
            anew=anew,
        ),
        inputs=embedded,
        gain=gains[1:2],
    )
    inner_low, residue, states = second["z"], second["residue"], second["states"]
    hidden_one, full_two, scale_two = second["own"], second["full"], second["scale"]
    gate_up = jnp.dot(full_two, w_gu, preferred_element_type=jnp.float32)

    def swiglu(paired):
        halves = paired.reshape(tokens, 2, -1)
        return jax.nn.silu(halves[:, 0]) * halves[:, 1]

    activated, act_pull = jax.vjp(swiglu, gate_up)
    act_low = activated.astype(jnp.bfloat16)
    third = transit(
        "norm",
        "rows",
        3,
        parts,
        slabs,
        w_down,
        tokens,
        size,
        left=act_low,
        inputs=hidden_one,
        gain=gains[2:3],
    )
    hidden_two, full_end, scale_end = third["own"], third["full"], third["scale"]
    local_targets = targets - head_index * vocab_part
    target_hits = columns[None, :] == local_targets[:, None]
    logits, stats = scores(
        full_end, table, jnp.broadcast_to(local_targets[:, None], (tokens, 128))
    )
    stats = share(7, stats[:, :, 0].reshape(-1, 128), ("head",)).reshape(parts, 3, tokens)
    highest = jnp.max(stats[:, 0], 0)
    exp_sum = jnp.sum(stats[:, 1] * jnp.exp(stats[:, 0] - highest[None]), 0)
    target_logit = jnp.sum(stats[:, 2], 0)
    totals = highest + jnp.log(exp_sum)
    counted = valid.astype(jnp.float32)
    d_logits = (
        (jnp.exp(logits - totals[:, None]) - target_hits.astype(jnp.float32)) * counted[:, None]
    ).astype(jnp.bfloat16)
    kept = (
        embedded,
        scale_one,
        full_one,
        (mixed, step_rate, initial_pairs, masks, residue, states),
        inner_low,
        hidden_one,
        scale_two,
        full_two,
        act_pull,
        act_low,
        hidden_two,
        scale_end,
        full_end,
        d_logits,
        local_ids,
    )
    return (jnp.sum((totals - target_logit) * counted), jnp.sum(counted), kept)


def slots_of(grad, order):
    parts = lax.axis_size("dp")
    shaped = grad.astype(jnp.bfloat16).reshape(parts, -1, grad.shape[1])
    return jnp.take(shaped, order, axis=0, mode="clip")


def column_slots_of(grad, order):
    parts = lax.axis_size("dp")
    shaped = grad.astype(jnp.bfloat16).reshape(grad.shape[0], parts, -1)
    return jnp.take(jnp.swapaxes(shaped, 0, 1), order, axis=0, mode="clip")


def scatter_dp(grad, dimension):
    return lax.psum_scatter(grad, "dp", scatter_dimension=dimension, tiled=True)


def rebanded(scale, band):
    rows = scale[:, 0].reshape(-1, 1, band)
    return jnp.broadcast_to(rows, (rows.shape[0], 8, band))


def layer_backward(kept, weights, gains, order):
    (
        embedded,
        scale_one,
        full_one,
        inner_kept,
        inner_low,
        hidden_one,
        scale_two,
        full_two,
        act_pull,
        act_low,
        hidden_two,
        scale_end,
        full_end,
        d_logits,
        local_ids,
    ) = kept
    w_qkv, w_out, w_gu, w_down, table = weights
    parts, slabs = lax.axis_size("head"), lax.axis_size("dp")
    tokens, size = embedded.shape
    chunks = tokens // ROWS
    wide_kind = jnp.float32
    grad_table = jnp.einsum("tv,td->vd", d_logits, full_end, preferred_element_type=wide_kind)
    grad_table = grad_table.astype(jnp.bfloat16)
    owned_table = scatter_dp(grad_table, 1)
    d_logits, grad_table = lax.optimization_barrier((d_logits, grad_table))
    fourth = transit(
        "grad",
        "rows",
        4,
        parts,
        slabs,
        table,
        tokens,
        size,
        left=d_logits,
        inputs=hidden_two,
        gain=gains[2:3],
        scale=rebanded(scale_end, 2 * ROWS),
        band=2 * ROWS,
    )
    d_two, d_down_in = fourth["own"], fourth["full"]
    d_down_in, owned_table = lax.optimization_barrier((d_down_in, owned_table))
    d_act = jnp.einsum("td,fd->tf", d_down_in, w_down, preferred_element_type=wide_kind)
    d_gate_up = act_pull(d_act)[0].astype(jnp.bfloat16)
    grad_down = jnp.einsum("tf,td->fd", act_low, d_down_in, preferred_element_type=wide_kind)
    slot_down = column_slots_of(grad_down, order[3])
    d_gate_up, slot_down = lax.optimization_barrier((d_gate_up, slot_down))
    owned_down = scatter_dp(slot_down, 0)
    fifth = transit(
        "grad_add",
        "turned",
        5,
        parts,
        slabs,
        w_gu,
        tokens,
        size,
        left=d_gate_up,
        inputs=hidden_one,
        gain=gains[1:2],
        scale=scale_two,
        added=d_two,
    )
    d_one, d_out_in = fifth["own"], fifth["full"]
    d_out_in, owned_down = lax.optimization_barrier((d_out_in, owned_down))
    d_inner = jnp.einsum("td,cd->tc", d_out_in, w_out, preferred_element_type=wide_kind)
    grad_gu = jnp.einsum("td,tc->dc", full_two, d_gate_up, preferred_element_type=wide_kind)
    slot_gu = slots_of(grad_gu, order[2])
    d_inner, slot_gu = lax.optimization_barrier((d_inner, slot_gu))
    owned_gu = scatter_dp(slot_gu, 0)
    d_mixed, grad_pairs, grad_step = mixer_backward(*inner_kept, d_inner)
    grad_init = head_blocks(grad_pairs)
    gate = jax.nn.sigmoid(gains[3])
    grad_rate = grad_step[0] * gate * (1.0 - gate) / (8 * P_SIZE)
    grad_out = jnp.einsum("tc,td->cd", inner_low, d_out_in, preferred_element_type=wide_kind)
    grad_qkv = jnp.einsum("td,tc->dc", full_one, d_mixed, preferred_element_type=wide_kind)
    slot_out = column_slots_of(grad_out, order[1])
    slot_qkv = slots_of(grad_qkv, order[0])
    d_mixed, slot_out, slot_qkv, owned_gu = lax.optimization_barrier(
        (d_mixed, slot_out, slot_qkv, owned_gu)
    )
    owned_out = scatter_dp(slot_out, 0)
    owned_qkv = scatter_dp(slot_qkv, 0)
    row_ids = jnp.moveaxis(local_ids.reshape(slabs, chunks // 2, 2, ROWS), 0, 2)
    row_ids = jnp.broadcast_to(
        row_ids.reshape(chunks // 2, 1, 2 * slabs * ROWS), (chunks // 2, 8, 2 * slabs * ROWS)
    )
    sixth = transit(
        "grad_add",
        "table",
        6,
        parts,
        slabs,
        w_qkv,
        tokens,
        size,
        left=d_mixed,
        inputs=embedded,
        gain=gains[0:1],
        scale=scale_one,
        added=d_one,
        ids=row_ids,
        entries=table.shape[0],
    )
    owned_table = owned_table.astype(wide_kind) + sixth["table_grad"]
    gain_rows = [sixth["gain_grad"][0], fifth["gain_grad"][0], fourth["gain_grad"][0], grad_rate]
    owned = tuple(
        piece.astype(wide_kind) for piece in (owned_qkv, owned_out, owned_gu, owned_down)
    )
    return owned + (owned_table,), grad_init, jnp.stack(gain_rows, 0)


def shards(
    token_ids,
    targets,
    valid,
    resets,
    owners,
    emb_master,
    emb_first,
    emb_second,
    qkv_master,
    qkv_left,
    qkv_right,
    qkv_left_root,
    qkv_right_root,
    out_master,
    out_left,
    out_right,
    out_left_root,
    out_right_root,
    gu_master,
    gu_left,
    gu_right,
    gu_left_root,
    gu_right_root,
    down_master,
    down_left,
    down_right,
    down_left_root,
    down_right_root,
    inner_init,
    inner_first,
    inner_second,
    gains,
    gains_first,
    gains_second,
):
    low = jnp.bfloat16
    dp_size, head_size = lax.axis_size("dp"), lax.axis_size("head")
    head_index = lax.axis_index("head")
    ids_rows = token_ids.astype(jnp.float32).reshape(-1, 128)
    gain_rows = jnp.pad(gains[0].reshape(-1, 128), ((0, 8 - gains.shape[1] // 128), (0, 0)))
    opening = share(8, jnp.concatenate([ids_rows, gain_rows], 0), ("dp", "head"))
    opening = opening.reshape(dp_size, head_size, -1, 128)
    local_ids = opening[:, 0, : ids_rows.shape[0]].reshape(dp_size, -1).astype(jnp.int32)
    local_ids = local_ids - head_index * emb_master.shape[0]
    gain_one = opening[0, :, ids_rows.shape[0] :].reshape(head_size, -1)
    gain_one = gain_one[:, : gains.shape[1]].reshape(-1)
    emb_low = emb_master.astype(low)

    def flat(array):
        return array.reshape(array.shape[1], -1)

    gathered = (
        lax.all_gather(flat(qkv_master).astype(low), "dp", axis=0),
        lax.all_gather(out_master.astype(low), "dp", axis=0, tiled=True),
        lax.all_gather(flat(gu_master).astype(low), "dp", axis=0),
        lax.all_gather(down_master.astype(low), "dp", axis=0, tiled=True),
        lax.all_gather(emb_low, "dp", axis=1, tiled=True),
    )
    w_qkv = jnp.take(gathered[0], owners[0], axis=0, mode="clip").reshape(D, -1)
    w_out = jnp.take(gathered[1], owners[1], axis=0, mode="clip")
    w_out = jnp.swapaxes(w_out, 0, 1).reshape(w_out.shape[1], D)
    w_gu = jnp.take(gathered[2], owners[2], axis=0, mode="clip").reshape(D, -1)
    w_down = jnp.take(gathered[3], owners[3], axis=0, mode="clip")
    w_down = jnp.swapaxes(w_down, 0, 1).reshape(w_down.shape[1], D)
    weights = (w_qkv, w_out, w_gu, w_down, gathered[4])
    loss_local, count_local, kept = layer_forward(
        local_ids, targets, valid, resets, emb_low, weights, inner_init, gains, gain_one, head_index
    )
    order = jnp.argsort(owners, axis=1)
    owned, grad_init, grad_gains = layer_backward(kept, weights, gains, order)
    init_rows = grad_init.size // 128
    numbers = jnp.zeros((8, 128), jnp.float32).at[0, 0].set(loss_local).at[0, 1].set(count_local)
    pieces = (grad_init.reshape(-1, 128), grad_gains.reshape(-1, 128), numbers)
    small = jnp.sum(share(9, jnp.concatenate(pieces, 0), ("dp",)), 0)
    loss_sum, count = small[-8, 0], small[-8, 1]
    small = (
        small[:init_rows].reshape(grad_init.shape),
        small[init_rows:-8].reshape(grad_gains.shape),
    )
    first_dp = (lax.axis_index("dp") == 0).astype(jnp.float32)
    squares = sum((jnp.sum(piece * piece) for piece in owned))
    squares = squares + first_dp * (jnp.sum(small[0] * small[0]) + jnp.sum(small[1] * small[1]))
    squares = share(10, jnp.broadcast_to(squares, (8, 128)), ("dp", "head"))
    squares_all = jnp.sum(squares[:, 0, 0])
    grad_norm = jnp.sqrt(squares_all) / count
    factor = jnp.minimum(1.0, CLIP_LIMIT / grad_norm) / count
    qkv_out = refresh(
        qkv_master, owned[0] * factor, qkv_left, qkv_right, qkv_left_root, qkv_right_root
    )
    out_out = refresh(
        out_master, owned[1] * factor, out_left, out_right, out_left_root, out_right_root
    )
    gu_out = refresh(gu_master, owned[2] * factor, gu_left, gu_right, gu_left_root, gu_right_root)
    down_out = refresh(
        down_master, owned[3] * factor, down_left, down_right, down_left_root, down_right_root
    )
    table_out = adamw(emb_master, owned[4] * factor, emb_first, emb_second, TABLE_RATE)
    init_out = adamw(inner_init, small[0] * factor, inner_first, inner_second, INITIAL_RATE)
    gain_out = adamw(gains, small[1] * factor, gains_first, gains_second, GAINS_RATE)
    return (
        (jnp.stack([loss_sum, count]), grad_norm)
        + table_out
        + qkv_out
        + out_out
        + gu_out
        + down_out
        + init_out
        + gain_out
    )


def solution(mesh):
    placed = (
        P("dp"),
        P("dp"),
        P("dp"),
        P("dp"),
        P(),
        P("head", "dp"),
        P("head", "dp"),
        P("head", "dp"),
        P("dp", None, None, "head"),
        P("dp", "head", None, None),
        P("dp", "head", None, None),
        P("dp", "head", None, None),
        P("dp", "head", None, None),
        P("dp", "head", None),
        P("dp", "head", None, None),
        P("dp", "head", None, None),
        P("dp", "head", None, None),
        P("dp", "head", None, None),
        P("dp", None, None, "head"),
        P("dp", "head", None, None),
        P("dp", "head", None, None),
        P("dp", "head", None, None),
        P("dp", "head", None, None),
        P("dp", "head", None),
        P("dp", "head", None, None),
        P("dp", "head", None, None),
        P("dp", "head", None, None),
        P("dp", "head", None, None),
        P("head", None, None),
        P("head", None, None),
        P("head", None, None),
        P(None, "head"),
        P(None, "head"),
        P(None, "head"),
    )
    return jax.shard_map(
        shards,
        mesh=mesh,
        in_specs=placed,
        out_specs=(
            P(),
            P(),
            P("head", "dp"),
            P("head", "dp"),
            P("head", "dp"),
            P("dp", None, None, "head"),
            P("dp", "head", None, None),
            P("dp", "head", None, None),
            P("dp", None, None, "head"),
            P("dp", "head", None),
            P("dp", "head", None, None),
            P("dp", "head", None, None),
            P("dp", "head", None),
            P("dp", None, None, "head"),
            P("dp", "head", None, None),
            P("dp", "head", None, None),
            P("dp", None, None, "head"),
            P("dp", "head", None),
            P("dp", "head", None, None),
            P("dp", "head", None, None),
            P("dp", "head", None),
            P("head", None, None),
            P("head", None, None),
            P("head", None, None),
            P(None, "head"),
            P(None, "head"),
            P(None, "head"),
        ),
        check_vma=False,
    )
```

```python
import functools

import jax
import jax.numpy as jnp
from jax import lax
from jax.experimental import pallas as pl
from jax.experimental.pallas import tpu as pltpu
from jax.sharding import PartitionSpec as P

D = 2048
P_SIZE = 64
MB = 16
STEP = 10


EPSILON = 1e-05
CLIP_LIMIT = 0.05
STAT_DECAY = 0.5
MATRIX_RATE = 0.4
TABLE_RATE = 0.3
INITIAL_RATE = 0.05
GAINS_RATE = 0.3
BETA_ONE = 0.9
BETA_TWO = 0.95
ADAM_EPSILON = 1e-08
WEIGHT_DECAY = 0.01


CHUNK = 64
PAIR = 2 * P_SIZE


def dot_ab(left, right):
    return lax.dot_general(left, right, (((1,), (0,)), ((), ())), preferred_element_type=jnp.float32)


def dot_abt(left, right):
    return lax.dot_general(left, right, (((1,), (1,)), ((), ())), preferred_element_type=jnp.float32)


def dot_atb(left, right):
    return lax.dot_general(left, right, (((0,), (0,)), ((), ())), preferred_element_type=jnp.float32)


def halves_of(value):
    high = value.astype(jnp.bfloat16)
    return (high, (value - high.astype(jnp.float32)).astype(jnp.bfloat16))


def wide(form, left, right):
    lefts = left if isinstance(left, tuple) else (left,)
    rights = right if isinstance(right, tuple) else (right,)
    total = form(lefts[0], rights[0])
    if len(rights) > 1:
        total = total + form(lefts[0], rights[1])
    if len(lefts) > 1:
        total = total + form(lefts[1], rights[0])
    return total


def each(pieces, change):
    return tuple(change(piece) for piece in pieces) if isinstance(pieces, tuple) else change(pieces)


def mixer_masks(resets, tokens):
    per_chunk = CHUNK // MB
    chunks = tokens // CHUNK
    segment = jnp.cumsum(resets.reshape(chunks, per_chunk), axis=1)
    segment = jnp.repeat(segment, MB, axis=1)
    same = segment[:, :, None] == segment[:, None, :]
    spot = jnp.arange(CHUNK, dtype=jnp.int32)
    causal = (spot[None, :] <= spot[:, None])[None]
    earlier = ((spot[None, :] // MB) < (spot[:, None] // MB))[None]
    causal = (same & causal).astype(jnp.float32)
    earlier = (same & earlier).astype(jnp.float32)
    first = (segment == 0).astype(jnp.float32).reshape(tokens, 1)
    last = (segment == segment[:, -1:]).astype(jnp.float32).reshape(tokens, 1)
    anew = (segment[:, -1] > 0).astype(jnp.float32)
    first = jnp.broadcast_to(first, (tokens, PAIR))
    last = jnp.broadcast_to(last, (tokens, PAIR))
    anew = jnp.broadcast_to(anew[:, None, None], (chunks, 8, PAIR))
    return causal, earlier, first, last, anew


def lane_helpers(rows):
    lanes = lax.broadcasted_iota(jnp.int32, (rows, PAIR), 1)
    low_lane = lanes < P_SIZE
    low_half = low_lane.astype(jnp.float32)
    high_half = 1.0 - low_half

    def stack(pieces):
        def one(piece):
            kind = piece.dtype
            return jnp.concatenate(
                [piece * low_half.astype(kind), piece * high_half.astype(kind)], 0
            )

        return each(pieces, one)

    def pick(product):
        return jnp.where(low_lane, product[:rows], product[rows:])

    return stack, pick


def diagonal_blocks():
    rows = lax.broadcasted_iota(jnp.int32, (PAIR, PAIR), 0) // P_SIZE
    columns = lax.broadcasted_iota(jnp.int32, (PAIR, PAIR), 1) // P_SIZE
    return (rows == columns).astype(jnp.float32)


def solve(matrix, rate_row, value, pick):
    rows = value.shape[0]
    powers = [(matrix, rate_row)]
    reach = 2
    while reach < CHUNK // MB:
        last, rate = powers[-1]
        low, high = halves_of(last[:rows]), halves_of(last[rows:])
        powers.append(
            (
                jnp.concatenate([wide(dot_ab, low, low), wide(dot_ab, high, high)], 0),
                rate * rate,
            )
        )
        reach = 2 * reach
    for index in range(len(powers) - 1, -1, -1):
        factor, rate = powers[index]
        moved = pick(wide(dot_ab, halves_of(factor), halves_of(value * rate)))
        value = value - moved if index == 0 else value + moved
    return value


def mixer_forward_chunk(
    qkv_ref,
    rate_ref,
    initial_ref,
    causal_ref,
    earlier_ref,
    first_ref,
    last_ref,
    anew_ref,
    z_ref,
    residue_ref,
    states_ref,
    state,
):
    pairs = initial_ref.shape[0]
    width = pairs * PAIR

    stack, pick = lane_helpers(CHUNK)
    blocks = diagonal_blocks()
    causal = causal_ref[0]
    causal = jnp.concatenate([causal, causal], 0)
    earlier = earlier_ref[0]
    earlier = jnp.concatenate([earlier, earlier], 0)
    first = first_ref[...] > 0.0
    last = last_ref[...]
    anew = anew_ref[0, 0:1, :]
    for pair in range(pairs):
        lanes = slice(pair * PAIR, (pair + 1) * PAIR)
        query = qkv_ref[:, lanes]
        key = qkv_ref[:, width + pair * PAIR : width + (pair + 1) * PAIR]
        value = qkv_ref[:, 2 * width + pair * PAIR : 2 * width + (pair + 1) * PAIR]
        rate = rate_ref[0:1, lanes]
        begin = state[pair]
        initial = initial_ref[pair]
        states_ref[0, pair] = begin
        products = dot_abt(jnp.concatenate([stack(key), stack(query)], 0), key)
        ties = products[: 2 * CHUNK] * earlier
        scores = products[2 * CHUNK :] * causal
        both = jnp.concatenate([key, query], 0)
        seen = wide(dot_ab, both, halves_of(begin))
        fresh = wide(dot_ab, both, halves_of(initial))
        key_seen = jnp.where(first, seen[:CHUNK], fresh[:CHUNK])
        query_seen = jnp.where(first, seen[CHUNK:], fresh[CHUNK:])
        key_wide = key.astype(jnp.float32)
        residue = solve(ties, rate, key_seen - (value.astype(jnp.float32) - key_wide), pick)
        residue_ref[:, lanes] = residue
        scaled = residue * rate
        scaled_parts = halves_of(scaled)
        output = query_seen - pick(wide(dot_ab, halves_of(scores), scaled_parts))
        z_ref[:, lanes] = output.astype(jnp.bfloat16)
        key_last = (key_wide * last).astype(jnp.bfloat16)
        base = jnp.where(anew > 0.0, initial, begin)
        state[pair] = base - blocks * wide(dot_atb, key_last, scaled_parts)


def mixer_backward_chunk(
    qkv_ref,
    rate_ref,
    initial_ref,
    causal_ref,
    earlier_ref,
    causal_turned_ref,
    earlier_turned_ref,
    first_ref,
    last_ref,
    anew_ref,
    residue_ref,
    states_ref,
    upstream_ref,
    grad_ref,
    grad_initial_ref,
    grad_rate_ref,
    carried,
):
    pairs = initial_ref.shape[0]
    width = pairs * PAIR

    stack, pick = lane_helpers(CHUNK)
    blocks = diagonal_blocks()

    def doubled(ref):
        return jnp.concatenate([ref[0], ref[0]], 0)

    causal, earlier = doubled(causal_ref), doubled(earlier_ref)
    causal_turned, earlier_turned = doubled(causal_turned_ref), doubled(earlier_turned_ref)
    first_wide = first_ref[...]
    first = first_wide > 0.0
    last = last_ref[...]
    anew = anew_ref[0, 0:1, :]
    low = jnp.bfloat16
    for pair in range(pairs):
        lanes = slice(pair * PAIR, (pair + 1) * PAIR)
        query = qkv_ref[:, lanes]
        key = qkv_ref[:, width + pair * PAIR : width + (pair + 1) * PAIR]
        rate = rate_ref[0:1, lanes]
        begin = halves_of(states_ref[0, pair])
        initial = halves_of(initial_ref[pair])
        after = carried[pair]
        after_parts = halves_of(after)
        residue = residue_ref[:, lanes]
        scaled = halves_of(residue * rate)
        upstream = upstream_ref[:, lanes]
        upstream_parts = halves_of(upstream)
        key_wide = key.astype(jnp.float32)
        query_wide = query.astype(jnp.float32)
        key_last = (key_wide * last).astype(low)
        key_stack = stack(key)
        products = dot_abt(key_stack, jnp.concatenate([key, query], 0))
        ties_turned = products[:, :CHUNK] * earlier_turned
        scores_turned = products[:, CHUNK:] * causal_turned
        pulled = pick(wide(dot_ab, halves_of(scores_turned), upstream_parts))
        pulled = pulled + wide(dot_ab, key_last, after_parts)
        grad_scaled = solve(ties_turned, rate, -pulled, pick)
        grad_rate_ref[0:1, lanes] += jnp.sum(grad_scaled * residue, 0, keepdims=True)
        grad_residue = grad_scaled * rate
        residue_parts = halves_of(grad_residue)
        joined = tuple(
            jnp.concatenate([one, two], 0) for one, two in zip(upstream_parts, residue_parts)
        )
        scaled_stack = stack(scaled)
        turned = wide(dot_abt, scaled_stack, joined)
        straight = wide(
            dot_abt,
            tuple(
                jnp.concatenate([stack(one), stack(two)], 0)
                for one, two in zip(upstream_parts, residue_parts)
            ),
            scaled,
        )
        grad_scores = -straight[: 2 * CHUNK] * causal
        grad_scores_turned = -turned[:, :CHUNK] * causal_turned
        grad_ties = -(straight[2 * CHUNK :] * earlier + turned[:, CHUNK:] * earlier_turned)
        seen = wide(dot_abt, joined, begin)
        fresh = wide(dot_abt, joined, initial)
        grad_query = jnp.where(first, seen[:CHUNK], fresh[:CHUNK])
        grad_query = grad_query + pick(wide(dot_ab, halves_of(grad_scores), key))
        grad_key = jnp.where(first, seen[CHUNK:], fresh[CHUNK:]) + grad_residue
        grad_key = grad_key + pick(
            wide(dot_ab, halves_of(grad_scores_turned), query)
            + wide(dot_ab, halves_of(grad_ties), key)
        )
        grad_key = grad_key - last * wide(dot_abt, scaled, after_parts)
        grad_ref[:, lanes] = grad_query.astype(low)
        grad_ref[:, width + pair * PAIR : width + (pair + 1) * PAIR] = grad_key.astype(low)
        grad_ref[:, 2 * width + pair * PAIR : 2 * width + (pair + 1) * PAIR] = (
            -grad_residue
        ).astype(low)
        fronts = jnp.concatenate([query_wide * first_wide, key_wide * first_wide], 0).astype(low)
        backs = jnp.concatenate(
            [query_wide * (1.0 - first_wide), key_wide * (1.0 - first_wide)], 0
        ).astype(low)
        kept_after = jnp.where(anew > 0.0, 0.0, after)
        carried[pair] = kept_after + blocks * wide(dot_atb, fronts, joined)
        grad_initial_ref[pair] += (after - kept_after) + blocks * wide(dot_atb, backs, joined)


def pair_blocks(matrices):
    heads = matrices.shape[0]
    split = matrices.reshape(heads // 2, 2, P_SIZE, P_SIZE)
    empty = jnp.zeros_like(split[:, 0])
    upper = jnp.concatenate([split[:, 0], empty], 2)
    lower = jnp.concatenate([empty, split[:, 1]], 2)
    return jnp.concatenate([upper, lower], 1)


def head_blocks(pairs):
    return jnp.stack([pairs[:, :P_SIZE, :P_SIZE], pairs[:, P_SIZE:, P_SIZE:]], 1).reshape(
        -1, P_SIZE, P_SIZE
    )


ROWS = 64
LAG = 2
MESH = pl.DeviceIdType.MESH


def across(column):
    return jnp.swapaxes(jnp.broadcast_to(column, (column.shape[0], 128)), 0, 1)[:8]


def down(row, width):
    turned = jnp.swapaxes(jnp.broadcast_to(row[:1], (128, row.shape[1])), 0, 1)
    return jnp.concatenate([turned] * (width // 128), 1) if width > 128 else turned


def transit_kernel(mode, form, parts, slabs, names, *all_refs):
    ref = dict(zip(names, all_refs))
    full_ref, partial, total = ref["full"], ref["partial"], ref["total"]
    pair_out, pair_in = ref["pair_out"], ref["pair_in"]
    from_low, from_high = ref["from_low"], ref["from_high"]
    places = parts // 2
    cross = form in ("lookup", "table")
    summing = mode != "plain"
    lefts = sum(name.startswith("left_buf") for name in names)
    size = total.shape[1]
    ring, band = partial.shape[0], partial.shape[1]
    me = lax.axis_index("head")
    mine_dp = lax.axis_index("dp")
    core = lax.rem(me, 2)
    spot = me // 2
    twin = {"head": me + 1 - 2 * core}
    upper = {"head": lax.rem(me + 2, parts)}
    lower = {"head": lax.rem(me + parts - 2, parts)}
    chunks = ref["up_in_sem"].shape[0]
    sum_at = LAG * places
    finish_at = sum_at + (LAG if summing else 0)
    reach_at = finish_at + LAG * (places - 1)
    close_at = reach_at + (2 * LAG if cross else LAG)

    def place_of(chunk):
        return chunks - 1 - chunk if form == "inner" else chunk

    def band_of(index):
        return pl.ds(pl.multiple_of(index * band, band), band)

    def rows_of(chunk):
        return band_of(place_of(chunk))

    def shard(index):
        return pl.ds(pl.multiple_of(index * size, 128), size)

    def remote(source, target, out_sem, in_sem, device):
        return pltpu.make_async_remote_copy(
            src_ref=source,
            dst_ref=target,
            send_sem=out_sem,
            recv_sem=in_sem,
            device_id=device,
            device_id_type=MESH,
        )

    def left_copies(chunk):
        half = lax.rem(chunk, 2)
        return [
            pltpu.make_async_copy(
                ref["left%d" % part].at[rows_of(chunk)],
                ref["left_buf%d" % part].at[half],
                ref["left_sem%d" % part].at[half],
            )
            for part in range(lefts)
        ]

    barrier = pltpu.get_barrier_semaphore()
    for offset in range(1, parts):
        pl.semaphore_signal(
            barrier, inc=1, device_id={"head": lax.rem(me + offset, parts)}, device_id_type=MESH
        )
    if cross:
        for offset in range(1, slabs):
            pl.semaphore_signal(
                barrier,
                inc=1,
                device_id={"dp": lax.rem(mine_dp + offset, slabs)},
                device_id_type=MESH,
            )
    for copy in left_copies(0):
        copy.start()
    if mode in ("grad", "grad_add"):
        ref["gain_grad"][...] = jnp.zeros_like(ref["gain_grad"])
    if form == "table":
        ref["table_grad"][...] = jnp.zeros_like(ref["table_grad"])
    pl.semaphore_wait(barrier, parts - 1 + (slabs - 1 if cross else 0))

    def valid(chunk):
        return jnp.logical_and(chunk >= 0, chunk < chunks)

    def pair_copy(chunk):
        slot = lax.rem(chunk, ring)
        return remote(
            pair_out.at[slot],
            pair_in.at[slot],
            ref["pair_out_sem"].at[slot],
            ref["pair_in_sem"].at[slot],
            twin,
        )

    def rise(chunk, place):
        slot = lax.rem(chunk, ring)
        part = from_low.at[slot, :, pl.ds((place + 1) * size, (places - 1 - place) * size)]
        return remote(part, part, ref["low_out_sem"].at[slot], ref["low_in_sem"].at[slot], upper)

    def fall(chunk, place):
        slot = lax.rem(chunk, ring)
        part = from_high.at[slot, :, pl.ds(0, place * size)]
        return remote(part, part, ref["high_out_sem"].at[slot], ref["high_in_sem"].at[slot], lower)

    def sums_copy(chunk, offset):
        slot = lax.rem(chunk, ring)
        return remote(
            ref["sums_out"].at[slot],
            ref["sums_in"].at[slot, offset - 1],
            ref["sums_out_sem"].at[slot],
            ref["sums_in_sem"].at[slot],
            {"head": lax.rem(me + offset, parts)},
        )

    def piece(chunk, source):
        if cross:
            return ref["stage"].at[rows_of(chunk), shard(source)]
        return full_ref.at[rows_of(chunk), shard(2 * source + core)]

    def climb(chunk, source, hop):
        part = piece(chunk, source)
        return remote(
            part,
            part,
            ref["up_out_sem"].at[chunk, hop - 1],
            ref["up_in_sem"].at[chunk, hop - 1],
            upper,
        )

    def sink(chunk, source, hop):
        part = piece(chunk, source)
        return remote(
            part,
            part,
            ref["down_out_sem"].at[chunk, hop - 1],
            ref["down_in_sem"].at[chunk, hop - 1],
            lower,
        )

    def target(chunk, giver):
        if form == "lookup":
            return full_ref.at[rows_of(chunk), shard(2 * giver + core)]
        return full_ref.at[chunk // 2, band_of(lax.rem(chunk, 2) * slabs + giver), shard(core)]

    def mirror(chunk, index):
        part = target(chunk, index) if cross else piece(chunk, index)
        return remote(
            part, part, ref["twin_out_sem"].at[chunk], ref["twin_in_sem"].at[chunk], twin
        )

    def hand_over(chunk, source):
        return remote(
            piece(chunk, source),
            target(chunk, mine_dp),
            ref["cross_out_sem"].at[chunk, source],
            ref["cross_in_sem"].at[chunk, mine_dp],
            {"dp": source},
        )

    def have(chunk, source):
        if not cross:
            mirror(chunk, source).start()
            return

        @pl.when(source != mine_dp)
        def _():
            hand_over(chunk, source).start()

        @pl.when(source == mine_dp)
        def _():
            values = ref["stage"][rows_of(chunk), shard(source)]
            if form == "lookup":
                full_ref[rows_of(chunk), shard(2 * mine_dp + core)] = values
            else:
                place_rows = band_of(lax.rem(chunk, 2) * slabs + mine_dp)
                full_ref[chunk // 2, place_rows, shard(core)] = values
            mirror(chunk, mine_dp).start()

    def receive(step):
        for hop in range(places):
            chunk = step - finish_at - LAG * (hop + 1)

            @pl.when(jnp.logical_and(valid(chunk), jnp.abs(spot - mine_dp) == hop))
            def _():
                for offset in range(1, slabs):
                    giver = lax.rem(mine_dp + offset, slabs)
                    part = target(chunk, giver)
                    remote(
                        part,
                        part,
                        ref["cross_out_sem"].at[chunk, giver],
                        ref["cross_in_sem"].at[chunk, giver],
                        twin,
                    ).wait_recv()
                    mirror(chunk, giver).start()

    def relay(step):
        for hop in range(1, places):
            chunk = step - finish_at - LAG * hop
            source = spot - hop

            @pl.when(jnp.logical_and(valid(chunk), source >= 0))
            def _():
                climb(chunk, source, hop).wait_recv()
                if hop < places - 1:

                    @pl.when(spot < places - 1)
                    def _():
                        climb(chunk, source, hop + 1).start()

                have(chunk, source)

            source_high = spot + hop

            @pl.when(jnp.logical_and(valid(chunk), source_high < places))
            def _():
                sink(chunk, source_high, hop).wait_recv()
                if hop < places - 1:

                    @pl.when(spot > 0)
                    def _():
                        sink(chunk, source_high, hop + 1).start()

                have(chunk, source_high)

    def finish_shard(step):
        chunk = step - finish_at

        @pl.when(valid(chunk))
        def _():
            slot = lax.rem(chunk, ring)
            rows = rows_of(chunk)
            if summing:
                sums_in = ref["sums_in"]
                pltpu.make_async_copy(
                    sums_in.at[slot], sums_in.at[slot], ref["sums_in_sem"].at[slot]
                ).wait()
                summed = ref["sums_out"][slot]
                for offset in range(1, parts):
                    summed = summed + sums_in[slot, offset - 1]
                gain = ref["gain"][0:1, :]
            if mode == "plain":
                result = total[...]
            elif mode == "norm":
                scale = lax.rsqrt(summed / D + EPSILON)
                ref["scale"][chunk] = scale
                result = ref["own"][rows, :] * down(scale, size) * gain
            else:
                scale = down(ref["scale"][place_of(chunk)], size)
                normed = ref["inputs"][rows, :] * scale
                inner = down(summed / D, size)
                result = scale * (ref["own"][rows, :] * gain - normed * inner)
                if mode == "grad_add":
                    result = result + ref["added"][rows, :]
                if form != "table":
                    ref["own"][rows, :] = result
            if cross:
                ref["stage"][rows, shard(spot)] = result.astype(jnp.bfloat16)
            else:
                full_ref[rows, shard(me)] = result.astype(jnp.bfloat16)

            @pl.when(spot < places - 1)
            def _():
                climb(chunk, spot, 1).start()

            @pl.when(spot > 0)
            def _():
                sink(chunk, spot, 1).start()

            have(chunk, spot)

    def add_pair(step):
        chunk = step - LAG

        @pl.when(valid(chunk))
        def _():
            slot = lax.rem(chunk, ring)
            pair_copy(chunk).wait_recv()
            partial[slot] = partial[slot] + pair_in[slot].astype(jnp.float32)

    def pass_on(step):
        for place in range(places):
            if place < places - 1:
                up_chunk = step - LAG * (1 + place)

                @pl.when(jnp.logical_and(valid(up_chunk), spot == place))
                def _():
                    slot = lax.rem(up_chunk, ring)
                    above = pl.ds((place + 1) * size, (places - 1 - place) * size)
                    values = partial[slot, :, above]
                    if place > 0:
                        rise(up_chunk, place - 1).wait_recv()
                        values = values + from_low[slot, :, above].astype(jnp.float32)
                    from_low[slot, :, above] = values.astype(jnp.bfloat16)
                    rise(up_chunk, place).start()

            if place > 0:
                down_chunk = step - LAG * (places - place)

                @pl.when(jnp.logical_and(valid(down_chunk), spot == place))
                def _():
                    slot = lax.rem(down_chunk, ring)
                    below = pl.ds(0, place * size)
                    values = partial[slot, :, below]
                    if place < places - 1:
                        fall(down_chunk, place + 1).wait_recv()
                        values = values + from_high[slot, :, below].astype(jnp.float32)
                    from_high[slot, :, below] = values.astype(jnp.bfloat16)
                    fall(down_chunk, place).start()

    def settle(step):
        chunk = step - sum_at - LAG

        @pl.when(valid(chunk))
        def _():
            pair_copy(chunk).wait_send()
            for place in range(places):

                @pl.when(spot == place)
                def _():
                    if place < places - 1:
                        rise(chunk, place).wait_send()
                    if place > 0:
                        fall(chunk, place).wait_send()

            if summing:
                slot = lax.rem(chunk, ring)
                sums_in = ref["sums_in"]
                pltpu.make_async_copy(
                    sums_in.at[slot], sums_in.at[slot], ref["sums_out_sem"].at[slot]
                ).wait()

    def sum_shard(step):
        chunk = step - sum_at

        @pl.when(valid(chunk))
        def _():
            slot = lax.rem(chunk, ring)
            rows = rows_of(chunk)
            mine = shard(spot)

            @pl.when(spot == places - 1)
            def _():
                rise(chunk, places - 2).wait_recv()

            @pl.when(spot == 0)
            def _():
                fall(chunk, 1).wait_recv()

            total[...] = partial[slot, :, mine]

            @pl.when(spot > 0)
            def _():
                total[...] += from_low[slot, :, mine].astype(jnp.float32)

            @pl.when(spot < places - 1)
            def _():
                total[...] += from_high[slot, :, mine].astype(jnp.float32)

            if not summing:
                return
            value = total[...]
            if mode == "norm":
                value = value + ref["inputs"][rows, :]
                column = jnp.sum(value * value, 1, keepdims=True)
            else:
                scale = down(ref["scale"][place_of(chunk)], size)
                normed = ref["inputs"][rows, :] * scale
                ref["gain_grad"][0:1, :] += jnp.sum(value * normed, 0, keepdims=True)
                column = jnp.sum(value * ref["gain"][0:1, :] * normed, 1, keepdims=True)
            ref["own"][rows, :] = value
            ref["sums_out"][slot] = across(column)
            for offset in range(1, parts):
                sums_copy(chunk, offset).start()

    def produce(step):
        chunk = step

        @pl.when(valid(chunk))
        def _():
            slot = lax.rem(chunk, ring)
            right_ref = ref["right0"]
            if form == "lookup":
                entries = right_ref.shape[0]
                ids = jnp.concatenate(
                    [ref["ids"][group, rows_of(chunk), 0:1] for group in range(slabs)], 0
                )
                spots = lax.broadcasted_iota(jnp.int32, (slabs * band, entries), 1)
                hits = (spots == ids).astype(jnp.bfloat16)
                other = dot_ab(hits, right_ref[:, shard(1 - core)]).astype(jnp.bfloat16)
                for group in range(slabs):
                    pair_out[slot, :, pl.ds(group * size, size)] = other[
                        group * band : (group + 1) * band
                    ]
                pair_copy(chunk).start()
                here = dot_ab(hits, right_ref[:, shard(core)])
                for group in range(slabs):
                    partial[slot, :, pl.ds(group * size, size)] = here[
                        group * band : (group + 1) * band
                    ]
                return
            half = lax.rem(chunk, 2)
            if form == "mixer":
                one = pl.ds(chunk, 1)
                here = rows_of(chunk)

                @pl.when(chunk == 0)
                def _():
                    ref["state"][...] = jnp.zeros_like(ref["state"])

                mixer_forward_chunk(
                    ref["qkv"].at[here],
                    ref["rate"],
                    ref["initial"],
                    ref["causal"].at[one],
                    ref["earlier"].at[one],
                    ref["first"].at[here],
                    ref["last"].at[here],
                    ref["anew"].at[one],
                    ref["z"].at[here],
                    ref["residue"].at[here],
                    ref["states"].at[one],
                    ref["state"],
                )
            else:
                for copy in left_copies(chunk):
                    copy.wait()

                @pl.when(chunk + 1 < chunks)
                def _():
                    for copy in left_copies(chunk + 1):
                        copy.start()

            def term(index):
                if form == "mixer":
                    return dot_ab(ref["z"][rows_of(chunk), :], right_ref[:, shard(index)])
                if form == "table":
                    return dot_abt(ref["left_buf0"][half], right_ref[shard(index), :])
                terms = [
                    dot_ab(ref["left_buf%d" % part][half], ref["right%d" % part][:, shard(index)])
                    for part in range(lefts)
                ]
                return sum(terms[1:], terms[0])

            for place in range(places):
                lanes = pl.ds(place * size, size)
                pair_out[slot, :, lanes] = term(2 * place + 1 - core).astype(jnp.bfloat16)
            pair_copy(chunk).start()
            for place in range(places):
                lanes = pl.ds(place * size, size)
                partial[slot, :, lanes] = term(2 * place + core)

    def close(step):
        chunk = step - close_at

        @pl.when(valid(chunk))
        def _():
            if form == "table":
                arrived = full_ref.at[chunk // 2, pl.ds(0, slabs * band), pl.ds(0, size)]
            else:
                arrived = full_ref.at[rows_of(chunk), pl.ds(0, places * size)]
            pltpu.make_async_copy(arrived, arrived, ref["twin_in_sem"].at[chunk]).wait()
            pltpu.make_async_copy(arrived, arrived, ref["twin_out_sem"].at[chunk]).wait()
            if cross:
                for offset in range(1, slabs):
                    hand_over(chunk, lax.rem(mine_dp + offset, slabs)).wait_send()
            for hop in range(1, places):
                source = spot - hop + 1

                @pl.when(jnp.logical_and(source >= 0, spot < places - 1))
                def _():
                    climb(chunk, source, hop).wait_send()

                source_high = spot + hop - 1

                @pl.when(jnp.logical_and(source_high < places, spot > 0))
                def _():
                    sink(chunk, source_high, hop).wait_send()

            if form == "lookup":
                rows = rows_of(chunk)
                ref["own"][rows, :] = full_ref[rows, shard(me)].astype(jnp.float32)
                values = full_ref[rows, :].astype(jnp.float32)
                scale = lax.rsqrt(jnp.sum(values * values, 1, keepdims=True) / D + EPSILON)
                ref["scale"][chunk] = across(scale)
                normed = (values * scale * ref["gain"][0:1, :]).astype(jnp.bfloat16)
                full_ref[rows, :] = normed
                ref["mixed"][rows, :] = dot_ab(normed, ref["project"][...]).astype(jnp.bfloat16)
            if form == "inner":
                rows, one = rows_of(chunk), pl.ds(place_of(chunk), 1)

                @pl.when(chunk == 0)
                def _():
                    for name in ("state", "grad_initial", "grad_rate"):
                        ref[name][...] = jnp.zeros_like(ref[name])

                ref["upstream"][...] = dot_abt(full_ref[rows, :], ref["project"][...])
                mixer_backward_chunk(
                    ref["qkv"].at[rows],
                    ref["rate"],
                    ref["initial"],
                    ref["causal"].at[one],
                    ref["earlier"].at[one],
                    ref["causal_turned"].at[one],
                    ref["earlier_turned"].at[one],
                    ref["first"].at[rows],
                    ref["last"].at[rows],
                    ref["anew"].at[one],
                    ref["residue"].at[rows],
                    ref["states"].at[one],
                    ref["upstream"],
                    ref["grad_mixed"].at[rows],
                    ref["grad_initial"],
                    ref["grad_rate"],
                    ref["state"],
                )
            if form == "table":
                @pl.when(lax.rem(chunk, 2) == 1)
                def _():
                    table_grad = ref["table_grad"]
                    entries = table_grad.shape[0]
                    pieces = 5 if entries % 80 == 0 else 1
                    block = entries // pieces
                    ids = ref["ids"][chunk // 2, 0:1, :]
                    values = full_ref[chunk // 2]
                    for index in range(pieces):
                        spots = index * block + lax.broadcasted_iota(
                            jnp.int32, (block, ids.shape[1]), 0
                        )
                        hits = (spots == ids).astype(jnp.bfloat16)
                        span = pl.ds(index * block, block)
                        table_grad[span, :] += dot_ab(hits, values)

    def advance(step, carried):
        relay(step)
        if summing:
            finish_shard(step)
        if cross:
            receive(step)
        add_pair(step)
        pass_on(step)
        settle(step)
        sum_shard(step)
        if not summing:
            finish_shard(step)
        produce(step)
        close(step)
        return carried

    lax.fori_loop(0, chunks + close_at, advance, 0)


def transit(
    mode,
    form,
    number,
    parts,
    slabs,
    right,
    tokens,
    size,
    left=None,
    inputs=None,
    gain=None,
    scale=None,
    added=None,
    ids=None,
    entries=None,
    mixer=None,
    project=None,
    band=ROWS,
):
    chunks = tokens // band
    places = parts // 2
    cross = form in ("lookup", "table")
    summing = mode != "plain"
    ring = min(chunks, LAG * (places + 1) + 2) if summing else chunks
    dma = pltpu.SemaphoreType.DMA
    low, wide_kind = jnp.bfloat16, jnp.float32
    vmem = pl.BlockSpec(memory_space=pltpu.VMEM)
    operands, specs, outputs, scratch = {}, [], {}, {}

    def take(name, array, spec=vmem):
        operands[name] = array
        specs.append(spec)

    rights = right if isinstance(right, tuple) else (right,)
    lefts = left if isinstance(left, tuple) else () if left is None else (left,)
    for part, array in enumerate(rights):
        take("right%d" % part, array)
    for part, array in enumerate(lefts):
        take("left%d" % part, array, pl.BlockSpec(memory_space=pl.ANY))
    if project is not None:
        take("project", project)
    if ids is not None:
        take("ids", ids)
    if mixer is not None:
        for name, array in mixer.items():
            take(name, array)
        pairs, width = mixer["initial"].shape[0], mixer["rate"].shape[1]
    if summing:
        take("inputs", inputs)
    take("gain", gain)
    if mode in ("grad", "grad_add"):
        take("scale", scale)
    if mode == "grad_add":
        take("added", added)

    if form != "table":
        outputs["own"] = ((tokens, size), wide_kind)
    if form != "table":
        outputs["full"] = ((tokens, parts * size), low)
    if mode in ("norm", "plain"):
        outputs["scale"] = ((chunks, 8, band), wide_kind)
    if mode in ("grad", "grad_add"):
        outputs["gain_grad"] = ((8, size), wide_kind)
    if form == "table":
        outputs["table_grad"] = ((entries, 2 * size), wide_kind)

    if form == "lookup":
        outputs["mixed"] = ((tokens, project.shape[1]), low)
    if form == "inner":
        outputs["grad_mixed"] = ((tokens, 3 * width), low)
        outputs["grad_initial"] = ((pairs, PAIR, PAIR), wide_kind)
        outputs["grad_rate"] = ((1, width), wide_kind)
        scratch["state"] = pltpu.VMEM((pairs, PAIR, PAIR), wide_kind)
        scratch["upstream"] = pltpu.VMEM((band, width), wide_kind)
    if form == "mixer":
        outputs["z"] = ((tokens, width), low)
        outputs["residue"] = ((tokens, width), wide_kind)
        outputs["states"] = ((chunks, pairs, PAIR, PAIR), wide_kind)
        scratch["state"] = pltpu.VMEM((pairs, PAIR, PAIR), wide_kind)
    span = places * size
    hops = max(places - 1, 1)
    if form == "table":
        scratch["own"] = pltpu.VMEM((tokens, size), wide_kind)
        scratch["full"] = pltpu.VMEM((chunks // 2, 2 * slabs * band, 2 * size), low)
    for part, array in enumerate(lefts):
        scratch["left_buf%d" % part] = pltpu.VMEM((2, band, array.shape[1]), low)
        scratch["left_sem%d" % part] = dma((2,))
    if cross:
        scratch["stage"] = pltpu.VMEM((tokens, span), low)
        scratch["cross_out_sem"] = dma((chunks, slabs))
        scratch["cross_in_sem"] = dma((chunks, slabs))
    if summing:
        scratch["sums_out"] = pltpu.VMEM((ring, 8, band), wide_kind)
        scratch["sums_in"] = pltpu.VMEM((ring, parts - 1, 8, band), wide_kind)
        scratch["sums_out_sem"] = dma((ring,))
        scratch["sums_in_sem"] = dma((ring,))
    scratch["total"] = pltpu.VMEM((band, size), wide_kind)
    scratch["partial"] = pltpu.VMEM((ring, band, span), wide_kind)
    for name in ("pair_out", "pair_in", "from_low", "from_high"):
        scratch[name] = pltpu.VMEM((ring, band, span), low)
    for name in ("pair_out", "pair_in", "low_out", "low_in", "high_out", "high_in"):
        scratch[name + "_sem"] = dma((ring,))
    for name in ("up_out", "up_in", "down_out", "down_in"):
        scratch[name + "_sem"] = dma((chunks, hops))
    scratch["twin_out_sem"] = dma((chunks,))
    scratch["twin_in_sem"] = dma((chunks,))

    depth = sum(array.size for array in rights) // (parts * size)
    names = tuple(operands) + tuple(outputs) + tuple(scratch)
    results = pl.pallas_call(
        functools.partial(transit_kernel, mode, form, parts, slabs, names),
        in_specs=specs,
        out_specs=[vmem] * len(outputs),
        out_shape=[jax.ShapeDtypeStruct(shape, kind) for shape, kind in outputs.values()],
        scratch_shapes=list(scratch.values()),
        compiler_params=pltpu.CompilerParams(
            collective_id=number, has_side_effects=True, vmem_limit_bytes=60 * 1024 * 1024
        ),
        cost_estimate=pl.CostEstimate(
            flops=2 * tokens * depth * parts * size,
            bytes_accessed=128 * tokens * parts * size,
            transcendentals=0,
        ),
        name="transit_" + form,
    )(*operands.values())
    return dict(zip(outputs, results))


def share_kernel(axes, block_ref, all_ref, out_sem, in_sem):
    counts = [lax.axis_size(axis) for axis in axes]
    places = [lax.axis_index(axis) for axis in axes]
    members = 1
    me = 0
    for count, place in zip(counts, places):
        members = members * count
        me = me * count + place

    def partner(offset):
        device, rest = {}, offset
        for axis, count, place in reversed(list(zip(axes, counts, places))):
            device[axis] = lax.rem(place + lax.rem(rest, count), count)
            rest = rest // count
        return device

    def send(offset):
        return pltpu.make_async_remote_copy(
            src_ref=block_ref,
            dst_ref=all_ref.at[me],
            send_sem=out_sem,
            recv_sem=in_sem,
            device_id=partner(offset),
            device_id_type=MESH,
        )

    barrier = pltpu.get_barrier_semaphore()

    def greet(offset, carried):
        pl.semaphore_signal(barrier, inc=1, device_id=partner(offset), device_id_type=MESH)
        return carried

    def start(offset, carried):
        send(offset).start()
        return carried

    lax.fori_loop(1, members, greet, 0)
    all_ref[me] = block_ref[...]
    pl.semaphore_wait(barrier, members - 1)
    lax.fori_loop(1, members, start, 0)
    arrived = all_ref.at[pl.ds(0, members - 1)]
    pltpu.make_async_copy(arrived, arrived, in_sem).wait()
    pltpu.make_async_copy(arrived, arrived, out_sem).wait()


def share(number, block, axes):
    members = 1
    for axis in axes:
        members = members * lax.axis_size(axis)
    vmem = pl.BlockSpec(memory_space=pltpu.VMEM)
    return pl.pallas_call(
        functools.partial(share_kernel, axes),
        in_specs=[vmem],
        out_specs=vmem,
        out_shape=jax.ShapeDtypeStruct((members,) + block.shape, block.dtype),
        scratch_shapes=[pltpu.SemaphoreType.DMA, pltpu.SemaphoreType.DMA],
        compiler_params=pltpu.CompilerParams(
            collective_id=number, has_side_effects=True, vmem_limit_bytes=16 * 1024 * 1024
        ),
        cost_estimate=pl.CostEstimate(
            flops=0, bytes_accessed=16 * 1024 * 1024, transcendentals=0
        ),
        name="share",
    )(block)


SCORE_ROWS = 256


def scores_kernel(rows_ref, table_ref, goal_ref, logits_ref, stats_ref):
    entries = table_ref.shape[0]
    edges = list(range(0, entries, 1024)) + [entries]
    peak = jnp.full((SCORE_ROWS, 1), -jnp.inf, jnp.float32)
    for low, high in zip(edges, edges[1:]):
        values = dot_abt(rows_ref[...], table_ref[low:high, :])
        logits_ref[:, low:high] = values
        peak = jnp.maximum(peak, jnp.max(values, 1, keepdims=True))
    exp_sum = jnp.zeros((SCORE_ROWS, 1), jnp.float32)
    picked = jnp.zeros((SCORE_ROWS, 1), jnp.float32)
    goal = goal_ref[:, 0:1]
    for low, high in zip(edges, edges[1:]):
        values = logits_ref[:, low:high]
        exp_sum = exp_sum + jnp.sum(jnp.exp(values - peak), 1, keepdims=True)
        spots = low + lax.broadcasted_iota(jnp.int32, values.shape, 1)
        picked = picked + jnp.sum(jnp.where(spots == goal, values, 0.0), 1, keepdims=True)
    stats_ref[0] = jnp.broadcast_to(peak, (SCORE_ROWS, 128))
    stats_ref[1] = jnp.broadcast_to(exp_sum, (SCORE_ROWS, 128))
    stats_ref[2] = jnp.broadcast_to(picked, (SCORE_ROWS, 128))


def scores(rows, table, goals):
    tokens, width = rows.shape
    entries = table.shape[0]
    return pl.pallas_call(
        scores_kernel,
        grid=(tokens // SCORE_ROWS,),
        in_specs=[
            pl.BlockSpec((SCORE_ROWS, width), lambda i: (i, 0)),
            pl.BlockSpec(memory_space=pltpu.VMEM),
            pl.BlockSpec((SCORE_ROWS, 128), lambda i: (i, 0)),
        ],
        out_specs=[
            pl.BlockSpec((SCORE_ROWS, entries), lambda i: (i, 0)),
            pl.BlockSpec((3, SCORE_ROWS, 128), lambda i: (0, i, 0)),
        ],
        out_shape=[
            jax.ShapeDtypeStruct((tokens, entries), jnp.float32),
            jax.ShapeDtypeStruct((3, tokens, 128), jnp.float32),
        ],
        compiler_params=pltpu.CompilerParams(
            dimension_semantics=("arbitrary",), vmem_limit_bytes=56 * 1024 * 1024
        ),
        cost_estimate=pl.CostEstimate(
            flops=2 * tokens * entries * width,
            bytes_accessed=2 * entries * width + 4 * tokens * entries,
            transcendentals=tokens * entries,
        ),
        name="scores",
    )(rows, table, goals)


def shampoo(tile_w, tile_g, left, right, left_root, right_root):
    low_g = tile_g.astype(jnp.bfloat16)

    def product(form, one, two):
        return jnp.einsum(
            form,
            one.astype(jnp.bfloat16),
            two.astype(jnp.bfloat16),
            preferred_element_type=jnp.float32,
        )

    new_left = STAT_DECAY * left + (1.0 - STAT_DECAY) * product("abrc,absc->abrs", low_g, low_g)
    new_right = STAT_DECAY * right + (1.0 - STAT_DECAY) * product("abrc,abrd->abcd", low_g, low_g)
    turned = product("abrs,absc->abrc", left_root, low_g)
    turned = product("abrc,abcd->abrd", turned, right_root)
    return (new_left, new_right, tile_w - MATRIX_RATE * (turned + WEIGHT_DECAY * tile_w))


def refresh(master, grad, left, right, left_root, right_root):
    rows = master.shape[1]
    new_left, new_right, new_w = shampoo(
        master.reshape(1, 1, rows, -1),
        grad.reshape(1, 1, rows, -1),
        left,
        right,
        left_root,
        right_root,
    )
    return (grad.reshape(master.shape), new_left, new_right, new_w.reshape(master.shape))


def refresh_rows(master, grad, left, right, left_root, right_root):
    _, rows, kinds, _ = master.shape
    low_g = grad.astype(jnp.bfloat16)

    def product(form, one, two):
        return jnp.einsum(
            form,
            one.astype(jnp.bfloat16),
            two.astype(jnp.bfloat16),
            preferred_element_type=jnp.float32,
        )

    def shaped(array):
        return jnp.transpose(array.reshape(kinds, -1, rows), (2, 0, 1))[None]

    master_rows = jnp.transpose(master[0], (1, 2, 0)).reshape(-1, rows)
    new_left = STAT_DECAY * left + (1.0 - STAT_DECAY) * product("cr,cs->rs", low_g, low_g)
    new_right = STAT_DECAY * right + (1.0 - STAT_DECAY) * product("cr,dr->cd", low_g, low_g)
    turned = product("rs,cs->cr", left_root[0, 0], low_g)
    turned = product("dr,dc->cr", turned, right_root[0, 0])
    new_w = master_rows - MATRIX_RATE * (turned + WEIGHT_DECAY * master_rows)
    return (shaped(grad), new_left, new_right, shaped(new_w))


def adamw(weight, grad, first, second, step_rate):
    new_first = BETA_ONE * first + (1.0 - BETA_ONE) * grad
    new_second = BETA_TWO * second + (1.0 - BETA_TWO) * grad * grad
    moved = (
        new_first
        / (1.0 - BETA_ONE**STEP)
        / (jnp.sqrt(new_second / (1.0 - BETA_TWO**STEP)) + ADAM_EPSILON)
    )
    return (new_first, new_second, weight - step_rate * (moved + WEIGHT_DECAY * weight))


def layer_forward(
    local_ids,
    targets,
    valid,
    resets,
    emb_low,
    w_qkv,
    later_weights,
    inner_init,
    gains,
    gain_one,
    head_index,
):
    parts, slabs = lax.axis_size("head"), lax.axis_size("dp")
    vocab_part = emb_low.shape[0]
    tokens, size = targets.shape[0], gains.shape[1]
    chunks = tokens // ROWS
    columns = jnp.arange(vocab_part, dtype=jnp.int32)
    spread_ids = jnp.broadcast_to(local_ids[:, :, None], (slabs, tokens, 128))
    first = transit(
        "plain",
        "lookup",
        1,
        parts,
        slabs,
        emb_low,
        tokens,
        size,
        ids=spread_ids,
        gain=gain_one[None],
        project=w_qkv,
    )
    embedded, full_one, scale_one = first["own"], first["full"], first["scale"]
    mixed = first["mixed"]
    w_out, w_gate, w_up, w_down, table, mixed = later_weights(mixed)
    step_rate = jax.nn.sigmoid(gains[3:4]) / (8 * P_SIZE)
    masks = mixer_masks(resets, tokens)
    initial_pairs = pair_blocks(inner_init)
    causal, earlier, before, after, anew = masks
    inner = dict(
        qkv=mixed,
        rate=step_rate,
        initial=initial_pairs,
        causal=causal,
        earlier=earlier,
        first=before,
        last=after,
        anew=anew,
    )
    second = transit(
        "norm",
        "mixer",
        2,
        parts,
        slabs,
        w_out,
        tokens,
        size,
        mixer=inner,
        inputs=embedded,
        gain=gains[1:2],
    )
    inner_low = second["z"]
    inner = dict(
        inner,
        causal_turned=jnp.swapaxes(causal, 1, 2),
        earlier_turned=jnp.swapaxes(earlier, 1, 2),
        residue=second["residue"],
        states=second["states"],
    )
    hidden_one, full_two, scale_two = second["own"], second["full"], second["scale"]
    gate = jnp.einsum("td,fd->tf", full_two, w_gate, preferred_element_type=jnp.float32)
    up = jnp.einsum("td,fd->tf", full_two, w_up, preferred_element_type=jnp.float32)
    activated, act_pull = jax.vjp(lambda one, two: jax.nn.silu(one) * two, gate, up)
    act_low = activated.astype(jnp.bfloat16)
    third = transit(
        "norm",
        "rows",
        3,
        parts,
        slabs,
        w_down,
        tokens,
        size,
        left=act_low,
        inputs=hidden_one,
        gain=gains[2:3],
    )
    hidden_two, full_end, scale_end = third["own"], third["full"], third["scale"]
    local_targets = targets - head_index * vocab_part
    target_hits = columns[None, :] == local_targets[:, None]
    logits, stats = scores(
        full_end, table, jnp.broadcast_to(local_targets[:, None], (tokens, 128))
    )
    stats = share(7, stats[:, :, 0].reshape(-1, 128), ("head",)).reshape(parts, 3, tokens)
    highest = jnp.max(stats[:, 0], 0)
    exp_sum = jnp.sum(stats[:, 1] * jnp.exp(stats[:, 0] - highest[None]), 0)
    target_logit = jnp.sum(stats[:, 2], 0)
    totals = highest + jnp.log(exp_sum)
    counted = valid.astype(jnp.float32)
    d_logits = (
        (jnp.exp(logits - totals[:, None]) - target_hits.astype(jnp.float32)) * counted[:, None]
    ).astype(jnp.bfloat16)
    kept = (
        embedded,
        scale_one,
        full_one,
        inner,
        inner_low,
        hidden_one,
        scale_two,
        full_two,
        act_pull,
        act_low,
        hidden_two,
        scale_end,
        full_end,
        d_logits,
        local_ids,
    )
    weights = (w_qkv, w_out, w_gate, w_up, w_down, table)
    return (jnp.sum((totals - target_logit) * counted), jnp.sum(counted), kept, weights)


def slots_of(grad, order):
    parts = lax.axis_size("dp")
    shaped = grad.astype(jnp.bfloat16).reshape(parts, -1, grad.shape[1])
    return jnp.take(shaped, order, axis=0, mode="clip")


def column_slots_of(grad, order):
    parts = lax.axis_size("dp")
    shaped = grad.astype(jnp.bfloat16).reshape(grad.shape[0], parts, -1)
    return jnp.take(jnp.swapaxes(shaped, 0, 1), order, axis=0, mode="clip")


def scatter_dp(grad, dimension):
    return lax.psum_scatter(grad, "dp", scatter_dimension=dimension, tiled=True)


def rebanded(scale, band):
    rows = scale[:, 0].reshape(-1, 1, band)
    return jnp.broadcast_to(rows, (rows.shape[0], 8, band))


def layer_backward(kept, weights, gains, order):
    (
        embedded,
        scale_one,
        full_one,
        inner,
        inner_low,
        hidden_one,
        scale_two,
        full_two,
        act_pull,
        act_low,
        hidden_two,
        scale_end,
        full_end,
        d_logits,
        local_ids,
    ) = kept
    w_qkv, w_out, w_gate, w_up, w_down, table = weights
    parts, slabs = lax.axis_size("head"), lax.axis_size("dp")
    tokens, size = embedded.shape
    chunks = tokens // ROWS
    wide_kind = jnp.float32
    grad_table = jnp.einsum("tv,td->vd", d_logits, full_end, preferred_element_type=wide_kind)
    grad_table = grad_table.astype(jnp.bfloat16)
    owned_table = scatter_dp(grad_table, 1)
    d_logits, grad_table = lax.optimization_barrier((d_logits, grad_table))
    fourth = transit(
        "grad",
        "rows",
        4,
        parts,
        slabs,
        table,
        tokens,
        size,
        left=d_logits,
        inputs=hidden_two,
        gain=gains[2:3],
        scale=rebanded(scale_end, 2 * ROWS),
        band=2 * ROWS,
    )
    d_two, d_down_in = fourth["own"], fourth["full"]
    d_down_in, owned_table = lax.optimization_barrier((d_down_in, owned_table))
    d_act = jnp.einsum("td,fd->tf", d_down_in, w_down, preferred_element_type=wide_kind)
    d_gate, d_up = act_pull(d_act)
    d_gate, d_up = d_gate.astype(jnp.bfloat16), d_up.astype(jnp.bfloat16)
    grad_down = jnp.einsum("tf,td->fd", act_low, d_down_in, preferred_element_type=wide_kind)
    slot_down = column_slots_of(grad_down, order[3])
    grad_gate = jnp.einsum("tf,td->fd", d_gate, full_two, preferred_element_type=wide_kind)
    grad_up = jnp.einsum("tf,td->fd", d_up, full_two, preferred_element_type=wide_kind)
    slot_gate = column_slots_of(grad_gate, order[2])
    slot_up = column_slots_of(grad_up, order[2])
    d_gate, d_up, slot_down, slot_gate, slot_up = lax.optimization_barrier(
        (d_gate, d_up, slot_down, slot_gate, slot_up)
    )
    owned_down = scatter_dp(slot_down, 0)
    owned_gate = scatter_dp(slot_gate, 0)
    owned_up = scatter_dp(slot_up, 0)
    fifth = transit(
        "grad_add",
        "inner",
        5,
        parts,
        slabs,
        (w_gate, w_up),
        tokens,
        size,
        left=(d_gate, d_up),
        inputs=hidden_one,
        gain=gains[1:2],
        scale=scale_two,
        added=d_two,
        mixer=inner,
        project=w_out,
    )
    d_one, d_out_in, d_mixed = fifth["own"], fifth["full"], fifth["grad_mixed"]
    grad_init = head_blocks(fifth["grad_initial"])
    gate = jax.nn.sigmoid(gains[3])
    grad_rate = fifth["grad_rate"][0] * gate * (1.0 - gate) / (8 * P_SIZE)
    d_mixed, owned_down, owned_gate, owned_up = lax.optimization_barrier(
        (d_mixed, owned_down, owned_gate, owned_up)
    )
    grad_out = jnp.einsum("tc,td->cd", inner_low, d_out_in, preferred_element_type=wide_kind)
    grad_qkv = jnp.einsum("td,tc->dc", full_one, d_mixed, preferred_element_type=wide_kind)
    slot_out = column_slots_of(grad_out, order[1])
    slot_qkv = slots_of(grad_qkv, order[0])
    d_mixed, slot_out, slot_qkv = lax.optimization_barrier((d_mixed, slot_out, slot_qkv))
    owned_out = scatter_dp(slot_out, 0)
    owned_qkv = scatter_dp(slot_qkv, 0)
    owned_gu = jnp.concatenate([owned_gate, owned_up], 1)
    row_ids = jnp.moveaxis(local_ids.reshape(slabs, chunks // 2, 2, ROWS), 0, 2)
    row_ids = jnp.broadcast_to(
        row_ids.reshape(chunks // 2, 1, 2 * slabs * ROWS), (chunks // 2, 8, 2 * slabs * ROWS)
    )
    sixth = transit(
        "grad_add",
        "table",
        6,
        parts,
        slabs,
        w_qkv,
        tokens,
        size,
        left=d_mixed,
        inputs=embedded,
        gain=gains[0:1],
        scale=scale_one,
        added=d_one,
        ids=row_ids,
        entries=table.shape[0],
    )
    owned_table = owned_table.astype(wide_kind) + sixth["table_grad"]
    gain_rows = [sixth["gain_grad"][0], fifth["gain_grad"][0], fourth["gain_grad"][0], grad_rate]
    owned = tuple(
        piece.astype(wide_kind) for piece in (owned_qkv, owned_out, owned_gu, owned_down)
    )
    return owned + (owned_table,), grad_init, jnp.stack(gain_rows, 0)


def shards(
    token_ids,
    targets,
    valid,
    resets,
    owners,
    emb_master,
    emb_first,
    emb_second,
    qkv_master,
    qkv_left,
    qkv_right,
    qkv_left_root,
    qkv_right_root,
    out_master,
    out_left,
    out_right,
    out_left_root,
    out_right_root,
    gu_master,
    gu_left,
    gu_right,
    gu_left_root,
    gu_right_root,
    down_master,
    down_left,
    down_right,
    down_left_root,
    down_right_root,
    inner_init,
    inner_first,
    inner_second,
    gains,
    gains_first,
    gains_second,
):
    low = jnp.bfloat16
    dp_size, head_size = lax.axis_size("dp"), lax.axis_size("head")
    head_index = lax.axis_index("head")
    ids_rows = token_ids.astype(jnp.float32).reshape(-1, 128)
    gain_rows = jnp.pad(gains[0].reshape(-1, 128), ((0, 8 - gains.shape[1] // 128), (0, 0)))
    opening = share(8, jnp.concatenate([ids_rows, gain_rows], 0), ("dp", "head"))
    opening = opening.reshape(dp_size, head_size, -1, 128)
    local_ids = opening[:, 0, : ids_rows.shape[0]].reshape(dp_size, -1).astype(jnp.int32)
    local_ids = local_ids - head_index * emb_master.shape[0]
    gain_one = opening[0, :, ids_rows.shape[0] :].reshape(head_size, -1)
    gain_one = gain_one[:, : gains.shape[1]].reshape(-1)
    emb_low = emb_master.astype(low)

    def flat(array):
        return array.reshape(array.shape[1], -1)

    gu_rows = jnp.transpose(gu_master[0], (1, 2, 0)).reshape(-1, gu_master.shape[1])
    hidden = gu_master.shape[3]
    all_qkv = lax.all_gather(flat(qkv_master).astype(low), "dp", axis=0)
    w_qkv = jnp.take(all_qkv, owners[0], axis=0, mode="clip").reshape(D, -1)

    def columns_of(slabs, owner):
        taken = jnp.take(slabs, owner, axis=0, mode="clip")
        return jnp.swapaxes(taken, 0, 1).reshape(taken.shape[1], D)

    _, out_low, gu_low, down_low = lax.optimization_barrier(
        (all_qkv, out_master[0].astype(low), gu_rows.astype(low), down_master[0].astype(low))
    )
    all_out = lax.all_gather(out_low, "dp", axis=0)
    all_gu = lax.all_gather(gu_low, "dp", axis=0)
    all_down = lax.all_gather(down_low, "dp", axis=0)

    def later_weights(mixed):
        mixed, wait_out, wait_gu, wait_down, wait_emb = lax.optimization_barrier(
            (mixed, all_out, all_gu, all_down, emb_low)
        )
        table = lax.all_gather(wait_emb, "dp", axis=1, tiled=True)
        w_gu = columns_of(wait_gu, owners[2])
        return (
            columns_of(wait_out, owners[1]),
            w_gu[:hidden],
            w_gu[hidden:],
            columns_of(wait_down, owners[3]),
            table,
            mixed,
        )

    loss_local, count_local, kept, weights = layer_forward(
        local_ids,
        targets,
        valid,
        resets,
        emb_low,
        w_qkv,
        later_weights,
        inner_init,
        gains,
        gain_one,
        head_index,
    )
    order = jnp.argsort(owners, axis=1)
    owned, grad_init, grad_gains = layer_backward(kept, weights, gains, order)
    init_rows = grad_init.size // 128
    numbers = jnp.zeros((8, 128), jnp.float32).at[0, 0].set(loss_local).at[0, 1].set(count_local)
    pieces = (grad_init.reshape(-1, 128), grad_gains.reshape(-1, 128), numbers)
    small = jnp.sum(share(9, jnp.concatenate(pieces, 0), ("dp",)), 0)
    loss_sum, count = small[-8, 0], small[-8, 1]
    small = (
        small[:init_rows].reshape(grad_init.shape),
        small[init_rows:-8].reshape(grad_gains.shape),
    )
    first_dp = (lax.axis_index("dp") == 0).astype(jnp.float32)
    squares = sum((jnp.sum(piece * piece) for piece in owned))
    squares = squares + first_dp * (jnp.sum(small[0] * small[0]) + jnp.sum(small[1] * small[1]))
    squares = share(10, jnp.broadcast_to(squares, (8, 128)), ("dp", "head"))
    squares_all = jnp.sum(squares[:, 0, 0])
    grad_norm = jnp.sqrt(squares_all) / count
    factor = jnp.minimum(1.0, CLIP_LIMIT / grad_norm) / count
    qkv_out = refresh(
        qkv_master, owned[0] * factor, qkv_left, qkv_right, qkv_left_root, qkv_right_root
    )
    out_out = refresh(
        out_master, owned[1] * factor, out_left, out_right, out_left_root, out_right_root
    )
    gu_out = refresh_rows(
        gu_master, owned[2][0] * factor, gu_left, gu_right, gu_left_root, gu_right_root
    )
    down_out = refresh(
        down_master, owned[3] * factor, down_left, down_right, down_left_root, down_right_root
    )
    table_out = adamw(emb_master, owned[4] * factor, emb_first, emb_second, TABLE_RATE)
    init_out = adamw(inner_init, small[0] * factor, inner_first, inner_second, INITIAL_RATE)
    gain_out = adamw(gains, small[1] * factor, gains_first, gains_second, GAINS_RATE)
    return (
        (jnp.stack([loss_sum, count]), grad_norm)
        + table_out
        + qkv_out
        + out_out
        + gu_out
        + down_out
        + init_out
        + gain_out
    )


def solution(mesh):
    placed = (
        P("dp"),
        P("dp"),
        P("dp"),
        P("dp"),
        P(),
        P("head", "dp"),
        P("head", "dp"),
        P("head", "dp"),
        P("dp", None, None, "head"),
        P("dp", "head", None, None),
        P("dp", "head", None, None),
        P("dp", "head", None, None),
        P("dp", "head", None, None),
        P("dp", "head", None),
        P("dp", "head", None, None),
        P("dp", "head", None, None),
        P("dp", "head", None, None),
        P("dp", "head", None, None),
        P("dp", None, None, "head"),
        P("dp", "head", None, None),
        P("dp", "head", None, None),
        P("dp", "head", None, None),
        P("dp", "head", None, None),
        P("dp", "head", None),
        P("dp", "head", None, None),
        P("dp", "head", None, None),
        P("dp", "head", None, None),
        P("dp", "head", None, None),
        P("head", None, None),
        P("head", None, None),
        P("head", None, None),
        P(None, "head"),
        P(None, "head"),
        P(None, "head"),
    )
    return jax.shard_map(
        shards,
        mesh=mesh,
        in_specs=placed,
        out_specs=(
            P(),
            P(),
            P("head", "dp"),
            P("head", "dp"),
            P("head", "dp"),
            P("dp", None, None, "head"),
            P("dp", "head", None, None),
            P("dp", "head", None, None),
            P("dp", None, None, "head"),
            P("dp", "head", None),
            P("dp", "head", None, None),
            P("dp", "head", None, None),
            P("dp", "head", None),
            P("dp", None, None, "head"),
            P("dp", "head", None, None),
            P("dp", "head", None, None),
            P("dp", None, None, "head"),
            P("dp", "head", None),
            P("dp", "head", None, None),
            P("dp", "head", None, None),
            P("dp", "head", None),
            P("head", None, None),
            P("head", None, None),
            P("head", None, None),
            P(None, "head"),
            P(None, "head"),
            P(None, "head"),
        ),
        check_vma=False,
    )
```

```python
import functools

import jax
import jax.numpy as jnp
from jax import lax
from jax.experimental import pallas as pl
from jax.experimental.pallas import tpu as pltpu
from jax.sharding import PartitionSpec as P

D = 2048
P_SIZE = 64
MB = 16
STEP = 10


EPSILON = 1e-05
CLIP_LIMIT = 0.05
STAT_DECAY = 0.5
MATRIX_RATE = 0.4
TABLE_RATE = 0.3
INITIAL_RATE = 0.05
GAINS_RATE = 0.3
BETA_ONE = 0.9
BETA_TWO = 0.95
ADAM_EPSILON = 1e-08
WEIGHT_DECAY = 0.01


CHUNK = 64
PAIR = 2 * P_SIZE


def dot_ab(left, right):
    return lax.dot_general(left, right, (((1,), (0,)), ((), ())), preferred_element_type=jnp.float32)


def dot_abt(left, right):
    return lax.dot_general(left, right, (((1,), (1,)), ((), ())), preferred_element_type=jnp.float32)


def dot_atb(left, right):
    return lax.dot_general(left, right, (((0,), (0,)), ((), ())), preferred_element_type=jnp.float32)


def halves_of(value):
    high = value.astype(jnp.bfloat16)
    return (high, (value - high.astype(jnp.float32)).astype(jnp.bfloat16))


def wide(form, left, right):
    lefts = left if isinstance(left, tuple) else (left,)
    rights = right if isinstance(right, tuple) else (right,)
    total = form(lefts[0], rights[0])
    if len(rights) > 1:
        total = total + form(lefts[0], rights[1])
    if len(lefts) > 1:
        total = total + form(lefts[1], rights[0])
    return total


def each(pieces, change):
    return tuple(change(piece) for piece in pieces) if isinstance(pieces, tuple) else change(pieces)


def mixer_masks(resets, tokens):
    per_chunk = CHUNK // MB
    chunks = tokens // CHUNK
    segment = jnp.cumsum(resets.reshape(chunks, per_chunk), axis=1)
    segment = jnp.repeat(segment, MB, axis=1)
    same = segment[:, :, None] == segment[:, None, :]
    spot = jnp.arange(CHUNK, dtype=jnp.int32)
    causal = (spot[None, :] <= spot[:, None])[None]
    earlier = ((spot[None, :] // MB) < (spot[:, None] // MB))[None]
    causal = (same & causal).astype(jnp.float32)
    earlier = (same & earlier).astype(jnp.float32)
    first = (segment == 0).astype(jnp.float32).reshape(tokens, 1)
    last = (segment == segment[:, -1:]).astype(jnp.float32).reshape(tokens, 1)
    anew = (segment[:, -1] > 0).astype(jnp.float32)
    first = jnp.broadcast_to(first, (tokens, PAIR))
    last = jnp.broadcast_to(last, (tokens, PAIR))
    anew = jnp.broadcast_to(anew[:, None, None], (chunks, 8, PAIR))
    return causal, earlier, first, last, anew


def lane_helpers(rows):
    lanes = lax.broadcasted_iota(jnp.int32, (rows, PAIR), 1)
    low_lane = lanes < P_SIZE
    low_half = low_lane.astype(jnp.float32)
    high_half = 1.0 - low_half

    def stack(pieces):
        def one(piece):
            kind = piece.dtype
            return jnp.concatenate(
                [piece * low_half.astype(kind), piece * high_half.astype(kind)], 0
            )

        return each(pieces, one)

    def pick(product):
        return jnp.where(low_lane, product[:rows], product[rows:])

    return stack, pick


def diagonal_blocks():
    rows = lax.broadcasted_iota(jnp.int32, (PAIR, PAIR), 0) // P_SIZE
    columns = lax.broadcasted_iota(jnp.int32, (PAIR, PAIR), 1) // P_SIZE
    return (rows == columns).astype(jnp.float32)


def solve(matrix, rate_row, value, pick):
    rows = value.shape[0]
    powers = [(matrix, rate_row)]
    reach = 2
    while reach < CHUNK // MB:
        last, rate = powers[-1]
        low, high = halves_of(last[:rows]), halves_of(last[rows:])
        powers.append(
            (
                jnp.concatenate([wide(dot_ab, low, low), wide(dot_ab, high, high)], 0),
                rate * rate,
            )
        )
        reach = 2 * reach
    for index in range(len(powers) - 1, -1, -1):
        factor, rate = powers[index]
        moved = pick(wide(dot_ab, halves_of(factor), halves_of(value * rate)))
        value = value - moved if index == 0 else value + moved
    return value


def mixer_forward_chunk(
    qkv_ref,
    rate_ref,
    initial_ref,
    causal_ref,
    earlier_ref,
    first_ref,
    last_ref,
    anew_ref,
    z_ref,
    residue_ref,
    states_ref,
    state,
):
    pairs = initial_ref.shape[0]
    width = pairs * PAIR

    stack, pick = lane_helpers(CHUNK)
    blocks = diagonal_blocks()
    causal = causal_ref[0]
    causal = jnp.concatenate([causal, causal], 0)
    earlier = earlier_ref[0]
    earlier = jnp.concatenate([earlier, earlier], 0)
    first = first_ref[...] > 0.0
    last = last_ref[...]
    anew = anew_ref[0, 0:1, :]
    for pair in range(pairs):
        lanes = slice(pair * PAIR, (pair + 1) * PAIR)
        query = qkv_ref[:, lanes]
        key = qkv_ref[:, width + pair * PAIR : width + (pair + 1) * PAIR]
        value = qkv_ref[:, 2 * width + pair * PAIR : 2 * width + (pair + 1) * PAIR]
        rate = rate_ref[0:1, lanes]
        begin = state[pair]
        initial = initial_ref[pair]
        states_ref[0, pair] = begin
        products = dot_abt(jnp.concatenate([stack(key), stack(query)], 0), key)
        ties = products[: 2 * CHUNK] * earlier
        scores = products[2 * CHUNK :] * causal
        both = jnp.concatenate([key, query], 0)
        seen = wide(dot_ab, both, halves_of(begin))
        fresh = wide(dot_ab, both, halves_of(initial))
        key_seen = jnp.where(first, seen[:CHUNK], fresh[:CHUNK])
        query_seen = jnp.where(first, seen[CHUNK:], fresh[CHUNK:])
        key_wide = key.astype(jnp.float32)
        residue = solve(ties, rate, key_seen - (value.astype(jnp.float32) - key_wide), pick)
        residue_ref[:, lanes] = residue
        scaled = residue * rate
        scaled_parts = halves_of(scaled)
        output = query_seen - pick(wide(dot_ab, halves_of(scores), scaled_parts))
        z_ref[:, lanes] = output.astype(jnp.bfloat16)
        key_last = (key_wide * last).astype(jnp.bfloat16)
        base = jnp.where(anew > 0.0, initial, begin)
        state[pair] = base - blocks * wide(dot_atb, key_last, scaled_parts)


def mixer_backward_chunk(
    qkv_ref,
    rate_ref,
    initial_ref,
    causal_ref,
    earlier_ref,
    causal_turned_ref,
    earlier_turned_ref,
    first_ref,
    last_ref,
    anew_ref,
    residue_ref,
    states_ref,
    upstream_ref,
    grad_ref,
    grad_initial_ref,
    grad_rate_ref,
    carried,
):
    pairs = initial_ref.shape[0]
    width = pairs * PAIR

    stack, pick = lane_helpers(CHUNK)
    blocks = diagonal_blocks()

    def doubled(ref):
        return jnp.concatenate([ref[0], ref[0]], 0)

    causal, earlier = doubled(causal_ref), doubled(earlier_ref)
    causal_turned, earlier_turned = doubled(causal_turned_ref), doubled(earlier_turned_ref)
    first_wide = first_ref[...]
    first = first_wide > 0.0
    last = last_ref[...]
    anew = anew_ref[0, 0:1, :]
    low = jnp.bfloat16
    for pair in range(pairs):
        lanes = slice(pair * PAIR, (pair + 1) * PAIR)
        query = qkv_ref[:, lanes]
        key = qkv_ref[:, width + pair * PAIR : width + (pair + 1) * PAIR]
        rate = rate_ref[0:1, lanes]
        begin = halves_of(states_ref[0, pair])
        initial = halves_of(initial_ref[pair])
        after = carried[pair]
        after_parts = halves_of(after)
        residue = residue_ref[:, lanes]
        scaled = halves_of(residue * rate)
        upstream = upstream_ref[:, lanes]
        upstream_parts = halves_of(upstream)
        key_wide = key.astype(jnp.float32)
        query_wide = query.astype(jnp.float32)
        key_last = (key_wide * last).astype(low)
        key_stack = stack(key)
        products = dot_abt(key_stack, jnp.concatenate([key, query], 0))
        ties_turned = products[:, :CHUNK] * earlier_turned
        scores_turned = products[:, CHUNK:] * causal_turned
        pulled = pick(wide(dot_ab, halves_of(scores_turned), upstream_parts))
        pulled = pulled + wide(dot_ab, key_last, after_parts)
        grad_scaled = solve(ties_turned, rate, -pulled, pick)
        grad_rate_ref[0:1, lanes] += jnp.sum(grad_scaled * residue, 0, keepdims=True)
        grad_residue = grad_scaled * rate
        residue_parts = halves_of(grad_residue)
        joined = tuple(
            jnp.concatenate([one, two], 0) for one, two in zip(upstream_parts, residue_parts)
        )
        turned = dot_abt(stack(scaled[0]), joined[0])
        straight = dot_abt(
            jnp.concatenate([stack(upstream_parts[0]), stack(residue_parts[0])], 0), scaled[0]
        )
        grad_scores = -straight[: 2 * CHUNK] * causal
        grad_scores_turned = -turned[:, :CHUNK] * causal_turned
        grad_ties = -(straight[2 * CHUNK :] * earlier + turned[:, CHUNK:] * earlier_turned)
        seen = dot_abt(joined[0], begin[0])
        fresh = dot_abt(joined[0], initial[0])
        grad_query = jnp.where(first, seen[:CHUNK], fresh[:CHUNK])
        grad_query = grad_query + pick(dot_ab(grad_scores.astype(low), key))
        grad_key = jnp.where(first, seen[CHUNK:], fresh[CHUNK:]) + grad_residue
        grad_key = grad_key + pick(
            dot_ab(grad_scores_turned.astype(low), query) + dot_ab(grad_ties.astype(low), key)
        )
        grad_key = grad_key - last * dot_abt(scaled[0], after_parts[0])
        grad_ref[:, lanes] = grad_query.astype(low)
        grad_ref[:, width + pair * PAIR : width + (pair + 1) * PAIR] = grad_key.astype(low)
        grad_ref[:, 2 * width + pair * PAIR : 2 * width + (pair + 1) * PAIR] = (
            -grad_residue
        ).astype(low)
        fronts = jnp.concatenate([query_wide * first_wide, key_wide * first_wide], 0).astype(low)
        backs = jnp.concatenate(
            [query_wide * (1.0 - first_wide), key_wide * (1.0 - first_wide)], 0
        ).astype(low)
        kept_after = jnp.where(anew > 0.0, 0.0, after)
        carried[pair] = kept_after + blocks * wide(dot_atb, fronts, joined)
        grad_initial_ref[pair] += (after - kept_after) + blocks * wide(dot_atb, backs, joined)


def pair_blocks(matrices):
    heads = matrices.shape[0]
    split = matrices.reshape(heads // 2, 2, P_SIZE, P_SIZE)
    empty = jnp.zeros_like(split[:, 0])
    upper = jnp.concatenate([split[:, 0], empty], 2)
    lower = jnp.concatenate([empty, split[:, 1]], 2)
    return jnp.concatenate([upper, lower], 1)


def head_blocks(pairs):
    return jnp.stack([pairs[:, :P_SIZE, :P_SIZE], pairs[:, P_SIZE:, P_SIZE:]], 1).reshape(
        -1, P_SIZE, P_SIZE
    )


ROWS = 64
LAG = 2
MESH = pl.DeviceIdType.MESH


def across(column):
    return jnp.swapaxes(jnp.broadcast_to(column, (column.shape[0], 128)), 0, 1)[:8]


def down(row, width):
    turned = jnp.swapaxes(jnp.broadcast_to(row[:1], (128, row.shape[1])), 0, 1)
    return jnp.concatenate([turned] * (width // 128), 1) if width > 128 else turned


def transit_kernel(mode, form, lag, parts, slabs, names, *all_refs):
    ref = dict(zip(names, all_refs))
    full_ref, partial, total = ref["full"], ref["partial"], ref["total"]
    pair_out, pair_in = ref["pair_out"], ref["pair_in"]
    from_low, from_high = ref["from_low"], ref["from_high"]
    places = parts // 2
    cross = form in ("lookup", "table")
    summing = mode != "plain"
    lefts = sum(name.startswith("left_buf") for name in names)
    size = total.shape[1]
    ring, band = partial.shape[0], partial.shape[1]
    me = lax.axis_index("head")
    mine_dp = lax.axis_index("dp")
    core = lax.rem(me, 2)
    spot = me // 2
    twin = {"head": me + 1 - 2 * core}
    upper = {"head": lax.rem(me + 2, parts)}
    lower = {"head": lax.rem(me + parts - 2, parts)}
    chunks = ref["up_in_sem"].shape[0]
    sum_at = 1 + lag * (places - 1)
    finish_at = sum_at + (lag if summing else 0)
    reach_at = finish_at + lag * (places - 1)
    close_at = reach_at + (lag + 1 if cross else 1)

    def place_of(chunk):
        return chunks - 1 - chunk if form == "inner" else chunk

    def band_of(index):
        return pl.ds(pl.multiple_of(index * band, band), band)

    def rows_of(chunk):
        return band_of(place_of(chunk))

    def shard(index):
        return pl.ds(pl.multiple_of(index * size, 128), size)

    def remote(source, target, out_sem, in_sem, device):
        return pltpu.make_async_remote_copy(
            src_ref=source,
            dst_ref=target,
            send_sem=out_sem,
            recv_sem=in_sem,
            device_id=device,
            device_id_type=MESH,
        )

    def left_copies(chunk):
        half = lax.rem(chunk, 2)
        return [
            pltpu.make_async_copy(
                ref["left%d" % part].at[rows_of(chunk)],
                ref["left_buf%d" % part].at[half],
                ref["left_sem%d" % part].at[half],
            )
            for part in range(lefts)
        ]

    barrier = pltpu.get_barrier_semaphore()
    for offset in range(1, parts):
        pl.semaphore_signal(
            barrier, inc=1, device_id={"head": lax.rem(me + offset, parts)}, device_id_type=MESH
        )
    if cross:
        for offset in range(1, slabs):
            pl.semaphore_signal(
                barrier,
                inc=1,
                device_id={"dp": lax.rem(mine_dp + offset, slabs)},
                device_id_type=MESH,
            )
    for copy in left_copies(0):
        copy.start()
    if mode in ("grad", "grad_add"):
        ref["gain_grad"][...] = jnp.zeros_like(ref["gain_grad"])
    if form == "table":
        ref["table_grad"][...] = jnp.zeros_like(ref["table_grad"])
    pl.semaphore_wait(barrier, parts - 1 + (slabs - 1 if cross else 0))

    def valid(chunk):
        return jnp.logical_and(chunk >= 0, chunk < chunks)

    def pair_copy(chunk):
        slot = lax.rem(chunk, ring)
        return remote(
            pair_out.at[slot],
            pair_in.at[slot],
            ref["pair_out_sem"].at[slot],
            ref["pair_in_sem"].at[slot],
            twin,
        )

    def rise(chunk, place):
        slot = lax.rem(chunk, ring)
        part = from_low.at[slot, :, pl.ds((place + 1) * size, (places - 1 - place) * size)]
        return remote(part, part, ref["low_out_sem"].at[slot], ref["low_in_sem"].at[slot], upper)

    def fall(chunk, place):
        slot = lax.rem(chunk, ring)
        part = from_high.at[slot, :, pl.ds(0, place * size)]
        return remote(part, part, ref["high_out_sem"].at[slot], ref["high_in_sem"].at[slot], lower)

    def sums_copy(chunk, offset):
        slot = lax.rem(chunk, ring)
        return remote(
            ref["sums_out"].at[slot],
            ref["sums_in"].at[slot, offset - 1],
            ref["sums_out_sem"].at[slot],
            ref["sums_in_sem"].at[slot],
            {"head": lax.rem(me + offset, parts)},
        )

    def piece(chunk, source):
        if cross:
            return ref["stage"].at[rows_of(chunk), shard(source)]
        return full_ref.at[rows_of(chunk), shard(2 * source + core)]

    def climb(chunk, source, hop):
        part = piece(chunk, source)
        return remote(
            part,
            part,
            ref["up_out_sem"].at[chunk, hop - 1],
            ref["up_in_sem"].at[chunk, hop - 1],
            upper,
        )

    def sink(chunk, source, hop):
        part = piece(chunk, source)
        return remote(
            part,
            part,
            ref["down_out_sem"].at[chunk, hop - 1],
            ref["down_in_sem"].at[chunk, hop - 1],
            lower,
        )

    def target(chunk, giver):
        if form == "lookup":
            return full_ref.at[rows_of(chunk), shard(2 * giver + core)]
        return full_ref.at[chunk // 2, band_of(lax.rem(chunk, 2) * slabs + giver), shard(core)]

    def mirror(chunk, index):
        part = target(chunk, index) if cross else piece(chunk, index)
        return remote(
            part, part, ref["twin_out_sem"].at[chunk], ref["twin_in_sem"].at[chunk], twin
        )

    def hand_over(chunk, source):
        return remote(
            piece(chunk, source),
            target(chunk, mine_dp),
            ref["cross_out_sem"].at[chunk, source],
            ref["cross_in_sem"].at[chunk, mine_dp],
            {"dp": source},
        )

    def have(chunk, source):
        if not cross:
            mirror(chunk, source).start()
            return

        @pl.when(source != mine_dp)
        def _():
            hand_over(chunk, source).start()

        @pl.when(source == mine_dp)
        def _():
            values = ref["stage"][rows_of(chunk), shard(source)]
            if form == "lookup":
                full_ref[rows_of(chunk), shard(2 * mine_dp + core)] = values
            else:
                place_rows = band_of(lax.rem(chunk, 2) * slabs + mine_dp)
                full_ref[chunk // 2, place_rows, shard(core)] = values
            mirror(chunk, mine_dp).start()

    def receive(step):
        for hop in range(places):
            chunk = step - finish_at - lag * (hop + 1)

            @pl.when(jnp.logical_and(valid(chunk), jnp.abs(spot - mine_dp) == hop))
            def _():
                for offset in range(1, slabs):
                    giver = lax.rem(mine_dp + offset, slabs)
                    part = target(chunk, giver)
                    remote(
                        part,
                        part,
                        ref["cross_out_sem"].at[chunk, giver],
                        ref["cross_in_sem"].at[chunk, giver],
                        twin,
                    ).wait_recv()
                    mirror(chunk, giver).start()

    def relay(step):
        for hop in range(1, places):
            chunk = step - finish_at - lag * hop
            source = spot - hop

            @pl.when(jnp.logical_and(valid(chunk), source >= 0))
            def _():
                climb(chunk, source, hop).wait_recv()
                if hop < places - 1:

                    @pl.when(spot < places - 1)
                    def _():
                        climb(chunk, source, hop + 1).start()

                have(chunk, source)

            source_high = spot + hop

            @pl.when(jnp.logical_and(valid(chunk), source_high < places))
            def _():
                sink(chunk, source_high, hop).wait_recv()
                if hop < places - 1:

                    @pl.when(spot > 0)
                    def _():
                        sink(chunk, source_high, hop + 1).start()

                have(chunk, source_high)

    def finish_shard(step):
        chunk = step - finish_at

        @pl.when(valid(chunk))
        def _():
            slot = lax.rem(chunk, ring)
            rows = rows_of(chunk)
            if summing:
                sums_in = ref["sums_in"]
                pltpu.make_async_copy(
                    sums_in.at[slot], sums_in.at[slot], ref["sums_in_sem"].at[slot]
                ).wait()
                summed = ref["sums_out"][slot]
                for offset in range(1, parts):
                    summed = summed + sums_in[slot, offset - 1]
                gain = ref["gain"][0:1, :]
            if mode == "plain":
                result = total[...]
            elif mode == "norm":
                scale = lax.rsqrt(summed / D + EPSILON)
                ref["scale"][chunk] = scale
                result = ref["own"][rows, :] * down(scale, size) * gain
            else:
                scale = down(ref["scale"][place_of(chunk)], size)
                normed = ref["inputs"][rows, :] * scale
                inner = down(summed / D, size)
                result = scale * (ref["own"][rows, :] * gain - normed * inner)
                if mode == "grad_add":
                    result = result + ref["added"][rows, :]
                if form != "table":
                    ref["own"][rows, :] = result
            if cross:
                ref["stage"][rows, shard(spot)] = result.astype(jnp.bfloat16)
            else:
                full_ref[rows, shard(me)] = result.astype(jnp.bfloat16)

            @pl.when(spot < places - 1)
            def _():
                climb(chunk, spot, 1).start()

            @pl.when(spot > 0)
            def _():
                sink(chunk, spot, 1).start()

            have(chunk, spot)

    def add_pair(step):
        chunk = step - 1

        @pl.when(valid(chunk))
        def _():
            slot = lax.rem(chunk, ring)
            pair_copy(chunk).wait_recv()
            partial[slot] = partial[slot] + pair_in[slot].astype(jnp.float32)

    def pass_on(step):
        for place in range(places):
            if place < places - 1:
                up_chunk = step - 1 - lag * place

                @pl.when(jnp.logical_and(valid(up_chunk), spot == place))
                def _():
                    slot = lax.rem(up_chunk, ring)
                    above = pl.ds((place + 1) * size, (places - 1 - place) * size)
                    values = partial[slot, :, above]
                    if place > 0:
                        rise(up_chunk, place - 1).wait_recv()
                        values = values + from_low[slot, :, above].astype(jnp.float32)
                    from_low[slot, :, above] = values.astype(jnp.bfloat16)
                    rise(up_chunk, place).start()

            if place > 0:
                down_chunk = step - 1 - lag * (places - 1 - place)

                @pl.when(jnp.logical_and(valid(down_chunk), spot == place))
                def _():
                    slot = lax.rem(down_chunk, ring)
                    below = pl.ds(0, place * size)
                    values = partial[slot, :, below]
                    if place < places - 1:
                        fall(down_chunk, place + 1).wait_recv()
                        values = values + from_high[slot, :, below].astype(jnp.float32)
                    from_high[slot, :, below] = values.astype(jnp.bfloat16)
                    fall(down_chunk, place).start()

    def settle(step):
        chunk = step - sum_at - lag

        @pl.when(valid(chunk))
        def _():
            pair_copy(chunk).wait_send()
            for place in range(places):

                @pl.when(spot == place)
                def _():
                    if place < places - 1:
                        rise(chunk, place).wait_send()
                    if place > 0:
                        fall(chunk, place).wait_send()

            if summing:
                slot = lax.rem(chunk, ring)
                sums_in = ref["sums_in"]
                pltpu.make_async_copy(
                    sums_in.at[slot], sums_in.at[slot], ref["sums_out_sem"].at[slot]
                ).wait()

    def sum_shard(step):
        chunk = step - sum_at

        @pl.when(valid(chunk))
        def _():
            slot = lax.rem(chunk, ring)
            rows = rows_of(chunk)
            mine = shard(spot)

            @pl.when(spot == places - 1)
            def _():
                rise(chunk, places - 2).wait_recv()

            @pl.when(spot == 0)
            def _():
                fall(chunk, 1).wait_recv()

            total[...] = partial[slot, :, mine]

            @pl.when(spot > 0)
            def _():
                total[...] += from_low[slot, :, mine].astype(jnp.float32)

            @pl.when(spot < places - 1)
            def _():
                total[...] += from_high[slot, :, mine].astype(jnp.float32)

            if not summing:
                return
            value = total[...]
            if mode == "norm":
                value = value + ref["inputs"][rows, :]
                column = jnp.sum(value * value, 1, keepdims=True)
            else:
                scale = down(ref["scale"][place_of(chunk)], size)
                normed = ref["inputs"][rows, :] * scale
                ref["gain_grad"][0:1, :] += jnp.sum(value * normed, 0, keepdims=True)
                column = jnp.sum(value * ref["gain"][0:1, :] * normed, 1, keepdims=True)
            ref["own"][rows, :] = value
            ref["sums_out"][slot] = across(column)
            for offset in range(1, parts):
                sums_copy(chunk, offset).start()

    def produce(step):
        chunk = step

        @pl.when(valid(chunk))
        def _():
            slot = lax.rem(chunk, ring)
            right_ref = ref["right0"]
            if form == "lookup":
                entries = right_ref.shape[0]
                ids = jnp.concatenate(
                    [ref["ids"][group, rows_of(chunk), 0:1] for group in range(slabs)], 0
                )
                spots = lax.broadcasted_iota(jnp.int32, (slabs * band, entries), 1)
                hits = (spots == ids).astype(jnp.bfloat16)
                other = dot_ab(hits, right_ref[:, shard(1 - core)]).astype(jnp.bfloat16)
                for group in range(slabs):
                    pair_out[slot, :, pl.ds(group * size, size)] = other[
                        group * band : (group + 1) * band
                    ]
                pair_copy(chunk).start()
                here = dot_ab(hits, right_ref[:, shard(core)])
                for group in range(slabs):
                    partial[slot, :, pl.ds(group * size, size)] = here[
                        group * band : (group + 1) * band
                    ]
                return
            half = lax.rem(chunk, 2)
            if form == "mixer":
                one = pl.ds(chunk, 1)
                here = rows_of(chunk)

                @pl.when(chunk == 0)
                def _():
                    ref["state"][...] = jnp.zeros_like(ref["state"])

                mixer_forward_chunk(
                    ref["qkv"].at[here],
                    ref["rate"],
                    ref["initial"],
                    ref["causal"].at[one],
                    ref["earlier"].at[one],
                    ref["first"].at[here],
                    ref["last"].at[here],
                    ref["anew"].at[one],
                    ref["z"].at[here],
                    ref["residue"].at[here],
                    ref["states"].at[one],
                    ref["state"],
                )
            else:
                for copy in left_copies(chunk):
                    copy.wait()

                @pl.when(chunk + 1 < chunks)
                def _():
                    for copy in left_copies(chunk + 1):
                        copy.start()

            def term(index):
                if form == "mixer":
                    return dot_ab(ref["z"][rows_of(chunk), :], right_ref[:, shard(index)])
                if form == "table":
                    return dot_abt(ref["left_buf0"][half], right_ref[shard(index), :])
                terms = [
                    dot_ab(ref["left_buf%d" % part][half], ref["right%d" % part][:, shard(index)])
                    for part in range(lefts)
                ]
                return sum(terms[1:], terms[0])

            for place in range(places):
                lanes = pl.ds(place * size, size)
                pair_out[slot, :, lanes] = term(2 * place + 1 - core).astype(jnp.bfloat16)
            pair_copy(chunk).start()
            for place in range(places):
                lanes = pl.ds(place * size, size)
                partial[slot, :, lanes] = term(2 * place + core)

    def close(step):
        chunk = step - close_at

        @pl.when(valid(chunk))
        def _():
            if form == "table":
                arrived = full_ref.at[chunk // 2, pl.ds(0, slabs * band), pl.ds(0, size)]
            else:
                arrived = full_ref.at[rows_of(chunk), pl.ds(0, places * size)]
            pltpu.make_async_copy(arrived, arrived, ref["twin_in_sem"].at[chunk]).wait()
            pltpu.make_async_copy(arrived, arrived, ref["twin_out_sem"].at[chunk]).wait()
            if cross:
                for offset in range(1, slabs):
                    hand_over(chunk, lax.rem(mine_dp + offset, slabs)).wait_send()
            for hop in range(1, places):
                source = spot - hop + 1

                @pl.when(jnp.logical_and(source >= 0, spot < places - 1))
                def _():
                    climb(chunk, source, hop).wait_send()

                source_high = spot + hop - 1

                @pl.when(jnp.logical_and(source_high < places, spot > 0))
                def _():
                    sink(chunk, source_high, hop).wait_send()

            if form == "lookup":
                rows = rows_of(chunk)
                ref["own"][rows, :] = full_ref[rows, shard(me)].astype(jnp.float32)
                values = full_ref[rows, :].astype(jnp.float32)
                scale = lax.rsqrt(jnp.sum(values * values, 1, keepdims=True) / D + EPSILON)
                ref["scale"][chunk] = across(scale)
                normed = (values * scale * ref["gain"][0:1, :]).astype(jnp.bfloat16)
                full_ref[rows, :] = normed
            if form == "inner":
                rows, one = rows_of(chunk), pl.ds(place_of(chunk), 1)

                @pl.when(chunk == 0)
                def _():
                    for name in ("state", "grad_initial", "grad_rate"):
                        ref[name][...] = jnp.zeros_like(ref[name])

                ref["upstream"][...] = dot_abt(full_ref[rows, :], ref["project"][...])
                mixer_backward_chunk(
                    ref["qkv"].at[rows],
                    ref["rate"],
                    ref["initial"],
                    ref["causal"].at[one],
                    ref["earlier"].at[one],
                    ref["causal_turned"].at[one],
                    ref["earlier_turned"].at[one],
                    ref["first"].at[rows],
                    ref["last"].at[rows],
                    ref["anew"].at[one],
                    ref["residue"].at[rows],
                    ref["states"].at[one],
                    ref["upstream"],
                    ref["grad_mixed"].at[rows],
                    ref["grad_initial"],
                    ref["grad_rate"],
                    ref["state"],
                )
            if form == "table":
                @pl.when(lax.rem(chunk, 2) == 1)
                def _():
                    table_grad = ref["table_grad"]
                    entries = table_grad.shape[0]
                    pieces = 5 if entries % 80 == 0 else 1
                    block = entries // pieces
                    ids = ref["ids"][chunk // 2, 0:1, :]
                    values = full_ref[chunk // 2]
                    for index in range(pieces):
                        spots = index * block + lax.broadcasted_iota(
                            jnp.int32, (block, ids.shape[1]), 0
                        )
                        hits = (spots == ids).astype(jnp.bfloat16)
                        span = pl.ds(index * block, block)
                        table_grad[span, :] += dot_ab(hits, values)

    def advance(step, carried):
        relay(step)
        if summing:
            finish_shard(step)
        if cross:
            receive(step)
        add_pair(step)
        pass_on(step)
        settle(step)
        sum_shard(step)
        if not summing:
            finish_shard(step)
        produce(step)
        close(step)
        return carried

    lax.fori_loop(0, chunks + close_at, advance, 0)


def transit(
    mode,
    form,
    number,
    parts,
    slabs,
    right,
    tokens,
    size,
    left=None,
    inputs=None,
    gain=None,
    scale=None,
    added=None,
    ids=None,
    entries=None,
    mixer=None,
    project=None,
    band=ROWS,
    lag=LAG,
):
    chunks = tokens // band
    places = parts // 2
    cross = form in ("lookup", "table")
    summing = mode != "plain"
    ring = min(chunks, lag * (places + 1) + 2) if summing else chunks
    dma = pltpu.SemaphoreType.DMA
    low, wide_kind = jnp.bfloat16, jnp.float32
    vmem = pl.BlockSpec(memory_space=pltpu.VMEM)
    operands, specs, outputs, scratch = {}, [], {}, {}

    def take(name, array, spec=vmem):
        operands[name] = array
        specs.append(spec)

    rights = right if isinstance(right, tuple) else (right,)
    lefts = left if isinstance(left, tuple) else () if left is None else (left,)
    for part, array in enumerate(rights):
        take("right%d" % part, array)
    for part, array in enumerate(lefts):
        take("left%d" % part, array, pl.BlockSpec(memory_space=pl.ANY))
    if project is not None:
        take("project", project)
    if ids is not None:
        take("ids", ids)
    if mixer is not None:
        for name, array in mixer.items():
            take(name, array)
        pairs, width = mixer["initial"].shape[0], mixer["rate"].shape[1]
    if summing:
        take("inputs", inputs)
    take("gain", gain)
    if mode in ("grad", "grad_add"):
        take("scale", scale)
    if mode == "grad_add":
        take("added", added)

    if form != "table":
        outputs["own"] = ((tokens, size), wide_kind)
    if form != "table":
        outputs["full"] = ((tokens, parts * size), low)
    if mode in ("norm", "plain"):
        outputs["scale"] = ((chunks, 8, band), wide_kind)
    if mode in ("grad", "grad_add"):
        outputs["gain_grad"] = ((8, size), wide_kind)
    if form == "table":
        outputs["table_grad"] = ((entries, 2 * size), wide_kind)

    if form == "inner":
        outputs["grad_mixed"] = ((tokens, 3 * width), low)
        outputs["grad_initial"] = ((pairs, PAIR, PAIR), wide_kind)
        outputs["grad_rate"] = ((1, width), wide_kind)
        scratch["state"] = pltpu.VMEM((pairs, PAIR, PAIR), wide_kind)
        scratch["upstream"] = pltpu.VMEM((band, width), wide_kind)
    if form == "mixer":
        outputs["z"] = ((tokens, width), low)
        outputs["residue"] = ((tokens, width), wide_kind)
        outputs["states"] = ((chunks, pairs, PAIR, PAIR), wide_kind)
        scratch["state"] = pltpu.VMEM((pairs, PAIR, PAIR), wide_kind)
    span = places * size
    hops = max(places - 1, 1)
    if form == "table":
        scratch["own"] = pltpu.VMEM((tokens, size), wide_kind)
        scratch["full"] = pltpu.VMEM((chunks // 2, 2 * slabs * band, 2 * size), low)
    for part, array in enumerate(lefts):
        scratch["left_buf%d" % part] = pltpu.VMEM((2, band, array.shape[1]), low)
        scratch["left_sem%d" % part] = dma((2,))
    if cross:
        scratch["stage"] = pltpu.VMEM((tokens, span), low)
        scratch["cross_out_sem"] = dma((chunks, slabs))
        scratch["cross_in_sem"] = dma((chunks, slabs))
    if summing:
        scratch["sums_out"] = pltpu.VMEM((ring, 8, band), wide_kind)
        scratch["sums_in"] = pltpu.VMEM((ring, parts - 1, 8, band), wide_kind)
        scratch["sums_out_sem"] = dma((ring,))
        scratch["sums_in_sem"] = dma((ring,))
    scratch["total"] = pltpu.VMEM((band, size), wide_kind)
    scratch["partial"] = pltpu.VMEM((ring, band, span), wide_kind)
    for name in ("pair_out", "pair_in", "from_low", "from_high"):
        scratch[name] = pltpu.VMEM((ring, band, span), low)
    for name in ("pair_out", "pair_in", "low_out", "low_in", "high_out", "high_in"):
        scratch[name + "_sem"] = dma((ring,))
    for name in ("up_out", "up_in", "down_out", "down_in"):
        scratch[name + "_sem"] = dma((chunks, hops))
    scratch["twin_out_sem"] = dma((chunks,))
    scratch["twin_in_sem"] = dma((chunks,))

    depth = sum(array.size for array in rights) // (parts * size)
    names = tuple(operands) + tuple(outputs) + tuple(scratch)
    results = pl.pallas_call(
        functools.partial(transit_kernel, mode, form, lag, parts, slabs, names),
        in_specs=specs,
        out_specs=[vmem] * len(outputs),
        out_shape=[jax.ShapeDtypeStruct(shape, kind) for shape, kind in outputs.values()],
        scratch_shapes=list(scratch.values()),
        compiler_params=pltpu.CompilerParams(
            collective_id=number, has_side_effects=True, vmem_limit_bytes=60 * 1024 * 1024
        ),
        cost_estimate=pl.CostEstimate(
            flops=2 * tokens * depth * parts * size,
            bytes_accessed=128 * tokens * parts * size,
            transcendentals=0,
        ),
        name="transit_" + form,
    )(*operands.values())
    return dict(zip(outputs, results))


def share_kernel(axes, block_ref, all_ref, out_sem, in_sem):
    counts = [lax.axis_size(axis) for axis in axes]
    places = [lax.axis_index(axis) for axis in axes]
    members = 1
    me = 0
    for count, place in zip(counts, places):
        members = members * count
        me = me * count + place

    def partner(offset):
        device, rest = {}, offset
        for axis, count, place in reversed(list(zip(axes, counts, places))):
            device[axis] = lax.rem(place + lax.rem(rest, count), count)
            rest = rest // count
        return device

    def send(offset):
        return pltpu.make_async_remote_copy(
            src_ref=block_ref,
            dst_ref=all_ref.at[me],
            send_sem=out_sem,
            recv_sem=in_sem,
            device_id=partner(offset),
            device_id_type=MESH,
        )

    barrier = pltpu.get_barrier_semaphore()

    def greet(offset, carried):
        pl.semaphore_signal(barrier, inc=1, device_id=partner(offset), device_id_type=MESH)
        return carried

    def start(offset, carried):
        send(offset).start()
        return carried

    lax.fori_loop(1, members, greet, 0)
    all_ref[me] = block_ref[...]
    pl.semaphore_wait(barrier, members - 1)
    lax.fori_loop(1, members, start, 0)
    arrived = all_ref.at[pl.ds(0, members - 1)]
    pltpu.make_async_copy(arrived, arrived, in_sem).wait()
    pltpu.make_async_copy(arrived, arrived, out_sem).wait()


def share(number, block, axes):
    members = 1
    for axis in axes:
        members = members * lax.axis_size(axis)
    vmem = pl.BlockSpec(memory_space=pltpu.VMEM)
    return pl.pallas_call(
        functools.partial(share_kernel, axes),
        in_specs=[vmem],
        out_specs=vmem,
        out_shape=jax.ShapeDtypeStruct((members,) + block.shape, block.dtype),
        scratch_shapes=[pltpu.SemaphoreType.DMA, pltpu.SemaphoreType.DMA],
        compiler_params=pltpu.CompilerParams(
            collective_id=number, has_side_effects=True, vmem_limit_bytes=16 * 1024 * 1024
        ),
        cost_estimate=pl.CostEstimate(
            flops=0, bytes_accessed=16 * 1024 * 1024, transcendentals=0
        ),
        name="share",
    )(block)


SCORE_ROWS = 256


def scores_kernel(rows_ref, table_ref, goal_ref, logits_ref, stats_ref):
    entries = table_ref.shape[0]
    edges = list(range(0, entries, 512)) + [entries]
    goal = goal_ref[:, 0:1]
    picked = jnp.zeros((SCORE_ROWS, 1), jnp.float32)
    peaks, sums = [], []
    for low, high in zip(edges, edges[1:]):
        values = dot_abt(rows_ref[...], table_ref[low:high, :])
        logits_ref[:, low:high] = values
        peaks.append(jnp.max(values, 1, keepdims=True))
        sums.append(jnp.sum(jnp.exp(values - peaks[-1]), 1, keepdims=True))
        spots = low + lax.broadcasted_iota(jnp.int32, values.shape, 1)
        picked = picked + jnp.sum(jnp.where(spots == goal, values, 0.0), 1, keepdims=True)
    peak = functools.reduce(jnp.maximum, peaks)
    exp_sum = sum(part * jnp.exp(top - peak) for part, top in zip(sums, peaks))
    stats_ref[0] = jnp.broadcast_to(peak, (SCORE_ROWS, 128))
    stats_ref[1] = jnp.broadcast_to(exp_sum, (SCORE_ROWS, 128))
    stats_ref[2] = jnp.broadcast_to(picked, (SCORE_ROWS, 128))


def scores(rows, table, goals):
    tokens, width = rows.shape
    entries = table.shape[0]
    return pl.pallas_call(
        scores_kernel,
        grid=(tokens // SCORE_ROWS,),
        in_specs=[
            pl.BlockSpec((SCORE_ROWS, width), lambda i: (i, 0)),
            pl.BlockSpec(memory_space=pltpu.VMEM),
            pl.BlockSpec((SCORE_ROWS, 128), lambda i: (i, 0)),
        ],
        out_specs=[
            pl.BlockSpec((SCORE_ROWS, entries), lambda i: (i, 0)),
            pl.BlockSpec((3, SCORE_ROWS, 128), lambda i: (0, i, 0)),
        ],
        out_shape=[
            jax.ShapeDtypeStruct((tokens, entries), jnp.float32),
            jax.ShapeDtypeStruct((3, tokens, 128), jnp.float32),
        ],
        compiler_params=pltpu.CompilerParams(
            dimension_semantics=("arbitrary",), vmem_limit_bytes=56 * 1024 * 1024
        ),
        cost_estimate=pl.CostEstimate(
            flops=2 * tokens * entries * width,
            bytes_accessed=2 * entries * width + 4 * tokens * entries,
            transcendentals=tokens * entries,
        ),
        name="scores",
    )(rows, table, goals)


def shampoo(tile_w, tile_g, left, right, left_root, right_root):
    low_g = tile_g.astype(jnp.bfloat16)

    def product(form, one, two):
        return jnp.einsum(
            form,
            one.astype(jnp.bfloat16),
            two.astype(jnp.bfloat16),
            preferred_element_type=jnp.float32,
        )

    new_left = STAT_DECAY * left + (1.0 - STAT_DECAY) * product("abrc,absc->abrs", low_g, low_g)
    new_right = STAT_DECAY * right + (1.0 - STAT_DECAY) * product("abrc,abrd->abcd", low_g, low_g)
    turned = product("abrs,absc->abrc", left_root, low_g)
    turned = product("abrc,abcd->abrd", turned, right_root)
    return (new_left, new_right, tile_w - MATRIX_RATE * (turned + WEIGHT_DECAY * tile_w))


def refresh(master, grad, left, right, left_root, right_root):
    rows = master.shape[1]
    new_left, new_right, new_w = shampoo(
        master.reshape(1, 1, rows, -1),
        grad.reshape(1, 1, rows, -1),
        left,
        right,
        left_root,
        right_root,
    )
    return (grad.reshape(master.shape), new_left, new_right, new_w.reshape(master.shape))


def refresh_rows(master, grad, left, right, left_root, right_root):
    _, rows, kinds, _ = master.shape
    low_g = grad.astype(jnp.bfloat16)

    def product(form, one, two):
        return jnp.einsum(
            form,
            one.astype(jnp.bfloat16),
            two.astype(jnp.bfloat16),
            preferred_element_type=jnp.float32,
        )

    def shaped(array):
        return jnp.transpose(array.reshape(kinds, -1, rows), (2, 0, 1))[None]

    master_rows = jnp.transpose(master[0], (1, 2, 0)).reshape(-1, rows)
    new_left = STAT_DECAY * left + (1.0 - STAT_DECAY) * product("cr,cs->rs", low_g, low_g)
    new_right = STAT_DECAY * right + (1.0 - STAT_DECAY) * product("cr,dr->cd", low_g, low_g)
    turned = product("rs,cs->cr", left_root[0, 0], low_g)
    turned = product("dr,dc->cr", turned, right_root[0, 0])
    new_w = master_rows - MATRIX_RATE * (turned + WEIGHT_DECAY * master_rows)
    return (shaped(grad), new_left, new_right, shaped(new_w))


def adamw(weight, grad, first, second, step_rate):
    new_first = BETA_ONE * first + (1.0 - BETA_ONE) * grad
    new_second = BETA_TWO * second + (1.0 - BETA_TWO) * grad * grad
    moved = (
        new_first
        / (1.0 - BETA_ONE**STEP)
        / (jnp.sqrt(new_second / (1.0 - BETA_TWO**STEP)) + ADAM_EPSILON)
    )
    return (new_first, new_second, weight - step_rate * (moved + WEIGHT_DECAY * weight))


def layer_forward(
    local_ids,
    targets,
    valid,
    resets,
    emb_low,
    later_weights,
    inner_init,
    gains,
    gain_one,
    head_index,
):
    parts, slabs = lax.axis_size("head"), lax.axis_size("dp")
    vocab_part = emb_low.shape[0]
    tokens, size = targets.shape[0], gains.shape[1]
    chunks = tokens // ROWS
    columns = jnp.arange(vocab_part, dtype=jnp.int32)
    spread_ids = jnp.broadcast_to(local_ids[:, :, None], (slabs, tokens, 128))
    first = transit(
        "plain",
        "lookup",
        1,
        parts,
        slabs,
        emb_low,
        tokens,
        size,
        ids=spread_ids,
        gain=gain_one[None],
        lag=3,
    )
    embedded, full_one, scale_one = first["own"], first["full"], first["scale"]
    full_one, w_qkv, w_out, w_gate, w_up, w_down, table = later_weights(full_one)
    mixed = jnp.dot(full_one, w_qkv, preferred_element_type=jnp.float32).astype(jnp.bfloat16)
    step_rate = jax.nn.sigmoid(gains[3:4]) / (8 * P_SIZE)
    masks = mixer_masks(resets, tokens)
    initial_pairs = pair_blocks(inner_init)
    causal, earlier, before, after, anew = masks
    inner = dict(
        qkv=mixed,
        rate=step_rate,
        initial=initial_pairs,
        causal=causal,
        earlier=earlier,
        first=before,
        last=after,
        anew=anew,
    )
    second = transit(
        "norm",
        "mixer",
        2,
        parts,
        slabs,
        w_out,
        tokens,
        size,
        mixer=inner,
        lag=3,
        inputs=embedded,
        gain=gains[1:2],
    )
    inner_low = second["z"]
    inner = dict(
        inner,
        causal_turned=jnp.swapaxes(causal, 1, 2),
        earlier_turned=jnp.swapaxes(earlier, 1, 2),
        residue=second["residue"],
        states=second["states"],
    )
    hidden_one, full_two, scale_two = second["own"], second["full"], second["scale"]
    gate = jnp.einsum("td,fd->tf", full_two, w_gate, preferred_element_type=jnp.float32)
    up = jnp.einsum("td,fd->tf", full_two, w_up, preferred_element_type=jnp.float32)
    activated, act_pull = jax.vjp(lambda one, two: jax.nn.silu(one) * two, gate, up)
    act_low = activated.astype(jnp.bfloat16)
    third = transit(
        "norm",
        "rows",
        3,
        parts,
        slabs,
        w_down,
        tokens,
        size,
        left=act_low,
        inputs=hidden_one,
        gain=gains[2:3],
    )
    hidden_two, full_end, scale_end = third["own"], third["full"], third["scale"]
    local_targets = targets - head_index * vocab_part
    target_hits = columns[None, :] == local_targets[:, None]
    logits, stats = scores(
        full_end, table, jnp.broadcast_to(local_targets[:, None], (tokens, 128))
    )
    stats = share(7, stats[:, :, 0].reshape(-1, 128), ("head",)).reshape(parts, 3, tokens)
    highest = jnp.max(stats[:, 0], 0)
    exp_sum = jnp.sum(stats[:, 1] * jnp.exp(stats[:, 0] - highest[None]), 0)
    target_logit = jnp.sum(stats[:, 2], 0)
    totals = highest + jnp.log(exp_sum)
    counted = valid.astype(jnp.float32)
    d_logits = (
        (jnp.exp(logits - totals[:, None]) - target_hits.astype(jnp.float32)) * counted[:, None]
    ).astype(jnp.bfloat16)
    kept = (
        embedded,
        scale_one,
        full_one,
        inner,
        inner_low,
        hidden_one,
        scale_two,
        full_two,
        act_pull,
        act_low,
        hidden_two,
        scale_end,
        full_end,
        d_logits,
        local_ids,
    )
    weights = (w_qkv, w_out, w_gate, w_up, w_down, table)
    return (jnp.sum((totals - target_logit) * counted), jnp.sum(counted), kept, weights)


def slots_of(grad, order):
    parts = lax.axis_size("dp")
    shaped = grad.astype(jnp.bfloat16).reshape(parts, -1, grad.shape[1])
    return jnp.take(shaped, order, axis=0, mode="clip")


def column_slots_of(grad, order):
    parts = lax.axis_size("dp")
    shaped = grad.astype(jnp.bfloat16).reshape(grad.shape[0], parts, -1)
    return jnp.take(jnp.swapaxes(shaped, 0, 1), order, axis=0, mode="clip")


def scatter_dp(grad, dimension):
    return lax.psum_scatter(grad, "dp", scatter_dimension=dimension, tiled=True)


def rebanded(scale, band):
    rows = scale[:, 0].reshape(-1, 1, band)
    return jnp.broadcast_to(rows, (rows.shape[0], 8, band))


def layer_backward(kept, weights, gains, order):
    (
        embedded,
        scale_one,
        full_one,
        inner,
        inner_low,
        hidden_one,
        scale_two,
        full_two,
        act_pull,
        act_low,
        hidden_two,
        scale_end,
        full_end,
        d_logits,
        local_ids,
    ) = kept
    w_qkv, w_out, w_gate, w_up, w_down, table = weights
    parts, slabs = lax.axis_size("head"), lax.axis_size("dp")
    tokens, size = embedded.shape
    chunks = tokens // ROWS
    wide_kind = jnp.float32
    grad_table = jnp.einsum("tv,td->vd", d_logits, full_end, preferred_element_type=wide_kind)
    grad_table = grad_table.astype(jnp.bfloat16)
    owned_table = scatter_dp(grad_table, 1)
    d_logits, grad_table = lax.optimization_barrier((d_logits, grad_table))
    fourth = transit(
        "grad",
        "rows",
        4,
        parts,
        slabs,
        table,
        tokens,
        size,
        left=d_logits,
        inputs=hidden_two,
        gain=gains[2:3],
        scale=rebanded(scale_end, 2 * ROWS),
        band=2 * ROWS,
    )
    d_two, d_down_in = fourth["own"], fourth["full"]
    d_down_in, owned_table = lax.optimization_barrier((d_down_in, owned_table))
    d_act = jnp.einsum("td,fd->tf", d_down_in, w_down, preferred_element_type=wide_kind)
    d_gate, d_up = act_pull(d_act)
    d_gate, d_up = d_gate.astype(jnp.bfloat16), d_up.astype(jnp.bfloat16)
    grad_down = jnp.einsum("tf,td->fd", act_low, d_down_in, preferred_element_type=wide_kind)
    slot_down = column_slots_of(grad_down, order[3])
    grad_gate = jnp.einsum("tf,td->fd", d_gate, full_two, preferred_element_type=wide_kind)
    grad_up = jnp.einsum("tf,td->fd", d_up, full_two, preferred_element_type=wide_kind)
    slot_gate = column_slots_of(grad_gate, order[2])
    slot_up = column_slots_of(grad_up, order[2])
    d_gate, d_up, slot_down, slot_gate, slot_up = lax.optimization_barrier(
        (d_gate, d_up, slot_down, slot_gate, slot_up)
    )
    owned_down = scatter_dp(slot_down, 0)
    owned_gate = scatter_dp(slot_gate, 0)
    owned_up = scatter_dp(slot_up, 0)
    fifth = transit(
        "grad_add",
        "inner",
        5,
        parts,
        slabs,
        (w_gate, w_up),
        tokens,
        size,
        left=(d_gate, d_up),
        inputs=hidden_one,
        gain=gains[1:2],
        scale=scale_two,
        added=d_two,
        mixer=inner,
        lag=3,
        project=w_out,
    )
    d_one, d_out_in, d_mixed = fifth["own"], fifth["full"], fifth["grad_mixed"]
    grad_init = head_blocks(fifth["grad_initial"])
    gate = jax.nn.sigmoid(gains[3])
    grad_rate = fifth["grad_rate"][0] * gate * (1.0 - gate) / (8 * P_SIZE)
    d_mixed, owned_down, owned_gate, owned_up = lax.optimization_barrier(
        (d_mixed, owned_down, owned_gate, owned_up)
    )
    grad_out = jnp.einsum("tc,td->cd", inner_low, d_out_in, preferred_element_type=wide_kind)
    grad_qkv = jnp.einsum("td,tc->dc", full_one, d_mixed, preferred_element_type=wide_kind)
    slot_out = column_slots_of(grad_out, order[1])
    slot_qkv = slots_of(grad_qkv, order[0])
    d_mixed, slot_out, slot_qkv = lax.optimization_barrier((d_mixed, slot_out, slot_qkv))
    owned_out = scatter_dp(slot_out, 0)
    owned_qkv = scatter_dp(slot_qkv, 0)
    owned_gu = jnp.concatenate([owned_gate, owned_up], 1)
    row_ids = jnp.moveaxis(local_ids.reshape(slabs, chunks // 2, 2, ROWS), 0, 2)
    row_ids = jnp.broadcast_to(
        row_ids.reshape(chunks // 2, 1, 2 * slabs * ROWS), (chunks // 2, 8, 2 * slabs * ROWS)
    )
    sixth = transit(
        "grad_add",
        "table",
        6,
        parts,
        slabs,
        w_qkv,
        tokens,
        size,
        left=d_mixed,
        inputs=embedded,
        gain=gains[0:1],
        scale=scale_one,
        added=d_one,
        ids=row_ids,
        entries=table.shape[0],
    )
    owned_table = owned_table.astype(wide_kind) + sixth["table_grad"]
    gain_rows = [sixth["gain_grad"][0], fifth["gain_grad"][0], fourth["gain_grad"][0], grad_rate]
    owned = tuple(
        piece.astype(wide_kind) for piece in (owned_qkv, owned_out, owned_gu, owned_down)
    )
    return owned + (owned_table,), grad_init, jnp.stack(gain_rows, 0)


def shards(
    token_ids,
    targets,
    valid,
    resets,
    owners,
    emb_master,
    emb_first,
    emb_second,
    qkv_master,
    qkv_left,
    qkv_right,
    qkv_left_root,
    qkv_right_root,
    out_master,
    out_left,
    out_right,
    out_left_root,
    out_right_root,
    gu_master,
    gu_left,
    gu_right,
    gu_left_root,
    gu_right_root,
    down_master,
    down_left,
    down_right,
    down_left_root,
    down_right_root,
    inner_init,
    inner_first,
    inner_second,
    gains,
    gains_first,
    gains_second,
):
    low = jnp.bfloat16
    dp_size, head_size = lax.axis_size("dp"), lax.axis_size("head")
    head_index = lax.axis_index("head")
    ids_rows = token_ids.astype(jnp.float32).reshape(-1, 128)
    gain_rows = jnp.pad(gains[0].reshape(-1, 128), ((0, 8 - gains.shape[1] // 128), (0, 0)))
    opening = share(8, jnp.concatenate([ids_rows, gain_rows], 0), ("dp", "head"))
    opening = opening.reshape(dp_size, head_size, -1, 128)
    local_ids = opening[:, 0, : ids_rows.shape[0]].reshape(dp_size, -1).astype(jnp.int32)
    local_ids = local_ids - head_index * emb_master.shape[0]
    gain_one = opening[0, :, ids_rows.shape[0] :].reshape(head_size, -1)
    gain_one = gain_one[:, : gains.shape[1]].reshape(-1)
    emb_low = emb_master.astype(low)

    def flat(array):
        return array.reshape(array.shape[1], -1)

    gu_rows = jnp.transpose(gu_master[0], (1, 2, 0)).reshape(-1, gu_master.shape[1])
    hidden = gu_master.shape[3]
    all_qkv = lax.all_gather(flat(qkv_master).astype(low), "dp", axis=0)
    all_out = lax.all_gather(out_master[0].astype(low), "dp", axis=0)
    all_gu = lax.all_gather(gu_rows.astype(low), "dp", axis=0)

    def columns_of(slabs, owner):
        taken = jnp.take(slabs, owner, axis=0, mode="clip")
        return jnp.swapaxes(taken, 0, 1).reshape(taken.shape[1], D)

    def later_weights(rows):
        rows, wait_qkv, wait_out, wait_gu, down_low, table_low = lax.optimization_barrier(
            (rows, all_qkv, all_out, all_gu, down_master[0].astype(low), emb_low)
        )
        w_qkv = jnp.take(wait_qkv, owners[0], axis=0, mode="clip").reshape(D, -1)
        all_down = lax.all_gather(down_low, "dp", axis=0)
        table = lax.all_gather(table_low, "dp", axis=1, tiled=True)
        w_gu = columns_of(wait_gu, owners[2])
        return (
            rows,
            w_qkv,
            columns_of(wait_out, owners[1]),
            w_gu[:hidden],
            w_gu[hidden:],
            columns_of(all_down, owners[3]),
            table,
        )

    loss_local, count_local, kept, weights = layer_forward(
        local_ids,
        targets,
        valid,
        resets,
        emb_low,
        later_weights,
        inner_init,
        gains,
        gain_one,
        head_index,
    )
    order = jnp.argsort(owners, axis=1)
    owned, grad_init, grad_gains = layer_backward(kept, weights, gains, order)
    init_rows = grad_init.size // 128
    numbers = jnp.zeros((8, 128), jnp.float32).at[0, 0].set(loss_local).at[0, 1].set(count_local)
    pieces = (grad_init.reshape(-1, 128), grad_gains.reshape(-1, 128), numbers)
    small = jnp.sum(share(9, jnp.concatenate(pieces, 0), ("dp",)), 0)
    loss_sum, count = small[-8, 0], small[-8, 1]
    small = (
        small[:init_rows].reshape(grad_init.shape),
        small[init_rows:-8].reshape(grad_gains.shape),
    )
    first_dp = (lax.axis_index("dp") == 0).astype(jnp.float32)
    squares = sum((jnp.sum(piece * piece) for piece in owned))
    squares = squares + first_dp * (jnp.sum(small[0] * small[0]) + jnp.sum(small[1] * small[1]))
    squares = share(10, jnp.broadcast_to(squares, (8, 128)), ("dp", "head"))
    squares_all = jnp.sum(squares[:, 0, 0])
    grad_norm = jnp.sqrt(squares_all) / count
    factor = jnp.minimum(1.0, CLIP_LIMIT / grad_norm) / count
    qkv_out = refresh(
        qkv_master, owned[0] * factor, qkv_left, qkv_right, qkv_left_root, qkv_right_root
    )
    out_out = refresh(
        out_master, owned[1] * factor, out_left, out_right, out_left_root, out_right_root
    )
    gu_out = refresh_rows(
        gu_master, owned[2][0] * factor, gu_left, gu_right, gu_left_root, gu_right_root
    )
    down_out = refresh(
        down_master, owned[3] * factor, down_left, down_right, down_left_root, down_right_root
    )
    table_out = adamw(emb_master, owned[4] * factor, emb_first, emb_second, TABLE_RATE)
    init_out = adamw(inner_init, small[0] * factor, inner_first, inner_second, INITIAL_RATE)
    gain_out = adamw(gains, small[1] * factor, gains_first, gains_second, GAINS_RATE)
    return (
        (jnp.stack([loss_sum, count]), grad_norm)
        + table_out
        + qkv_out
        + out_out
        + gu_out
        + down_out
        + init_out
        + gain_out
    )


def solution(mesh):
    placed = (
        P("dp"),
        P("dp"),
        P("dp"),
        P("dp"),
        P(),
        P("head", "dp"),
        P("head", "dp"),
        P("head", "dp"),
        P("dp", None, None, "head"),
        P("dp", "head", None, None),
        P("dp", "head", None, None),
        P("dp", "head", None, None),
        P("dp", "head", None, None),
        P("dp", "head", None),
        P("dp", "head", None, None),
        P("dp", "head", None, None),
        P("dp", "head", None, None),
        P("dp", "head", None, None),
        P("dp", None, None, "head"),
        P("dp", "head", None, None),
        P("dp", "head", None, None),
        P("dp", "head", None, None),
        P("dp", "head", None, None),
        P("dp", "head", None),
        P("dp", "head", None, None),
        P("dp", "head", None, None),
        P("dp", "head", None, None),
        P("dp", "head", None, None),
        P("head", None, None),
        P("head", None, None),
        P("head", None, None),
        P(None, "head"),
        P(None, "head"),
        P(None, "head"),
    )
    return jax.shard_map(
        shards,
        mesh=mesh,
        in_specs=placed,
        out_specs=(
            P(),
            P(),
            P("head", "dp"),
            P("head", "dp"),
            P("head", "dp"),
            P("dp", None, None, "head"),
            P("dp", "head", None, None),
            P("dp", "head", None, None),
            P("dp", None, None, "head"),
            P("dp", "head", None),
            P("dp", "head", None, None),
            P("dp", "head", None, None),
            P("dp", "head", None),
            P("dp", None, None, "head"),
            P("dp", "head", None, None),
            P("dp", "head", None, None),
            P("dp", None, None, "head"),
            P("dp", "head", None),
            P("dp", "head", None, None),
            P("dp", "head", None, None),
            P("dp", "head", None),
            P("head", None, None),
            P("head", None, None),
            P("head", None, None),
            P(None, "head"),
            P(None, "head"),
            P(None, "head"),
        ),
        check_vma=False,
    )
```

```python
import functools

import jax
import jax.numpy as jnp
from jax import lax
from jax.experimental import pallas as pl
from jax.experimental.pallas import tpu as pltpu
from jax.sharding import PartitionSpec as P

D = 2048
P_SIZE = 64
MB = 16
STEP = 10


EPSILON = 1e-05
CLIP_LIMIT = 0.05
STAT_DECAY = 0.5
MATRIX_RATE = 0.4
TABLE_RATE = 0.3
INITIAL_RATE = 0.05
GAINS_RATE = 0.3
BETA_ONE = 0.9
BETA_TWO = 0.95
ADAM_EPSILON = 1e-08
WEIGHT_DECAY = 0.01


CHUNK = 64
PAIR = 2 * P_SIZE


def dot_ab(left, right):
    return lax.dot_general(left, right, (((1,), (0,)), ((), ())), preferred_element_type=jnp.float32)


def dot_abt(left, right):
    return lax.dot_general(left, right, (((1,), (1,)), ((), ())), preferred_element_type=jnp.float32)


def dot_atb(left, right):
    return lax.dot_general(left, right, (((0,), (0,)), ((), ())), preferred_element_type=jnp.float32)


def halves_of(value):
    high = value.astype(jnp.bfloat16)
    return (high, (value - high.astype(jnp.float32)).astype(jnp.bfloat16))


def wide(form, left, right):
    lefts = left if isinstance(left, tuple) else (left,)
    rights = right if isinstance(right, tuple) else (right,)
    total = form(lefts[0], rights[0])
    if len(rights) > 1:
        total = total + form(lefts[0], rights[1])
    if len(lefts) > 1:
        total = total + form(lefts[1], rights[0])
    return total


def each(pieces, change):
    return tuple(change(piece) for piece in pieces) if isinstance(pieces, tuple) else change(pieces)


def mixer_masks(resets, tokens):
    per_chunk = CHUNK // MB
    chunks = tokens // CHUNK
    segment = jnp.cumsum(resets.reshape(chunks, per_chunk), axis=1)
    segment = jnp.repeat(segment, MB, axis=1)
    same = segment[:, :, None] == segment[:, None, :]
    spot = jnp.arange(CHUNK, dtype=jnp.int32)
    causal = (spot[None, :] <= spot[:, None])[None]
    earlier = ((spot[None, :] // MB) < (spot[:, None] // MB))[None]
    causal = (same & causal).astype(jnp.float32)
    earlier = (same & earlier).astype(jnp.float32)
    first = (segment == 0).astype(jnp.float32).reshape(tokens, 1)
    last = (segment == segment[:, -1:]).astype(jnp.float32).reshape(tokens, 1)
    anew = (segment[:, -1] > 0).astype(jnp.float32)
    first = jnp.broadcast_to(first, (tokens, PAIR))
    last = jnp.broadcast_to(last, (tokens, PAIR))
    anew = jnp.broadcast_to(anew[:, None, None], (chunks, 8, PAIR))
    return causal, earlier, first, last, anew


def lane_helpers(rows):
    lanes = lax.broadcasted_iota(jnp.int32, (rows, PAIR), 1)
    low_lane = lanes < P_SIZE
    low_half = low_lane.astype(jnp.float32)
    high_half = 1.0 - low_half

    def stack(pieces):
        def one(piece):
            kind = piece.dtype
            return jnp.concatenate(
                [piece * low_half.astype(kind), piece * high_half.astype(kind)], 0
            )

        return each(pieces, one)

    def pick(product):
        return jnp.where(low_lane, product[:rows], product[rows:])

    return stack, pick


def diagonal_blocks():
    rows = lax.broadcasted_iota(jnp.int32, (PAIR, PAIR), 0) // P_SIZE
    columns = lax.broadcasted_iota(jnp.int32, (PAIR, PAIR), 1) // P_SIZE
    return (rows == columns).astype(jnp.float32)


def solve(matrix, rate_row, value, pick):
    rows = value.shape[0]
    powers = [(matrix, rate_row)]
    reach = 2
    while reach < CHUNK // MB:
        last, rate = powers[-1]
        low, high = halves_of(last[:rows]), halves_of(last[rows:])
        powers.append(
            (
                jnp.concatenate([wide(dot_ab, low, low), wide(dot_ab, high, high)], 0),
                rate * rate,
            )
        )
        reach = 2 * reach
    for index in range(len(powers) - 1, -1, -1):
        factor, rate = powers[index]
        moved = pick(wide(dot_ab, halves_of(factor), halves_of(value * rate)))
        value = value - moved if index == 0 else value + moved
    return value


def mixer_forward_chunk(
    qkv_ref,
    rate_ref,
    initial_ref,
    causal_ref,
    earlier_ref,
    first_ref,
    last_ref,
    anew_ref,
    z_ref,
    residue_ref,
    states_ref,
    state,
):
    pairs = initial_ref.shape[0]
    width = pairs * PAIR

    stack, pick = lane_helpers(CHUNK)
    blocks = diagonal_blocks()
    causal = causal_ref[0]
    causal = jnp.concatenate([causal, causal], 0)
    earlier = earlier_ref[0]
    earlier = jnp.concatenate([earlier, earlier], 0)
    first = first_ref[...] > 0.0
    last = last_ref[...]
    anew = anew_ref[0, 0:1, :]
    for pair in range(pairs):
        lanes = slice(pair * PAIR, (pair + 1) * PAIR)
        query = qkv_ref[:, lanes]
        key = qkv_ref[:, width + pair * PAIR : width + (pair + 1) * PAIR]
        value = qkv_ref[:, 2 * width + pair * PAIR : 2 * width + (pair + 1) * PAIR]
        rate = rate_ref[0:1, lanes]
        begin = state[pair]
        initial = initial_ref[pair]
        states_ref[0, pair] = begin
        products = dot_abt(jnp.concatenate([stack(key), stack(query)], 0), key)
        ties = products[: 2 * CHUNK] * earlier
        scores = products[2 * CHUNK :] * causal
        both = jnp.concatenate([key, query], 0)
        seen = wide(dot_ab, both, halves_of(begin))
        fresh = wide(dot_ab, both, halves_of(initial))
        key_seen = jnp.where(first, seen[:CHUNK], fresh[:CHUNK])
        query_seen = jnp.where(first, seen[CHUNK:], fresh[CHUNK:])
        key_wide = key.astype(jnp.float32)
        residue = solve(ties, rate, key_seen - (value.astype(jnp.float32) - key_wide), pick)
        residue_ref[:, lanes] = residue
        scaled = residue * rate
        scaled_parts = halves_of(scaled)
        output = query_seen - pick(wide(dot_ab, halves_of(scores), scaled_parts))
        z_ref[:, lanes] = output.astype(jnp.bfloat16)
        key_last = (key_wide * last).astype(jnp.bfloat16)
        base = jnp.where(anew > 0.0, initial, begin)
        state[pair] = base - blocks * wide(dot_atb, key_last, scaled_parts)


def mixer_backward_chunk(
    qkv_ref,
    rate_ref,
    initial_ref,
    causal_ref,
    earlier_ref,
    causal_turned_ref,
    earlier_turned_ref,
    first_ref,
    last_ref,
    anew_ref,
    residue_ref,
    states_ref,
    upstream_ref,
    grad_ref,
    grad_initial_ref,
    grad_rate_ref,
    carried,
):
    pairs = initial_ref.shape[0]
    width = pairs * PAIR

    stack, pick = lane_helpers(CHUNK)
    blocks = diagonal_blocks()

    def doubled(ref):
        return jnp.concatenate([ref[0], ref[0]], 0)

    causal, earlier = doubled(causal_ref), doubled(earlier_ref)
    causal_turned, earlier_turned = doubled(causal_turned_ref), doubled(earlier_turned_ref)
    first_wide = first_ref[...]
    first = first_wide > 0.0
    last = last_ref[...]
    anew = anew_ref[0, 0:1, :]
    low = jnp.bfloat16
    for pair in range(pairs):
        lanes = slice(pair * PAIR, (pair + 1) * PAIR)
        query = qkv_ref[:, lanes]
        key = qkv_ref[:, width + pair * PAIR : width + (pair + 1) * PAIR]
        rate = rate_ref[0:1, lanes]
        begin = halves_of(states_ref[0, pair])
        initial = halves_of(initial_ref[pair])
        after = carried[pair]
        after_parts = halves_of(after)
        residue = residue_ref[:, lanes]
        scaled = halves_of(residue * rate)
        upstream = upstream_ref[:, lanes]
        upstream_parts = halves_of(upstream)
        key_wide = key.astype(jnp.float32)
        query_wide = query.astype(jnp.float32)
        key_last = (key_wide * last).astype(low)
        key_stack = stack(key)
        products = dot_abt(key_stack, jnp.concatenate([key, query], 0))
        ties_turned = products[:, :CHUNK] * earlier_turned
        scores_turned = products[:, CHUNK:] * causal_turned
        pulled = pick(wide(dot_ab, halves_of(scores_turned), upstream_parts))
        pulled = pulled + wide(dot_ab, key_last, after_parts)
        grad_scaled = solve(ties_turned, rate, -pulled, pick)
        grad_rate_ref[0:1, lanes] += jnp.sum(grad_scaled * residue, 0, keepdims=True)
        grad_residue = grad_scaled * rate
        residue_parts = halves_of(grad_residue)
        joined = tuple(
            jnp.concatenate([one, two], 0) for one, two in zip(upstream_parts, residue_parts)
        )
        turned = dot_abt(stack(scaled[0]), joined[0])
        straight = dot_abt(
            jnp.concatenate([stack(upstream_parts[0]), stack(residue_parts[0])], 0), scaled[0]
        )
        grad_scores = -straight[: 2 * CHUNK] * causal
        grad_scores_turned = -turned[:, :CHUNK] * causal_turned
        grad_ties = -(straight[2 * CHUNK :] * earlier + turned[:, CHUNK:] * earlier_turned)
        seen = dot_abt(joined[0], begin[0])
        fresh = dot_abt(joined[0], initial[0])
        grad_query = jnp.where(first, seen[:CHUNK], fresh[:CHUNK])
        grad_query = grad_query + pick(dot_ab(grad_scores.astype(low), key))
        grad_key = jnp.where(first, seen[CHUNK:], fresh[CHUNK:]) + grad_residue
        grad_key = grad_key + pick(
            dot_ab(grad_scores_turned.astype(low), query) + dot_ab(grad_ties.astype(low), key)
        )
        grad_key = grad_key - last * dot_abt(scaled[0], after_parts[0])
        grad_ref[:, lanes] = grad_query.astype(low)
        grad_ref[:, width + pair * PAIR : width + (pair + 1) * PAIR] = grad_key.astype(low)
        grad_ref[:, 2 * width + pair * PAIR : 2 * width + (pair + 1) * PAIR] = (
            -grad_residue
        ).astype(low)
        fronts = jnp.concatenate([query_wide * first_wide, key_wide * first_wide], 0).astype(low)
        backs = jnp.concatenate(
            [query_wide * (1.0 - first_wide), key_wide * (1.0 - first_wide)], 0
        ).astype(low)
        kept_after = jnp.where(anew > 0.0, 0.0, after)
        carried[pair] = kept_after + blocks * wide(dot_atb, fronts, joined)
        grad_initial_ref[pair] += (after - kept_after) + blocks * wide(dot_atb, backs, joined)


def pair_blocks(matrices):
    heads = matrices.shape[0]
    split = matrices.reshape(heads // 2, 2, P_SIZE, P_SIZE)
    empty = jnp.zeros_like(split[:, 0])
    upper = jnp.concatenate([split[:, 0], empty], 2)
    lower = jnp.concatenate([empty, split[:, 1]], 2)
    return jnp.concatenate([upper, lower], 1)


def head_blocks(pairs):
    return jnp.stack([pairs[:, :P_SIZE, :P_SIZE], pairs[:, P_SIZE:, P_SIZE:]], 1).reshape(
        -1, P_SIZE, P_SIZE
    )


ROWS = 64
LAG = 2
MESH = pl.DeviceIdType.MESH


def across(column):
    return jnp.swapaxes(jnp.broadcast_to(column, (column.shape[0], 128)), 0, 1)[:8]


def down(row, width):
    turned = jnp.swapaxes(jnp.broadcast_to(row[:1], (128, row.shape[1])), 0, 1)
    return jnp.concatenate([turned] * (width // 128), 1) if width > 128 else turned


def transit_kernel(mode, form, lag, parts, slabs, names, *all_refs):
    ref = dict(zip(names, all_refs))
    full_ref, partial, total = ref["full"], ref["partial"], ref["total"]
    pair_out, pair_in = ref["pair_out"], ref["pair_in"]
    from_low, from_high = ref["from_low"], ref["from_high"]
    places = parts // 2
    cross = form in ("lookup", "table")
    summing = mode != "plain"
    lefts = sum(name.startswith("left_buf") for name in names)
    size = total.shape[1]
    ring, band = partial.shape[0], partial.shape[1]
    me = lax.axis_index("head")
    mine_dp = lax.axis_index("dp")
    core = lax.rem(me, 2)
    spot = me // 2
    twin = {"head": me + 1 - 2 * core}
    upper = {"head": lax.rem(me + 2, parts)}
    lower = {"head": lax.rem(me + parts - 2, parts)}
    chunks = ref["up_in_sem"].shape[0]
    sum_at = 1 + lag * (places - 1)
    finish_at = sum_at + (lag if summing else 0)
    reach_at = finish_at + lag * (places - 1)
    close_at = reach_at + (lag + 1 if cross else 1)

    def place_of(chunk):
        return chunks - 1 - chunk if form == "inner" else chunk

    def band_of(index):
        return pl.ds(pl.multiple_of(index * band, band), band)

    def rows_of(chunk):
        return band_of(place_of(chunk))

    def shard(index):
        return pl.ds(pl.multiple_of(index * size, 128), size)

    def remote(source, target, out_sem, in_sem, device):
        return pltpu.make_async_remote_copy(
            src_ref=source,
            dst_ref=target,
            send_sem=out_sem,
            recv_sem=in_sem,
            device_id=device,
            device_id_type=MESH,
        )

    def left_copies(chunk):
        half = lax.rem(chunk, 2)
        return [
            pltpu.make_async_copy(
                ref["left%d" % part].at[rows_of(chunk)],
                ref["left_buf%d" % part].at[half],
                ref["left_sem%d" % part].at[half],
            )
            for part in range(lefts)
        ]

    barrier = pltpu.get_barrier_semaphore()
    for offset in range(1, parts):
        pl.semaphore_signal(
            barrier, inc=1, device_id={"head": lax.rem(me + offset, parts)}, device_id_type=MESH
        )
    if cross:
        for offset in range(1, slabs):
            pl.semaphore_signal(
                barrier,
                inc=1,
                device_id={"dp": lax.rem(mine_dp + offset, slabs)},
                device_id_type=MESH,
            )
    for copy in left_copies(0):
        copy.start()
    if mode in ("grad", "grad_add"):
        ref["gain_grad"][...] = jnp.zeros_like(ref["gain_grad"])
    if form == "table":
        ref["table_grad"][...] = jnp.zeros_like(ref["table_grad"])
    pl.semaphore_wait(barrier, parts - 1 + (slabs - 1 if cross else 0))

    def valid(chunk):
        return jnp.logical_and(chunk >= 0, chunk < chunks)

    def pair_copy(chunk):
        slot = lax.rem(chunk, ring)
        return remote(
            pair_out.at[slot],
            pair_in.at[slot],
            ref["pair_out_sem"].at[slot],
            ref["pair_in_sem"].at[slot],
            twin,
        )

    def rise(chunk, place):
        slot = lax.rem(chunk, ring)
        part = from_low.at[slot, pl.ds(place + 1, places - 1 - place)]
        return remote(part, part, ref["low_out_sem"].at[slot], ref["low_in_sem"].at[slot], upper)

    def fall(chunk, place):
        slot = lax.rem(chunk, ring)
        part = from_high.at[slot, pl.ds(0, place)]
        return remote(part, part, ref["high_out_sem"].at[slot], ref["high_in_sem"].at[slot], lower)

    def sums_copy(chunk, offset):
        slot = lax.rem(chunk, ring)
        return remote(
            ref["sums_out"].at[slot],
            ref["sums_in"].at[slot, offset - 1],
            ref["sums_out_sem"].at[slot],
            ref["sums_in_sem"].at[slot],
            {"head": lax.rem(me + offset, parts)},
        )

    def piece(chunk, source):
        if cross:
            return ref["stage"].at[source, rows_of(chunk)]
        return ref["shards"].at[2 * source + core, rows_of(chunk)]

    def climb(chunk, source, hop):
        part = piece(chunk, source)
        return remote(
            part,
            part,
            ref["up_out_sem"].at[chunk, hop - 1],
            ref["up_in_sem"].at[chunk, hop - 1],
            upper,
        )

    def sink(chunk, source, hop):
        part = piece(chunk, source)
        return remote(
            part,
            part,
            ref["down_out_sem"].at[chunk, hop - 1],
            ref["down_in_sem"].at[chunk, hop - 1],
            lower,
        )

    def target(chunk, giver):
        if form == "lookup":
            return ref["shards"].at[2 * giver + core, rows_of(chunk)]
        return full_ref.at[chunk // 2, band_of(lax.rem(chunk, 2) * slabs + giver), shard(core)]

    def mirror(chunk, index):
        part = target(chunk, index) if cross else piece(chunk, index)
        return remote(
            part, part, ref["twin_out_sem"].at[chunk], ref["twin_in_sem"].at[chunk], twin
        )

    def hand_over(chunk, source):
        return remote(
            piece(chunk, source),
            target(chunk, mine_dp),
            ref["cross_out_sem"].at[chunk, source],
            ref["cross_in_sem"].at[chunk, mine_dp],
            {"dp": source},
        )

    def have(chunk, source):
        if not cross:
            mirror(chunk, source).start()
            return

        @pl.when(source != mine_dp)
        def _():
            hand_over(chunk, source).start()

        @pl.when(source == mine_dp)
        def _():
            values = ref["stage"][source, rows_of(chunk), :]
            if form == "lookup":
                ref["shards"][2 * mine_dp + core, rows_of(chunk), :] = values
            else:
                place_rows = band_of(lax.rem(chunk, 2) * slabs + mine_dp)
                full_ref[chunk // 2, place_rows, shard(core)] = values
            mirror(chunk, mine_dp).start()

    def receive(step):
        for hop in range(places):
            chunk = step - finish_at - lag * (hop + 1)

            @pl.when(jnp.logical_and(valid(chunk), jnp.abs(spot - mine_dp) == hop))
            def _():
                for offset in range(1, slabs):
                    giver = lax.rem(mine_dp + offset, slabs)
                    part = target(chunk, giver)
                    remote(
                        part,
                        part,
                        ref["cross_out_sem"].at[chunk, giver],
                        ref["cross_in_sem"].at[chunk, giver],
                        twin,
                    ).wait_recv()
                    mirror(chunk, giver).start()

    def relay(step):
        for hop in range(1, places):
            chunk = step - finish_at - lag * hop
            source = spot - hop

            @pl.when(jnp.logical_and(valid(chunk), source >= 0))
            def _():
                climb(chunk, source, hop).wait_recv()
                if hop < places - 1:

                    @pl.when(spot < places - 1)
                    def _():
                        climb(chunk, source, hop + 1).start()

                have(chunk, source)

            source_high = spot + hop

            @pl.when(jnp.logical_and(valid(chunk), source_high < places))
            def _():
                sink(chunk, source_high, hop).wait_recv()
                if hop < places - 1:

                    @pl.when(spot > 0)
                    def _():
                        sink(chunk, source_high, hop + 1).start()

                have(chunk, source_high)

    def finish_shard(step):
        chunk = step - finish_at

        @pl.when(valid(chunk))
        def _():
            slot = lax.rem(chunk, ring)
            rows = rows_of(chunk)
            if summing:
                sums_in = ref["sums_in"]
                pltpu.make_async_copy(
                    sums_in.at[slot], sums_in.at[slot], ref["sums_in_sem"].at[slot]
                ).wait()
                summed = ref["sums_out"][slot]
                for offset in range(1, parts):
                    summed = summed + sums_in[slot, offset - 1]
                gain = ref["gain"][0:1, :]
            if mode == "plain":
                result = total[...]
            elif mode == "norm":
                scale = lax.rsqrt(summed / D + EPSILON)
                ref["scale"][chunk] = scale
                result = ref["own"][rows, :] * down(scale, size) * gain
            else:
                scale = down(ref["scale"][place_of(chunk)], size)
                normed = ref["inputs"][rows, :] * scale
                inner = down(summed / D, size)
                result = scale * (ref["own"][rows, :] * gain - normed * inner)
                if mode == "grad_add":
                    result = result + ref["added"][rows, :]
                if form != "table":
                    ref["own"][rows, :] = result
            if cross:
                ref["stage"][spot, rows, :] = result.astype(jnp.bfloat16)
            else:
                ref["shards"][me, rows, :] = result.astype(jnp.bfloat16)

            @pl.when(spot < places - 1)
            def _():
                climb(chunk, spot, 1).start()

            @pl.when(spot > 0)
            def _():
                sink(chunk, spot, 1).start()

            have(chunk, spot)

    def add_pair(step):
        chunk = step - 1

        @pl.when(valid(chunk))
        def _():
            slot = lax.rem(chunk, ring)
            pair_copy(chunk).wait_recv()
            partial[slot] = partial[slot] + pair_in[slot].astype(jnp.float32)

    def pass_on(step):
        for place in range(places):
            if place < places - 1:
                up_chunk = step - 1 - lag * place

                @pl.when(jnp.logical_and(valid(up_chunk), spot == place))
                def _():
                    slot = lax.rem(up_chunk, ring)
                    if place > 0:
                        rise(up_chunk, place - 1).wait_recv()
                    for above in range(place + 1, places):
                        values = partial[slot, :, pl.ds(above * size, size)]
                        if place > 0:
                            values = values + from_low[slot, above].astype(jnp.float32)
                        from_low[slot, above] = values.astype(jnp.bfloat16)
                    rise(up_chunk, place).start()

            if place > 0:
                down_chunk = step - 1 - lag * (places - 1 - place)

                @pl.when(jnp.logical_and(valid(down_chunk), spot == place))
                def _():
                    slot = lax.rem(down_chunk, ring)
                    if place < places - 1:
                        fall(down_chunk, place + 1).wait_recv()
                    for below in range(place):
                        values = partial[slot, :, pl.ds(below * size, size)]
                        if place < places - 1:
                            values = values + from_high[slot, below].astype(jnp.float32)
                        from_high[slot, below] = values.astype(jnp.bfloat16)
                    fall(down_chunk, place).start()

    def settle(step):
        chunk = step - sum_at - lag

        @pl.when(valid(chunk))
        def _():
            pair_copy(chunk).wait_send()
            for place in range(places):

                @pl.when(spot == place)
                def _():
                    if place < places - 1:
                        rise(chunk, place).wait_send()
                    if place > 0:
                        fall(chunk, place).wait_send()

            if summing:
                slot = lax.rem(chunk, ring)
                sums_in = ref["sums_in"]
                pltpu.make_async_copy(
                    sums_in.at[slot], sums_in.at[slot], ref["sums_out_sem"].at[slot]
                ).wait()

    def sum_shard(step):
        chunk = step - sum_at

        @pl.when(valid(chunk))
        def _():
            slot = lax.rem(chunk, ring)
            rows = rows_of(chunk)
            mine = shard(spot)

            @pl.when(spot == places - 1)
            def _():
                rise(chunk, places - 2).wait_recv()

            @pl.when(spot == 0)
            def _():
                fall(chunk, 1).wait_recv()

            total[...] = partial[slot, :, mine]

            @pl.when(spot > 0)
            def _():
                total[...] += from_low[slot, spot].astype(jnp.float32)

            @pl.when(spot < places - 1)
            def _():
                total[...] += from_high[slot, spot].astype(jnp.float32)

            if not summing:
                return
            value = total[...]
            if mode == "norm":
                value = value + ref["inputs"][rows, :]
                column = jnp.sum(value * value, 1, keepdims=True)
            else:
                scale = down(ref["scale"][place_of(chunk)], size)
                normed = ref["inputs"][rows, :] * scale
                ref["gain_grad"][0:1, :] += jnp.sum(value * normed, 0, keepdims=True)
                column = jnp.sum(value * ref["gain"][0:1, :] * normed, 1, keepdims=True)
            ref["own"][rows, :] = value
            ref["sums_out"][slot] = across(column)
            for offset in range(1, parts):
                sums_copy(chunk, offset).start()

    def produce(step):
        chunk = step

        @pl.when(valid(chunk))
        def _():
            slot = lax.rem(chunk, ring)
            right_ref = ref["right0"]
            if form == "lookup":
                entries = right_ref.shape[0]
                ids = jnp.concatenate(
                    [ref["ids"][group, rows_of(chunk), 0:1] for group in range(slabs)], 0
                )
                spots = lax.broadcasted_iota(jnp.int32, (slabs * band, entries), 1)
                hits = (spots == ids).astype(jnp.bfloat16)
                other = dot_ab(hits, right_ref[:, shard(1 - core)]).astype(jnp.bfloat16)
                for group in range(slabs):
                    pair_out[slot, :, pl.ds(group * size, size)] = other[
                        group * band : (group + 1) * band
                    ]
                pair_copy(chunk).start()
                here = dot_ab(hits, right_ref[:, shard(core)])
                for group in range(slabs):
                    partial[slot, :, pl.ds(group * size, size)] = here[
                        group * band : (group + 1) * band
                    ]
                return
            half = lax.rem(chunk, 2)
            if form == "mixer":
                one = pl.ds(chunk, 1)
                here = rows_of(chunk)

                @pl.when(chunk == 0)
                def _():
                    ref["state"][...] = jnp.zeros_like(ref["state"])

                mixer_forward_chunk(
                    ref["qkv"].at[here],
                    ref["rate"],
                    ref["initial"],
                    ref["causal"].at[one],
                    ref["earlier"].at[one],
                    ref["first"].at[here],
                    ref["last"].at[here],
                    ref["anew"].at[one],
                    ref["z"].at[here],
                    ref["residue"].at[here],
                    ref["states"].at[one],
                    ref["state"],
                )
            else:
                for copy in left_copies(chunk):
                    copy.wait()

                @pl.when(chunk + 1 < chunks)
                def _():
                    for copy in left_copies(chunk + 1):
                        copy.start()

            def term(index):
                if form == "mixer":
                    return dot_ab(ref["z"][rows_of(chunk), :], right_ref[:, shard(index)])
                if form == "table":
                    return dot_abt(ref["left_buf0"][half], right_ref[shard(index), :])
                terms = [
                    dot_ab(ref["left_buf%d" % part][half], ref["right%d" % part][:, shard(index)])
                    for part in range(lefts)
                ]
                return sum(terms[1:], terms[0])

            for place in range(places):
                lanes = pl.ds(place * size, size)
                pair_out[slot, :, lanes] = term(2 * place + 1 - core).astype(jnp.bfloat16)
            pair_copy(chunk).start()
            for place in range(places):
                lanes = pl.ds(place * size, size)
                partial[slot, :, lanes] = term(2 * place + core)

    def close(step):
        chunk = step - close_at

        @pl.when(valid(chunk))
        def _():
            if form == "table":
                arrived = full_ref.at[chunk // 2, pl.ds(0, slabs * band), pl.ds(0, size)]
            else:
                arrived = ref["shards"].at[pl.ds(0, places), rows_of(chunk)]
            pltpu.make_async_copy(arrived, arrived, ref["twin_in_sem"].at[chunk]).wait()
            pltpu.make_async_copy(arrived, arrived, ref["twin_out_sem"].at[chunk]).wait()
            if cross:
                for offset in range(1, slabs):
                    hand_over(chunk, lax.rem(mine_dp + offset, slabs)).wait_send()
            for hop in range(1, places):
                source = spot - hop + 1

                @pl.when(jnp.logical_and(source >= 0, spot < places - 1))
                def _():
                    climb(chunk, source, hop).wait_send()

                source_high = spot + hop - 1

                @pl.when(jnp.logical_and(source_high < places, spot > 0))
                def _():
                    sink(chunk, source_high, hop).wait_send()

            if form != "table":
                for index in range(parts):
                    full_ref[rows_of(chunk), pl.ds(index * size, size)] = ref["shards"][
                        index, rows_of(chunk), :
                    ]
            if form == "lookup":
                rows = rows_of(chunk)
                ref["own"][rows, :] = full_ref[rows, shard(me)].astype(jnp.float32)
                values = full_ref[rows, :].astype(jnp.float32)
                scale = lax.rsqrt(jnp.sum(values * values, 1, keepdims=True) / D + EPSILON)
                ref["scale"][chunk] = across(scale)
                normed = (values * scale * ref["gain"][0:1, :]).astype(jnp.bfloat16)
                full_ref[rows, :] = normed
            if form == "inner":
                rows, one = rows_of(chunk), pl.ds(place_of(chunk), 1)

                @pl.when(chunk == 0)
                def _():
                    for name in ("state", "grad_initial", "grad_rate"):
                        ref[name][...] = jnp.zeros_like(ref[name])

                ref["upstream"][...] = dot_abt(full_ref[rows, :], ref["project"][...])
                mixer_backward_chunk(
                    ref["qkv"].at[rows],
                    ref["rate"],
                    ref["initial"],
                    ref["causal"].at[one],
                    ref["earlier"].at[one],
                    ref["causal_turned"].at[one],
                    ref["earlier_turned"].at[one],
                    ref["first"].at[rows],
                    ref["last"].at[rows],
                    ref["anew"].at[one],
                    ref["residue"].at[rows],
                    ref["states"].at[one],
                    ref["upstream"],
                    ref["grad_mixed"].at[rows],
                    ref["grad_initial"],
                    ref["grad_rate"],
                    ref["state"],
                )
            if form == "table":
                @pl.when(lax.rem(chunk, 2) == 1)
                def _():
                    table_grad = ref["table_grad"]
                    entries = table_grad.shape[0]
                    pieces = 5 if entries % 80 == 0 else 1
                    block = entries // pieces
                    ids = ref["ids"][chunk // 2, 0:1, :]
                    values = full_ref[chunk // 2]
                    for index in range(pieces):
                        spots = index * block + lax.broadcasted_iota(
                            jnp.int32, (block, ids.shape[1]), 0
                        )
                        hits = (spots == ids).astype(jnp.bfloat16)
                        span = pl.ds(index * block, block)
                        table_grad[span, :] += dot_ab(hits, values)

    def advance(step, carried):
        relay(step)
        if summing:
            finish_shard(step)
        if cross:
            receive(step)
        add_pair(step)
        pass_on(step)
        settle(step)
        sum_shard(step)
        if not summing:
            finish_shard(step)
        produce(step)
        close(step)
        return carried

    lax.fori_loop(0, chunks + close_at, advance, 0)


def transit(
    mode,
    form,
    number,
    parts,
    slabs,
    right,
    tokens,
    size,
    left=None,
    inputs=None,
    gain=None,
    scale=None,
    added=None,
    ids=None,
    entries=None,
    mixer=None,
    project=None,
    band=ROWS,
    lag=LAG,
):
    chunks = tokens // band
    places = parts // 2
    cross = form in ("lookup", "table")
    summing = mode != "plain"
    ring = min(chunks, lag * (places + 1) + 2) if summing else chunks
    dma = pltpu.SemaphoreType.DMA
    low, wide_kind = jnp.bfloat16, jnp.float32
    vmem = pl.BlockSpec(memory_space=pltpu.VMEM)
    operands, specs, outputs, scratch = {}, [], {}, {}

    def take(name, array, spec=vmem):
        operands[name] = array
        specs.append(spec)

    rights = right if isinstance(right, tuple) else (right,)
    lefts = left if isinstance(left, tuple) else () if left is None else (left,)
    for part, array in enumerate(rights):
        take("right%d" % part, array)
    for part, array in enumerate(lefts):
        take("left%d" % part, array, pl.BlockSpec(memory_space=pl.ANY))
    if project is not None:
        take("project", project)
    if ids is not None:
        take("ids", ids)
    if mixer is not None:
        for name, array in mixer.items():
            take(name, array)
        pairs, width = mixer["initial"].shape[0], mixer["rate"].shape[1]
    if summing:
        take("inputs", inputs)
    take("gain", gain)
    if mode in ("grad", "grad_add"):
        take("scale", scale)
    if mode == "grad_add":
        take("added", added)

    if form != "table":
        outputs["own"] = ((tokens, size), wide_kind)
    if form != "table":
        outputs["full"] = ((tokens, parts * size), low)
    if mode in ("norm", "plain"):
        outputs["scale"] = ((chunks, 8, band), wide_kind)
    if mode in ("grad", "grad_add"):
        outputs["gain_grad"] = ((8, size), wide_kind)
    if form == "table":
        outputs["table_grad"] = ((entries, 2 * size), wide_kind)

    if form == "inner":
        outputs["grad_mixed"] = ((tokens, 3 * width), low)
        outputs["grad_initial"] = ((pairs, PAIR, PAIR), wide_kind)
        outputs["grad_rate"] = ((1, width), wide_kind)
        scratch["state"] = pltpu.VMEM((pairs, PAIR, PAIR), wide_kind)
        scratch["upstream"] = pltpu.VMEM((band, width), wide_kind)
    if form == "mixer":
        outputs["z"] = ((tokens, width), low)
        outputs["residue"] = ((tokens, width), wide_kind)
        outputs["states"] = ((chunks, pairs, PAIR, PAIR), wide_kind)
        scratch["state"] = pltpu.VMEM((pairs, PAIR, PAIR), wide_kind)
    span = places * size
    hops = max(places - 1, 1)
    if form == "table":
        scratch["own"] = pltpu.VMEM((tokens, size), wide_kind)
        scratch["full"] = pltpu.VMEM((chunks // 2, 2 * slabs * band, 2 * size), low)
    for part, array in enumerate(lefts):
        scratch["left_buf%d" % part] = pltpu.VMEM((2, band, array.shape[1]), low)
        scratch["left_sem%d" % part] = dma((2,))
    if form != "table":
        scratch["shards"] = pltpu.VMEM((parts, tokens, size), low)
    if cross:
        scratch["stage"] = pltpu.VMEM((places, tokens, size), low)
        scratch["cross_out_sem"] = dma((chunks, slabs))
        scratch["cross_in_sem"] = dma((chunks, slabs))
    if summing:
        scratch["sums_out"] = pltpu.VMEM((ring, 8, band), wide_kind)
        scratch["sums_in"] = pltpu.VMEM((ring, parts - 1, 8, band), wide_kind)
        scratch["sums_out_sem"] = dma((ring,))
        scratch["sums_in_sem"] = dma((ring,))
    scratch["total"] = pltpu.VMEM((band, size), wide_kind)
    scratch["partial"] = pltpu.VMEM((ring, band, span), wide_kind)
    for name in ("pair_out", "pair_in"):
        scratch[name] = pltpu.VMEM((ring, band, span), low)
    for name in ("from_low", "from_high"):
        scratch[name] = pltpu.VMEM((ring, places, band, size), low)
    for name in ("pair_out", "pair_in", "low_out", "low_in", "high_out", "high_in"):
        scratch[name + "_sem"] = dma((ring,))
    for name in ("up_out", "up_in", "down_out", "down_in"):
        scratch[name + "_sem"] = dma((chunks, hops))
    scratch["twin_out_sem"] = dma((chunks,))
    scratch["twin_in_sem"] = dma((chunks,))

    depth = sum(array.size for array in rights) // (parts * size)
    names = tuple(operands) + tuple(outputs) + tuple(scratch)
    results = pl.pallas_call(
        functools.partial(transit_kernel, mode, form, lag, parts, slabs, names),
        in_specs=specs,
        out_specs=[vmem] * len(outputs),
        out_shape=[jax.ShapeDtypeStruct(shape, kind) for shape, kind in outputs.values()],
        scratch_shapes=list(scratch.values()),
        compiler_params=pltpu.CompilerParams(
            collective_id=number, has_side_effects=True, vmem_limit_bytes=60 * 1024 * 1024
        ),
        cost_estimate=pl.CostEstimate(
            flops=2 * tokens * depth * parts * size,
            bytes_accessed=128 * tokens * parts * size,
            transcendentals=0,
        ),
        name="transit_" + form,
    )(*operands.values())
    return dict(zip(outputs, results))


def share_kernel(axes, block_ref, all_ref, out_sem, in_sem):
    counts = [lax.axis_size(axis) for axis in axes]
    places = [lax.axis_index(axis) for axis in axes]
    members = 1
    me = 0
    for count, place in zip(counts, places):
        members = members * count
        me = me * count + place

    def partner(offset):
        device, rest = {}, offset
        for axis, count, place in reversed(list(zip(axes, counts, places))):
            device[axis] = lax.rem(place + lax.rem(rest, count), count)
            rest = rest // count
        return device

    def send(offset):
        return pltpu.make_async_remote_copy(
            src_ref=block_ref,
            dst_ref=all_ref.at[me],
            send_sem=out_sem,
            recv_sem=in_sem,
            device_id=partner(offset),
            device_id_type=MESH,
        )

    barrier = pltpu.get_barrier_semaphore()

    def greet(offset, carried):
        pl.semaphore_signal(barrier, inc=1, device_id=partner(offset), device_id_type=MESH)
        return carried

    def start(offset, carried):
        send(offset).start()
        return carried

    lax.fori_loop(1, members, greet, 0)
    all_ref[me] = block_ref[...]
    pl.semaphore_wait(barrier, members - 1)
    lax.fori_loop(1, members, start, 0)
    arrived = all_ref.at[pl.ds(0, members - 1)]
    pltpu.make_async_copy(arrived, arrived, in_sem).wait()
    pltpu.make_async_copy(arrived, arrived, out_sem).wait()


def share(number, block, axes):
    members = 1
    for axis in axes:
        members = members * lax.axis_size(axis)
    vmem = pl.BlockSpec(memory_space=pltpu.VMEM)
    return pl.pallas_call(
        functools.partial(share_kernel, axes),
        in_specs=[vmem],
        out_specs=vmem,
        out_shape=jax.ShapeDtypeStruct((members,) + block.shape, block.dtype),
        scratch_shapes=[pltpu.SemaphoreType.DMA, pltpu.SemaphoreType.DMA],
        compiler_params=pltpu.CompilerParams(
            collective_id=number, has_side_effects=True, vmem_limit_bytes=16 * 1024 * 1024
        ),
        cost_estimate=pl.CostEstimate(
            flops=0, bytes_accessed=16 * 1024 * 1024, transcendentals=0
        ),
        name="share",
    )(block)


SCORE_ROWS = 256


def scores_kernel(rows_ref, table_ref, goal_ref, logits_ref, stats_ref):
    entries = table_ref.shape[0]
    edges = list(range(0, entries, 512)) + [entries]
    goal = goal_ref[:, 0:1]
    picked = jnp.zeros((SCORE_ROWS, 1), jnp.float32)
    peaks, sums = [], []
    for low, high in zip(edges, edges[1:]):
        values = dot_abt(rows_ref[...], table_ref[low:high, :])
        logits_ref[:, low:high] = values
        peaks.append(jnp.max(values, 1, keepdims=True))
        sums.append(jnp.sum(jnp.exp(values - peaks[-1]), 1, keepdims=True))
        spots = low + lax.broadcasted_iota(jnp.int32, values.shape, 1)
        picked = picked + jnp.sum(jnp.where(spots == goal, values, 0.0), 1, keepdims=True)
    peak = functools.reduce(jnp.maximum, peaks)
    exp_sum = sum(part * jnp.exp(top - peak) for part, top in zip(sums, peaks))
    stats_ref[0] = jnp.broadcast_to(peak, (SCORE_ROWS, 128))
    stats_ref[1] = jnp.broadcast_to(exp_sum, (SCORE_ROWS, 128))
    stats_ref[2] = jnp.broadcast_to(picked, (SCORE_ROWS, 128))


def scores(rows, table, goals):
    tokens, width = rows.shape
    entries = table.shape[0]
    return pl.pallas_call(
        scores_kernel,
        grid=(tokens // SCORE_ROWS,),
        in_specs=[
            pl.BlockSpec((SCORE_ROWS, width), lambda i: (i, 0)),
            pl.BlockSpec(memory_space=pltpu.VMEM),
            pl.BlockSpec((SCORE_ROWS, 128), lambda i: (i, 0)),
        ],
        out_specs=[
            pl.BlockSpec((SCORE_ROWS, entries), lambda i: (i, 0)),
            pl.BlockSpec((3, SCORE_ROWS, 128), lambda i: (0, i, 0)),
        ],
        out_shape=[
            jax.ShapeDtypeStruct((tokens, entries), jnp.float32),
            jax.ShapeDtypeStruct((3, tokens, 128), jnp.float32),
        ],
        compiler_params=pltpu.CompilerParams(
            dimension_semantics=("arbitrary",), vmem_limit_bytes=56 * 1024 * 1024
        ),
        cost_estimate=pl.CostEstimate(
            flops=2 * tokens * entries * width,
            bytes_accessed=2 * entries * width + 4 * tokens * entries,
            transcendentals=tokens * entries,
        ),
        name="scores",
    )(rows, table, goals)


def shampoo(tile_w, tile_g, left, right, left_root, right_root):
    low_g = tile_g.astype(jnp.bfloat16)

    def product(form, one, two):
        return jnp.einsum(
            form,
            one.astype(jnp.bfloat16),
            two.astype(jnp.bfloat16),
            preferred_element_type=jnp.float32,
        )

    new_left = STAT_DECAY * left + (1.0 - STAT_DECAY) * product("abrc,absc->abrs", low_g, low_g)
    new_right = STAT_DECAY * right + (1.0 - STAT_DECAY) * product("abrc,abrd->abcd", low_g, low_g)
    turned = product("abrs,absc->abrc", left_root, low_g)
    turned = product("abrc,abcd->abrd", turned, right_root)
    return (new_left, new_right, tile_w - MATRIX_RATE * (turned + WEIGHT_DECAY * tile_w))


def refresh(master, grad, left, right, left_root, right_root):
    rows = master.shape[1]
    new_left, new_right, new_w = shampoo(
        master.reshape(1, 1, rows, -1),
        grad.reshape(1, 1, rows, -1),
        left,
        right,
        left_root,
        right_root,
    )
    return (grad.reshape(master.shape), new_left, new_right, new_w.reshape(master.shape))


def refresh_rows(master, grad, left, right, left_root, right_root):
    _, rows, kinds, _ = master.shape
    low_g = grad.astype(jnp.bfloat16)

    def product(form, one, two):
        return jnp.einsum(
            form,
            one.astype(jnp.bfloat16),
            two.astype(jnp.bfloat16),
            preferred_element_type=jnp.float32,
        )

    def shaped(array):
        return jnp.transpose(array.reshape(kinds, -1, rows), (2, 0, 1))[None]

    master_rows = jnp.transpose(master[0], (1, 2, 0)).reshape(-1, rows)
    new_left = STAT_DECAY * left + (1.0 - STAT_DECAY) * product("cr,cs->rs", low_g, low_g)
    new_right = STAT_DECAY * right + (1.0 - STAT_DECAY) * product("cr,dr->cd", low_g, low_g)
    turned = product("rs,cs->cr", left_root[0, 0], low_g)
    turned = product("dr,dc->cr", turned, right_root[0, 0])
    new_w = master_rows - MATRIX_RATE * (turned + WEIGHT_DECAY * master_rows)
    return (shaped(grad), new_left, new_right, shaped(new_w))


def adamw(weight, grad, first, second, step_rate):
    new_first = BETA_ONE * first + (1.0 - BETA_ONE) * grad
    new_second = BETA_TWO * second + (1.0 - BETA_TWO) * grad * grad
    moved = (
        new_first
        / (1.0 - BETA_ONE**STEP)
        / (jnp.sqrt(new_second / (1.0 - BETA_TWO**STEP)) + ADAM_EPSILON)
    )
    return (new_first, new_second, weight - step_rate * (moved + WEIGHT_DECAY * weight))


def layer_forward(
    local_ids,
    targets,
    valid,
    resets,
    emb_low,
    later_weights,
    inner_init,
    gains,
    gain_one,
    head_index,
):
    parts, slabs = lax.axis_size("head"), lax.axis_size("dp")
    vocab_part = emb_low.shape[0]
    tokens, size = targets.shape[0], gains.shape[1]
    chunks = tokens // ROWS
    columns = jnp.arange(vocab_part, dtype=jnp.int32)
    spread_ids = jnp.broadcast_to(local_ids[:, :, None], (slabs, tokens, 128))
    first = transit(
        "plain",
        "lookup",
        1,
        parts,
        slabs,
        emb_low,
        tokens,
        size,
        ids=spread_ids,
        gain=gain_one[None],
    )
    embedded, full_one, scale_one = first["own"], first["full"], first["scale"]
    full_one, w_qkv, w_out, w_gate, w_up, w_down, table = later_weights(full_one)
    mixed = jnp.dot(full_one, w_qkv, preferred_element_type=jnp.float32).astype(jnp.bfloat16)
    step_rate = jax.nn.sigmoid(gains[3:4]) / (8 * P_SIZE)
    masks = mixer_masks(resets, tokens)
    initial_pairs = pair_blocks(inner_init)
    causal, earlier, before, after, anew = masks
    inner = dict(
        qkv=mixed,
        rate=step_rate,
        initial=initial_pairs,
        causal=causal,
        earlier=earlier,
        first=before,
        last=after,
        anew=anew,
    )
    second = transit(
        "norm",
        "mixer",
        2,
        parts,
        slabs,
        w_out,
        tokens,
        size,
        mixer=inner,
        inputs=embedded,
        gain=gains[1:2],
    )
    inner_low = second["z"]
    inner = dict(
        inner,
        causal_turned=jnp.swapaxes(causal, 1, 2),
        earlier_turned=jnp.swapaxes(earlier, 1, 2),
        residue=second["residue"],
        states=second["states"],
    )
    hidden_one, full_two, scale_two = second["own"], second["full"], second["scale"]
    gate = jnp.einsum("td,fd->tf", full_two, w_gate, preferred_element_type=jnp.float32)
    up = jnp.einsum("td,fd->tf", full_two, w_up, preferred_element_type=jnp.float32)
    activated, act_pull = jax.vjp(lambda one, two: jax.nn.silu(one) * two, gate, up)
    act_low = activated.astype(jnp.bfloat16)
    third = transit(
        "norm",
        "rows",
        3,
        parts,
        slabs,
        w_down,
        tokens,
        size,
        left=act_low,
        inputs=hidden_one,
        gain=gains[2:3],
    )
    hidden_two, full_end, scale_end = third["own"], third["full"], third["scale"]
    local_targets = targets - head_index * vocab_part
    target_hits = columns[None, :] == local_targets[:, None]
    logits, stats = scores(
        full_end, table, jnp.broadcast_to(local_targets[:, None], (tokens, 128))
    )
    stats = share(7, stats[:, :, 0].reshape(-1, 128), ("head",)).reshape(parts, 3, tokens)
    highest = jnp.max(stats[:, 0], 0)
    exp_sum = jnp.sum(stats[:, 1] * jnp.exp(stats[:, 0] - highest[None]), 0)
    target_logit = jnp.sum(stats[:, 2], 0)
    totals = highest + jnp.log(exp_sum)
    counted = valid.astype(jnp.float32)
    d_logits = (
        (jnp.exp(logits - totals[:, None]) - target_hits.astype(jnp.float32)) * counted[:, None]
    ).astype(jnp.bfloat16)
    kept = (
        embedded,
        scale_one,
        full_one,
        inner,
        inner_low,
        hidden_one,
        scale_two,
        full_two,
        act_pull,
        act_low,
        hidden_two,
        scale_end,
        full_end,
        d_logits,
        local_ids,
    )
    weights = (w_qkv, w_out, w_gate, w_up, w_down, table)
    return (jnp.sum((totals - target_logit) * counted), jnp.sum(counted), kept, weights)


def slots_of(grad, order):
    parts = lax.axis_size("dp")
    shaped = grad.astype(jnp.bfloat16).reshape(parts, -1, grad.shape[1])
    return jnp.take(shaped, order, axis=0, mode="clip")


def column_slots_of(grad, order):
    parts = lax.axis_size("dp")
    shaped = grad.astype(jnp.bfloat16).reshape(grad.shape[0], parts, -1)
    return jnp.take(jnp.swapaxes(shaped, 0, 1), order, axis=0, mode="clip")


def scatter_dp(grad, dimension):
    return lax.psum_scatter(grad, "dp", scatter_dimension=dimension, tiled=True)


def rebanded(scale, band):
    rows = scale[:, 0].reshape(-1, 1, band)
    return jnp.broadcast_to(rows, (rows.shape[0], 8, band))


def layer_backward(kept, weights, gains, order):
    (
        embedded,
        scale_one,
        full_one,
        inner,
        inner_low,
        hidden_one,
        scale_two,
        full_two,
        act_pull,
        act_low,
        hidden_two,
        scale_end,
        full_end,
        d_logits,
        local_ids,
    ) = kept
    w_qkv, w_out, w_gate, w_up, w_down, table = weights
    parts, slabs = lax.axis_size("head"), lax.axis_size("dp")
    tokens, size = embedded.shape
    chunks = tokens // ROWS
    wide_kind = jnp.float32
    grad_table = jnp.einsum("tv,td->vd", d_logits, full_end, preferred_element_type=wide_kind)
    grad_table = grad_table.astype(jnp.bfloat16)
    owned_table = scatter_dp(grad_table, 1)
    d_logits, grad_table = lax.optimization_barrier((d_logits, grad_table))
    fourth = transit(
        "grad",
        "rows",
        4,
        parts,
        slabs,
        table,
        tokens,
        size,
        left=d_logits,
        inputs=hidden_two,
        gain=gains[2:3],
        scale=rebanded(scale_end, 2 * ROWS),
        band=2 * ROWS,
    )
    d_two, d_down_in = fourth["own"], fourth["full"]
    d_down_in, owned_table = lax.optimization_barrier((d_down_in, owned_table))
    d_act = jnp.einsum("td,fd->tf", d_down_in, w_down, preferred_element_type=wide_kind)
    d_gate, d_up = act_pull(d_act)
    d_gate, d_up = d_gate.astype(jnp.bfloat16), d_up.astype(jnp.bfloat16)
    grad_down = jnp.einsum("tf,td->fd", act_low, d_down_in, preferred_element_type=wide_kind)
    slot_down = column_slots_of(grad_down, order[3])
    grad_gate = jnp.einsum("tf,td->fd", d_gate, full_two, preferred_element_type=wide_kind)
    grad_up = jnp.einsum("tf,td->fd", d_up, full_two, preferred_element_type=wide_kind)
    slot_gate = column_slots_of(grad_gate, order[2])
    slot_up = column_slots_of(grad_up, order[2])
    d_gate, d_up, slot_down, slot_gate, slot_up = lax.optimization_barrier(
        (d_gate, d_up, slot_down, slot_gate, slot_up)
    )
    owned_down = scatter_dp(slot_down, 0)
    owned_gate = scatter_dp(slot_gate, 0)
    owned_up = scatter_dp(slot_up, 0)
    fifth = transit(
        "grad_add",
        "inner",
        5,
        parts,
        slabs,
        (w_gate, w_up),
        tokens,
        size,
        left=(d_gate, d_up),
        inputs=hidden_one,
        gain=gains[1:2],
        scale=scale_two,
        added=d_two,
        mixer=inner,
        project=w_out,
    )
    d_one, d_out_in, d_mixed = fifth["own"], fifth["full"], fifth["grad_mixed"]
    grad_init = head_blocks(fifth["grad_initial"])
    gate = jax.nn.sigmoid(gains[3])
    grad_rate = fifth["grad_rate"][0] * gate * (1.0 - gate) / (8 * P_SIZE)
    d_mixed, owned_down, owned_gate, owned_up = lax.optimization_barrier(
        (d_mixed, owned_down, owned_gate, owned_up)
    )
    grad_out = jnp.einsum("tc,td->cd", inner_low, d_out_in, preferred_element_type=wide_kind)
    grad_qkv = jnp.einsum("td,tc->dc", full_one, d_mixed, preferred_element_type=wide_kind)
    slot_out = column_slots_of(grad_out, order[1])
    slot_qkv = slots_of(grad_qkv, order[0])
    d_mixed, slot_out, slot_qkv = lax.optimization_barrier((d_mixed, slot_out, slot_qkv))
    owned_out = scatter_dp(slot_out, 0)
    owned_qkv = scatter_dp(slot_qkv, 0)
    owned_gu = jnp.concatenate([owned_gate, owned_up], 1)
    row_ids = jnp.moveaxis(local_ids.reshape(slabs, chunks // 2, 2, ROWS), 0, 2)
    row_ids = jnp.broadcast_to(
        row_ids.reshape(chunks // 2, 1, 2 * slabs * ROWS), (chunks // 2, 8, 2 * slabs * ROWS)
    )
    sixth = transit(
        "grad_add",
        "table",
        6,
        parts,
        slabs,
        w_qkv,
        tokens,
        size,
        left=d_mixed,
        inputs=embedded,
        gain=gains[0:1],
        scale=scale_one,
        added=d_one,
        ids=row_ids,
        entries=table.shape[0],
    )
    owned_table = owned_table.astype(wide_kind) + sixth["table_grad"]
    gain_rows = [sixth["gain_grad"][0], fifth["gain_grad"][0], fourth["gain_grad"][0], grad_rate]
    owned = tuple(
        piece.astype(wide_kind) for piece in (owned_qkv, owned_out, owned_gu, owned_down)
    )
    return owned + (owned_table,), grad_init, jnp.stack(gain_rows, 0)


def shards(
    token_ids,
    targets,
    valid,
    resets,
    owners,
    emb_master,
    emb_first,
    emb_second,
    qkv_master,
    qkv_left,
    qkv_right,
    qkv_left_root,
    qkv_right_root,
    out_master,
    out_left,
    out_right,
    out_left_root,
    out_right_root,
    gu_master,
    gu_left,
    gu_right,
    gu_left_root,
    gu_right_root,
    down_master,
    down_left,
    down_right,
    down_left_root,
    down_right_root,
    inner_init,
    inner_first,
    inner_second,
    gains,
    gains_first,
    gains_second,
):
    low = jnp.bfloat16
    dp_size, head_size = lax.axis_size("dp"), lax.axis_size("head")
    head_index = lax.axis_index("head")
    ids_rows = token_ids.astype(jnp.float32).reshape(-1, 128)
    gain_rows = jnp.pad(gains[0].reshape(-1, 128), ((0, 8 - gains.shape[1] // 128), (0, 0)))
    opening = share(8, jnp.concatenate([ids_rows, gain_rows], 0), ("dp", "head"))
    opening = opening.reshape(dp_size, head_size, -1, 128)
    local_ids = opening[:, 0, : ids_rows.shape[0]].reshape(dp_size, -1).astype(jnp.int32)
    local_ids = local_ids - head_index * emb_master.shape[0]
    gain_one = opening[0, :, ids_rows.shape[0] :].reshape(head_size, -1)
    gain_one = gain_one[:, : gains.shape[1]].reshape(-1)
    emb_low = emb_master.astype(low)

    def flat(array):
        return array.reshape(array.shape[1], -1)

    gu_rows = jnp.transpose(gu_master[0], (1, 2, 0)).reshape(-1, gu_master.shape[1])
    hidden = gu_master.shape[3]
    all_qkv = lax.all_gather(flat(qkv_master).astype(low), "dp", axis=0)
    all_out = lax.all_gather(out_master[0].astype(low), "dp", axis=0)
    all_gu = lax.all_gather(gu_rows.astype(low), "dp", axis=0)

    def columns_of(slabs, owner):
        taken = jnp.take(slabs, owner, axis=0, mode="clip")
        return jnp.swapaxes(taken, 0, 1).reshape(taken.shape[1], D)

    def later_weights(rows):
        rows, wait_qkv, wait_out, wait_gu, down_low, table_low = lax.optimization_barrier(
            (rows, all_qkv, all_out, all_gu, down_master[0].astype(low), emb_low)
        )
        w_qkv = jnp.take(wait_qkv, owners[0], axis=0, mode="clip").reshape(D, -1)
        all_down = lax.all_gather(down_low, "dp", axis=0)
        table = lax.all_gather(table_low, "dp", axis=1, tiled=True)
        w_gu = columns_of(wait_gu, owners[2])
        return (
            rows,
            w_qkv,
            columns_of(wait_out, owners[1]),
            w_gu[:hidden],
            w_gu[hidden:],
            columns_of(all_down, owners[3]),
            table,
        )

    loss_local, count_local, kept, weights = layer_forward(
        local_ids,
        targets,
        valid,
        resets,
        emb_low,
        later_weights,
        inner_init,
        gains,
        gain_one,
        head_index,
    )
    order = jnp.argsort(owners, axis=1)
    owned, grad_init, grad_gains = layer_backward(kept, weights, gains, order)
    init_rows = grad_init.size // 128
    numbers = jnp.zeros((8, 128), jnp.float32).at[0, 0].set(loss_local).at[0, 1].set(count_local)
    pieces = (grad_init.reshape(-1, 128), grad_gains.reshape(-1, 128), numbers)
    small = jnp.sum(share(9, jnp.concatenate(pieces, 0), ("dp",)), 0)
    loss_sum, count = small[-8, 0], small[-8, 1]
    small = (
        small[:init_rows].reshape(grad_init.shape),
        small[init_rows:-8].reshape(grad_gains.shape),
    )
    first_dp = (lax.axis_index("dp") == 0).astype(jnp.float32)
    squares = sum((jnp.sum(piece * piece) for piece in owned))
    squares = squares + first_dp * (jnp.sum(small[0] * small[0]) + jnp.sum(small[1] * small[1]))
    squares = share(10, jnp.broadcast_to(squares, (8, 128)), ("dp", "head"))
    squares_all = jnp.sum(squares[:, 0, 0])
    grad_norm = jnp.sqrt(squares_all) / count
    factor = jnp.minimum(1.0, CLIP_LIMIT / grad_norm) / count
    qkv_out = refresh(
        qkv_master, owned[0] * factor, qkv_left, qkv_right, qkv_left_root, qkv_right_root
    )
    out_out = refresh(
        out_master, owned[1] * factor, out_left, out_right, out_left_root, out_right_root
    )
    gu_out = refresh_rows(
        gu_master, owned[2][0] * factor, gu_left, gu_right, gu_left_root, gu_right_root
    )
    down_out = refresh(
        down_master, owned[3] * factor, down_left, down_right, down_left_root, down_right_root
    )
    table_out = adamw(emb_master, owned[4] * factor, emb_first, emb_second, TABLE_RATE)
    init_out = adamw(inner_init, small[0] * factor, inner_first, inner_second, INITIAL_RATE)
    gain_out = adamw(gains, small[1] * factor, gains_first, gains_second, GAINS_RATE)
    return (
        (jnp.stack([loss_sum, count]), grad_norm)
        + table_out
        + qkv_out
        + out_out
        + gu_out
        + down_out
        + init_out
        + gain_out
    )


def solution(mesh):
    placed = (
        P("dp"),
        P("dp"),
        P("dp"),
        P("dp"),
        P(),
        P("head", "dp"),
        P("head", "dp"),
        P("head", "dp"),
        P("dp", None, None, "head"),
        P("dp", "head", None, None),
        P("dp", "head", None, None),
        P("dp", "head", None, None),
        P("dp", "head", None, None),
        P("dp", "head", None),
        P("dp", "head", None, None),
        P("dp", "head", None, None),
        P("dp", "head", None, None),
        P("dp", "head", None, None),
        P("dp", None, None, "head"),
        P("dp", "head", None, None),
        P("dp", "head", None, None),
        P("dp", "head", None, None),
        P("dp", "head", None, None),
        P("dp", "head", None),
        P("dp", "head", None, None),
        P("dp", "head", None, None),
        P("dp", "head", None, None),
        P("dp", "head", None, None),
        P("head", None, None),
        P("head", None, None),
        P("head", None, None),
        P(None, "head"),
        P(None, "head"),
        P(None, "head"),
    )
    return jax.shard_map(
        shards,
        mesh=mesh,
        in_specs=placed,
        out_specs=(
            P(),
            P(),
            P("head", "dp"),
            P("head", "dp"),
            P("head", "dp"),
            P("dp", None, None, "head"),
            P("dp", "head", None, None),
            P("dp", "head", None, None),
            P("dp", None, None, "head"),
            P("dp", "head", None),
            P("dp", "head", None, None),
            P("dp", "head", None, None),
            P("dp", "head", None),
            P("dp", None, None, "head"),
            P("dp", "head", None, None),
            P("dp", "head", None, None),
            P("dp", None, None, "head"),
            P("dp", "head", None),
            P("dp", "head", None, None),
            P("dp", "head", None, None),
            P("dp", "head", None),
            P("head", None, None),
            P("head", None, None),
            P("head", None, None),
            P(None, "head"),
            P(None, "head"),
            P(None, "head"),
        ),
        check_vma=False,
    )
```
